32 devices in a mesh: rep: 16 (over z, x, core), shard: 2 (over y).
Axes of the slice: x: 2, y: 2, z: 4, core: 2. Of those that a mesh axis runs over, the one named last changes fastest.
Arguments:
- tokens: bfloat16 [7168, 1536], P(('rep', 'shard')), may hold values from -6 to 6
- norm_gain: bfloat16 [1536], P('shard'), may hold values from 0.5 to 1.5
- w_query: bfloat16 [1536, 1536], P('shard'), may hold values from -0.15625 to 0.15625
- key_weight: bfloat16 [1536, 512], P('shard'), may hold values from -0.15625 to 0.15625
- value_weight: bfloat16 [1536, 512], P('shard'), may hold values from -0.15625 to 0.15625
- w_out: bfloat16 [1536, 1536], P(None, 'shard'), may hold values from -1.25 to 1.25
- ffn_gain: bfloat16 [1536], P('shard'), may hold values from 0.5 to 1.5
- w_router: bfloat16 [1536, 16], P('shard'), may hold values from -0.1875 to 0.1875
- w_gate: bfloat16 [16, 1536, 512], P('shard'), may hold values from -0.15625 to 0.15625
- w_up: bfloat16 [16, 1536, 512], P('shard'), may hold values from -0.15625 to 0.15625
- w_down: bfloat16 [16, 512, 1536], P('shard'), may hold values from -0.5 to 0.5
- parents: int32 [16, 13], P('rep'), may hold values from 0 to 4, as said below
- routes: int32 [7168, 8], P(('rep', 'shard')), may hold values from 0 to 15, all different within a row; in each aligned block of 224 rows (0 to 223, 224 to 447, ...) at most 126 rows name the same one
- cotangent: bfloat16 [7168, 1536], P(('rep', 'shard')), may hold values from -6 to 6
Outputs:
- output: bfloat16 [7168, 1536], P(('rep', 'shard'))
- input_grad: bfloat16 [7168, 1536], P(('rep', 'shard'))
- grad_norm_gain: float32 [1536], P('shard')
- grad_query: float32 [1536, 1536], P('shard')
- grad_key: float32 [1536, 512], P('shard')
- grad_value: float32 [1536, 512], P('shard')
- grad_out: float32 [1536, 1536], P(None, 'shard')
- grad_ffn_gain: float32 [1536], P('shard')
- grad_router: float32 [1536, 16], P('shard')
- grad_gate: float32 [16, 1536, 512], P('shard', 'rep')
- grad_up: float32 [16, 1536, 512], P('shard', 'rep')
- grad_down: float32 [16, 512, 1536], P('shard', None, 'rep')
The draws below stay inside these ranges and needn't reach their ends.
Inputs may be any that keep to these rules, and one draw needn't show every extreme that they name: `parents`: segments 0 to 4 have parent 0 (the trunk is its own parent, 1 to 4 are branches); each of segments 5 to 12 (leaves) names a branch. `routes`: among the 224 tokens of one device no expert is named more than 126 times, a bound that some block reaches; a token names 8 different experts.
All inputs are finite; a program needn't handle non-finite values.
Results may differ from the reference program's by a relative error of at most 0.022.
Values may be sent and summed in bfloat16 or wider, within the bound.
No kernel may reach another device: no remote copies, remote signals or barrier semaphores. Data moves between devices by JAX's collectives and lax.ppermute only.
A program may use at most 384 MiB of HBM per device.

```python
import math
import jax
import jax.numpy as jnp
import numpy as np
from jax import lax

MODEL_DIM = 1536
QUERY_HEADS = 24
KEY_VALUE_HEADS = 8
HEAD_DIM = 64
FF = 512
TOP = 8
EXPERTS = 16
DEVICE_TOKENS = 224
CAP = 126
TREE_TOKENS = 448
TREES = 16
TOKENS = 7168
N_SHARD = 2


def draw_parents(key, part):
    key = jax.random.fold_in(key, 7)
    leaves = jax.random.randint(key, (TREES, 8), 1, 5).astype(jnp.int32)
    return jnp.concatenate([jnp.zeros((TREES, 5), jnp.int32), leaves], axis=1)


def levels(key, shape, pieces, smallest, high):
    def one(dim, parts):
        draws = jax.random.uniform(jax.random.fold_in(jax.random.fold_in(key, 6), dim), (parts,), jnp.float32, smallest / len(pieces), high / len(pieces))
        return jnp.repeat(jnp.exp(draws), shape[dim] // parts).reshape((-1,) + (1,) * (len(shape) - dim - 1))

    loudness = one(*pieces[0])
    for cut in pieces[1:]:
        loudness = loudness * one(*cut)
    return loudness


def deal_out(own_key, own, number, rows, count, top, limit, skew):
    order = jax.random.permutation(own_key, count)
    packed, usual = shares(count, rows * top, limit, skew, True), shares(count, rows * top, limit, skew, False)
    places = jnp.arange(count)

    def named(tallies, offset_by):
        used = int((tallies > 0).sum())
        fixed = max(1, used // 4)
        moved = fixed + (places - fixed + offset_by * (used - fixed)) % max(1, count - fixed)
        return jnp.zeros((count,), jnp.int32).at[order[jnp.where(places < fixed, places, moved)]].set(jnp.asarray(tallies, jnp.int32))

    tallies = jnp.where(number % 4 == 0, named(packed, number // 4), named(usual, number - number // 4 - 1))
    mixed = jax.random.permutation(jax.random.fold_in(own, 3), count)
    donor, receiver = mixed[0:count // 2 * 2:2], mixed[1:count // 2 * 2:2]
    margin = jnp.minimum(tallies[donor] - 1, limit - tallies[receiver]) // 2
    margin = jnp.where((donor == order[0]) | (receiver == order[0]) | (tallies[receiver] == 0), 0, jnp.maximum(margin, 0))
    moved = jax.random.randint(jax.random.fold_in(own, 4), (count // 2,), 0, 1 << 20) % (margin + 1)
    tallies = tallies.at[donor].add(-moved).at[receiver].add(moved)
    items = jnp.searchsorted(jnp.cumsum(tallies), jnp.arange(rows * top), side="right").astype(jnp.int32)
    listing = items.reshape(top, rows).T
    listing = listing[jax.random.permutation(jax.random.fold_in(own, 1), rows)]
    offset_by = jax.random.randint(jax.random.fold_in(own, 2), (rows, 1), 0, top)
    return jnp.take_along_axis(listing, (jnp.arange(top)[None, :] + offset_by) % top, axis=1)


def shares(count, total, most, skew, full):
    loads = [(1 << 20) // math.isqrt(grade ** skew) + 1 for grade in range(1, count + 1)]
    largest = most if full else min(most, max(-(-total // count), total * loads[0] // sum(loads)))
    least = 1 if total - largest >= count - 1 else 0
    counts, spare = [largest] + [least] * (count - 1), total - largest - least * (count - 1)
    while spare > 0:
        free = [i for i in range(1, count) if counts[i] < largest] or [i for i in range(1, count) if counts[i] < most]
        pool, left = sum([loads[i] for i in free]), spare
        for i in free:
            more = min(most - counts[i], max(1, left * loads[i] // pool), spare)
            counts[i] = counts[i] + more
            spare = spare - more
    return np.array(counts)


def centred(key, shape, width, limit, split=(), kind=jnp.bfloat16):
    level = levels(key, shape, split, -0.22, 0.18) if split else 1.0
    drawn = jax.random.normal(key, shape, jnp.float32) * width * level
    return jnp.minimum(jnp.maximum(drawn, -limit), limit).astype(kind)


def setup_inputs(seed: int = 0) -> dict:
    seeds = jax.random.split(jax.random.key(seed), 15)
    tokens = centred(seeds[0], (TOKENS, MODEL_DIM), 1.0, 6.0, ((0, 32),))
    norm_gain = jnp.clip(1.0 + 0.1 * jax.random.normal(seeds[1], (MODEL_DIM,), jnp.float32), 0.5, 1.5).astype(jnp.bfloat16)
    w_query = centred(seeds[2], (MODEL_DIM, QUERY_HEADS * HEAD_DIM), MODEL_DIM ** -0.5, 0.15625, ((0, 2),))
    key_weight = centred(seeds[3], (MODEL_DIM, KEY_VALUE_HEADS * HEAD_DIM), MODEL_DIM ** -0.5, 0.15625, ((0, 2),))
    value_weight = centred(seeds[4], (MODEL_DIM, KEY_VALUE_HEADS * HEAD_DIM), MODEL_DIM ** -0.5, 0.15625, ((0, 2),))
    w_out = centred(seeds[5], (QUERY_HEADS * HEAD_DIM, MODEL_DIM), (max(QUERY_HEADS * HEAD_DIM // 64, 1)) ** -0.5, 1.25, ((1, 2),))
    ffn_gain = jnp.clip(1.0 + 0.1 * jax.random.normal(seeds[6], (MODEL_DIM,), jnp.float32), 0.5, 1.5).astype(jnp.bfloat16)
    w_router = centred(seeds[7], (MODEL_DIM, EXPERTS), (0.5 * MODEL_DIM ** -0.5), 0.1875, ((0, 2),))
    w_gate = centred(seeds[8], (EXPERTS, MODEL_DIM, FF), MODEL_DIM ** -0.5, 0.15625, ((0, 2),))
    w_up = centred(seeds[9], (EXPERTS, MODEL_DIM, FF), MODEL_DIM ** -0.5, 0.15625, ((0, 2),))
    w_down = centred(seeds[10], (EXPERTS, FF, MODEL_DIM), (FF // 4) ** -0.5, 0.5, ((0, 2),))
    parents = draw_parents(jax.random.fold_in(seeds[14], 71), 0)
    routes_keys = jax.random.split(jax.random.fold_in(seeds[12], 1), TOKENS // DEVICE_TOKENS)
    routes_turns = jax.random.permutation(jax.random.fold_in(seeds[12], 3), TOKENS // DEVICE_TOKENS)
    routes = jax.vmap(lambda own, number: deal_out(jax.random.fold_in(seeds[12], 2), own, number, DEVICE_TOKENS, EXPERTS, TOP, CAP, 1))(routes_keys, routes_turns).reshape((TOKENS, TOP))
    cotangent = centred(seeds[13], (TOKENS, MODEL_DIM), 1.0, 6.0, ((0, 32),))
    return dict(tokens=tokens, norm_gain=norm_gain, w_query=w_query, key_weight=key_weight, value_weight=value_weight, w_out=w_out, ffn_gain=ffn_gain, w_router=w_router, w_gate=w_gate, w_up=w_up, w_down=w_down, parents=parents, routes=routes, cotangent=cotangent)


EPS = 1e-06

@jax.custom_vjp
def reduced_cast(v):
    return lax.optimization_barrier(v.astype(jnp.bfloat16)).astype(jnp.float32)

@jax.custom_vjp
def reduced_cast_back(v):
    return v

def low_keep(v):
    return (reduced_cast(v), None)

def low_pass(kept, grad):
    return (grad,)

def back_keep(v):
    return (v, None)

def back_low(kept, grad):
    return (reduced_cast(grad),)
reduced_cast.defvjp(low_keep, low_pass)
reduced_cast_back.defvjp(back_keep, back_low)

def exact_product(form, left, right):
    return jnp.einsum(form, left, right, precision=lax.Precision.HIGHEST)

def tree_layout(position, seg_len):
    trunk_len = 4 * seg_len
    beyond = position - trunk_len
    segment = jnp.where(position < trunk_len, 0, 1 + beyond // seg_len).astype(jnp.int32)
    inner = jnp.where(segment <= 4, trunk_len + beyond % seg_len, trunk_len + seg_len + beyond % seg_len)
    depth_position = jnp.where(position < trunk_len, position, inner).astype(jnp.int32)
    return (segment, depth_position)

def lookup(segment, parents_row):
    labels = jnp.arange(parents_row.shape[0], dtype=jnp.int32)
    picked = jnp.where(segment[:, None] == labels[None, :], parents_row[None, :], 0)
    return lax.optimization_barrier(jnp.sum(picked, axis=1)).astype(jnp.int32)

def tree_mask(query_index, key_index, parents_row, seg_len):
    query_seg, unused_depth = tree_layout(query_index, seg_len)
    key_seg, other_depth = tree_layout(key_index, seg_len)
    parent_one = lookup(query_seg, parents_row)
    parent_two = lookup(parent_one, parents_row)
    key_row = key_seg[None, :]
    related = (key_row == query_seg[:, None]) | (key_row == parent_one[:, None]) | (key_row == parent_two[:, None])
    return related & (key_index[None, :] <= query_index[:, None])

def apply_rotary(values, depth_position):
    half_dim = values.shape[-1] // 2
    frequency = 10000.0 ** (-2.0 * jnp.arange(half_dim, dtype=jnp.float32) / (2 * half_dim))
    angles = depth_position.astype(jnp.float32)[:, None] * frequency[None, :]
    cosine = jnp.cos(angles)[:, None, :]
    sine_part = jnp.sin(angles)[:, None, :]
    first_half = values[..., :half_dim]
    second_half = values[..., half_dim:]
    return jnp.concatenate([first_half * cosine - second_half * sine_part, second_half * cosine + first_half * sine_part], axis=-1)

def slot_targets(flat_routes):
    expert_hot = (flat_routes[:, None] == jnp.arange(EXPERTS, dtype=jnp.int32)[None, :]).astype(jnp.int32)
    rank_before = jnp.cumsum(expert_hot, axis=0) - expert_hot
    slot_index = lax.optimization_barrier(jnp.sum(rank_before * expert_hot, axis=1))
    return (flat_routes * CAP + slot_index).astype(jnp.int32)

def layer_forward(inputs, gain_one, query_w, key_w, value_weight_cast, out_w, gain_two, router_w, gate_w, up_w, down_w, parents_row, route_rows):
    seg_len = TREE_TOKENS // 16
    score_scale = HEAD_DIM ** (-0.5)
    positions = jnp.arange(TREE_TOKENS, dtype=jnp.int32)
    segment_ids, depth_position = tree_layout(positions, seg_len)
    inv_one = lax.rsqrt(lax.optimization_barrier(jnp.mean(inputs * inputs, axis=-1, keepdims=True)) + EPS)
    hidden_first = reduced_cast(inputs * inv_one * gain_one)
    query_raw = reduced_cast_back(exact_product('sw,wg->sg', hidden_first, query_w))
    key_unrotated = reduced_cast_back(exact_product('sw,wg->sg', hidden_first, key_w))
    value_every_head = reduced_cast(reduced_cast_back(exact_product('sw,wg->sg', hidden_first, value_weight_cast))).reshape(TREE_TOKENS, KEY_VALUE_HEADS, HEAD_DIM)
    query_rotated = reduced_cast(apply_rotary(query_raw.reshape(TREE_TOKENS, QUERY_HEADS, HEAD_DIM), depth_position))
    key_rotated = reduced_cast(apply_rotary(key_unrotated.reshape(TREE_TOKENS, KEY_VALUE_HEADS, HEAD_DIM), depth_position))
    query_tiles = query_rotated.reshape(TREE_TOKENS // DEVICE_TOKENS, DEVICE_TOKENS, KEY_VALUE_HEADS, QUERY_HEADS // KEY_VALUE_HEADS, HEAD_DIM)
    offsets = jnp.arange(TREE_TOKENS // DEVICE_TOKENS, dtype=jnp.int32) * DEVICE_TOKENS

    def attend_block(operands):
        query_part, offset = operands
        visible = tree_mask(offset + jnp.arange(DEVICE_TOKENS, dtype=jnp.int32), positions, parents_row, seg_len)
        raw_scores = exact_product('qhgd,khd->hgqk', query_part, key_rotated)
        scores = reduced_cast_back(raw_scores) * score_scale
        scores = jnp.where(visible[None, None], scores, -1e+30)
        row_peak = lax.optimization_barrier(jnp.max(scores, axis=-1, keepdims=True))
        exp_scores = jnp.exp(scores - row_peak)
        weights_row = exp_scores / lax.optimization_barrier(jnp.sum(exp_scores, axis=-1, keepdims=True))
        return exact_product('hgqk,khd->qhgd', reduced_cast(weights_row), value_every_head)
    attended = lax.map(jax.checkpoint(attend_block), (query_tiles, offsets))
    mixed_heads = reduced_cast(reduced_cast_back(attended.reshape(TREE_TOKENS, QUERY_HEADS * HEAD_DIM)))
    branch = reduced_cast_back(exact_product('te,ed->td', mixed_heads, out_w))
    middle = inputs + branch
    inv_two = lax.rsqrt(lax.optimization_barrier(jnp.mean(middle * middle, axis=-1, keepdims=True)) + EPS)
    hidden_two = reduced_cast(middle * inv_two * gain_two)
    logits = reduced_cast_back(exact_product('sw,wg->sg', hidden_two, router_w))
    chosen = jnp.take_along_axis(logits, route_rows, axis=1)
    gates = jax.nn.softmax(chosen, axis=-1)
    destination = jax.vmap(slot_targets)(route_rows.reshape(N_SHARD, DEVICE_TOKENS * TOP))
    source = jnp.arange(DEVICE_TOKENS * TOP, dtype=jnp.int32) // TOP
    hidden_blocks = hidden_two.reshape(N_SHARD, DEVICE_TOKENS, MODEL_DIM)

    def fill_slots(hidden_block, targets):
        return jnp.zeros((EXPERTS * CAP, MODEL_DIM), jnp.float32).at[targets].set(hidden_block[source])
    buffer = jax.vmap(fill_slots)(hidden_blocks, destination).reshape(N_SHARD, EXPERTS, CAP, MODEL_DIM)
    gate_pre = reduced_cast_back(exact_product('secd,edf->secf', buffer, gate_w))
    up_pre = reduced_cast_back(exact_product('secd,edf->secf', buffer, up_w))
    hidden_mid = reduced_cast(jax.nn.silu(gate_pre) * up_pre)
    expert_out = reduced_cast_back(exact_product('secf,efd->secd', hidden_mid, down_w)).reshape(N_SHARD, EXPERTS * CAP, MODEL_DIM)
    paired = jax.vmap(lambda outs_block, targets: outs_block[targets])(expert_out, destination).reshape(TREE_TOKENS, TOP, MODEL_DIM)
    mixture = lax.optimization_barrier(jnp.sum(gates[..., None] * paired, axis=1))
    return middle + mixture

def reference(tokens, norm_gain, w_query, key_weight, value_weight, w_out, ffn_gain, w_router, w_gate, w_up, w_down, parents, routes, cotangent):
    weights = (norm_gain.astype(jnp.float32), w_query.astype(jnp.float32), key_weight.astype(jnp.float32), value_weight.astype(jnp.float32), w_out.astype(jnp.float32), ffn_gain.astype(jnp.float32), w_router.astype(jnp.float32), w_gate.astype(jnp.float32), w_up.astype(jnp.float32), w_down.astype(jnp.float32))
    tree_inputs = tokens.astype(jnp.float32).reshape(TREES, TREE_TOKENS, MODEL_DIM)
    tree_cot = cotangent.astype(jnp.float32).reshape(TREES, TREE_TOKENS, MODEL_DIM)
    tree_routes = routes.reshape(TREES, TREE_TOKENS, TOP)

    def tree_step(carried, tree_items):
        inputs, cot_tree, route_rows, parents_row = tree_items

        def wrapped(inputs_arg, *weight_args):
            return layer_forward(inputs_arg, *weight_args, parents_row, route_rows)
        output_tree, pullback = jax.vjp(wrapped, inputs, *weights)
        gradients = pullback(cot_tree)
        carried = tuple((total_part + grad_part for total_part, grad_part in zip(carried, gradients[1:])))
        return (carried, (output_tree, gradients[0]))
    initial = tuple((jnp.zeros_like(weight) for weight in weights))
    totals, (outputs, input_grads) = lax.scan(tree_step, initial, (tree_inputs, tree_cot, tree_routes, parents))
    return (outputs.reshape(TOKENS, MODEL_DIM).astype(jnp.bfloat16), input_grads.reshape(TOKENS, MODEL_DIM).astype(jnp.bfloat16), totals[0], totals[1], totals[2], totals[3], totals[4], totals[5], totals[6], totals[7], totals[8], totals[9])
```

```python
import jax
import jax.numpy as jnp
from jax import lax
from jax.sharding import PartitionSpec as P

HEAD_DIM = 64
EPS = 1e-06
BF = jnp.bfloat16
F32 = jnp.float32


def tree_layout(position, seg_len):
    trunk_len = 4 * seg_len
    beyond = position - trunk_len
    segment = jnp.where(position < trunk_len, 0, 1 + beyond // seg_len)
    inner = jnp.where(
        segment <= 4, trunk_len + beyond % seg_len, trunk_len + seg_len + beyond % seg_len
    )
    depth_position = jnp.where(position < trunk_len, position, inner)
    return (segment, depth_position)


def lookup(segment, parents_row):
    labels = jnp.arange(parents_row.shape[0], dtype=jnp.int32)
    picked = jnp.where(segment[:, None] == labels[None, :], parents_row[None, :], 0)
    return jnp.sum(picked, axis=1)


def tree_mask(query_index, key_index, parents_row, seg_len):
    query_seg, _ = tree_layout(query_index, seg_len)
    key_seg, _ = tree_layout(key_index, seg_len)
    parent_one = lookup(query_seg, parents_row)
    parent_two = lookup(parent_one, parents_row)
    key_row = key_seg[None, :]
    related = (
        (key_row == query_seg[:, None])
        | (key_row == parent_one[:, None])
        | (key_row == parent_two[:, None])
    )
    return related & (key_index[None, :] <= query_index[:, None])


def angle_tables(depth_position, half_dim):
    frequency = 10000.0 ** (-2.0 * jnp.arange(half_dim, dtype=F32) / (2 * half_dim))
    angles = depth_position.astype(F32)[:, None] * frequency[None, :]
    return (jnp.cos(angles)[:, None, :], jnp.sin(angles)[:, None, :])


def rotate(values, tables, sign):
    cosine, sine = tables
    half = values.shape[-1] // 2
    first = values[..., :half]
    second = values[..., half:]
    return jnp.concatenate(
        [first * cosine - sign * second * sine, second * cosine + sign * first * sine], axis=-1
    )


def dot(a, b, dims):
    return lax.dot_general(a, b, (dims, ((), ())), preferred_element_type=F32)


def nn(a, b):
    return dot(a, b, ((1,), (0,)))


def nt(a, b):
    return dot(a, b, ((1,), (1,)))


def tn(a, b):
    return dot(a, b, ((0,), (0,)))


class Mesh:
    def __init__(self):
        self.groups = lax.axis_size("shard")
        self.member = lax.axis_index("shard")
        self.reps = lax.axis_size("rep")
        self.rep = lax.axis_index("rep")
        self.core = self.rep % 2
        self.chip = self.rep // 2
        self.chips = self.reps // 2
        rows = self.chips // 2
        order = [2 * z for z in range(rows)] + [2 * z + 1 for z in range(rows - 1, -1, -1)]
        self.ring = []
        for place, chip in enumerate(order):
            after, before = order[(place + 1) % self.chips], order[place - 1]
            self.ring += [(2 * chip, 2 * after), (2 * chip + 1, 2 * before + 1)]
        self.place = jnp.where(
            self.chip % 2 == 0, self.chip // 2, self.chips - 1 - self.chip // 2
        )
        self.way = 1 - 2 * self.core

    def chip_at(self, place):
        place = place % self.chips
        rows = self.chips // 2
        return jnp.where(place < rows, 2 * place, 2 * (self.chips - 1 - place) + 1)

    def swap_shard(self, v):
        return lax.ppermute(v, "shard", [(0, 1), (1, 0)])

    def swap_core(self, v):
        return lax.ppermute(v, "rep", [(r, r ^ 1) for r in range(self.reps)])

    def along_ring(self, v):
        return lax.ppermute(v, "rep", self.ring)

    def part(self, v, axis, which):
        size = v.shape[axis] // self.groups
        return lax.dynamic_slice_in_dim(v, which * size, size, axis)

    def gather(self, v, axis):
        if self.groups != 2:
            return lax.all_gather(v, "shard", axis=axis, tiled=True)
        other = self.swap_shard(v)
        return self.in_order(self.member, v, other, axis)

    def in_order(self, which, mine, other, axis):
        return jnp.where(
            which == 0,
            jnp.concatenate([mine, other], axis),
            jnp.concatenate([other, mine], axis),
        )

    def exchange(self, v, split_axis, concat_axis):
        if self.groups != 2:
            return lax.all_to_all(v, "shard", split_axis, concat_axis, tiled=True)
        other = self.swap_shard(self.part(v, split_axis, 1 - self.member))
        mine = self.part(v, split_axis, self.member)
        return self.in_order(self.member, mine, other, concat_axis)

    def scatter(self, v, axis):
        if self.groups != 2:
            return lax.psum_scatter(
                v.astype(BF), "shard", scatter_dimension=axis, tiled=True
            ).astype(F32)
        other = self.swap_shard(self.part(v, axis, 1 - self.member).astype(BF))
        return self.part(v, axis, self.member).astype(F32) + other.astype(F32)

    def total(self, v):
        if self.groups != 2:
            return lax.psum(v, "shard")
        return v + self.swap_shard(v)

    def ring_scatter(self, own):
        held = own(self.chip_at(self.place - self.way))
        for step in range(self.chips - 1):
            came = self.along_ring(held)
            mine = own(self.chip_at(self.place - self.way * (step + 2)))
            held = (came.astype(F32) + mine.astype(F32)).astype(BF)
        return held

    def ring_gather(self, held, axis):
        size = held.shape[axis]
        shape = list(held.shape)
        shape[axis] = size * self.chips
        whole = jnp.zeros(shape, held.dtype)
        whole = lax.dynamic_update_slice_in_dim(
            whole, held, self.chip_at(self.place) * size, axis
        )
        for step in range(self.chips - 1):
            held = self.along_ring(held)
            at = self.chip_at(self.place - self.way * (step + 1)) * size
            whole = lax.dynamic_update_slice_in_dim(whole, held, at, axis)
        return whole

    def all_reduce(self, v):
        half = v.shape[0] // 2
        v = v.astype(BF)
        mine = lax.dynamic_slice_in_dim(v, self.core * half, half, 0)
        other = self.swap_core(
            lax.dynamic_slice_in_dim(v, (1 - self.core) * half, half, 0)
        )
        both = (mine.astype(F32) + other.astype(F32)).astype(BF)
        chunk = half // self.chips
        held = self.ring_scatter(
            lambda chip: lax.dynamic_slice_in_dim(both, chip * chunk, chunk, 0)
        )
        whole = self.ring_gather(held, 0)
        return self.in_order(self.core, whole, self.swap_core(whole), 0).astype(F32)

    def butterfly(self, v):
        bit = 1
        while bit < self.reps:
            v = v + lax.ppermute(v, "rep", [(r, r ^ bit) for r in range(self.reps)])
            bit *= 2
        return v


def local(
    tokens,
    norm_gain,
    w_query,
    key_weight,
    value_weight,
    w_out,
    ffn_gain,
    w_router,
    w_gate,
    w_up,
    w_down,
    parents,
    routes,
    cotangent,
):
    me = Mesh()
    tok_rows, width = tokens.shape
    tree_len = tok_rows * me.groups
    seg_len = tree_len // 16
    columns = width // me.groups
    q_heads = w_query.shape[1] // HEAD_DIM // me.groups
    kv_heads = key_weight.shape[1] // HEAD_DIM // me.groups
    per_key = q_heads // kv_heads
    experts = w_gate.shape[0] * me.groups
    per_core = w_gate.shape[0] // 2
    hidden = w_gate.shape[2]
    scale = HEAD_DIM ** (-0.5)
    q_width, k_width = q_heads * HEAD_DIM, kv_heads * HEAD_DIM

    own_rows = tokens.astype(F32)
    inv_rows = lax.rsqrt(jnp.mean(own_rows * own_rows, axis=-1, keepdims=True) + EPS)
    inputs = me.exchange(tokens, 1, 0).astype(F32)
    inv_one = me.gather(inv_rows, 0)
    normed_one = inputs * inv_one
    gain_one = norm_gain.astype(F32)
    hidden_first = (normed_one * gain_one).astype(BF)
    raw_q = me.scatter(nn(hidden_first, w_query), 1)
    raw_k = me.scatter(nn(hidden_first, key_weight), 1)
    value_low = me.scatter(nn(hidden_first, value_weight), 1).astype(BF)

    route_hot = jnp.any(
        routes[:, :, None] == jnp.arange(experts, dtype=jnp.int32)[None, None, :], axis=1
    ).astype(F32)
    routed = me.gather(route_hot, 0)
    gain_two = ffn_gain.astype(F32)
    gain_two_full = me.gather(ffn_gain, 0).astype(F32)
    router_full = me.gather(w_router, 0)
    grad_tree = me.gather(cotangent, 0)
    grad_all = jnp.concatenate([grad_tree, me.swap_core(grad_tree)], 0)
    routed_other = me.swap_core(routed)

    index = jnp.arange(tree_len, dtype=jnp.int32)
    _, depth = tree_layout(index, seg_len)
    tables = angle_tables(depth, HEAD_DIM // 2)
    visible = tree_mask(index, index, parents[0], seg_len)

    def heads(v):
        return v.reshape(tree_len, -1, HEAD_DIM)

    query_rot = rotate(heads(raw_q), tables, 1.0).astype(BF)
    key_rot = rotate(heads(raw_k), tables, 1.0).astype(BF)
    query_h = query_rot.reshape(tree_len, kv_heads, per_key, HEAD_DIM).transpose(1, 2, 0, 3)
    key_h = key_rot.transpose(1, 0, 2)
    value_h = heads(value_low).transpose(1, 0, 2)

    def scores_of(q, k):
        s = jnp.einsum("gqd,kd->gqk", q, k, preferred_element_type=F32) * scale
        return jnp.where(visible[None], s, -1e30)

    def head_forward(operands):
        q, k, v = operands
        s = scores_of(q, k)
        peak = jnp.max(s, axis=-1, keepdims=True)
        e = jnp.exp(s - peak)
        total = jnp.sum(e, axis=-1, keepdims=True)
        probs = (e / total).astype(BF)
        return (
            jnp.einsum("gqk,kd->gqd", probs, v, preferred_element_type=F32),
            peak + jnp.log(total),
        )

    attended_h, log_total = lax.map(head_forward, (query_h, key_h, value_h))
    attended = attended_h.transpose(2, 0, 1, 3).reshape(tree_len, q_width).astype(BF)
    attended_full = me.gather(attended, 1)
    middle = inputs + nn(attended_full, w_out)
    squares = me.total(jnp.sum(middle * middle, axis=-1, keepdims=True))
    inv_two = lax.rsqrt(squares / width + EPS)
    normed_two = middle * inv_two
    hidden_own = (normed_two * gain_two).astype(BF)
    hidden_tree = me.gather(hidden_own, 1)
    hidden_all = jnp.concatenate([hidden_tree, me.swap_core(hidden_tree)], 0)

    def gates_of(h, on):
        logits = nn(h, router_full)
        logits = jnp.where(on > 0, logits, -1e30)
        peak = jnp.max(logits, axis=-1, keepdims=True)
        e = jnp.exp(logits - peak) * on
        return e / jnp.sum(e, axis=-1, keepdims=True)

    gates_all = gates_of(hidden_all, jnp.concatenate([routed, routed_other], 0))
    gates = gates_all[:tree_len]

    mixed = jnp.zeros((2 * tree_len, width), F32)
    grad_hidden = jnp.zeros((2 * tree_len, width), F32)
    grad_gate_columns = []
    sums = []
    for j in range(per_core):
        which = me.core * per_core + j
        gate_w = lax.dynamic_index_in_dim(w_gate, which, 0, keepdims=False)
        up_w = lax.dynamic_index_in_dim(w_up, which, 0, keepdims=False)
        down_w = lax.dynamic_index_in_dim(w_down, which, 0, keepdims=False)
        gate = lax.dynamic_slice_in_dim(
            gates_all, me.member * (2 * per_core) + which, 1, 1
        )
        gate_pre = nn(hidden_all, gate_w)
        up_pre = nn(hidden_all, up_w)
        grad_mid = nt(grad_all, down_w)
        sig = jax.nn.sigmoid(gate_pre)
        silu = gate_pre * sig
        mid = silu * up_pre
        grad_gate_columns.append(jnp.sum(grad_mid * mid, axis=-1, keepdims=True))
        act = (gate * mid).astype(BF)
        mixed = mixed + nn(act, down_w)
        grad_mid = gate * grad_mid
        grad_gate_pre = (grad_mid * up_pre * sig * (1.0 + gate_pre * (1.0 - sig))).astype(BF)
        grad_up_pre = (grad_mid * silu).astype(BF)
        grad_hidden = grad_hidden + nt(grad_gate_pre, gate_w) + nt(grad_up_pre, up_w)
        own = jnp.stack(
            [
                tn(hidden_all, grad_gate_pre).astype(BF),
                tn(hidden_all, grad_up_pre).astype(BF),
                tn(grad_all, act).astype(BF),
            ]
        )
        chunk = width // me.chips
        sums.append(
            me.ring_scatter(
                lambda chip, own=own: lax.dynamic_slice_in_dim(own, chip * chunk, chunk, 1)
            )
        )

    def over_cores(v):
        return v[:tree_len] + me.swap_core(v[tree_len:].astype(BF)).astype(F32)

    mixed = over_cores(mixed)
    grad_hidden = over_cores(grad_hidden)
    placed = lax.dynamic_update_slice_in_dim(
        jnp.zeros((tree_len, width), F32), middle, me.member * columns, 1
    )
    result = me.scatter(mixed + placed, 0).astype(BF)

    own_columns = jnp.concatenate(grad_gate_columns, 1)
    both = me.in_order(
        me.core, own_columns[:tree_len], me.swap_core(own_columns[tree_len:]), 1
    )
    grad_gates = me.gather(both, 1)
    grad_logits = (
        gates * (grad_gates - jnp.sum(gates * grad_gates, axis=-1, keepdims=True))
    ).astype(BF)
    grad_router = tn(hidden_own, grad_logits)
    grad_hidden_two = nt(grad_logits, w_router) + me.scatter(grad_hidden, 1)
    grad_gain_two = jnp.sum(grad_hidden_two * normed_two, axis=0)
    scaled = grad_hidden_two * gain_two
    mean = me.total(jnp.sum(scaled * normed_two, axis=-1, keepdims=True)) / width
    grad_own = me.part(grad_tree, 1, me.member).astype(F32)
    grad_middle = grad_own + inv_two * (scaled - normed_two * mean)
    grad_branch = grad_middle.astype(BF)
    grad_out = me.all_reduce(tn(attended_full, grad_branch))
    grad_attended = me.scatter(nt(grad_branch, w_out), 1).astype(BF)

    grad_h = grad_attended.reshape(tree_len, kv_heads, per_key, HEAD_DIM).transpose(1, 2, 0, 3)

    def head_backward(operands):
        q, k, v, g, log_one = operands
        probs = jnp.exp(scores_of(q, k) - log_one)
        probs_low = probs.astype(BF)
        grad_probs = jnp.einsum("gqd,kd->gqk", g, v, preferred_element_type=F32)
        grad_v = jnp.einsum("gqk,gqd->kd", probs_low, g, preferred_element_type=F32)
        delta = jnp.sum(probs * grad_probs, axis=-1, keepdims=True)
        grad_s = (probs * (grad_probs - delta) * scale).astype(BF)
        grad_q = jnp.einsum("gqk,kd->gqd", grad_s, k, preferred_element_type=F32)
        grad_k = jnp.einsum("gqk,gqd->kd", grad_s, q, preferred_element_type=F32)
        return (grad_q, grad_k, grad_v)

    grad_q, grad_k, grad_v = lax.map(head_backward, (query_h, key_h, value_h, grad_h, log_total))
    grad_q = grad_q.transpose(2, 0, 1, 3).reshape(tree_len, q_heads, HEAD_DIM)
    grad_q = rotate(grad_q, tables, -1.0).reshape(tree_len, q_width).astype(BF)
    grad_k = rotate(grad_k.transpose(1, 0, 2), tables, -1.0)
    grad_k = grad_k.reshape(tree_len, k_width).astype(BF)
    grad_v = grad_v.transpose(1, 0, 2).reshape(tree_len, k_width).astype(BF)
    grad_q_full = me.gather(grad_q, 1)
    grad_k_full = me.gather(grad_k, 1)
    grad_v_full = me.gather(grad_v, 1)
    grad_query = me.all_reduce(tn(hidden_first, grad_q_full))
    grad_key = me.all_reduce(tn(hidden_first, grad_k_full))
    grad_value = me.all_reduce(tn(hidden_first, grad_v_full))
    grad_hidden_one = (
        nt(grad_q_full, w_query) + nt(grad_k_full, key_weight) + nt(grad_v_full, value_weight)
    )
    grad_gain_one = jnp.sum(grad_hidden_one * normed_one, axis=0)
    scaled = grad_hidden_one * gain_one
    mean = me.total(jnp.sum(scaled * normed_one, axis=-1, keepdims=True)) / width
    input_grad = (grad_middle + inv_one * (scaled - normed_one * mean)).astype(BF)
    input_grad = me.exchange(input_grad, 0, 1)

    small = me.butterfly(
        jnp.concatenate([grad_gain_one[None], grad_gain_two[None], grad_router.T], 0)
    )

    stacked = jnp.stack(sums)
    half = width // me.reps
    mine = lax.dynamic_slice_in_dim(stacked, me.core * half, half, 2)
    other = me.swap_core(
        lax.dynamic_slice_in_dim(stacked, (1 - me.core) * half, half, 2)
    )
    ordered = me.in_order(me.core, mine, other, 0).astype(F32)

    return (
        result,
        input_grad,
        small[0],
        grad_query,
        grad_key,
        grad_value,
        grad_out,
        small[1],
        small[2:].T,
        ordered[:, 0],
        ordered[:, 1],
        ordered[:, 2].transpose(0, 2, 1),
    )


def solution(mesh):
    return jax.shard_map(
        local,
        mesh=mesh,
        in_specs=(
            P(("rep", "shard"), None),
            P("shard"),
            P("shard", None),
            P("shard", None),
            P("shard", None),
            P(None, "shard"),
            P("shard"),
            P("shard", None),
            P("shard", None, None),
            P("shard", None, None),
            P("shard", None, None),
            P("rep", None),
            P(("rep", "shard"), None),
            P(("rep", "shard"), None),
        ),
        out_specs=(
            P(("rep", "shard"), None),
            P(("rep", "shard"), None),
            P("shard"),
            P("shard", None),
            P("shard", None),
            P("shard", None),
            P(None, "shard"),
            P("shard"),
            P("shard", None),
            P("shard", "rep", None),
            P("shard", "rep", None),
            P("shard", None, "rep"),
        ),
        check_vma=False,
    )
```

```python
import functools

import jax
import jax.numpy as jnp
from jax import lax
from jax.experimental import pallas as pl
from jax.experimental.pallas import tpu as pltpu
from jax.sharding import PartitionSpec as P

HEAD_DIM = 64
LANES = 128
EPS = 1e-06
BF = jnp.bfloat16
F32 = jnp.float32
VMEM_LIMIT = 60 << 20


def tree_layout(position, seg_len):
    trunk_len = 4 * seg_len
    beyond = position - trunk_len
    segment = jnp.where(position < trunk_len, 0, 1 + beyond // seg_len)
    inner = jnp.where(
        segment <= 4, trunk_len + beyond % seg_len, trunk_len + seg_len + beyond % seg_len
    )
    depth_position = jnp.where(position < trunk_len, position, inner)
    return (segment, depth_position)


def lookup(segment, parents_row):
    labels = jnp.arange(parents_row.shape[0], dtype=jnp.int32)
    picked = jnp.where(segment[:, None] == labels[None, :], parents_row[None, :], 0)
    return jnp.sum(picked, axis=1)


def tree_mask(query_index, key_index, parents_row, seg_len):
    query_seg, _ = tree_layout(query_index, seg_len)
    key_seg, _ = tree_layout(key_index, seg_len)
    parent_one = lookup(query_seg, parents_row)
    parent_two = lookup(parent_one, parents_row)
    key_row = key_seg[None, :]
    related = (
        (key_row == query_seg[:, None])
        | (key_row == parent_one[:, None])
        | (key_row == parent_two[:, None])
    )
    return related & (key_index[None, :] <= query_index[:, None])


def angle_tables(depth_position):
    half = HEAD_DIM // 2
    frequency = 10000.0 ** (-2.0 * jnp.arange(half, dtype=F32) / HEAD_DIM)
    angles = depth_position.astype(F32)[:, None] * frequency[None, :]
    cosine, sine = jnp.cos(angles), jnp.sin(angles)
    return (
        jnp.concatenate([cosine] * 4, 1),
        jnp.concatenate([-sine, sine, -sine, sine], 1),
    )


def dot(a, b, dims):
    return lax.dot_general(a, b, (dims, ((), ())), preferred_element_type=F32)


def nn(a, b):
    return dot(a, b, ((1,), (0,)))


def nt(a, b):
    return dot(a, b, ((1,), (1,)))


def tn(a, b):
    return dot(a, b, ((0,), (0,)))


class Mesh:
    def __init__(self):
        self.groups = lax.axis_size("shard")
        self.member = lax.axis_index("shard")
        self.reps = lax.axis_size("rep")
        self.rep = lax.axis_index("rep")
        self.core = self.rep % 2
        self.chip = self.rep // 2
        self.chips = self.reps // 2
        rows = self.chips // 2
        order = [2 * z for z in range(rows)] + [2 * z + 1 for z in range(rows - 1, -1, -1)]
        self.ring = []
        for place, chip in enumerate(order):
            after, before = order[(place + 1) % self.chips], order[place - 1]
            self.ring += [(2 * chip, 2 * after), (2 * chip + 1, 2 * before + 1)]
        self.place = jnp.where(
            self.chip % 2 == 0, self.chip // 2, self.chips - 1 - self.chip // 2
        )
        self.way = 1 - 2 * self.core

    def chip_at(self, place):
        place = place % self.chips
        rows = self.chips // 2
        return jnp.where(place < rows, 2 * place, 2 * (self.chips - 1 - place) + 1)

    def swap_shard(self, v):
        return lax.ppermute(v, "shard", [(0, 1), (1, 0)])

    def swap_core(self, v):
        return lax.ppermute(v, "rep", [(r, r ^ 1) for r in range(self.reps)])

    def along_ring(self, v):
        return lax.ppermute(v, "rep", self.ring)

    def part(self, v, axis, which):
        size = v.shape[axis] // self.groups
        return lax.dynamic_slice_in_dim(v, which * size, size, axis)

    def gather(self, v, axis):
        if self.groups != 2:
            return lax.all_gather(v, "shard", axis=axis, tiled=True)
        other = self.swap_shard(v)
        return self.in_order(self.member, v, other, axis)

    def in_order(self, which, mine, other, axis):
        return jnp.where(
            which == 0,
            jnp.concatenate([mine, other], axis),
            jnp.concatenate([other, mine], axis),
        )

    def exchange(self, v, split_axis, concat_axis):
        if self.groups != 2:
            return lax.all_to_all(v, "shard", split_axis, concat_axis, tiled=True)
        other = self.swap_shard(self.part(v, split_axis, 1 - self.member))
        mine = self.part(v, split_axis, self.member)
        return self.in_order(self.member, mine, other, concat_axis)

    def scatter(self, v, axis):
        if self.groups != 2:
            return lax.psum_scatter(
                v.astype(BF), "shard", scatter_dimension=axis, tiled=True
            ).astype(F32)
        other = self.swap_shard(self.part(v, axis, 1 - self.member).astype(BF))
        return self.part(v, axis, self.member).astype(F32) + other.astype(F32)

    def total(self, v):
        if self.groups != 2:
            return lax.psum(v, "shard")
        return v + self.swap_shard(v)

    def ring_scatter(self, own):
        held = own(self.chip_at(self.place - self.way))
        for step in range(self.chips - 1):
            came = self.along_ring(held)
            mine = own(self.chip_at(self.place - self.way * (step + 2)))
            held = (came.astype(F32) + mine.astype(F32)).astype(BF)
        return held

    def ring_gather(self, held, axis):
        size = held.shape[axis]
        shape = list(held.shape)
        shape[axis] = size * self.chips
        whole = jnp.zeros(shape, held.dtype)
        whole = lax.dynamic_update_slice_in_dim(
            whole, held, self.chip_at(self.place) * size, axis
        )
        for step in range(self.chips - 1):
            held = self.along_ring(held)
            at = self.chip_at(self.place - self.way * (step + 1)) * size
            whole = lax.dynamic_update_slice_in_dim(whole, held, at, axis)
        return whole

    def all_reduce(self, v):
        half = v.shape[0] // 2
        v = v.astype(BF)
        mine = lax.dynamic_slice_in_dim(v, self.core * half, half, 0)
        other = self.swap_core(
            lax.dynamic_slice_in_dim(v, (1 - self.core) * half, half, 0)
        )
        both = (mine.astype(F32) + other.astype(F32)).astype(BF)
        chunk = half // self.chips
        held = self.ring_scatter(
            lambda chip: lax.dynamic_slice_in_dim(both, chip * chunk, chunk, 0)
        )
        whole = self.ring_gather(held, 0)
        return self.in_order(self.core, whole, self.swap_core(whole), 0).astype(F32)

    def butterfly(self, v):
        bit = 1
        while bit < self.reps:
            v = v + lax.ppermute(v, "rep", [(r, r ^ bit) for r in range(self.reps)])
            bit *= 2
        return v


def pairs(heads):
    return -(-heads // 2)


def rope(v, cos, sin, back):
    lane = lax.broadcasted_iota(jnp.int32, (1, LANES), 1)
    first = lane % HEAD_DIM < HEAD_DIM // 2
    out = []
    for i in range(v.shape[1] // LANES):
        x = v[:, i * LANES : (i + 1) * LANES]
        other = jnp.where(
            first,
            pltpu.roll(x, LANES - HEAD_DIM // 2, 1),
            pltpu.roll(x, HEAD_DIM // 2, 1),
        )
        out.append(x * cos - other * sin if back else x * cos + other * sin)
    return out


def halves(x, parity):
    low = lax.broadcasted_iota(jnp.int32, (1, LANES), 1) < HEAD_DIM
    zero = jnp.zeros_like(x)
    turned = pltpu.roll(x, HEAD_DIM, 1)
    a, b = (x, turned) if parity == 0 else (turned, x)
    return jnp.where(low, a, zero).astype(BF), jnp.where(low, zero, b).astype(BF)


def attend_kernel(
    q_heads, kv_heads, own_ref, came_ref, cos_ref, sin_ref, bias_ref,
    out_ref, lse_ref, q_ref, k_ref, v_ref,
):
    per = q_heads // kv_heads
    rows = own_ref.shape[0]
    qp, kp = pairs(q_heads), pairs(kv_heads)
    cos, sin = cos_ref[...], sin_ref[...]
    raw = own_ref[...].astype(F32) + came_ref[...].astype(F32)
    scale = HEAD_DIM**-0.5
    q = [(t * scale).astype(BF) for t in rope(raw[:, : qp * LANES], cos, sin, False)]
    keys = rope(raw[:, qp * LANES : (qp + kp) * LANES], cos, sin, False)
    for i in range(qp):
        q_ref[:, i * LANES : (i + 1) * LANES] = q[i]
    ks, vs = [], []
    for g in range(kv_heads):
        at = (qp + kp + g // 2) * LANES
        ks.append(halves(keys[g // 2], g % 2))
        vs.append(halves(raw[:, at : at + LANES], g % 2))
        for p in range(2):
            k_ref[g, p] = ks[g][p]
            v_ref[g, p] = vs[g][p]
    half = rows // 2
    for lo, n in ((0, half), (half, rows)):
        bias = bias_ref[lo : lo + half, :n]
        for i in range(qp):
            out = jnp.zeros((half, LANES), F32)
            for h in range(2 * i, min(2 * i + 2, q_heads)):
                g, p = h // per, h % 2
                s = nt(q[i][lo : lo + half], ks[g][p][:n]) + bias
                peak = jnp.max(s, axis=-1, keepdims=True)
                e = jnp.exp(s - peak)
                total = jnp.sum(e, axis=-1, keepdims=True)
                lse_ref[lo : lo + half, h : h + 1] = peak + jnp.log(total)
                out = out + nn((e * (1.0 / total)).astype(BF), vs[g][p][:n])
            out_ref[lo : lo + half, i * LANES : (i + 1) * LANES] = out.astype(BF)


def attend(own, came, cos, sin, bias, q_heads, kv_heads):
    rows = own.shape[0]
    qp = pairs(q_heads)
    return pl.pallas_call(
        functools.partial(attend_kernel, q_heads, kv_heads),
        out_shape=[
            jax.ShapeDtypeStruct((rows, qp * LANES), BF),
            jax.ShapeDtypeStruct((rows, LANES), F32),
            jax.ShapeDtypeStruct((rows, qp * LANES), BF),
            jax.ShapeDtypeStruct((kv_heads, 2, rows, LANES), BF),
            jax.ShapeDtypeStruct((kv_heads, 2, rows, LANES), BF),
        ],
        compiler_params=pltpu.CompilerParams(vmem_limit_bytes=VMEM_LIMIT),
        cost_estimate=pl.CostEstimate(
            flops=1200 * rows * rows * q_heads,
            bytes_accessed=8 << 20,
            transcendentals=rows * rows * q_heads,
        ),
    )(own, came, cos, sin, bias)


def attend_back_kernel(
    q_heads, kv_heads, own_ref, came_ref, q_ref, k_ref, v_ref, lse_ref,
    cos_ref, sin_ref, bias_ref, out_ref,
):
    per = q_heads // kv_heads
    rows = own_ref.shape[0]
    qp, kp = pairs(q_heads), pairs(kv_heads)
    cos, sin = cos_ref[...], sin_ref[...]
    scale = HEAD_DIM**-0.5
    low = lax.broadcasted_iota(jnp.int32, (1, LANES), 1) < HEAD_DIM
    grad = (own_ref[...].astype(F32) + came_ref[...].astype(F32)).astype(BF)
    lse = lse_ref[...].T
    half = rows // 2

    def put(at, v):
        out_ref[:, at * LANES : (at + 1) * LANES] = v.astype(BF)

    def blocks():
        return [
            [[jnp.zeros((half, LANES), F32) for _ in range(2)] for _ in range(2)]
            for _ in range(kv_heads)
        ]

    dk, dv = blocks(), blocks()
    for i in range(qp):
        parts = []
        for lo, n in ((0, half), (half, rows)):
            q = q_ref[lo : lo + half, i * LANES : (i + 1) * LANES]
            go = grad[lo : lo + half, i * LANES : (i + 1) * LANES]
            bias = bias_ref[:n, lo : lo + half]
            dq = jnp.zeros((half, LANES), F32)
            for h in range(2 * i, min(2 * i + 2, q_heads)):
                g, p = h // per, h % 2
                k, v = k_ref[g, p, :n], v_ref[g, p, :n]
                s = nt(k, q) + bias
                probs = jnp.exp(s - lse[h : h + 1, lo : lo + half])
                dp = nt(v, go)
                delta = jnp.sum(probs * dp, axis=0, keepdims=True)
                ds = (probs * (dp - delta)).astype(BF)
                dq = dq + tn(ds, k)
                ck, cv = nn(ds, q), nn(probs.astype(BF), go)
                for b in range(n // half):
                    dk[g][p][b] = dk[g][p][b] + ck[b * half : (b + 1) * half]
                    dv[g][p][b] = dv[g][p][b] + cv[b * half : (b + 1) * half]
            parts.append(dq * scale)
        put(i, rope(jnp.concatenate(parts, 0), cos, sin, True)[0])

    def packed(d, j):
        got = jnp.zeros((rows, LANES), F32)
        for g in range(2 * j, min(2 * j + 2, kv_heads)):
            a, b = (jnp.concatenate(d[g][p], 0) for p in range(2))
            a, b = jnp.where(low, a, 0.0), jnp.where(low, 0.0, b)
            if g % 2 == 0:
                got = got + a + pltpu.roll(b, HEAD_DIM, 1)
            else:
                got = got + b + pltpu.roll(a, HEAD_DIM, 1)
        return got

    for j in range(kp):
        put(qp + j, rope(packed(dk, j), cos, sin, True)[0])
        put(qp + kp + j, packed(dv, j))


def attend_back(own, came, q, k, v, lse, cos, sin, bias, q_heads, kv_heads):
    rows = own.shape[0]
    lanes = (pairs(q_heads) + 2 * pairs(kv_heads)) * LANES
    return pl.pallas_call(
        functools.partial(attend_back_kernel, q_heads, kv_heads),
        out_shape=jax.ShapeDtypeStruct((rows, lanes), BF),
        compiler_params=pltpu.CompilerParams(vmem_limit_bytes=VMEM_LIMIT),
        cost_estimate=pl.CostEstimate(
            flops=1600 * rows * rows * q_heads,
            bytes_accessed=8 << 20,
            transcendentals=rows * rows * q_heads,
        ),
    )(own, came, q, k, v, lse, cos, sin, bias)


def expert_grads_kernel(
    chained, where, h_ref, g_ref, on_ref, wg_ref, wu_ref, wd_ref, *refs
):
    if chained:
        gg_in, refs = refs[0], refs[2:]
    mid_ref, gg_ref, own_ref, *acc = refs
    step, steps = pl.program_id(0), pl.num_programs(0)
    h, g = h_ref[...], g_ref[...]
    lane = lax.broadcasted_iota(jnp.int32, (1, on_ref.shape[1]), 1) == where[1]
    on = jnp.sum(jnp.where(lane, on_ref[...], 0.0), axis=-1, keepdims=True)
    gate_pre = nn(h, wg_ref[0])
    up_pre = nn(h, wu_ref[0])
    grad_mid = nt(g, wd_ref[0])
    sig = 1.0 / (1.0 + jnp.exp(-gate_pre))
    silu = gate_pre * sig
    mid = silu * up_pre
    column = jnp.where(lane, jnp.sum(grad_mid * mid, axis=-1, keepdims=True), 0.0)
    gg_ref[...] = gg_in[...] + column if chained else column
    act = (on * mid).astype(BF)
    grad_mid = on * grad_mid
    ggp = (grad_mid * up_pre * (sig * (1.0 + gate_pre * (1.0 - sig)))).astype(BF)
    gup = (grad_mid * silu).astype(BF)
    mid_ref[0, 0] = act
    mid_ref[0, 1] = ggp
    mid_ref[0, 2] = gup
    if not acc:
        own_ref[0] = tn(h, ggp).astype(BF)
        own_ref[1] = tn(h, gup).astype(BF)
        own_ref[2] = tn(g, act).astype(BF)
        return
    acc = acc[0]

    @pl.when(step == 0)
    def _():
        acc[...] = jnp.zeros_like(acc)

    acc[0] += tn(h, ggp)
    acc[1] += tn(h, gup)
    acc[2] += tn(g, act)

    @pl.when(step == steps - 1)
    def _():
        own_ref[...] = acc[...].astype(BF)


def expert_grads(j, per_core, which, column, h, g, on, w_gate, w_up, w_down, before):
    rows, width = h.shape
    hidden = w_gate.shape[2]
    experts = on.shape[1]
    tile = rows if rows <= 896 else 448
    steps = rows // tile

    def row(i, w):
        return (i, 0)

    def weight(i, w):
        return (w[0], 0, 0)

    chained = before is not None
    return pl.pallas_call(
        functools.partial(expert_grads_kernel, chained),
        grid_spec=pltpu.PrefetchScalarGridSpec(
            num_scalar_prefetch=1,
            grid=(steps,),
            in_specs=[
                pl.BlockSpec((tile, width), row),
                pl.BlockSpec((tile, width), row),
                pl.BlockSpec((tile, experts), row),
                pl.BlockSpec((1, width, hidden), weight),
                pl.BlockSpec((1, width, hidden), weight),
                pl.BlockSpec((1, hidden, width), weight),
            ]
            + [pl.BlockSpec((tile, experts), row), pl.BlockSpec(memory_space=pl.ANY)] * chained,
            out_specs=[
                pl.BlockSpec((1, 3, tile, hidden), lambda i, w: (j, 0, i, 0)),
                pl.BlockSpec((tile, experts), row),
                pl.BlockSpec((3, width, hidden), lambda i, w: (0, 0, 0)),
            ],
            scratch_shapes=[pltpu.VMEM((3, width, hidden), F32)] * (steps > 1),
        ),
        out_shape=[
            jax.ShapeDtypeStruct((per_core, 3, rows, hidden), BF),
            jax.ShapeDtypeStruct((rows, experts), F32),
            jax.ShapeDtypeStruct((3, width, hidden), BF),
        ],
        input_output_aliases={8: 0} if chained else {},
        compiler_params=pltpu.CompilerParams(vmem_limit_bytes=VMEM_LIMIT),
        cost_estimate=pl.CostEstimate(
            flops=20 * rows * width * hidden,
            bytes_accessed=20 << 20,
            transcendentals=rows * hidden,
        ),
    )(
        jnp.stack([which, column]).astype(jnp.int32),
        h, g, on, w_gate, w_up, w_down, *((before[1], before[0]) if chained else ()),
    )


def expert_sums_kernel(first, mid_ref, wg_ref, wu_ref, wd_ref, mix_ref, gh_ref, mix_acc, gh_acc):
    e, count = pl.program_id(1), pl.num_programs(1)
    mix = nn(mid_ref[0, 0], wd_ref[0])
    gh = nt(mid_ref[0, 1], wg_ref[0]) + nt(mid_ref[0, 2], wu_ref[0])

    @pl.when(e == 0)
    def _():
        mix_acc[...] = mix
        gh_acc[...] = gh

    @pl.when(e > 0)
    def _():
        mix_acc[...] += mix
        gh_acc[...] += gh

    @pl.when(e == count - 1)
    def _():
        mix_ref[...] = mix_acc[...].astype(BF)
        gh_ref[...] = gh_acc[...].astype(BF)


def expert_sums(first, mid, tree, w_gate, w_up, w_down):
    count, _, rows, hidden = mid.shape
    width = w_gate.shape[1]
    rows //= 2
    tile = 448
    tiles = rows // tile

    def weight(i, e, f):
        return (f[0] + e, 0, 0)

    out = pl.BlockSpec((tile, width), lambda i, e, f: (i, 0))
    return pl.pallas_call(
        expert_sums_kernel,
        grid_spec=pltpu.PrefetchScalarGridSpec(
            num_scalar_prefetch=1,
            grid=(tiles, count),
            in_specs=[
                pl.BlockSpec((1, 3, tile, hidden), lambda i, e, f: (e, 0, tree * tiles + i, 0)),
                pl.BlockSpec((1, width, hidden), weight),
                pl.BlockSpec((1, width, hidden), weight),
                pl.BlockSpec((1, hidden, width), weight),
            ],
            out_specs=[out, out],
            scratch_shapes=[pltpu.VMEM((tile, width), F32), pltpu.VMEM((tile, width), F32)],
        ),
        out_shape=[jax.ShapeDtypeStruct((rows, width), BF)] * 2,
        compiler_params=pltpu.CompilerParams(vmem_limit_bytes=VMEM_LIMIT),
        cost_estimate=pl.CostEstimate(
            flops=10 * count * rows * width * hidden,
            bytes_accessed=30 << 20,
            transcendentals=0,
        ),
    )(jnp.reshape(first, (1,)).astype(jnp.int32), mid, w_gate, w_up, w_down)


def local(
    tokens,
    norm_gain,
    w_query,
    key_weight,
    value_weight,
    w_out,
    ffn_gain,
    w_router,
    w_gate,
    w_up,
    w_down,
    parents,
    routes,
    cotangent,
):
    me = Mesh()
    tok_rows, width = tokens.shape
    tree_len = tok_rows * me.groups
    seg_len = tree_len // 16
    columns = width // me.groups
    q_heads = w_query.shape[1] // HEAD_DIM // me.groups
    kv_heads = key_weight.shape[1] // HEAD_DIM // me.groups
    per_key = q_heads // kv_heads
    experts = w_gate.shape[0] * me.groups
    per_core = w_gate.shape[0] // 2
    q_width, k_width = q_heads * HEAD_DIM, kv_heads * HEAD_DIM
    q_lanes, k_lanes = pairs(q_heads) * LANES, pairs(kv_heads) * LANES
    lanes = q_lanes + 2 * k_lanes

    blocks = []
    for j in range(me.groups):
        for weight, size, room in (
            (w_query, q_width, q_lanes),
            (key_weight, k_width, k_lanes),
            (value_weight, k_width, k_lanes),
        ):
            block = weight[:, j * size : (j + 1) * size]
            blocks.append(jnp.pad(block, ((0, 0), (0, room - size))))
    weights = jnp.concatenate(blocks, 1)

    own_rows = tokens.astype(F32)
    inv_rows = lax.rsqrt(jnp.mean(own_rows * own_rows, axis=-1, keepdims=True) + EPS)
    inputs = me.exchange(tokens, 1, 0).astype(F32)
    inv_one = me.gather(inv_rows, 0)
    normed_one = inputs * inv_one
    gain_one = norm_gain.astype(F32)
    hidden_first = (normed_one * gain_one).astype(BF)
    if me.groups == 2:
        theirs = nn(hidden_first, me.part(weights, 1, 1 - me.member)).astype(BF)
        came = me.swap_shard(theirs)
        own = nn(hidden_first, me.part(weights, 1, me.member))
    else:
        own = me.scatter(nn(hidden_first, weights), 1)
        came = jnp.zeros(own.shape, BF)

    route_hot = jnp.any(
        routes[:, :, None] == jnp.arange(experts, dtype=jnp.int32)[None, None, :], axis=1
    ).astype(F32)
    routed = me.gather(route_hot, 0)
    gain_two = ffn_gain.astype(F32)
    gain_two_full = me.gather(ffn_gain, 0).astype(F32)
    router_full = me.gather(w_router, 0)
    grad_tree = me.gather(cotangent, 0)
    grad_all = jnp.concatenate([grad_tree, me.swap_core(grad_tree)], 0)
    routed_other = me.swap_core(routed)

    index = jnp.arange(tree_len, dtype=jnp.int32)
    _, depth = tree_layout(index, seg_len)
    cos, sin = angle_tables(depth)
    visible = tree_mask(index, index, parents[0], seg_len)
    bias = jnp.where(visible, 0.0, -1e30).astype(F32)
    attended, lse, query, key, value = attend(own, came, cos, sin, bias, q_heads, kv_heads)
    attended_full = me.gather(attended[:, :q_width], 1)
    middle = inputs + nn(attended_full, w_out)
    squares = me.total(jnp.sum(middle * middle, axis=-1, keepdims=True))
    inv_two = lax.rsqrt(squares / width + EPS)
    normed_two = middle * inv_two
    hidden_own = (normed_two * gain_two).astype(BF)
    hidden_tree = me.gather(hidden_own, 1)
    hidden_all = jnp.concatenate([hidden_tree, me.swap_core(hidden_tree)], 0)

    def gates_of(h, on):
        logits = nn(h, router_full)
        logits = jnp.where(on > 0, logits, -1e30)
        peak = jnp.max(logits, axis=-1, keepdims=True)
        e = jnp.exp(logits - peak) * on
        return e / jnp.sum(e, axis=-1, keepdims=True)

    gates_all = gates_of(hidden_all, jnp.concatenate([routed, routed_other], 0))
    gates = gates_all[:tree_len]

    first = me.core * per_core
    before = None
    sums = []
    chunk = width // me.chips
    for j in range(per_core):
        mid, own_columns, grads = expert_grads(
            j, per_core, first + j, me.member * (2 * per_core) + first + j,
            hidden_all, grad_all, gates_all, w_gate, w_up, w_down, before,
        )
        before = (mid, own_columns)
        sums.append(
            me.ring_scatter(
                lambda chip, grads=grads: lax.dynamic_slice_in_dim(grads, chip * chunk, chunk, 1)
            )
        )
    mixed_other, grad_other = expert_sums(first, mid, 1, w_gate, w_up, w_down)
    mixed_own, grad_own = expert_sums(first, mid, 0, w_gate, w_up, w_down)

    grad_hidden = grad_own.astype(F32) + me.swap_core(grad_other).astype(F32)
    mixed = mixed_own.astype(F32) + me.swap_core(mixed_other).astype(F32)
    placed = lax.dynamic_update_slice_in_dim(
        jnp.zeros((tree_len, width), F32), middle, me.member * columns, 1
    )
    result = me.scatter(mixed + placed, 0).astype(BF)

    grad_gates = me.total(own_columns[:tree_len] + me.swap_core(own_columns[tree_len:]))
    grad_logits = (
        gates * (grad_gates - jnp.sum(gates * grad_gates, axis=-1, keepdims=True))
    ).astype(BF)
    grad_router = tn(hidden_own, grad_logits)
    grad_hidden_two = nt(grad_logits, w_router) + me.scatter(grad_hidden, 1)
    grad_gain_two = jnp.sum(grad_hidden_two * normed_two, axis=0)
    scaled = grad_hidden_two * gain_two
    mean = me.total(jnp.sum(scaled * normed_two, axis=-1, keepdims=True)) / width
    grad_columns = me.part(grad_tree, 1, me.member).astype(F32)
    grad_middle = grad_columns + inv_two * (scaled - normed_two * mean)
    grad_branch = grad_middle.astype(BF)
    grad_out = me.all_reduce(tn(attended_full, grad_branch))
    grad_attended = nt(grad_branch, w_out)
    if me.groups == 2:
        own = me.part(grad_attended, 1, me.member)
        came = me.swap_shard(me.part(grad_attended, 1, 1 - me.member).astype(BF))
    else:
        own = me.scatter(grad_attended, 1)
        own = jnp.pad(own, ((0, 0), (0, q_lanes - q_width)))
        came = jnp.zeros(own.shape, BF)
    grad_heads = attend_back(
        own, came, query, key, value, lse, cos, sin, bias.T, q_heads, kv_heads
    )
    grad_full = me.gather(grad_heads, 1)
    grad_weights = me.all_reduce(tn(hidden_first, grad_full))
    grad_weights = grad_weights.reshape(columns, me.groups, lanes)

    def picked(start, size):
        return grad_weights[:, :, start : start + size].reshape(columns, me.groups * size)

    grad_query = picked(0, q_width)
    grad_key = picked(q_lanes, k_width)
    grad_value = picked(q_lanes + k_lanes, k_width)
    grad_hidden_one = nt(grad_full, weights)
    grad_gain_one = jnp.sum(grad_hidden_one * normed_one, axis=0)
    scaled = grad_hidden_one * gain_one
    mean = me.total(jnp.sum(scaled * normed_one, axis=-1, keepdims=True)) / width
    input_grad = (grad_middle + inv_one * (scaled - normed_one * mean)).astype(BF)
    input_grad = me.exchange(input_grad, 0, 1)

    small = me.butterfly(
        jnp.concatenate([grad_gain_one[None], grad_gain_two[None], grad_router.T], 0)
    )

    stacked = jnp.stack(sums)
    half = width // me.reps
    mine = lax.dynamic_slice_in_dim(stacked, me.core * half, half, 2)
    other = me.swap_core(
        lax.dynamic_slice_in_dim(stacked, (1 - me.core) * half, half, 2)
    )
    ordered = me.in_order(me.core, mine, other, 0).astype(F32)

    return (
        result,
        input_grad,
        small[0],
        grad_query,
        grad_key,
        grad_value,
        grad_out,
        small[1],
        small[2:].T,
        ordered[:, 0],
        ordered[:, 1],
        ordered[:, 2].transpose(0, 2, 1),
    )


def solution(mesh):
    return jax.shard_map(
        local,
        mesh=mesh,
        in_specs=(
            P(("rep", "shard"), None),
            P("shard"),
            P("shard", None),
            P("shard", None),
            P("shard", None),
            P(None, "shard"),
            P("shard"),
            P("shard", None),
            P("shard", None, None),
            P("shard", None, None),
            P("shard", None, None),
            P("rep", None),
            P(("rep", "shard"), None),
            P(("rep", "shard"), None),
        ),
        out_specs=(
            P(("rep", "shard"), None),
            P(("rep", "shard"), None),
            P("shard"),
            P("shard", None),
            P("shard", None),
            P("shard", None),
            P(None, "shard"),
            P("shard"),
            P("shard", None),
            P("shard", "rep", None),
            P("shard", "rep", None),
            P("shard", None, "rep"),
        ),
        check_vma=False,
    )
```

```python
import functools

import jax
import jax.numpy as jnp
from jax import lax
from jax.experimental import pallas as pl
from jax.experimental.pallas import tpu as pltpu
from jax.sharding import PartitionSpec as P

HEAD_DIM = 64
LANES = 128
EPS = 1e-06
BF = jnp.bfloat16
F32 = jnp.float32
VMEM_LIMIT = 60 << 20


def tree_layout(position, seg_len):
    trunk_len = 4 * seg_len
    beyond = position - trunk_len
    segment = jnp.where(position < trunk_len, 0, 1 + beyond // seg_len)
    inner = jnp.where(
        segment <= 4, trunk_len + beyond % seg_len, trunk_len + seg_len + beyond % seg_len
    )
    depth_position = jnp.where(position < trunk_len, position, inner)
    return (segment, depth_position)


def lookup(segment, parents_row):
    labels = jnp.arange(parents_row.shape[0], dtype=jnp.int32)
    picked = jnp.where(segment[:, None] == labels[None, :], parents_row[None, :], 0)
    return jnp.sum(picked, axis=1)


def tree_mask(query_index, key_index, parents_row, seg_len):
    query_seg, _ = tree_layout(query_index, seg_len)
    key_seg, _ = tree_layout(key_index, seg_len)
    parent_one = lookup(query_seg, parents_row)
    parent_two = lookup(parent_one, parents_row)
    key_row = key_seg[None, :]
    related = (
        (key_row == query_seg[:, None])
        | (key_row == parent_one[:, None])
        | (key_row == parent_two[:, None])
    )
    return related & (key_index[None, :] <= query_index[:, None])


def angle_tables(depth_position):
    half = HEAD_DIM // 2
    frequency = 10000.0 ** (-2.0 * jnp.arange(half, dtype=F32) / HEAD_DIM)
    angles = depth_position.astype(F32)[:, None] * frequency[None, :]
    cosine, sine = jnp.cos(angles), jnp.sin(angles)
    return (
        jnp.concatenate([cosine] * 4, 1),
        jnp.concatenate([-sine, sine, -sine, sine], 1),
    )


def dot(a, b, dims):
    return lax.dot_general(a, b, (dims, ((), ())), preferred_element_type=F32)


def nn(a, b):
    return dot(a, b, ((1,), (0,)))


def nt(a, b):
    return dot(a, b, ((1,), (1,)))


def tn(a, b):
    return dot(a, b, ((0,), (0,)))


class Mesh:
    def __init__(self):
        self.groups = lax.axis_size("shard")
        self.member = lax.axis_index("shard")
        self.reps = lax.axis_size("rep")
        self.rep = lax.axis_index("rep")
        self.core = self.rep % 2
        self.chip = self.rep // 2
        self.chips = self.reps // 2
        rows = self.chips // 2
        order = [2 * z for z in range(rows)] + [2 * z + 1 for z in range(rows - 1, -1, -1)]
        self.ring = []
        for place, chip in enumerate(order):
            after, before = order[(place + 1) % self.chips], order[place - 1]
            self.ring += [(2 * chip, 2 * after), (2 * chip + 1, 2 * before + 1)]
        self.place = jnp.where(
            self.chip % 2 == 0, self.chip // 2, self.chips - 1 - self.chip // 2
        )
        self.way = 1 - 2 * self.core

    def chip_at(self, place):
        place = place % self.chips
        rows = self.chips // 2
        return jnp.where(place < rows, 2 * place, 2 * (self.chips - 1 - place) + 1)

    def swap_shard(self, v):
        return lax.ppermute(v, "shard", [(0, 1), (1, 0)])

    def swap_core(self, v):
        return lax.ppermute(v, "rep", [(r, r ^ 1) for r in range(self.reps)])

    def along_ring(self, v):
        return lax.ppermute(v, "rep", self.ring)

    def part(self, v, axis, which):
        size = v.shape[axis] // self.groups
        return lax.dynamic_slice_in_dim(v, which * size, size, axis)

    def gather(self, v, axis):
        if self.groups != 2:
            return lax.all_gather(v, "shard", axis=axis, tiled=True)
        other = self.swap_shard(v)
        return self.in_order(self.member, v, other, axis)

    def in_order(self, which, mine, other, axis):
        return jnp.where(
            which == 0,
            jnp.concatenate([mine, other], axis),
            jnp.concatenate([other, mine], axis),
        )

    def exchange(self, v, split_axis, concat_axis):
        if self.groups != 2:
            return lax.all_to_all(v, "shard", split_axis, concat_axis, tiled=True)
        other = self.swap_shard(self.part(v, split_axis, 1 - self.member))
        mine = self.part(v, split_axis, self.member)
        return self.in_order(self.member, mine, other, concat_axis)

    def scatter(self, v, axis):
        if self.groups != 2:
            return lax.psum_scatter(
                v.astype(BF), "shard", scatter_dimension=axis, tiled=True
            ).astype(F32)
        other = self.swap_shard(self.part(v, axis, 1 - self.member).astype(BF))
        return self.part(v, axis, self.member).astype(F32) + other.astype(F32)

    def total(self, v):
        if self.groups != 2:
            return lax.psum(v, "shard")
        return v + self.swap_shard(v)

    def ring_sum(self, v):
        chunk = v.shape[0] // self.chips
        ring = Scatter(self, lambda chip: lax.dynamic_slice_in_dim(v, chip * chunk, chunk, 0))
        for _ in range(self.chips - 1):
            ring.start()
            ring.finish()
        ring = Gather(self, ring.held)
        for _ in range(self.chips - 1):
            ring.start()
            ring.finish()
        return ring.whole

    def all_reduce(self, v):
        half = v.shape[0] // 2
        v = v.astype(BF)
        mine = lax.dynamic_slice_in_dim(v, self.core * half, half, 0)
        other = self.swap_core(
            lax.dynamic_slice_in_dim(v, (1 - self.core) * half, half, 0)
        )
        whole = self.ring_sum((mine.astype(F32) + other.astype(F32)).astype(BF))
        return self.in_order(self.core, whole, self.swap_core(whole), 0).astype(F32)

    def butterfly(self, v):
        bit = 1
        while bit < self.reps:
            v = v + lax.ppermute(v, "rep", [(r, r ^ bit) for r in range(self.reps)])
            bit *= 2
        return v


class Scatter:
    def __init__(self, me, own):
        self.me, self.own, self.hops = me, own, 0
        self.held = own(me.chip_at(me.place - me.way))

    def start(self, *deps):
        self.came = self.me.along_ring(tie(self.held, deps))

    def finish(self):
        self.hops += 1
        mine = self.own(self.me.chip_at(self.me.place - self.me.way * (self.hops + 1)))
        self.held = (self.came.astype(F32) + mine.astype(F32)).astype(BF)
        return self.came


class Gather:
    def __init__(self, me, held):
        self.me, self.held, self.hops = me, held, 0
        self.size = held.shape[0]
        whole = jnp.zeros((self.size * me.chips, held.shape[1]), held.dtype)
        self.whole = self.put(whole, me.place)

    def put(self, whole, place):
        at = self.me.chip_at(place) * self.size
        return lax.dynamic_update_slice_in_dim(whole, self.held, at, 0)

    def start(self, *deps):
        self.came = self.me.along_ring(tie(self.held, deps))

    def finish(self):
        self.hops += 1
        self.held = self.came
        self.whole = self.put(self.whole, self.me.place - self.me.way * self.hops)
        return self.came


def pairs(heads):
    return -(-heads // 2)


def rope(v, cos, sin, back):
    lane = lax.broadcasted_iota(jnp.int32, (1, LANES), 1)
    first = lane % HEAD_DIM < HEAD_DIM // 2
    out = []
    for i in range(v.shape[1] // LANES):
        x = v[:, i * LANES : (i + 1) * LANES]
        other = jnp.where(
            first,
            pltpu.roll(x, LANES - HEAD_DIM // 2, 1),
            pltpu.roll(x, HEAD_DIM // 2, 1),
        )
        out.append(x * cos - other * sin if back else x * cos + other * sin)
    return out


def halves(x, parity):
    low = lax.broadcasted_iota(jnp.int32, (1, LANES), 1) < HEAD_DIM
    zero = jnp.zeros_like(x)
    turned = pltpu.roll(x, HEAD_DIM, 1)
    a, b = (x, turned) if parity == 0 else (turned, x)
    return jnp.where(low, a, zero).astype(BF), jnp.where(low, zero, b).astype(BF)


def attend_kernel(
    q_heads, kv_heads, own_ref, came_ref, cos_ref, sin_ref, bias_ref, along_ref,
    out_ref, lse_ref, q_ref, k_ref, v_ref, sent_ref,
):
    sent_ref[...] = along_ref[...]
    per = q_heads // kv_heads
    rows = own_ref.shape[0]
    qp, kp = pairs(q_heads), pairs(kv_heads)
    cos, sin = cos_ref[...], sin_ref[...]
    raw = own_ref[...].astype(F32) + came_ref[...].astype(F32)
    scale = HEAD_DIM**-0.5
    q = [(t * scale).astype(BF) for t in rope(raw[:, : qp * LANES], cos, sin, False)]
    keys = rope(raw[:, qp * LANES : (qp + kp) * LANES], cos, sin, False)
    for i in range(qp):
        q_ref[:, i * LANES : (i + 1) * LANES] = q[i]
    ks, vs = [], []
    for g in range(kv_heads):
        at = (qp + kp + g // 2) * LANES
        ks.append(halves(keys[g // 2], g % 2))
        vs.append(halves(raw[:, at : at + LANES], g % 2))
        for p in range(2):
            k_ref[g, p] = ks[g][p]
            v_ref[g, p] = vs[g][p]
    half = rows // 2
    for lo, n in ((0, half), (half, rows)):
        bias = bias_ref[lo : lo + half, :n]
        for i in range(qp):
            out = jnp.zeros((half, LANES), F32)
            for h in range(2 * i, min(2 * i + 2, q_heads)):
                g, p = h // per, h % 2
                s = nt(q[i][lo : lo + half], ks[g][p][:n]) + bias
                peak = jnp.max(s, axis=-1, keepdims=True)
                e = jnp.exp(s - peak)
                total = jnp.sum(e, axis=-1, keepdims=True)
                lse_ref[lo : lo + half, h : h + 1] = peak + jnp.log(total)
                out = out + nn((e * (1.0 / total)).astype(BF), vs[g][p][:n])
            out_ref[lo : lo + half, i * LANES : (i + 1) * LANES] = out.astype(BF)


def attend(own, came, cos, sin, bias, along, q_heads, kv_heads):
    rows = own.shape[0]
    qp = pairs(q_heads)
    return pl.pallas_call(
        functools.partial(attend_kernel, q_heads, kv_heads),
        out_shape=[
            jax.ShapeDtypeStruct((rows, qp * LANES), BF),
            jax.ShapeDtypeStruct((rows, LANES), F32),
            jax.ShapeDtypeStruct((rows, qp * LANES), BF),
            jax.ShapeDtypeStruct((kv_heads, 2, rows, LANES), BF),
            jax.ShapeDtypeStruct((kv_heads, 2, rows, LANES), BF),
            jax.ShapeDtypeStruct(along.shape, along.dtype),
        ],
        compiler_params=pltpu.CompilerParams(vmem_limit_bytes=VMEM_LIMIT),
        cost_estimate=pl.CostEstimate(
            flops=1200 * rows * rows * q_heads,
            bytes_accessed=8 << 20,
            transcendentals=rows * rows * q_heads,
        ),
    )(own, came, cos, sin, bias, along)


def attend_back_kernel(
    q_heads, kv_heads, own_ref, came_ref, q_ref, k_ref, v_ref, lse_ref,
    cos_ref, sin_ref, bias_ref, *refs,
):
    per = q_heads // kv_heads
    rows = own_ref.shape[0]
    qp, kp = pairs(q_heads), pairs(kv_heads)
    cos, sin = cos_ref[...], sin_ref[...]
    scale = HEAD_DIM**-0.5
    low = lax.broadcasted_iota(jnp.int32, (1, LANES), 1) < HEAD_DIM
    grad = (own_ref[...].astype(F32) + came_ref[...].astype(F32)).astype(BF)
    lse = lse_ref[...].T
    half = rows // 2
    out_ref = refs[-1]

    def put(at, v):
        out_ref[:, at * LANES : (at + 1) * LANES] = v.astype(BF)

    def blocks():
        return [
            [[jnp.zeros((half, LANES), F32) for _ in range(2)] for _ in range(2)]
            for _ in range(kv_heads)
        ]

    dk, dv = blocks(), blocks()
    for i in range(qp):
        parts = []
        for lo, n in ((0, half), (half, rows)):
            q = q_ref[lo : lo + half, i * LANES : (i + 1) * LANES]
            go = grad[lo : lo + half, i * LANES : (i + 1) * LANES]
            bias = bias_ref[:n, lo : lo + half]
            dq = jnp.zeros((half, LANES), F32)
            for h in range(2 * i, min(2 * i + 2, q_heads)):
                g, p = h // per, h % 2
                k, v = k_ref[g, p, :n], v_ref[g, p, :n]
                s = nt(k, q) + bias
                probs = jnp.exp(s - lse[h : h + 1, lo : lo + half])
                dp = nt(v, go)
                delta = jnp.sum(probs * dp, axis=0, keepdims=True)
                ds = (probs * (dp - delta)).astype(BF)
                dq = dq + tn(ds, k)
                ck, cv = nn(ds, q), nn(probs.astype(BF), go)
                for b in range(n // half):
                    dk[g][p][b] = dk[g][p][b] + ck[b * half : (b + 1) * half]
                    dv[g][p][b] = dv[g][p][b] + cv[b * half : (b + 1) * half]
            parts.append(dq * scale)
        put(i, rope(jnp.concatenate(parts, 0), cos, sin, True)[0])

    def packed(d, j):
        got = jnp.zeros((rows, LANES), F32)
        for g in range(2 * j, min(2 * j + 2, kv_heads)):
            a, b = (jnp.concatenate(d[g][p], 0) for p in range(2))
            a, b = jnp.where(low, a, 0.0), jnp.where(low, 0.0, b)
            if g % 2 == 0:
                got = got + a + pltpu.roll(b, HEAD_DIM, 1)
            else:
                got = got + b + pltpu.roll(a, HEAD_DIM, 1)
        return got

    for j in range(kp):
        put(qp + j, rope(packed(dk, j), cos, sin, True)[0])
        put(qp + kp + j, packed(dv, j))


def attend_back(own, came, q, k, v, lse, cos, sin, bias, q_heads, kv_heads, deps):
    rows = own.shape[0]
    lanes = (pairs(q_heads) + 2 * pairs(kv_heads)) * LANES
    specs, deps = after(deps)
    return pl.pallas_call(
        functools.partial(attend_back_kernel, q_heads, kv_heads),
        in_specs=[pl.BlockSpec(memory_space=pltpu.VMEM)] * 9 + specs,
        out_shape=jax.ShapeDtypeStruct((rows, lanes), BF),
        compiler_params=pltpu.CompilerParams(vmem_limit_bytes=VMEM_LIMIT),
        cost_estimate=pl.CostEstimate(
            flops=1600 * rows * rows * q_heads,
            bytes_accessed=8 << 20,
            transcendentals=rows * rows * q_heads,
        ),
    )(own, came, q, k, v, lse, cos, sin, bias, *deps)


def after(arrays):
    return [pl.BlockSpec(memory_space=pl.ANY)] * len(arrays), tuple(arrays)


def row_tile(rows):
    return rows if rows <= 896 else 448


def params():
    return pltpu.CompilerParams(vmem_limit_bytes=VMEM_LIMIT)


def cost(flops, megabytes, transcendentals=0):
    return pl.CostEstimate(
        flops=int(flops), bytes_accessed=megabytes << 20, transcendentals=int(transcendentals)
    )


def to_row(column):
    rows = column.shape[0]
    return jnp.broadcast_to(column, (rows, LANES)).T[:1]


def to_column(row):
    return jnp.broadcast_to(row, (LANES, row.shape[1])).T[:, :1]


def put_column(ref, column):
    rows = column.shape[0]
    row = to_row(column)
    high = row.astype(BF)
    low = (row - high.astype(F32)).astype(BF)
    line = lax.broadcasted_iota(jnp.int32, (16, rows), 0)
    ref[rows : rows + 16, :] = jnp.zeros((16, ref.shape[1]), BF)
    ref[rows : rows + 16, :rows] = jnp.where(
        line == 0, high.astype(F32), jnp.where(line == 1, low.astype(F32), 0.0)
    ).astype(BF)


def get_column(ref):
    rows = ref.shape[0] - 16
    last = ref[rows : rows + 16, :rows].astype(F32)
    return to_column(last[0:1] + last[1:2])


def split_kernel(where, x_ref, packet_ref, along_ref, theirs_ref, mine_ref, sent_ref, gone_ref):
    rows, size = x_ref.shape[0], mine_ref.shape[1]
    sent_ref[...] = packet_ref[...]
    gone_ref[...] = along_ref[...]
    x = x_ref[...].astype(F32)
    squares = jnp.sum(x * x, axis=-1, keepdims=True)
    for ref, member in ((theirs_ref, 1 - where[0]), (mine_ref, where[0])):
        ref[:rows, :] = x_ref[:, pl.ds(pl.multiple_of(member * size, LANES), size)]
        put_column(ref, squares)


def split(member, x, packet, along):
    rows, width = x.shape
    out = jax.ShapeDtypeStruct((rows + 16, width // 2), BF)
    return pl.pallas_call(
        split_kernel,
        in_specs=[pl.BlockSpec(memory_space=pltpu.SMEM)]
        + [pl.BlockSpec(memory_space=pltpu.VMEM)] * 3,
        out_shape=[
            out,
            out,
            jax.ShapeDtypeStruct(packet.shape, BF),
            jax.ShapeDtypeStruct(along.shape, BF),
        ],
        compiler_params=params(),
        cost_estimate=cost(0, 2),
    )(jnp.reshape(member, (1,)), x, packet, along)


def heads_product(hidden, member, part, parts, weights):
    found = []
    for w in weights:
        size = w.shape[1] // (2 * parts)
        at = pl.ds(pl.multiple_of((member * parts + part) * size, LANES), size)
        found.append(nn(hidden, w[:, at]))
    return jnp.concatenate(found, 1)


def project_theirs_kernel(parts, where, mine_ref, came_ref, gain_ref, wq, wk, wv, *refs):
    outs, (hidden_ref, x_ref, inv_ref) = refs[:parts], refs[parts:]
    rows, columns = mine_ref.shape[0] - 16, mine_ref.shape[1]
    gain = gain_ref[...].astype(F32)
    for message, member in ((mine_ref, where[0]), (came_ref, 1 - where[0])):
        at = pl.ds(pl.multiple_of(member * rows, 16), rows)
        inv = lax.rsqrt(get_column(message) / (2 * columns) + EPS)
        inv_ref[at, :] = inv
        x = message[:rows, :]
        x_ref[at, :] = x
        hidden_ref[at, :] = (x.astype(F32) * inv * gain).astype(BF)
    for part in range(parts):
        outs[part][...] = heads_product(
            hidden_ref[...], 1 - where[0], part, parts, (wq, wk, wv)
        ).astype(BF)


def project_theirs(member, parts, mine, came, gain, weights):
    rows, columns = 2 * (mine.shape[0] - 16), mine.shape[1]
    lanes = sum(w.shape[1] for w in weights) // (2 * parts)
    return pl.pallas_call(
        functools.partial(project_theirs_kernel, parts),
        in_specs=[pl.BlockSpec(memory_space=pltpu.SMEM)]
        + [pl.BlockSpec(memory_space=pltpu.VMEM)] * 6,
        out_shape=[jax.ShapeDtypeStruct((rows, lanes), BF)] * parts
        + [
            jax.ShapeDtypeStruct((rows, columns), BF),
            jax.ShapeDtypeStruct((rows, columns), BF),
            jax.ShapeDtypeStruct((rows, 1), F32),
        ],
        compiler_params=params(),
        cost_estimate=cost(4 * rows * columns * lanes * parts, 6),
    )(jnp.reshape(member, (1,)), mine, came, gain, *weights)


def project_own_kernel(parts, where, hidden_ref, wq, wk, wv, *refs):
    for part in range(parts):
        refs[part - parts][...] = heads_product(
            hidden_ref[...], where[0], part, parts, (wq, wk, wv)
        )


def project_own(member, parts, hidden, weights, deps):
    rows, columns = hidden.shape
    lanes = sum(w.shape[1] for w in weights) // (2 * parts)
    specs, deps = after(deps)
    return pl.pallas_call(
        functools.partial(project_own_kernel, parts),
        in_specs=[pl.BlockSpec(memory_space=pltpu.SMEM)]
        + [pl.BlockSpec(memory_space=pltpu.VMEM)] * 4
        + specs,
        out_shape=[jax.ShapeDtypeStruct((rows, lanes), F32)] * parts,
        compiler_params=params(),
        cost_estimate=cost(4 * rows * columns * lanes * parts, 6),
    )(jnp.reshape(member, (1,)), hidden, *weights, *deps)


def project_back_kernel(
    parts, where, x_ref, inv_ref, gain_ref, wq_ref, wk_ref, wv_ref, *refs
):
    grads = refs[: 2 * parts]
    scaled_ref, sums_ref, gain_grad_ref = refs[-3:]
    total = jnp.zeros(x_ref.shape, F32)
    for part in range(parts):
        for grad, member in ((grads[2 * part], where[0]), (grads[2 * part + 1], 1 - where[0])):
            start = 0
            for w in (wq_ref, wk_ref, wv_ref):
                size = w.shape[1] // (2 * parts)
                at = pl.ds(pl.multiple_of((member * parts + part) * size, LANES), size)
                total += nt(grad[:, start : start + size], w[:, at])
                start += size
    normed = x_ref[...].astype(F32) * inv_ref[...]
    scaled = total * gain_ref[...].astype(F32)
    scaled_ref[...] = scaled
    sums_ref[...] = jnp.sum(scaled * normed, axis=-1, keepdims=True)
    gain_grad_ref[...] = jnp.sum(total * normed, axis=0, keepdims=True)


def project_back(member, x, inv, gain, weights, grads, deps):
    rows, columns = x.shape
    parts = len(grads)
    flat = [a for pair in grads for a in pair]
    specs, deps = after(deps)
    whole = pl.BlockSpec(memory_space=pltpu.VMEM)
    return pl.pallas_call(
        functools.partial(project_back_kernel, parts),
        in_specs=[pl.BlockSpec(memory_space=pltpu.SMEM)] + [whole] * (6 + len(flat)) + specs,
        out_shape=[
            jax.ShapeDtypeStruct((rows, columns), F32),
            jax.ShapeDtypeStruct((rows, 1), F32),
            jax.ShapeDtypeStruct((1, columns), F32),
        ],
        compiler_params=params(),
        cost_estimate=cost(2 * rows * columns * sum(w.shape[1] for w in weights), 10),
    )(jnp.reshape(member, (1,)), x, inv, gain, *weights, *flat, *deps)


def weight_grads_kernel(where, *refs):
    hidden, out_ref = refs[:2], refs[-1]
    size = refs[2].shape[1]
    out_ref[:, 2 * size :] = refs[10][...]
    for core in range(2):

        @pl.when(where[1] == core)
        def _():
            for i, member in ((0, where[0]), (1, 1 - where[0])):
                total = sum(tn(hidden[t][...], refs[2 + 4 * t + 2 * core + i][...]) for t in range(2))
                at = pl.ds(pl.multiple_of(member * size, LANES), size)
                out_ref[:, at] = total.astype(BF)


def weight_grads(member, core, hidden, grads, beside, deps):
    columns = hidden[0].shape[1]
    flat = [a for tree in grads for pair in tree for a in pair]
    rows, lanes = flat[0].shape
    specs, deps = after(deps)
    return pl.pallas_call(
        weight_grads_kernel,
        in_specs=[pl.BlockSpec(memory_space=pltpu.SMEM)]
        + [pl.BlockSpec(memory_space=pltpu.VMEM)] * (3 + len(flat))
        + specs,
        out_shape=jax.ShapeDtypeStruct((columns, 2 * lanes + beside.shape[1]), BF),
        compiler_params=params(),
        cost_estimate=cost(8 * rows * columns * lanes, 8),
    )(jnp.stack([member, core]), *hidden, *flat, beside, *deps)


def middle_kernel(count, where, *refs):
    pieces, (w_ref, x_ref) = refs[:count], refs[count : count + 2]
    middle_ref, low_ref, squares_ref = refs[-3:]
    total = x_ref[...].astype(F32)
    for i, piece in enumerate(pieces):
        size = piece.shape[1]
        total += nn(piece[...], w_ref[pl.ds(pl.multiple_of(where[i], 64), size), :])
    squares = jnp.sum(total * total, axis=-1, keepdims=True)
    middle_ref[...] = total
    low_ref[: total.shape[0], :] = total.astype(BF)
    squares_ref[...] = squares
    if low_ref.shape[0] > total.shape[0]:
        put_column(low_ref, squares)


def middle_of(pieces, where, w_out, x, packed):
    rows, columns = x.shape
    tile = rows if packed else 448
    more = 16 if packed else 0

    def row(i, w):
        return (i, 0)

    return pl.pallas_call(
        functools.partial(middle_kernel, len(pieces)),
        grid_spec=pltpu.PrefetchScalarGridSpec(
            num_scalar_prefetch=1,
            grid=(rows // tile,),
            in_specs=[pl.BlockSpec((tile, p.shape[1]), row) for p in pieces]
            + [
                pl.BlockSpec(w_out.shape, lambda i, w: (0, 0)),
                pl.BlockSpec((tile, columns), row),
            ],
            out_specs=[
                pl.BlockSpec((tile, columns), row),
                pl.BlockSpec((tile + more, columns), row),
                pl.BlockSpec((tile, 1), row),
            ],
        ),
        out_shape=[
            jax.ShapeDtypeStruct((rows, columns), F32),
            jax.ShapeDtypeStruct((rows + more, columns), BF),
            jax.ShapeDtypeStruct((rows, 1), F32),
        ],
        compiler_params=params(),
        cost_estimate=cost(2 * rows * columns * w_out.shape[0], 6),
    )(where, *pieces, w_out, x)


def hidden_kernel(count, parts, width, where, *refs):
    gain_ref, router_ref = refs[:2]
    h_ref, gates_ref = refs[-2:]
    for tree in range(2):
        mine = refs[2 + tree * (count + parts + 1) :]
        pieces, squares, on = mine[:count], mine[count : count + parts], mine[count + parts][...]
        total = squares[0][...]
        for more in squares[1:]:
            total += more[...]
        inv = lax.rsqrt(total / width + EPS)
        for i, piece in enumerate(pieces):
            size = piece.shape[1]
            at = pl.ds(pl.multiple_of(where[i] * size, LANES), size)
            gain = gain_ref[:, at].astype(F32)
            h_ref[tree, :, at] = (piece[...].astype(F32) * inv * gain).astype(BF)
        logits = jnp.where(on > 0, nn(h_ref[tree], router_ref[...]), -1e30)
        peak = jnp.max(logits, axis=-1, keepdims=True)
        e = jnp.exp(logits - peak) * on
        gates_ref[tree] = e / jnp.sum(e, axis=-1, keepdims=True)


def hidden_of(trees, where, gain, router):
    pieces, squares, on = trees[0]
    rows = on.shape[0]
    width, experts = router.shape
    tile = 448

    def row(i, w):
        return (i, 0)

    def all_of(i, w):
        return (0, 0)

    def both(i, w):
        return (0, i, 0)

    specs = [pl.BlockSpec((tile, p.shape[1]), row) for p in (*pieces, *squares, on)]
    return pl.pallas_call(
        functools.partial(hidden_kernel, len(pieces), len(squares), width),
        grid_spec=pltpu.PrefetchScalarGridSpec(
            num_scalar_prefetch=1,
            grid=(rows // tile,),
            in_specs=[pl.BlockSpec((1, width), all_of), pl.BlockSpec((width, experts), all_of)]
            + specs
            + specs,
            out_specs=[
                pl.BlockSpec((2, tile, width), both),
                pl.BlockSpec((2, tile, experts), both),
            ],
        ),
        out_shape=[
            jax.ShapeDtypeStruct((2, rows, width), BF),
            jax.ShapeDtypeStruct((2, rows, experts), F32),
        ],
        compiler_params=params(),
        cost_estimate=cost(4 * rows * width * 256, 8, rows * 32),
    )(where, gain, router, *(a for p, q, o in trees for a in (*p, *q, o)))


PACKET_ROWS = 48


def hidden_packed_kernel(where, *refs):
    h_ref, gates_ref, inv_ref, on_ref = refs[8:]
    member = (where[0], 1 - where[0])
    for tree in range(2):
        messages, packets = refs[4 * tree : 4 * tree + 2], refs[4 * tree + 2 : 4 * tree + 4]
        rows, columns = messages[0].shape[0] - 16, messages[0].shape[1]
        squares = get_column(messages[0]) + get_column(messages[1])
        inv = lax.rsqrt(squares / (2 * columns) + EPS)
        if tree == 0:
            inv_ref[...] = inv
        logits = 0.0
        for i in range(2):
            at = pl.ds(pl.multiple_of(member[i] * columns, LANES), columns)
            gain = packets[i][16:32, :].astype(F32)[:1]
            h = (messages[i][:rows, :].astype(F32) * inv * gain).astype(BF)
            h_ref[tree, :, at] = h
            logits = logits + nt(h, packets[i][:16, :])
            tokens = rows // 2
            on_ref[pl.ds(pl.multiple_of(member[i] * tokens, 16), tokens), :] = (
                packets[i][32:48, :tokens].astype(F32).T
            )
        on = on_ref[...]
        logits = jnp.where(on > 0, logits, -1e30)
        peak = jnp.max(logits, axis=-1, keepdims=True)
        e = jnp.exp(logits - peak) * on
        gates_ref[tree] = e / jnp.sum(e, axis=-1, keepdims=True)


def hidden_packed(member, trees):
    rows, columns = trees[0][0].shape[0] - 16, trees[0][0].shape[1]
    return pl.pallas_call(
        hidden_packed_kernel,
        in_specs=[pl.BlockSpec(memory_space=pltpu.SMEM)]
        + [pl.BlockSpec(memory_space=pltpu.VMEM)] * 8,
        out_shape=[
            jax.ShapeDtypeStruct((2, rows, 2 * columns), BF),
            jax.ShapeDtypeStruct((2, rows, 16), F32),
            jax.ShapeDtypeStruct((rows, 1), F32),
        ],
        scratch_shapes=[pltpu.VMEM((rows, 16), F32)],
        compiler_params=params(),
        cost_estimate=cost(4 * rows * columns * 256, 8),
    )(jnp.reshape(member, (1,)), *(a for tree in trees for a in tree))


def expert_grads_kernel(
    chained, steps, where, h_ref, g_ref, on_ref, wg_ref, wu_ref, wd_ref, *refs
):
    mid_ref, gg_ref, own_ref = refs[-3:] if steps == 1 else refs[-4:-1]
    step = pl.program_id(0)
    h, g = h_ref[...], g_ref[...]
    lane = lax.broadcasted_iota(jnp.int32, (1, on_ref.shape[1]), 1) == where[1]
    on = jnp.sum(jnp.where(lane, on_ref[...], 0.0), axis=-1, keepdims=True)
    gate_pre = nn(h, wg_ref[0])
    up_pre = nn(h, wu_ref[0])
    grad_mid = nt(g, wd_ref[0])
    sig = 1.0 / (1.0 + jnp.exp(-gate_pre))
    silu = gate_pre * sig
    mid = silu * up_pre
    column = jnp.where(lane, jnp.sum(grad_mid * mid, axis=-1, keepdims=True), 0.0)
    gg_ref[...] = refs[0][...] + column if chained else column
    act = (on * mid).astype(BF)
    grad_mid = on * grad_mid
    ggp = (grad_mid * up_pre * (sig * (1.0 + gate_pre * (1.0 - sig)))).astype(BF)
    gup = (grad_mid * silu).astype(BF)
    mid_ref[0, 0] = act
    mid_ref[0, 1] = ggp
    mid_ref[0, 2] = gup
    if steps == 1:
        own_ref[0] = tn(h, ggp).astype(BF)
        own_ref[1] = tn(h, gup).astype(BF)
        own_ref[2] = tn(g, act).astype(BF)
        return
    acc = refs[-1]

    @pl.when(step == 0)
    def _():
        acc[...] = jnp.zeros_like(acc)

    acc[0] += tn(h, ggp)
    acc[1] += tn(h, gup)
    acc[2] += tn(g, act)

    @pl.when(step == steps - 1)
    def _():
        own_ref[...] = acc[...].astype(BF)


def expert_grads(
    j, per_core, which, column, h, g, on, w_gate, w_up, w_down, before, slot, slots, deps
):
    rows, width = h.shape
    hidden = w_gate.shape[2]
    experts = on.shape[1]
    tile = row_tile(rows)
    steps = rows // tile

    def row(i, w):
        return (i, 0)

    def weight(i, w):
        return (w[0], 0, 0)

    chained = before is not None
    more = [pl.BlockSpec((tile, experts), row), pl.BlockSpec(memory_space=pl.ANY)] * chained
    aliases = {8: 0} if chained else {}
    if slot:
        aliases[9] = 2
        deps = (before[2], *deps)
    specs, deps = after(deps)
    return pl.pallas_call(
        functools.partial(expert_grads_kernel, chained, steps),
        grid_spec=pltpu.PrefetchScalarGridSpec(
            num_scalar_prefetch=1,
            grid=(steps,),
            in_specs=[
                pl.BlockSpec((tile, width), row),
                pl.BlockSpec((tile, width), row),
                pl.BlockSpec((tile, experts), row),
                pl.BlockSpec((1, width, hidden), weight),
                pl.BlockSpec((1, width, hidden), weight),
                pl.BlockSpec((1, hidden, width), weight),
            ]
            + more
            + specs,
            out_specs=[
                pl.BlockSpec((1, 3, tile, hidden), lambda i, w: (j, 0, i, 0)),
                pl.BlockSpec((tile, experts), row),
                pl.BlockSpec((3, width, hidden), lambda i, w: (slot, 0, 0)),
            ],
            scratch_shapes=[pltpu.VMEM((3, width, hidden), F32)] * (steps > 1),
        ),
        out_shape=[
            jax.ShapeDtypeStruct((per_core, 3, rows, hidden), BF),
            jax.ShapeDtypeStruct((rows, experts), F32),
            jax.ShapeDtypeStruct((3 * slots, width, hidden), BF),
        ],
        input_output_aliases=aliases,
        compiler_params=params(),
        cost_estimate=cost(16 * rows * width * hidden, 20, rows * hidden),
    )(
        jnp.stack([which, column]).astype(jnp.int32),
        h, g, on, w_gate, w_up, w_down,
        *((before[1], before[0]) if chained else ()),
        *deps,
    )


def expert_hidden_kernel(given, split, where, gate_ref, up_ref, wg_ref, wu_ref, *refs):
    e, count = pl.program_id(1), pl.num_programs(1)
    acc = refs[-1]
    part = nt(gate_ref[0, 0], wg_ref[0]) + nt(up_ref[0, 0], wu_ref[0])

    @pl.when(e == 0)
    def _():
        acc[...] = part + refs[0][...].astype(F32) if given else part

    @pl.when(e > 0)
    def _():
        acc[...] += part

    @pl.when(e == count - 1)
    def _():
        if not split:
            refs[-2][...] = acc[...].astype(BF)
            return
        size = refs[-2].shape[1]
        for out, member in ((refs[-3], where[1]), (refs[-2], 1 - where[1])):
            at = pl.ds(pl.multiple_of(member * size, LANES), size)
            out[...] = acc[:, at].astype(BF)


def expert_hidden(first, member, mid, tree, w_gate, w_up, came, split, deps):
    count, _, rows, hidden = mid.shape
    width = w_gate.shape[1]
    rows //= 2
    tile = 448
    tiles = rows // tile

    def weight(i, e, f):
        return (f[0] + e, 0, 0)

    def row(i, e, f):
        return (i, 0)

    given = [came] if came is not None else []
    specs, deps = after(deps)
    outs = 2 if split else 1
    return pl.pallas_call(
        functools.partial(expert_hidden_kernel, bool(given), split),
        grid_spec=pltpu.PrefetchScalarGridSpec(
            num_scalar_prefetch=1,
            grid=(tiles, count),
            in_specs=[
                pl.BlockSpec((1, 1, tile, hidden), lambda i, e, f: (e, 1, tree * tiles + i, 0)),
                pl.BlockSpec((1, 1, tile, hidden), lambda i, e, f: (e, 2, tree * tiles + i, 0)),
                pl.BlockSpec((1, width, hidden), weight),
                pl.BlockSpec((1, width, hidden), weight),
            ]
            + [pl.BlockSpec((tile, width), row) for _ in given]
            + specs,
            out_specs=[pl.BlockSpec((tile, width // outs), row)] * outs,
            scratch_shapes=[pltpu.VMEM((tile, width), F32)],
        ),
        out_shape=[jax.ShapeDtypeStruct((rows, width // outs), BF)] * outs,
        compiler_params=params(),
        cost_estimate=cost(6 * count * rows * width * hidden, 20),
    )(jnp.stack([first, member]).astype(jnp.int32), mid, mid, w_gate, w_up, *given, *deps)


def expert_mix_kernel(first, mid_ref, wd_ref, *refs):
    e, count = pl.program_id(1), pl.num_programs(1)
    acc = refs[-1]
    part = nn(mid_ref[0, 0], wd_ref[0])

    @pl.when(e == 0)
    def _():
        acc[...] = part

    @pl.when(e > 0)
    def _():
        acc[...] += part

    @pl.when(e == count - 1)
    def _():
        refs[-2][...] = acc[...].astype(BF)


def expert_mix(first, mid, tree, w_down, deps):
    count, _, rows, hidden = mid.shape
    width = w_down.shape[2]
    rows //= 2
    tile = 448
    tiles = rows // tile
    specs, deps = after(deps)
    return pl.pallas_call(
        expert_mix_kernel,
        grid_spec=pltpu.PrefetchScalarGridSpec(
            num_scalar_prefetch=1,
            grid=(tiles, count),
            in_specs=[
                pl.BlockSpec((1, 1, tile, hidden), lambda i, e, f: (e, 0, tree * tiles + i, 0)),
                pl.BlockSpec((1, hidden, width), lambda i, e, f: (f[0] + e, 0, 0)),
            ]
            + specs,
            out_specs=pl.BlockSpec((tile, width), lambda i, e, f: (i, 0)),
            scratch_shapes=[pltpu.VMEM((tile, width), F32)],
        ),
        out_shape=jax.ShapeDtypeStruct((rows, width), BF),
        compiler_params=params(),
        cost_estimate=cost(3 * count * rows * width * hidden, 10),
    )(jnp.reshape(first, (1,)).astype(jnp.int32), mid, w_down, *deps)


def out_grads_kernel(parts, where, *refs):
    branch, out_ref = refs[4 * parts : 4 * parts + 2], refs[-1]
    for own in range(2):

        @pl.when(where[0] == own)
        def _():
            for part in range(parts):
                at = (1 - own) * parts + part
                total = sum(
                    tn(refs[2 * parts * t + at][...], branch[t][...]) for t in range(2)
                )
                size = total.shape[0]
                out_ref[part * size : (part + 1) * size, :] = total.astype(BF)


def out_grads(own, attended, branch):
    parts = len(attended[0]) // 2
    size, columns = attended[0][0].shape[1], branch[0].shape[1]
    return pl.pallas_call(
        functools.partial(out_grads_kernel, parts),
        in_specs=[pl.BlockSpec(memory_space=pltpu.SMEM)]
        + [pl.BlockSpec(memory_space=pltpu.VMEM)] * (4 * parts + 2),
        out_shape=jax.ShapeDtypeStruct((parts * size, columns), BF),
        compiler_params=params(),
        cost_estimate=cost(4 * branch[0].shape[0] * columns * size * parts, 8),
    )(jnp.reshape(own, (1,)).astype(jnp.int32), *attended[0], *attended[1], *branch)


def tie_kernel(*refs):
    pass


def tie(v, deps):
    if not deps:
        return v
    specs, deps = after((v, *deps))
    return pl.pallas_call(
        tie_kernel,
        in_specs=specs,
        out_specs=pl.BlockSpec(memory_space=pl.ANY),
        out_shape=jax.ShapeDtypeStruct(v.shape, v.dtype),
        input_output_aliases={0: 0},
        cost_estimate=cost(0, 0),
    )(*deps)


def norm_back_kernel(
    mine_ref, came_ref, logits_ref, router_ref, middle_ref, inv_ref, gain_ref, *refs
):
    scaled_ref, sums_ref, gain_grad_ref = refs[-3:]
    total = mine_ref[...].astype(F32) + came_ref[...].astype(F32)
    total += nt(logits_ref[...], router_ref[...])
    normed = middle_ref[...] * inv_ref[...]
    scaled = total * gain_ref[...].astype(F32)
    scaled_ref[...] = scaled
    sums_ref[...] = jnp.sum(scaled * normed, axis=-1, keepdims=True)
    gain_grad_ref[...] = jnp.sum(total * normed, axis=0, keepdims=True)


def norm_back(mine, came, logits, router, middle, inv, gain, deps):
    rows, columns = middle.shape
    specs, deps = after(deps)
    return pl.pallas_call(
        norm_back_kernel,
        in_specs=[pl.BlockSpec(memory_space=pltpu.VMEM)] * 7 + specs,
        out_shape=[
            jax.ShapeDtypeStruct((rows, columns), F32),
            jax.ShapeDtypeStruct((rows, 1), F32),
            jax.ShapeDtypeStruct((1, columns), F32),
        ],
        compiler_params=params(),
        cost_estimate=cost(512 * rows * columns, 6),
    )(mine, came, logits, router, middle, inv, gain, *deps)


def branch_kernel(parts, where, grad_ref, scaled_ref, middle_ref, inv_ref, m_ref, c_ref, w_ref, *refs):
    full_ref, low_ref = refs[-2 - 2 * parts : -2 * parts]
    theirs, own = refs[-2 * parts : -parts], refs[-parts:]
    columns = middle_ref.shape[1]
    inv = inv_ref[...]
    mean = (m_ref[...] + c_ref[...]) / (2 * columns)
    at = pl.ds(pl.multiple_of(where[0] * columns, LANES), columns)
    grad = grad_ref[:, at].astype(F32)
    grad += inv * (scaled_ref[...] - middle_ref[...] * inv * mean)
    full_ref[...] = grad
    low = grad.astype(BF)
    low_ref[...] = low
    for outs, member in ((theirs, 1 - where[0]), (own, where[0])):
        for part in range(parts):
            size = outs[part].shape[1]
            rows = pl.ds(pl.multiple_of((member * parts + part) * size, 16), size)
            outs[part][...] = nt(low, w_ref[rows, :]).astype(outs[part].dtype)


def branch_back(member, parts, grad, scaled, middle, inv, sums_mine, sums_came, w_out, deps):
    rows, columns = middle.shape
    size = w_out.shape[0] // (2 * parts)
    specs, deps = after(deps)
    vmem = pl.BlockSpec(memory_space=pltpu.VMEM)
    first = pl.BlockSpec((rows, grad.shape[1]), lambda i: (0, 0))
    outs = [
        jax.ShapeDtypeStruct((rows, columns), F32),
        jax.ShapeDtypeStruct((rows, columns), BF),
        *[jax.ShapeDtypeStruct((rows, size), BF)] * parts,
        *[jax.ShapeDtypeStruct((rows, size), F32)] * parts,
    ]
    return pl.pallas_call(
        functools.partial(branch_kernel, parts),
        grid=(1,),
        in_specs=[pl.BlockSpec(memory_space=pltpu.SMEM), first] + [vmem] * 6 + specs,
        out_specs=[pl.BlockSpec(o.shape, lambda i: (0, 0)) for o in outs],
        out_shape=outs,
        compiler_params=params(),
        cost_estimate=cost(2 * rows * columns * w_out.shape[0], 10),
    )(
        jnp.reshape(member, (1,)),
        grad, scaled, middle, inv, sums_mine, sums_came, w_out, *deps,
    )


def finish_kernel(layout, where, *refs):
    outs, last = refs[2:-1], refs[-1]
    for g in range(2):
        for out, to, start, size in layout[g]:
            at = slice(start, start + size)
            v = jnp.where(where[0] == g, refs[0][:, at], refs[1][:, at])
            outs[out][:, to : to + size] = v.astype(F32)
    start = refs[0].shape[1] - last.shape[2]
    last[where[0]] = refs[0][:, start:].astype(F32)
    last[1 - where[0]] = refs[1][:, start:].astype(F32)


def finish(core, mine, other, layout, widths, out_width):
    rows, columns = mine.shape
    tile = rows // 4

    def row(i, w):
        return (i, 0)

    return pl.pallas_call(
        functools.partial(finish_kernel, layout),
        grid_spec=pltpu.PrefetchScalarGridSpec(
            num_scalar_prefetch=1,
            grid=(4,),
            in_specs=[pl.BlockSpec((tile, columns), row)] * 2,
            out_specs=[pl.BlockSpec((tile, w), row) for w in widths]
            + [pl.BlockSpec((2, tile, out_width), lambda i, w: (0, i, 0))],
        ),
        out_shape=[jax.ShapeDtypeStruct((rows, w), F32) for w in widths]
        + [jax.ShapeDtypeStruct((2, rows, out_width), F32)],
        compiler_params=params(),
        cost_estimate=cost(0, 12),
    )(jnp.reshape(core, (1,)).astype(jnp.int32), mine, other)


def finish_experts_kernel(per_core, half, where, *refs):
    mine, came, outs = refs[:per_core], refs[per_core : 2 * per_core], refs[2 * per_core :]
    rows = pl.ds(pl.multiple_of(where[0] * half, 16), half)
    for j in range(per_core):
        for source, at in ((mine, where[0] * per_core + j), ((came), (1 - where[0]) * per_core + j)):
            v = source[j][:, rows, :].astype(F32)
            outs[0][at] = v[0]
            outs[1][at] = v[1]
            outs[2][at] = v[2]


def finish_experts(core, mine, came):
    per_core = len(mine)
    _, rows, hidden = mine[0].shape
    half = rows // 2
    whole = pl.BlockSpec(memory_space=pltpu.VMEM)
    return pl.pallas_call(
        functools.partial(finish_experts_kernel, per_core, half),
        in_specs=[pl.BlockSpec(memory_space=pltpu.SMEM)] + [whole] * (2 * per_core),
        out_shape=[
            jax.ShapeDtypeStruct((2 * per_core, half, hidden), F32),
            jax.ShapeDtypeStruct((2 * per_core, half, hidden), F32),
            jax.ShapeDtypeStruct((2 * per_core, half, hidden), F32),
        ],
        compiler_params=params(),
        cost_estimate=cost(0, 10),
    )(jnp.reshape(core, (1,)), *mine, *came)


def local(
    tokens,
    norm_gain,
    w_query,
    key_weight,
    value_weight,
    w_out,
    ffn_gain,
    w_router,
    w_gate,
    w_up,
    w_down,
    parents,
    routes,
    cotangent,
):
    me = Mesh()
    paired = me.groups == 2
    tok_rows, width = tokens.shape
    tree_len = tok_rows * me.groups
    seg_len = tree_len // 16
    columns = width // me.groups
    all_q, all_k = w_query.shape[1], key_weight.shape[1]
    q_width, k_width = all_q // me.groups, all_k // me.groups
    kv_heads = k_width // HEAD_DIM
    parts = kv_heads // 2 if kv_heads % 2 == 0 else 1
    q_part, k_part = q_width // parts, k_width // parts
    gq, gk = q_part // HEAD_DIM, k_part // HEAD_DIM
    q_room, k_room = pairs(gq) * LANES, pairs(gk) * LANES
    lanes = q_room + 2 * k_room
    experts = w_gate.shape[0] * me.groups
    per_core = w_gate.shape[0] // 2
    partner = 1 - me.member

    def heads_of(member):
        found = []
        for weight, size, room in (
            (w_query, q_width, q_room),
            (key_weight, k_width, k_room),
            (value_weight, k_width, k_room),
        ):
            block = lax.dynamic_slice_in_dim(weight, member * size, size, 1)
            found.append(jnp.pad(block, ((0, 0), (0, room - size))))
        return jnp.concatenate(found, 1)

    projections = (w_query, key_weight, value_weight)
    gain_row = norm_gain[None]
    own, came = [], []
    along = jnp.split(cotangent, 2, 0)
    grad_came = []
    if paired:
        hot = jnp.any(
            routes.T[:, None, :] == jnp.arange(experts, dtype=jnp.int32)[None, :, None], axis=0
        )
        packet = jnp.concatenate(
            [
                w_router.T,
                jnp.pad(ffn_gain[None], ((0, 15), (0, 0))),
                jnp.pad(hot.astype(BF), ((0, 0), (0, columns - tok_rows))),
            ],
            0,
        )
        x_theirs, x_mine, packet_sent, gone = split(me.member, tokens, packet, along[0])
        x_came = me.swap_shard(x_theirs)
        grad_came.append(me.swap_shard(gone))
        packets = [packet_sent, me.swap_shard(packet_sent)]
        *theirs, hidden_first, x_columns, inv_one = project_theirs(
            me.member, parts, x_mine, x_came, gain_row, projections
        )
        came = [me.swap_shard(v) for v in theirs]
        own = project_own(me.member, parts, hidden_first, projections, (theirs[-1],))
    else:
        every_head = jnp.concatenate([heads_of(j) for j in range(me.groups)], 1)
        own_rows = tokens.astype(F32)
        inv_rows = lax.rsqrt(jnp.mean(own_rows * own_rows, axis=-1, keepdims=True) + EPS)
        x_columns = me.exchange(tokens, 1, 0)
        inv_one = me.gather(inv_rows, 0)
        hidden_first = (x_columns.astype(F32) * inv_one * norm_gain.astype(F32)).astype(BF)
        own.append(me.scatter(nn(hidden_first, every_head), 1))
        came.append(jnp.zeros(own[-1].shape, BF))

    gain_two = ffn_gain.astype(F32)

    index = jnp.arange(tree_len, dtype=jnp.int32)
    _, depth = tree_layout(index, seg_len)
    cos, sin = angle_tables(depth)
    visible = tree_mask(index, index, parents[0], seg_len)
    bias = jnp.where(visible, 0.0, -1e30).astype(F32)

    attended, lse, query, key, value, att_came = [], [], [], [], [], []
    for part in range(parts):
        a, b, c, d, e, f = attend(
            own[part], came[part], cos, sin, bias, along[1] if part == parts - 1 else cos, gq, gk
        )
        attended.append(a)
        lse.append(b)
        query.append(c)
        key.append(d)
        value.append(e)
        if paired:
            att_came.append(me.swap_shard(a))
    if paired:
        grad_came.append(me.swap_shard(f))
        mine = [cotangent, me.swap_core(cotangent)]
        others = [*grad_came, *(me.swap_core(v) for v in grad_came)]
        grad_all = jnp.where(
            me.member == 0,
            jnp.concatenate([mine[0], *others[:2], mine[1], *others[2:]], 0),
            jnp.concatenate([*others[:2], mine[0], *others[2:], mine[1]], 0),
        )
        starts = [
            member * q_width + part * q_part
            for member in (me.member, partner)
            for part in range(parts)
        ]
        middle, middle_low, squares = middle_of(
            attended + att_came, jnp.stack(starts).astype(jnp.int32), w_out, x_columns, True
        )
        attended_full = me.in_order(
            me.member, jnp.concatenate(attended, 1), jnp.concatenate(att_came, 1), 1
        )
        messages = [middle_low, me.swap_shard(middle_low)]
        hidden_all, gates_all, inv_two = hidden_packed(
            me.member,
            [
                (*messages, *packets),
                (*(me.swap_core(v) for v in messages), *(me.swap_core(v) for v in packets)),
            ],
        )
    else:
        grad_tree = me.gather(cotangent, 0)
        grad_all = jnp.concatenate([grad_tree, me.swap_core(grad_tree)], 0)
        attended_full = me.gather(attended[0][:, :q_width], 1)
        where = jnp.zeros((1,), jnp.int32)
        middle, middle_low, squares = middle_of([attended_full], where, w_out, x_columns, False)
        route_hot = jnp.any(
            routes[:, :, None] == jnp.arange(experts, dtype=jnp.int32)[None, None, :], axis=1
        ).astype(F32)
        routed = me.gather(route_hot, 0)
        middle_low, squares = me.gather(middle_low, 1), me.total(squares)
        hidden_all, gates_all = hidden_of(
            [
                ([middle_low], [squares], routed),
                (
                    [me.swap_core(middle_low)],
                    [me.swap_core(squares)],
                    me.swap_core(routed),
                ),
            ],
            where,
            me.gather(ffn_gain, 0)[None],
            me.gather(w_router, 0),
        )
        inv_two = lax.rsqrt(squares / width + EPS)
    grad_tree = grad_all[:tree_len]
    gates = gates_all[0]
    hidden_all = hidden_all.reshape(2 * tree_len, width)
    gates_all = gates_all.reshape(2 * tree_len, experts)
    normed_two = middle * inv_two
    hidden_own = (normed_two * gain_two).astype(BF)

    first = me.core * per_core
    chunk = width // me.chips
    def gates_grad(own_columns):
        grad = me.total(own_columns[:tree_len] + me.swap_core(own_columns[tree_len:]))
        return (gates * (grad - jnp.sum(gates * grad, axis=-1, keepdims=True))).astype(BF)

    def output_of(mixed_own, mixed_other, *deps):
        mixed = mixed_own.astype(F32) + me.swap_core(mixed_other).astype(F32)
        placed = lax.dynamic_update_slice_in_dim(
            jnp.zeros((tree_len, width), F32), middle, me.member * columns, 1
        )
        return me.scatter(tie((mixed + placed).astype(BF), deps), 0).astype(BF)

    def input_of(grad_middle, scaled, row_sums):
        normed = x_columns.astype(F32) * inv_one
        grad = grad_middle + inv_one * (scaled - normed * (me.total(row_sums) / width))
        return me.exchange(grad.astype(BF), 0, 1)

    flipped = bias.T
    if not paired:
        before, rings = None, []
        for j in range(per_core):
            before = expert_grads(
                j, per_core, first + j, me.member * (2 * per_core) + first + j,
                hidden_all, grad_all, gates_all, w_gate, w_up, w_down, before, 0, 1, (),
            )
            mid, own_columns, grads = before
            ring = Scatter(me, lambda chip: lax.dynamic_slice_in_dim(grads, chip * chunk, chunk, 1))
            for _ in range(me.chips - 1):
                ring.start()
                ring.finish()
            rings.append(ring.held)
        grad_logits = gates_grad(own_columns)
        (grad_other,) = expert_hidden(first, me.member, mid, 1, w_gate, w_up, None, False, ())
        (grad_own,) = expert_hidden(
            first, me.member, mid, 0, w_gate, w_up, me.swap_core(grad_other), False, ()
        )
        mixed_other = expert_mix(first, mid, 1, w_down, ())
        mixed_own = expert_mix(first, mid, 0, w_down, ())
        result = output_of(mixed_own, mixed_other)
        grad_hidden_two = nt(grad_logits, w_router) + me.scatter(grad_own, 1)
        grad_gain_two = jnp.sum(grad_hidden_two * normed_two, axis=0)[None]
        scaled = grad_hidden_two * gain_two
        mean = me.total(jnp.sum(scaled * normed_two, axis=-1, keepdims=True)) / width
        grad_columns = me.part(grad_tree, 1, me.member).astype(F32)
        grad_middle = grad_columns + inv_two * (scaled - normed_two * mean)
        grad_branch = grad_middle.astype(BF)
        own = me.scatter(nt(grad_branch, w_out), 1)
        own = jnp.pad(own, ((0, 0), (0, q_room - q_width)))
        grad_heads = attend_back(
            own, jnp.zeros(own.shape, BF), query[0], key[0], value[0], lse[0],
            cos, sin, flipped, gq, gk, (),
        )
        grad_out = me.all_reduce(tn(attended_full, grad_branch))
        grad_full = me.gather(grad_heads, 1)
        every = me.all_reduce(tn(hidden_first, grad_full))
        every = every.reshape(columns, me.groups, lanes)
        grad_query, grad_key, grad_value = (
            every[:, :, start : start + size].reshape(columns, me.groups * size)
            for start, size in ((0, q_width), (q_room, k_width), (q_room + k_room, k_width))
        )
        grad_hidden_one = nt(grad_full, every_head)
        normed_one = x_columns.astype(F32) * inv_one
        grad_gain_one = jnp.sum(grad_hidden_one * normed_one, axis=0)[None]
        scaled = grad_hidden_one * norm_gain.astype(F32)
        row_sums = jnp.sum(scaled * normed_one, axis=-1, keepdims=True)
        input_grad = input_of(grad_middle, scaled, row_sums)
        grad_router = tn(hidden_own, grad_logits)
        small = me.butterfly(jnp.concatenate([grad_gain_one, grad_gain_two, grad_router.T], 0))
        sums = rings
        grad_gate, grad_up, grad_down = finish_experts(
            me.core, sums, [me.swap_core(v) for v in sums]
        )
    else:

        def expert(j, before, deps):
            return expert_grads(
                j, per_core, first + j, me.member * (2 * per_core) + first + j,
                hidden_all, grad_all, gates_all, w_gate, w_up, w_down, before, j % 2, 2, deps,
            )

        def ring_of(grads):
            return Scatter(me, lambda chip: lax.dynamic_slice_in_dim(grads, chip * chunk, chunk, 1))

        one = expert(1, expert(0, None, ()), ())
        ring_a = ring_of(one[2])
        ring_a.start()
        two = expert(2, one, ())
        a = ring_a.finish()
        ring_a.start(two[1])
        mid, own_columns, grads = expert(3, two, (a,))
        ring_b = ring_of(grads)
        a = ring_a.finish()
        ring_a.start(own_columns)
        ring_b.start()
        grad_logits = gates_grad(own_columns)
        (grad_other,) = expert_hidden(first, me.member, mid, 1, w_gate, w_up, None, False, (a,))
        a, b = ring_a.finish(), ring_b.finish()
        ring_a.start(grad_other)
        ring_b.start(grad_other)
        grad_mine, grad_theirs = expert_hidden(
            first, me.member, mid, 0, w_gate, w_up, me.swap_core(grad_other), True, (a, b)
        )
        hidden_came = me.swap_shard(grad_theirs)
        a, b = ring_a.finish(), ring_b.finish()
        ring_a.start(grad_mine)
        ring_b.start(grad_mine)
        mixed_other = expert_mix(first, mid, 1, w_down, (grad_mine, a, b))
        mixed_own = expert_mix(first, mid, 0, w_down, (mixed_other, grad_logits))
        scaled, row_sums, grad_gain_two = norm_back(
            grad_mine, hidden_came, grad_logits, w_router, middle, inv_two, ffn_gain[None],
            (mixed_own,),
        )
        sums_came = me.swap_shard(row_sums)
        a = ring_a.finish()
        ring_a.start(scaled)
        grad_middle, grad_branch, *both = branch_back(
            me.member, parts, grad_all, scaled, middle, inv_two, row_sums, sums_came, w_out, (a,)
        )
        came = [me.swap_shard(v) for v in both[:parts]]
        own = both[parts:]
        b = ring_b.finish()
        ring_b.start(grad_branch)
        grad_out = out_grads(
            me.core == me.member,
            [attended + att_came, [me.swap_core(v) for v in attended + att_came]],
            [grad_branch, me.swap_core(grad_branch)],
        )
        a = ring_a.finish()
        ring_a.start(grad_out)
        heads_a = attend_back(
            own[0], came[0], query[0], key[0], value[0], lse[0], cos, sin, flipped, gq, gk,
            (b, a, grad_out),
        )
        back_a = me.swap_shard(heads_a)
        b = ring_b.finish()
        ring_b.start(heads_a)
        heads_b = attend_back(
            own[1], came[1], query[1], key[1], value[1], lse[1], cos, sin, flipped, gq, gk,
            (b, heads_a),
        )
        back_b = me.swap_shard(heads_b)
        a = ring_a.finish()
        grad_pairs = [(heads_a, back_a), (heads_b, back_b)]
        grads_mine = weight_grads(
            me.member,
            me.core,
            (hidden_first, me.swap_core(hidden_first)),
            (grad_pairs, [tuple(me.swap_core(v) for v in pair) for pair in grad_pairs]),
            grad_out,
            (a,),
        )
        head_chunk = grads_mine.shape[0] // me.chips
        ring_w = Scatter(
            me, lambda chip: lax.dynamic_slice_in_dim(grads_mine, chip * head_chunk, head_chunk, 0)
        )
        ring_w.start()
        grad_router = tn(hidden_own, grad_logits)
        beside = {}
        hops = me.chips - 1
        for hop in range(1, 2 * hops):
            w = ring_w.finish()
            if hop == hops:
                ring_w = Gather(me, ring_w.held)
            if hop == 4:
                result = output_of(mixed_own, mixed_other, w)
                beside[12] = (result,)
            if hop == hops:
                scaled, row_sums, grad_gain_one = project_back(
                    me.member, x_columns, inv_one, gain_row, projections, grad_pairs, (w,)
                )
                input_grad = input_of(grad_middle, scaled, row_sums)
                small = me.butterfly(
                    jnp.concatenate([grad_gain_one, grad_gain_two, grad_router.T], 0)
                )
                beside[hop + 1] = (scaled,)
                beside[hop + 4] = (small,)
                beside[hop + 6] = (input_grad,)
            deps = beside.get(hop, ())
            if hop in (1, 3, 5) and ring_b.hops < hops:
                deps = (*deps, ring_b.finish())
                if ring_b.hops < hops:
                    ring_b.start(w)
                else:
                    sums = [h for r in (ring_a, ring_b) for h in jnp.split(r.held, 2, 0)]
                    experts_done = finish_experts(me.core, sums, [me.swap_core(v) for v in sums])
                    beside[hop + 5] = (*beside.get(hop + 5, ()), experts_done[0])
            ring_w.start(*deps)
        ring_w.finish()
        grad_gate, grad_up, grad_down = experts_done
        layout = [
            [
                (out, j * step + part * size, j * lanes + start, size)
                for j in range(2)
                for out, step, start, size in (
                    (0, q_width, 0, q_part),
                    (1, k_width, q_room, k_part),
                    (2, k_width, q_room + k_room, k_part),
                )
            ]
            for part in range(parts)
        ]
        grad_query, grad_key, grad_value, grad_out = finish(
            me.core, ring_w.whole, me.swap_core(ring_w.whole), layout, (all_q, all_k, all_k), columns
        )
        grad_out = grad_out.reshape(-1, columns)

    return (
        result,
        input_grad,
        small[0],
        grad_query,
        grad_key,
        grad_value,
        grad_out,
        small[1],
        small[2:].T,
        grad_gate,
        grad_up,
        grad_down.transpose(0, 2, 1),
    )


def solution(mesh):
    return jax.shard_map(
        local,
        mesh=mesh,
        in_specs=(
            P(("rep", "shard"), None),
            P("shard"),
            P("shard", None),
            P("shard", None),
            P("shard", None),
            P(None, "shard"),
            P("shard"),
            P("shard", None),
            P("shard", None, None),
            P("shard", None, None),
            P("shard", None, None),
            P("rep", None),
            P(("rep", "shard"), None),
            P(("rep", "shard"), None),
        ),
        out_specs=(
            P(("rep", "shard"), None),
            P(("rep", "shard"), None),
            P("shard"),
            P("shard", None),
            P("shard", None),
            P("shard", None),
            P(None, "shard"),
            P("shard"),
            P("shard", None),
            P("shard", "rep", None),
            P("shard", "rep", None),
            P("shard", None, "rep"),
        ),
        check_vma=False,
    )
```

```python
import functools

import jax
import jax.numpy as jnp
from jax import lax
from jax.experimental import pallas as pl
from jax.experimental.pallas import tpu as pltpu
from jax.sharding import PartitionSpec as P

HEAD_DIM = 64
LANES = 128
EPS = 1e-06
BF = jnp.bfloat16
F32 = jnp.float32
VMEM_LIMIT = 60 << 20


def tree_layout(position, seg_len):
    trunk_len = 4 * seg_len
    beyond = position - trunk_len
    segment = jnp.where(position < trunk_len, 0, 1 + beyond // seg_len)
    inner = jnp.where(
        segment <= 4, trunk_len + beyond % seg_len, trunk_len + seg_len + beyond % seg_len
    )
    depth_position = jnp.where(position < trunk_len, position, inner)
    return (segment, depth_position)


def lookup(segment, parents_row):
    labels = jnp.arange(parents_row.shape[0], dtype=jnp.int32)
    picked = jnp.where(segment[:, None] == labels[None, :], parents_row[None, :], 0)
    return jnp.sum(picked, axis=1)


def tree_mask(query_index, key_index, parents_row, seg_len):
    query_seg, _ = tree_layout(query_index, seg_len)
    key_seg, _ = tree_layout(key_index, seg_len)
    parent_one = lookup(query_seg, parents_row)
    parent_two = lookup(parent_one, parents_row)
    key_row = key_seg[None, :]
    related = (
        (key_row == query_seg[:, None])
        | (key_row == parent_one[:, None])
        | (key_row == parent_two[:, None])
    )
    return related & (key_index[None, :] <= query_index[:, None])


def angle_tables(depth_position):
    half = HEAD_DIM // 2
    frequency = 10000.0 ** (-2.0 * jnp.arange(half, dtype=F32) / HEAD_DIM)
    angles = depth_position.astype(F32)[:, None] * frequency[None, :]
    cosine, sine = jnp.cos(angles), jnp.sin(angles)
    return (
        jnp.concatenate([cosine] * 4, 1),
        jnp.concatenate([-sine, sine, -sine, sine], 1),
    )


def dot(a, b, dims):
    return lax.dot_general(a, b, (dims, ((), ())), preferred_element_type=F32)


def nn(a, b):
    return dot(a, b, ((1,), (0,)))


def nt(a, b):
    return dot(a, b, ((1,), (1,)))


def tn(a, b):
    return dot(a, b, ((0,), (0,)))


class Mesh:
    def __init__(self):
        self.groups = lax.axis_size("shard")
        self.member = lax.axis_index("shard")
        self.reps = lax.axis_size("rep")
        self.rep = lax.axis_index("rep")
        self.core = self.rep % 2
        self.chip = self.rep // 2
        self.chips = self.reps // 2
        rows = self.chips // 2
        order = [2 * z for z in range(rows)] + [2 * z + 1 for z in range(rows - 1, -1, -1)]
        self.ring = []
        for place, chip in enumerate(order):
            after, before = order[(place + 1) % self.chips], order[place - 1]
            self.ring += [(2 * chip, 2 * after), (2 * chip + 1, 2 * before + 1)]
        self.place = jnp.where(
            self.chip % 2 == 0, self.chip // 2, self.chips - 1 - self.chip // 2
        )
        self.way = 1 - 2 * self.core

    def chip_at(self, place):
        place = place % self.chips
        rows = self.chips // 2
        return jnp.where(place < rows, 2 * place, 2 * (self.chips - 1 - place) + 1)

    def swap_shard(self, v):
        return lax.ppermute(v, "shard", [(0, 1), (1, 0)])

    def swap_core(self, v):
        return lax.ppermute(v, "rep", [(r, r ^ 1) for r in range(self.reps)])

    def along_ring(self, v):
        return lax.ppermute(v, "rep", self.ring)

    def part(self, v, axis, which):
        size = v.shape[axis] // self.groups
        return lax.dynamic_slice_in_dim(v, which * size, size, axis)

    def gather(self, v, axis):
        if self.groups != 2:
            return lax.all_gather(v, "shard", axis=axis, tiled=True)
        other = self.swap_shard(v)
        return self.in_order(self.member, v, other, axis)

    def in_order(self, which, mine, other, axis):
        return jnp.where(
            which == 0,
            jnp.concatenate([mine, other], axis),
            jnp.concatenate([other, mine], axis),
        )

    def exchange(self, v, split_axis, concat_axis):
        if self.groups != 2:
            return lax.all_to_all(v, "shard", split_axis, concat_axis, tiled=True)
        other = self.swap_shard(self.part(v, split_axis, 1 - self.member))
        mine = self.part(v, split_axis, self.member)
        return self.in_order(self.member, mine, other, concat_axis)

    def scatter(self, v, axis):
        if self.groups != 2:
            return lax.psum_scatter(
                v.astype(BF), "shard", scatter_dimension=axis, tiled=True
            ).astype(F32)
        other = self.swap_shard(self.part(v, axis, 1 - self.member).astype(BF))
        return self.part(v, axis, self.member).astype(F32) + other.astype(F32)

    def total(self, v):
        if self.groups != 2:
            return lax.psum(v, "shard")
        return v + self.swap_shard(v)

    def ring_sum(self, v):
        chunk = v.shape[0] // self.chips
        ring = Scatter(self, lambda chip: lax.dynamic_slice_in_dim(v, chip * chunk, chunk, 0))
        for _ in range(self.chips - 1):
            ring.start()
            ring.finish()
        ring = Gather(self, ring.held)
        for _ in range(self.chips - 1):
            ring.start()
            ring.finish()
        return ring.whole

    def all_reduce(self, v):
        half = v.shape[0] // 2
        v = v.astype(BF)
        mine = lax.dynamic_slice_in_dim(v, self.core * half, half, 0)
        other = self.swap_core(
            lax.dynamic_slice_in_dim(v, (1 - self.core) * half, half, 0)
        )
        whole = self.ring_sum((mine.astype(F32) + other.astype(F32)).astype(BF))
        return self.in_order(self.core, whole, self.swap_core(whole), 0).astype(F32)

    def butterfly(self, v):
        bit = 1
        while bit < self.reps:
            v = v + lax.ppermute(v, "rep", [(r, r ^ bit) for r in range(self.reps)])
            bit *= 2
        return v


class Scatter:
    def __init__(self, me, own):
        self.me, self.own, self.hops = me, own, 0
        self.held = own(me.chip_at(me.place - me.way))

    def start(self, *deps):
        sent = tie(self.held, deps)
        self.came = self.me.along_ring(sent)
        return sent

    def hop(self, *deps):
        self.finish(*deps)
        return self.start()

    def finish(self, *deps):
        self.hops += 1
        self.came = tie(self.came, deps)
        mine = self.own(self.me.chip_at(self.me.place - self.me.way * (self.hops + 1)))
        self.held = (self.came.astype(F32) + mine.astype(F32)).astype(BF)
        return self.came


class Gather:
    def __init__(self, me, held):
        self.me, self.held, self.hops = me, held, 0
        self.size = held.shape[0]
        whole = jnp.zeros((self.size * me.chips, held.shape[1]), held.dtype)
        self.whole = self.put(whole, me.place)

    def put(self, whole, place):
        at = self.me.chip_at(place) * self.size
        return lax.dynamic_update_slice_in_dim(whole, self.held, at, 0)

    def start(self, *deps):
        self.came = self.me.along_ring(tie(self.held, deps))

    def finish(self):
        self.hops += 1
        self.held = self.came
        self.whole = self.put(self.whole, self.me.place - self.me.way * self.hops)
        return self.came


def pairs(heads):
    return -(-heads // 2)


def rope(v, cos, sin, back):
    lane = lax.broadcasted_iota(jnp.int32, (1, LANES), 1)
    first = lane % HEAD_DIM < HEAD_DIM // 2
    out = []
    for i in range(v.shape[1] // LANES):
        x = v[:, i * LANES : (i + 1) * LANES]
        other = jnp.where(
            first,
            pltpu.roll(x, LANES - HEAD_DIM // 2, 1),
            pltpu.roll(x, HEAD_DIM // 2, 1),
        )
        out.append(x * cos - other * sin if back else x * cos + other * sin)
    return out


def halves(x, parity):
    low = lax.broadcasted_iota(jnp.int32, (1, LANES), 1) < HEAD_DIM
    zero = jnp.zeros_like(x)
    turned = pltpu.roll(x, HEAD_DIM, 1)
    a, b = (x, turned) if parity == 0 else (turned, x)
    return jnp.where(low, a, zero).astype(BF), jnp.where(low, zero, b).astype(BF)


def attend_kernel(
    q_heads, kv_heads, own_ref, came_ref, cos_ref, sin_ref, bias_ref, along_ref,
    out_ref, lse_ref, q_ref, k_ref, v_ref, sent_ref,
):
    sent_ref[...] = along_ref[...]
    per = q_heads // kv_heads
    rows = own_ref.shape[0]
    qp, kp = pairs(q_heads), pairs(kv_heads)
    cos, sin = cos_ref[...], sin_ref[...]
    raw = own_ref[...].astype(F32) + came_ref[...].astype(F32)
    scale = HEAD_DIM**-0.5
    q = [(t * scale).astype(BF) for t in rope(raw[:, : qp * LANES], cos, sin, False)]
    keys = rope(raw[:, qp * LANES : (qp + kp) * LANES], cos, sin, False)
    for i in range(qp):
        q_ref[:, i * LANES : (i + 1) * LANES] = q[i]
    ks, vs = [], []
    for g in range(kv_heads):
        at = (qp + kp + g // 2) * LANES
        ks.append(halves(keys[g // 2], g % 2))
        vs.append(halves(raw[:, at : at + LANES], g % 2))
        for p in range(2):
            k_ref[g, p] = ks[g][p]
            v_ref[g, p] = vs[g][p]
    half = rows // 2
    for lo, n in ((0, half), (half, rows)):
        bias = bias_ref[lo : lo + half, :n]
        for i in range(qp):
            out = jnp.zeros((half, LANES), F32)
            for h in range(2 * i, min(2 * i + 2, q_heads)):
                g, p = h // per, h % 2
                s = nt(q[i][lo : lo + half], ks[g][p][:n]) + bias
                peak = jnp.max(s, axis=-1, keepdims=True)
                e = jnp.exp(s - peak)
                total = jnp.sum(e, axis=-1, keepdims=True)
                lse_ref[lo : lo + half, h : h + 1] = peak + jnp.log(total)
                out = out + nn((e * (1.0 / total)).astype(BF), vs[g][p][:n])
            out_ref[lo : lo + half, i * LANES : (i + 1) * LANES] = out.astype(BF)


def attend(own, came, cos, sin, bias, along, q_heads, kv_heads):
    rows = own.shape[0]
    qp = pairs(q_heads)
    return pl.pallas_call(
        functools.partial(attend_kernel, q_heads, kv_heads),
        out_shape=[
            jax.ShapeDtypeStruct((rows, qp * LANES), BF),
            jax.ShapeDtypeStruct((rows, LANES), F32),
            jax.ShapeDtypeStruct((rows, qp * LANES), BF),
            jax.ShapeDtypeStruct((kv_heads, 2, rows, LANES), BF),
            jax.ShapeDtypeStruct((kv_heads, 2, rows, LANES), BF),
            jax.ShapeDtypeStruct(along.shape, along.dtype),
        ],
        compiler_params=pltpu.CompilerParams(vmem_limit_bytes=VMEM_LIMIT),
        cost_estimate=pl.CostEstimate(
            flops=1200 * rows * rows * q_heads,
            bytes_accessed=8 << 20,
            transcendentals=rows * rows * q_heads,
        ),
    )(own, came, cos, sin, bias, along)


def attend_back_kernel(
    q_heads, kv_heads, own_ref, came_ref, q_ref, k_ref, v_ref, lse_ref,
    cos_ref, sin_ref, bias_ref, *refs,
):
    per = q_heads // kv_heads
    rows = own_ref.shape[0]
    qp, kp = pairs(q_heads), pairs(kv_heads)
    cos, sin = cos_ref[...], sin_ref[...]
    scale = HEAD_DIM**-0.5
    low = lax.broadcasted_iota(jnp.int32, (1, LANES), 1) < HEAD_DIM
    grad = (own_ref[...].astype(F32) + came_ref[...].astype(F32)).astype(BF)
    lse = lse_ref[...].T
    half = rows // 2
    out_ref = refs[-1]

    def put(at, v):
        out_ref[:, at * LANES : (at + 1) * LANES] = v.astype(BF)

    def blocks():
        return [
            [[jnp.zeros((half, LANES), F32) for _ in range(2)] for _ in range(2)]
            for _ in range(kv_heads)
        ]

    dk, dv = blocks(), blocks()
    for i in range(qp):
        parts = []
        for lo, n in ((0, half), (half, rows)):
            q = q_ref[lo : lo + half, i * LANES : (i + 1) * LANES]
            go = grad[lo : lo + half, i * LANES : (i + 1) * LANES]
            bias = bias_ref[:n, lo : lo + half]
            dq = jnp.zeros((half, LANES), F32)
            for h in range(2 * i, min(2 * i + 2, q_heads)):
                g, p = h // per, h % 2
                k, v = k_ref[g, p, :n], v_ref[g, p, :n]
                s = nt(k, q) + bias
                probs = jnp.exp(s - lse[h : h + 1, lo : lo + half])
                dp = nt(v, go)
                delta = jnp.sum(probs * dp, axis=0, keepdims=True)
                ds = (probs * (dp - delta)).astype(BF)
                dq = dq + tn(ds, k)
                ck, cv = nn(ds, q), nn(probs.astype(BF), go)
                for b in range(n // half):
                    dk[g][p][b] = dk[g][p][b] + ck[b * half : (b + 1) * half]
                    dv[g][p][b] = dv[g][p][b] + cv[b * half : (b + 1) * half]
            parts.append(dq * scale)
        put(i, rope(jnp.concatenate(parts, 0), cos, sin, True)[0])

    def packed(d, j):
        got = jnp.zeros((rows, LANES), F32)
        for g in range(2 * j, min(2 * j + 2, kv_heads)):
            a, b = (jnp.concatenate(d[g][p], 0) for p in range(2))
            a, b = jnp.where(low, a, 0.0), jnp.where(low, 0.0, b)
            if g % 2 == 0:
                got = got + a + pltpu.roll(b, HEAD_DIM, 1)
            else:
                got = got + b + pltpu.roll(a, HEAD_DIM, 1)
        return got

    for j in range(kp):
        put(qp + j, rope(packed(dk, j), cos, sin, True)[0])
        put(qp + kp + j, packed(dv, j))


def attend_back(own, came, q, k, v, lse, cos, sin, bias, q_heads, kv_heads, deps):
    rows = own.shape[0]
    lanes = (pairs(q_heads) + 2 * pairs(kv_heads)) * LANES
    specs, deps = after(deps)
    return pl.pallas_call(
        functools.partial(attend_back_kernel, q_heads, kv_heads),
        in_specs=[pl.BlockSpec(memory_space=pltpu.VMEM)] * 9 + specs,
        out_shape=jax.ShapeDtypeStruct((rows, lanes), BF),
        compiler_params=pltpu.CompilerParams(vmem_limit_bytes=VMEM_LIMIT),
        cost_estimate=pl.CostEstimate(
            flops=1600 * rows * rows * q_heads,
            bytes_accessed=8 << 20,
            transcendentals=rows * rows * q_heads,
        ),
    )(own, came, q, k, v, lse, cos, sin, bias, *deps)


def after(arrays):
    return [pl.BlockSpec(memory_space=pl.ANY)] * len(arrays), tuple(arrays)


def row_tile(rows):
    return rows if rows <= 896 else 448


def params():
    return pltpu.CompilerParams(vmem_limit_bytes=VMEM_LIMIT)


def cost(flops, megabytes, transcendentals=0):
    return pl.CostEstimate(
        flops=int(flops), bytes_accessed=megabytes << 20, transcendentals=int(transcendentals)
    )


def to_row(column):
    rows = column.shape[0]
    return jnp.broadcast_to(column, (rows, LANES)).T[:1]


def to_column(row):
    return jnp.broadcast_to(row, (LANES, row.shape[1])).T[:, :1]


def put_column(ref, column):
    rows = column.shape[0]
    row = to_row(column)
    high = row.astype(BF)
    low = (row - high.astype(F32)).astype(BF)
    line = lax.broadcasted_iota(jnp.int32, (16, rows), 0)
    ref[rows : rows + 16, :] = jnp.zeros((16, ref.shape[1]), BF)
    ref[rows : rows + 16, :rows] = jnp.where(
        line == 0, high.astype(F32), jnp.where(line == 1, low.astype(F32), 0.0)
    ).astype(BF)


def get_column(ref):
    rows = ref.shape[0] - 16
    last = ref[rows : rows + 16, :rows].astype(F32)
    return to_column(last[0:1] + last[1:2])


def split_kernel(where, x_ref, packet_ref, along_ref, theirs_ref, mine_ref, sent_ref, gone_ref):
    rows, size = x_ref.shape[0], mine_ref.shape[1]
    sent_ref[...] = packet_ref[...]
    gone_ref[...] = along_ref[...]
    x = x_ref[...].astype(F32)
    squares = jnp.sum(x * x, axis=-1, keepdims=True)
    for ref, member in ((theirs_ref, 1 - where[0]), (mine_ref, where[0])):
        ref[:rows, :] = x_ref[:, pl.ds(pl.multiple_of(member * size, LANES), size)]
        put_column(ref, squares)


def split(member, x, packet, along):
    rows, width = x.shape
    out = jax.ShapeDtypeStruct((rows + 16, width // 2), BF)
    return pl.pallas_call(
        split_kernel,
        in_specs=[pl.BlockSpec(memory_space=pltpu.SMEM)]
        + [pl.BlockSpec(memory_space=pltpu.VMEM)] * 3,
        out_shape=[
            out,
            out,
            jax.ShapeDtypeStruct(packet.shape, BF),
            jax.ShapeDtypeStruct(along.shape, BF),
        ],
        compiler_params=params(),
        cost_estimate=cost(0, 2),
    )(jnp.reshape(member, (1,)), x, packet, along)


def heads_product(hidden, member, part, parts, weights):
    found = []
    for w in weights:
        size = w.shape[1] // (2 * parts)
        at = pl.ds(pl.multiple_of((member * parts + part) * size, LANES), size)
        found.append(nn(hidden, w[:, at]))
    return jnp.concatenate(found, 1)


def project_theirs_kernel(parts, where, mine_ref, came_ref, gain_ref, wq, wk, wv, *refs):
    outs, (hidden_ref, x_ref, inv_ref) = refs[:parts], refs[parts:]
    rows, columns = mine_ref.shape[0] - 16, mine_ref.shape[1]
    gain = gain_ref[...].astype(F32)
    for message, member in ((mine_ref, where[0]), (came_ref, 1 - where[0])):
        at = pl.ds(pl.multiple_of(member * rows, 16), rows)
        inv = lax.rsqrt(get_column(message) / (2 * columns) + EPS)
        inv_ref[at, :] = inv
        x = message[:rows, :]
        x_ref[at, :] = x
        hidden_ref[at, :] = (x.astype(F32) * inv * gain).astype(BF)
    for part in range(parts):
        outs[part][...] = heads_product(
            hidden_ref[...], 1 - where[0], part, parts, (wq, wk, wv)
        ).astype(BF)


def project_theirs(member, parts, mine, came, gain, weights):
    rows, columns = 2 * (mine.shape[0] - 16), mine.shape[1]
    lanes = sum(w.shape[1] for w in weights) // (2 * parts)
    return pl.pallas_call(
        functools.partial(project_theirs_kernel, parts),
        in_specs=[pl.BlockSpec(memory_space=pltpu.SMEM)]
        + [pl.BlockSpec(memory_space=pltpu.VMEM)] * 6,
        out_shape=[jax.ShapeDtypeStruct((rows, lanes), BF)] * parts
        + [
            jax.ShapeDtypeStruct((rows, columns), BF),
            jax.ShapeDtypeStruct((rows, columns), BF),
            jax.ShapeDtypeStruct((rows, 1), F32),
        ],
        compiler_params=params(),
        cost_estimate=cost(4 * rows * columns * lanes * parts, 6),
    )(jnp.reshape(member, (1,)), mine, came, gain, *weights)


def project_own_kernel(parts, where, hidden_ref, wq, wk, wv, *refs):
    for part in range(parts):
        refs[part - parts][...] = heads_product(
            hidden_ref[...], where[0], part, parts, (wq, wk, wv)
        )


def project_own(member, parts, hidden, weights, deps):
    rows, columns = hidden.shape
    lanes = sum(w.shape[1] for w in weights) // (2 * parts)
    specs, deps = after(deps)
    return pl.pallas_call(
        functools.partial(project_own_kernel, parts),
        in_specs=[pl.BlockSpec(memory_space=pltpu.SMEM)]
        + [pl.BlockSpec(memory_space=pltpu.VMEM)] * 4
        + specs,
        out_shape=[jax.ShapeDtypeStruct((rows, lanes), F32)] * parts,
        compiler_params=params(),
        cost_estimate=cost(4 * rows * columns * lanes * parts, 6),
    )(jnp.reshape(member, (1,)), hidden, *weights, *deps)


def project_back_kernel(
    parts, where, x_ref, inv_ref, gain_ref, wq_ref, wk_ref, wv_ref, *refs
):
    grads = refs[: 2 * parts]
    scaled_ref, sums_ref, gain_grad_ref = refs[-3:]
    total = jnp.zeros(x_ref.shape, F32)
    for part in range(parts):
        for grad, member in ((grads[2 * part], where[0]), (grads[2 * part + 1], 1 - where[0])):
            start = 0
            for w in (wq_ref, wk_ref, wv_ref):
                size = w.shape[1] // (2 * parts)
                at = pl.ds(pl.multiple_of((member * parts + part) * size, LANES), size)
                total += nt(grad[:, start : start + size], w[:, at])
                start += size
    normed = x_ref[...].astype(F32) * inv_ref[...]
    scaled = total * gain_ref[...].astype(F32)
    scaled_ref[...] = scaled
    sums_ref[...] = jnp.sum(scaled * normed, axis=-1, keepdims=True)
    gain_grad_ref[...] = jnp.sum(total * normed, axis=0, keepdims=True)


def project_back(member, x, inv, gain, weights, grads, deps):
    rows, columns = x.shape
    parts = len(grads)
    flat = [a for pair in grads for a in pair]
    specs, deps = after(deps)
    whole = pl.BlockSpec(memory_space=pltpu.VMEM)
    return pl.pallas_call(
        functools.partial(project_back_kernel, parts),
        in_specs=[pl.BlockSpec(memory_space=pltpu.SMEM)] + [whole] * (6 + len(flat)) + specs,
        out_shape=[
            jax.ShapeDtypeStruct((rows, columns), F32),
            jax.ShapeDtypeStruct((rows, 1), F32),
            jax.ShapeDtypeStruct((1, columns), F32),
        ],
        compiler_params=params(),
        cost_estimate=cost(2 * rows * columns * sum(w.shape[1] for w in weights), 10),
    )(jnp.reshape(member, (1,)), x, inv, gain, *weights, *flat, *deps)


def weight_grads_kernel(where, *refs):
    hidden, out_ref = refs[:2], refs[-1]
    size = refs[2].shape[1]
    out_ref[:, 2 * size :] = refs[10][...]
    for core in range(2):

        @pl.when(where[1] == core)
        def _():
            for i, member in ((0, where[0]), (1, 1 - where[0])):
                total = sum(tn(hidden[t][...], refs[2 + 4 * t + 2 * core + i][...]) for t in range(2))
                at = pl.ds(pl.multiple_of(member * size, LANES), size)
                out_ref[:, at] = total.astype(BF)


def weight_grads(member, core, hidden, grads, beside, deps):
    columns = hidden[0].shape[1]
    flat = [a for tree in grads for pair in tree for a in pair]
    rows, lanes = flat[0].shape
    specs, deps = after(deps)
    return pl.pallas_call(
        weight_grads_kernel,
        in_specs=[pl.BlockSpec(memory_space=pltpu.SMEM)]
        + [pl.BlockSpec(memory_space=pltpu.VMEM)] * (3 + len(flat))
        + specs,
        out_shape=jax.ShapeDtypeStruct((columns, 2 * lanes + beside.shape[1]), BF),
        compiler_params=params(),
        cost_estimate=cost(8 * rows * columns * lanes, 8),
    )(jnp.stack([member, core]), *hidden, *flat, beside, *deps)


def middle_kernel(count, where, *refs):
    pieces, (w_ref, x_ref) = refs[:count], refs[count : count + 2]
    middle_ref, low_ref, squares_ref = refs[-3:]
    total = x_ref[...].astype(F32)
    for i, piece in enumerate(pieces):
        size = piece.shape[1]
        total += nn(piece[...], w_ref[pl.ds(pl.multiple_of(where[i], 64), size), :])
    squares = jnp.sum(total * total, axis=-1, keepdims=True)
    middle_ref[...] = total
    low_ref[: total.shape[0], :] = total.astype(BF)
    squares_ref[...] = squares
    if low_ref.shape[0] > total.shape[0]:
        put_column(low_ref, squares)


def middle_of(pieces, where, w_out, x, packed):
    rows, columns = x.shape
    tile = rows if packed else 448
    more = 16 if packed else 0

    def row(i, w):
        return (i, 0)

    return pl.pallas_call(
        functools.partial(middle_kernel, len(pieces)),
        grid_spec=pltpu.PrefetchScalarGridSpec(
            num_scalar_prefetch=1,
            grid=(rows // tile,),
            in_specs=[pl.BlockSpec((tile, p.shape[1]), row) for p in pieces]
            + [
                pl.BlockSpec(w_out.shape, lambda i, w: (0, 0)),
                pl.BlockSpec((tile, columns), row),
            ],
            out_specs=[
                pl.BlockSpec((tile, columns), row),
                pl.BlockSpec((tile + more, columns), row),
                pl.BlockSpec((tile, 1), row),
            ],
        ),
        out_shape=[
            jax.ShapeDtypeStruct((rows, columns), F32),
            jax.ShapeDtypeStruct((rows + more, columns), BF),
            jax.ShapeDtypeStruct((rows, 1), F32),
        ],
        compiler_params=params(),
        cost_estimate=cost(2 * rows * columns * w_out.shape[0], 6),
    )(where, *pieces, w_out, x)


def hidden_kernel(count, parts, width, where, *refs):
    gain_ref, router_ref = refs[:2]
    h_ref, gates_ref = refs[-2:]
    for tree in range(2):
        mine = refs[2 + tree * (count + parts + 1) :]
        pieces, squares, on = mine[:count], mine[count : count + parts], mine[count + parts][...]
        total = squares[0][...]
        for more in squares[1:]:
            total += more[...]
        inv = lax.rsqrt(total / width + EPS)
        for i, piece in enumerate(pieces):
            size = piece.shape[1]
            at = pl.ds(pl.multiple_of(where[i] * size, LANES), size)
            gain = gain_ref[:, at].astype(F32)
            h_ref[tree, :, at] = (piece[...].astype(F32) * inv * gain).astype(BF)
        logits = jnp.where(on > 0, nn(h_ref[tree], router_ref[...]), -1e30)
        peak = jnp.max(logits, axis=-1, keepdims=True)
        e = jnp.exp(logits - peak) * on
        gates_ref[tree] = e / jnp.sum(e, axis=-1, keepdims=True)


def hidden_of(trees, where, gain, router):
    pieces, squares, on = trees[0]
    rows = on.shape[0]
    width, experts = router.shape
    tile = 448

    def row(i, w):
        return (i, 0)

    def all_of(i, w):
        return (0, 0)

    def both(i, w):
        return (0, i, 0)

    specs = [pl.BlockSpec((tile, p.shape[1]), row) for p in (*pieces, *squares, on)]
    return pl.pallas_call(
        functools.partial(hidden_kernel, len(pieces), len(squares), width),
        grid_spec=pltpu.PrefetchScalarGridSpec(
            num_scalar_prefetch=1,
            grid=(rows // tile,),
            in_specs=[pl.BlockSpec((1, width), all_of), pl.BlockSpec((width, experts), all_of)]
            + specs
            + specs,
            out_specs=[
                pl.BlockSpec((2, tile, width), both),
                pl.BlockSpec((2, tile, experts), both),
            ],
        ),
        out_shape=[
            jax.ShapeDtypeStruct((2, rows, width), BF),
            jax.ShapeDtypeStruct((2, rows, experts), F32),
        ],
        compiler_params=params(),
        cost_estimate=cost(4 * rows * width * 256, 8, rows * 32),
    )(where, gain, router, *(a for p, q, o in trees for a in (*p, *q, o)))


PACKET_ROWS = 48


def hidden_packed_kernel(where, *refs):
    h_ref, gates_ref, slots_ref, inv_ref, on_ref = refs[8:]
    count = refs[0].shape[0] // 2 - 8
    before = (
        lax.broadcasted_iota(jnp.int32, (count, count), 0)
        < lax.broadcasted_iota(jnp.int32, (count, count), 1)
    )
    before = jnp.where(before, 1.0, 0.0).astype(BF)
    member = (where[0], 1 - where[0])
    for tree in range(2):
        messages, packets = refs[4 * tree : 4 * tree + 2], refs[4 * tree + 2 : 4 * tree + 4]
        rows, columns = messages[0].shape[0] - 16, messages[0].shape[1]
        squares = get_column(messages[0]) + get_column(messages[1])
        inv = lax.rsqrt(squares / (2 * columns) + EPS)
        if tree == 0:
            inv_ref[...] = inv
        logits = 0.0
        for i in range(2):
            at = pl.ds(pl.multiple_of(member[i] * columns, LANES), columns)
            gain = packets[i][16:32, :].astype(F32)[:1]
            h = (messages[i][:rows, :].astype(F32) * inv * gain).astype(BF)
            h_ref[tree, :, at] = h
            logits = logits + nt(h, packets[i][:16, :])
            tokens = rows // 2
            on_ref[pl.ds(pl.multiple_of(member[i] * tokens, 16), tokens), :] = (
                packets[i][32:48, :tokens].astype(F32).T
            )
        on = on_ref[...]
        logits = jnp.where(on > 0, logits, -1e30)
        peak = jnp.max(logits, axis=-1, keepdims=True)
        e = jnp.exp(logits - peak) * on
        gates = (e / jnp.sum(e, axis=-1, keepdims=True)).T
        for i in range(2):
            at = gates[:, i * count : (i + 1) * count]
            gates_ref[2 * tree + i] = at
            routed = jnp.where(at > 0.0, 1.0, 0.0).astype(BF)
            slots_ref[2 * tree + i] = nn(routed, before).astype(jnp.int32)


def hidden_packed(member, trees):
    rows, columns = trees[0][0].shape[0] - 16, trees[0][0].shape[1]
    return pl.pallas_call(
        hidden_packed_kernel,
        in_specs=[pl.BlockSpec(memory_space=pltpu.SMEM)]
        + [pl.BlockSpec(memory_space=pltpu.VMEM)] * 8,
        out_shape=[
            jax.ShapeDtypeStruct((2, rows, 2 * columns), BF),
            jax.ShapeDtypeStruct((4, 16, rows // 2), F32),
            jax.ShapeDtypeStruct((4, 16, rows // 2), jnp.int32),
            jax.ShapeDtypeStruct((rows, 1), F32),
        ],
        scratch_shapes=[pltpu.VMEM((rows, 16), F32)],
        compiler_params=params(),
        cost_estimate=cost(4 * rows * columns * 256, 8),
    )(jnp.reshape(member, (1,)), *(a for tree in trees for a in tree))


def expert_grads_kernel(
    chained, steps, where, h_ref, g_ref, on_ref, wg_ref, wu_ref, wd_ref, *refs
):
    mid_ref, gg_ref, own_ref = refs[-3:] if steps == 1 else refs[-4:-1]
    step = pl.program_id(0)
    h, g = h_ref[...], g_ref[...]
    lane = lax.broadcasted_iota(jnp.int32, (1, on_ref.shape[1]), 1) == where[1]
    on = jnp.sum(jnp.where(lane, on_ref[...], 0.0), axis=-1, keepdims=True)
    gate_pre = nn(h, wg_ref[0])
    up_pre = nn(h, wu_ref[0])
    grad_mid = nt(g, wd_ref[0])
    sig = 1.0 / (1.0 + jnp.exp(-gate_pre))
    silu = gate_pre * sig
    mid = silu * up_pre
    column = jnp.where(lane, jnp.sum(grad_mid * mid, axis=-1, keepdims=True), 0.0)
    gg_ref[...] = refs[0][...] + column if chained else column
    act = (on * mid).astype(BF)
    grad_mid = on * grad_mid
    ggp = (grad_mid * up_pre * (sig * (1.0 + gate_pre * (1.0 - sig)))).astype(BF)
    gup = (grad_mid * silu).astype(BF)
    mid_ref[0, 0] = act
    mid_ref[0, 1] = ggp
    mid_ref[0, 2] = gup
    if steps == 1:
        own_ref[0] = tn(h, ggp).astype(BF)
        own_ref[1] = tn(h, gup).astype(BF)
        own_ref[2] = tn(g, act).astype(BF)
        return
    acc = refs[-1]

    @pl.when(step == 0)
    def _():
        acc[...] = jnp.zeros_like(acc)

    acc[0] += tn(h, ggp)
    acc[1] += tn(h, gup)
    acc[2] += tn(g, act)

    @pl.when(step == steps - 1)
    def _():
        own_ref[...] = acc[...].astype(BF)


def expert_grads(
    j, per_core, which, column, h, g, on, w_gate, w_up, w_down, before, slot, slots, deps
):
    rows, width = h.shape
    hidden = w_gate.shape[2]
    experts = on.shape[1]
    tile = row_tile(rows)
    steps = rows // tile

    def row(i, w):
        return (i, 0)

    def weight(i, w):
        return (w[0], 0, 0)

    chained = before is not None
    more = [pl.BlockSpec((tile, experts), row), pl.BlockSpec(memory_space=pl.ANY)] * chained
    aliases = {8: 0} if chained else {}
    if slot:
        aliases[9] = 2
        deps = (before[2], *deps)
    specs, deps = after(deps)
    return pl.pallas_call(
        functools.partial(expert_grads_kernel, chained, steps),
        grid_spec=pltpu.PrefetchScalarGridSpec(
            num_scalar_prefetch=1,
            grid=(steps,),
            in_specs=[
                pl.BlockSpec((tile, width), row),
                pl.BlockSpec((tile, width), row),
                pl.BlockSpec((tile, experts), row),
                pl.BlockSpec((1, width, hidden), weight),
                pl.BlockSpec((1, width, hidden), weight),
                pl.BlockSpec((1, hidden, width), weight),
            ]
            + more
            + specs,
            out_specs=[
                pl.BlockSpec((1, 3, tile, hidden), lambda i, w: (j, 0, i, 0)),
                pl.BlockSpec((tile, experts), row),
                pl.BlockSpec((3, width, hidden), lambda i, w: (slot, 0, 0)),
            ],
            scratch_shapes=[pltpu.VMEM((3, width, hidden), F32)] * (steps > 1),
        ),
        out_shape=[
            jax.ShapeDtypeStruct((per_core, 3, rows, hidden), BF),
            jax.ShapeDtypeStruct((rows, experts), F32),
            jax.ShapeDtypeStruct((3 * slots, width, hidden), BF),
        ],
        input_output_aliases=aliases,
        compiler_params=params(),
        cost_estimate=cost(16 * rows * width * hidden, 20, rows * hidden),
    )(
        jnp.stack([which, column]).astype(jnp.int32),
        h, g, on, w_gate, w_up, w_down,
        *((before[1], before[0]) if chained else ()),
        *deps,
    )


def expert_hidden_kernel(given, split, where, gate_ref, up_ref, wg_ref, wu_ref, *refs):
    e, count = pl.program_id(1), pl.num_programs(1)
    acc = refs[-1]
    part = nt(gate_ref[0, 0], wg_ref[0]) + nt(up_ref[0, 0], wu_ref[0])

    @pl.when(e == 0)
    def _():
        acc[...] = part + refs[0][...].astype(F32) if given else part

    @pl.when(e > 0)
    def _():
        acc[...] += part

    @pl.when(e == count - 1)
    def _():
        if not split:
            refs[-2][...] = acc[...].astype(BF)
            return
        size = refs[-2].shape[1]
        for out, member in ((refs[-3], where[1]), (refs[-2], 1 - where[1])):
            at = pl.ds(pl.multiple_of(member * size, LANES), size)
            out[...] = acc[:, at].astype(BF)


def expert_hidden(first, member, mid, tree, w_gate, w_up, came, split, deps):
    count, _, rows, hidden = mid.shape
    width = w_gate.shape[1]
    rows //= 2
    tile = 448
    tiles = rows // tile

    def weight(i, e, f):
        return (f[0] + e, 0, 0)

    def row(i, e, f):
        return (i, 0)

    given = [came] if came is not None else []
    specs, deps = after(deps)
    outs = 2 if split else 1
    return pl.pallas_call(
        functools.partial(expert_hidden_kernel, bool(given), split),
        grid_spec=pltpu.PrefetchScalarGridSpec(
            num_scalar_prefetch=1,
            grid=(tiles, count),
            in_specs=[
                pl.BlockSpec((1, 1, tile, hidden), lambda i, e, f: (e, 1, tree * tiles + i, 0)),
                pl.BlockSpec((1, 1, tile, hidden), lambda i, e, f: (e, 2, tree * tiles + i, 0)),
                pl.BlockSpec((1, width, hidden), weight),
                pl.BlockSpec((1, width, hidden), weight),
            ]
            + [pl.BlockSpec((tile, width), row) for _ in given]
            + specs,
            out_specs=[pl.BlockSpec((tile, width // outs), row)] * outs,
            scratch_shapes=[pltpu.VMEM((tile, width), F32)],
        ),
        out_shape=[jax.ShapeDtypeStruct((rows, width // outs), BF)] * outs,
        compiler_params=params(),
        cost_estimate=cost(6 * count * rows * width * hidden, 20),
    )(jnp.stack([first, member]).astype(jnp.int32), mid, mid, w_gate, w_up, *given, *deps)


def expert_mix_kernel(first, mid_ref, wd_ref, *refs):
    e, count = pl.program_id(1), pl.num_programs(1)
    acc = refs[-1]
    part = nn(mid_ref[0, 0], wd_ref[0])

    @pl.when(e == 0)
    def _():
        acc[...] = part

    @pl.when(e > 0)
    def _():
        acc[...] += part

    @pl.when(e == count - 1)
    def _():
        refs[-2][...] = acc[...].astype(BF)


def expert_mix(first, mid, tree, w_down, deps):
    count, _, rows, hidden = mid.shape
    width = w_down.shape[2]
    rows //= 2
    tile = 448
    tiles = rows // tile
    specs, deps = after(deps)
    return pl.pallas_call(
        expert_mix_kernel,
        grid_spec=pltpu.PrefetchScalarGridSpec(
            num_scalar_prefetch=1,
            grid=(tiles, count),
            in_specs=[
                pl.BlockSpec((1, 1, tile, hidden), lambda i, e, f: (e, 0, tree * tiles + i, 0)),
                pl.BlockSpec((1, hidden, width), lambda i, e, f: (f[0] + e, 0, 0)),
            ]
            + specs,
            out_specs=pl.BlockSpec((tile, width), lambda i, e, f: (i, 0)),
            scratch_shapes=[pltpu.VMEM((tile, width), F32)],
        ),
        out_shape=jax.ShapeDtypeStruct((rows, width), BF),
        compiler_params=params(),
        cost_estimate=cost(3 * count * rows * width * hidden, 10),
    )(jnp.reshape(first, (1,)).astype(jnp.int32), mid, w_down, *deps)


def out_grads_kernel(parts, where, *refs):
    branch, out_ref = refs[4 * parts : 4 * parts + 2], refs[-1]
    for own in range(2):

        @pl.when(where[0] == own)
        def _():
            for part in range(parts):
                at = (1 - own) * parts + part
                total = sum(
                    tn(refs[2 * parts * t + at][...], branch[t][...]) for t in range(2)
                )
                size = total.shape[0]
                out_ref[part * size : (part + 1) * size, :] = total.astype(BF)


def out_grads(own, attended, branch, deps):
    parts = len(attended[0]) // 2
    size, columns = attended[0][0].shape[1], branch[0].shape[1]
    specs, deps = after(deps)
    return pl.pallas_call(
        functools.partial(out_grads_kernel, parts),
        in_specs=[pl.BlockSpec(memory_space=pltpu.SMEM)]
        + [pl.BlockSpec(memory_space=pltpu.VMEM)] * (4 * parts + 2)
        + specs,
        out_shape=jax.ShapeDtypeStruct((parts * size, columns), BF),
        compiler_params=params(),
        cost_estimate=cost(4 * branch[0].shape[0] * columns * size * parts, 8),
    )(jnp.reshape(own, (1,)).astype(jnp.int32), *attended[0], *attended[1], *branch, *deps)


def tie_kernel(*refs):
    pass


def tie(v, deps):
    if not deps:
        return v
    specs, deps = after((v, *deps))
    return pl.pallas_call(
        tie_kernel,
        in_specs=specs,
        out_specs=pl.BlockSpec(memory_space=pl.ANY),
        out_shape=jax.ShapeDtypeStruct(v.shape, v.dtype),
        input_output_aliases={0: 0},
        cost_estimate=cost(0, 0),
    )(*deps)


def norm_back_kernel(
    mine_ref, came_ref, logits_ref, router_ref, middle_ref, inv_ref, gain_ref, *refs
):
    scaled_ref, sums_ref, gain_grad_ref = refs[-3:]
    total = mine_ref[...].astype(F32) + came_ref[...].astype(F32)
    total += nt(logits_ref[...], router_ref[...])
    normed = middle_ref[...] * inv_ref[...]
    scaled = total * gain_ref[...].astype(F32)
    scaled_ref[...] = scaled
    sums_ref[...] = jnp.sum(scaled * normed, axis=-1, keepdims=True)
    gain_grad_ref[...] = jnp.sum(total * normed, axis=0, keepdims=True)


def norm_back(mine, came, logits, router, middle, inv, gain, deps):
    rows, columns = middle.shape
    specs, deps = after(deps)
    return pl.pallas_call(
        norm_back_kernel,
        in_specs=[pl.BlockSpec(memory_space=pltpu.VMEM)] * 7 + specs,
        out_shape=[
            jax.ShapeDtypeStruct((rows, columns), F32),
            jax.ShapeDtypeStruct((rows, 1), F32),
            jax.ShapeDtypeStruct((1, columns), F32),
        ],
        compiler_params=params(),
        cost_estimate=cost(512 * rows * columns, 6),
    )(mine, came, logits, router, middle, inv, gain, *deps)


def branch_kernel(parts, where, grad_ref, scaled_ref, middle_ref, inv_ref, m_ref, c_ref, w_ref, *refs):
    full_ref, low_ref = refs[-2 - 2 * parts : -2 * parts]
    theirs, own = refs[-2 * parts : -parts], refs[-parts:]
    columns = middle_ref.shape[1]
    inv = inv_ref[...]
    mean = (m_ref[...] + c_ref[...]) / (2 * columns)
    at = pl.ds(pl.multiple_of(where[0] * columns, LANES), columns)
    grad = grad_ref[:, at].astype(F32)
    grad += inv * (scaled_ref[...] - middle_ref[...] * inv * mean)
    full_ref[...] = grad
    low = grad.astype(BF)
    low_ref[...] = low
    for outs, member in ((theirs, 1 - where[0]), (own, where[0])):
        for part in range(parts):
            size = outs[part].shape[1]
            rows = pl.ds(pl.multiple_of((member * parts + part) * size, 16), size)
            outs[part][...] = nt(low, w_ref[rows, :]).astype(outs[part].dtype)


def branch_back(member, parts, grad, scaled, middle, inv, sums_mine, sums_came, w_out, deps):
    rows, columns = middle.shape
    size = w_out.shape[0] // (2 * parts)
    specs, deps = after(deps)
    vmem = pl.BlockSpec(memory_space=pltpu.VMEM)
    first = pl.BlockSpec((rows, grad.shape[1]), lambda i: (0, 0))
    outs = [
        jax.ShapeDtypeStruct((rows, columns), F32),
        jax.ShapeDtypeStruct((rows, columns), BF),
        *[jax.ShapeDtypeStruct((rows, size), BF)] * parts,
        *[jax.ShapeDtypeStruct((rows, size), F32)] * parts,
    ]
    return pl.pallas_call(
        functools.partial(branch_kernel, parts),
        grid=(1,),
        in_specs=[pl.BlockSpec(memory_space=pltpu.SMEM), first] + [vmem] * 6 + specs,
        out_specs=[pl.BlockSpec(o.shape, lambda i: (0, 0)) for o in outs],
        out_shape=outs,
        compiler_params=params(),
        cost_estimate=cost(2 * rows * columns * w_out.shape[0], 10),
    )(
        jnp.reshape(member, (1,)),
        grad, scaled, middle, inv, sums_mine, sums_came, w_out, *deps,
    )


SLOTS = 128


def picked(gates_ref, slots_ref, block, expert):
    gates = gates_ref[block, pl.ds(expert, 1), :]
    slots = slots_ref[block, pl.ds(expert, 1), :]
    slot = lax.broadcasted_iota(jnp.int32, (SLOTS, gates.shape[1]), 0)
    return (slot == slots) & (gates > 0.0), gates


def one_hot(hit):
    return jnp.where(hit, 1.0, 0.0).astype(BF)


def expert_pair_kernel(
    chained, where, h_ref, g_ref, gates_ref, slots_ref, wg_ref, wu_ref, wd_ref, *refs
):
    mid_ref, gg_ref, own_ref, he_ref, ge_ref = refs[-5:]
    step = pl.program_id(0)
    expert = where[1] + step

    @pl.when(step == 0)
    def _():
        gg_ref[...] = refs[0][...] if chained else jnp.zeros_like(gg_ref)

    count = gates_ref.shape[2]
    hits, scales = [], []
    for b in range(4):
        hit, gates = picked(gates_ref, slots_ref, b, expert)
        pick = one_hot(hit)
        to = slice(b * SLOTS, (b + 1) * SLOTS)
        at = slice(b * count, (b + 1) * count)
        he_ref[to, :] = nn(pick, h_ref[at, :]).astype(BF)
        ge_ref[to, :] = nn(pick, g_ref[at, :]).astype(BF)
        hits.append(hit)
        scales.append(jnp.sum(jnp.where(hit, gates, 0.0), axis=-1, keepdims=True))
    on = jnp.concatenate(scales, 0)
    h, g = he_ref[...], ge_ref[...]
    gate_pre = nn(h, wg_ref[0])
    up_pre = nn(h, wu_ref[0])
    grad_mid = nt(g, wd_ref[0])
    sig = 1.0 / (1.0 + jnp.exp(-gate_pre))
    silu = gate_pre * sig
    mid = silu * up_pre
    column = jnp.sum(grad_mid * mid, axis=-1, keepdims=True)
    for b in range(4):
        part = jnp.where(hits[b], column[b * SLOTS : (b + 1) * SLOTS], 0.0)
        gg_ref[b, pl.ds(expert, 1), :] = jnp.sum(part, axis=0, keepdims=True)
    act = (on * mid).astype(BF)
    grad_mid = on * grad_mid
    ggp = (grad_mid * up_pre * (sig * (1.0 + gate_pre * (1.0 - sig)))).astype(BF)
    gup = (grad_mid * silu).astype(BF)
    mid_ref[0, 0] = act
    mid_ref[0, 1] = ggp
    mid_ref[0, 2] = gup
    own_ref[0] = tn(h, ggp).astype(BF)
    own_ref[1] = tn(h, gup).astype(BF)
    own_ref[2] = tn(g, act).astype(BF)


def expert_pair(pair, per_core, first, column, h, g, gates, slots, w_gate, w_up, w_down, before, deps):
    rows, width = h.shape
    hidden = w_gate.shape[2]

    def all_of(i, w):
        return (0, 0)

    def every(i, w):
        return (0, 0, 0)

    def weight(i, w):
        return (w[0] + i, 0, 0)

    chained = before is not None
    more = [pl.BlockSpec(gates.shape, every), pl.BlockSpec(memory_space=pl.ANY)] * chained
    specs, deps = after(deps)
    return pl.pallas_call(
        functools.partial(expert_pair_kernel, chained),
        grid_spec=pltpu.PrefetchScalarGridSpec(
            num_scalar_prefetch=1,
            grid=(2,),
            in_specs=[
                pl.BlockSpec((rows, width), all_of),
                pl.BlockSpec((rows, width), all_of),
                pl.BlockSpec(gates.shape, every),
                pl.BlockSpec(gates.shape, every),
                pl.BlockSpec((1, width, hidden), weight),
                pl.BlockSpec((1, width, hidden), weight),
                pl.BlockSpec((1, hidden, width), weight),
            ]
            + more
            + specs,
            out_specs=[
                pl.BlockSpec((1, 3, 4 * SLOTS, hidden), lambda i, w: (2 * pair + i, 0, 0, 0)),
                pl.BlockSpec(gates.shape, every),
                pl.BlockSpec((3, width, hidden), lambda i, w: (i, 0, 0)),
            ],
            scratch_shapes=[pltpu.VMEM((4 * SLOTS, width), BF)] * 2,
        ),
        out_shape=[
            jax.ShapeDtypeStruct((per_core, 3, 4 * SLOTS, hidden), BF),
            jax.ShapeDtypeStruct(gates.shape, F32),
            jax.ShapeDtypeStruct((6, width, hidden), BF),
        ],
        input_output_aliases={9: 0} if chained else {},
        compiler_params=params(),
        cost_estimate=cost(24 * 4 * SLOTS * width * hidden, 24, rows * hidden),
    )(
        jnp.stack([first, column]).astype(jnp.int32),
        h, g, gates, slots, w_gate, w_up, w_down,
        *((before[1], before[0]) if chained else ()),
        *deps,
    )


def add_picked(acc, tree, column, gates_ref, slots_ref, outs):
    step, steps = pl.program_id(0), pl.num_programs(0)
    count = gates_ref.shape[2]
    for b in range(2):
        pick = jnp.concatenate(
            [
                one_hot(picked(gates_ref, slots_ref, 2 * tree + b, column + 2 * step + i)[0])
                for i in range(2)
            ],
            0,
        )
        rows = jnp.concatenate([out[b * SLOTS : (b + 1) * SLOTS] for out in outs], 0)
        at = slice(b * count, (b + 1) * count)
        acc[at, :] += tn(pick, rows)


def pair_hidden_kernel(given, tree, where, gates_ref, slots_ref, gp_ref, up_ref, wg_ref, wu_ref, *refs):
    step, acc = pl.program_id(0), refs[-1]

    @pl.when(step == 0)
    def _():
        acc[...] = refs[0][...].astype(F32) if given else jnp.zeros_like(acc)

    outs = [
        (nt(gp_ref[i, 0], wg_ref[i]) + nt(up_ref[i, 0], wu_ref[i])).astype(BF) for i in range(2)
    ]
    add_picked(acc, tree, where[1], gates_ref, slots_ref, outs)

    @pl.when(step == pl.num_programs(0) - 1)
    def _():
        if not given:
            refs[-2][...] = acc[...].astype(BF)
            return
        size = refs[-2].shape[1]
        for out, member in ((refs[-3], where[2]), (refs[-2], 1 - where[2])):
            at = pl.ds(pl.multiple_of(member * size, LANES), size)
            out[...] = acc[:, at].astype(BF)


def pair_hidden(first, column, member, tree, gates, slots, mid, w_gate, w_up, came, deps):
    count, _, rows, hidden = mid.shape
    width = w_gate.shape[1]
    tokens = 2 * gates.shape[2]
    given = [came] if came is not None else []

    def weight(i, w):
        return (w[0] + i, 0, 0)

    def every(i, w):
        return (0, 0, 0)

    def all_of(i, w):
        return (0, 0)

    specs, deps = after(deps)
    outs = 1 + len(given)
    return pl.pallas_call(
        functools.partial(pair_hidden_kernel, bool(given), tree),
        grid_spec=pltpu.PrefetchScalarGridSpec(
            num_scalar_prefetch=1,
            grid=(count // 2,),
            in_specs=[
                pl.BlockSpec(gates.shape, every),
                pl.BlockSpec(gates.shape, every),
                pl.BlockSpec((2, 1, rows // 2, hidden), lambda i, w: (i, 1, tree, 0)),
                pl.BlockSpec((2, 1, rows // 2, hidden), lambda i, w: (i, 2, tree, 0)),
                pl.BlockSpec((2, width, hidden), weight),
                pl.BlockSpec((2, width, hidden), weight),
            ]
            + [pl.BlockSpec((tokens, width), all_of) for _ in given]
            + specs,
            out_specs=[pl.BlockSpec((tokens, width // outs), all_of)] * outs,
            scratch_shapes=[pltpu.VMEM((tokens, width), F32)],
        ),
        out_shape=[jax.ShapeDtypeStruct((tokens, width // outs), BF)] * outs,
        compiler_params=params(),
        cost_estimate=cost(6 * count * rows * width * hidden, 16),
    )(
        jnp.stack([first // 2, column, member]).astype(jnp.int32),
        gates, slots, mid, mid, w_gate, w_up, *given, *deps,
    )


def pair_mix_kernel(tree, where, gates_ref, slots_ref, act_ref, wd_ref, *refs):
    step, acc = pl.program_id(0), refs[-1]

    @pl.when(step == 0)
    def _():
        acc[...] = jnp.zeros_like(acc)

    outs = [nn(act_ref[i, 0], wd_ref[i]).astype(BF) for i in range(2)]
    add_picked(acc, tree, where[1], gates_ref, slots_ref, outs)

    @pl.when(step == pl.num_programs(0) - 1)
    def _():
        refs[-2][...] = acc[...].astype(BF)


def pair_mix(first, column, tree, gates, slots, mid, w_down, deps):
    count, _, rows, hidden = mid.shape
    width = w_down.shape[2]
    tokens = 2 * gates.shape[2]

    def every(i, w):
        return (0, 0, 0)

    specs, deps = after(deps)
    return pl.pallas_call(
        functools.partial(pair_mix_kernel, tree),
        grid_spec=pltpu.PrefetchScalarGridSpec(
            num_scalar_prefetch=1,
            grid=(count // 2,),
            in_specs=[
                pl.BlockSpec(gates.shape, every),
                pl.BlockSpec(gates.shape, every),
                pl.BlockSpec((2, 1, rows // 2, hidden), lambda i, w: (i, 0, tree, 0)),
                pl.BlockSpec((2, hidden, width), lambda i, w: (w[0] + i, 0, 0)),
            ]
            + specs,
            out_specs=pl.BlockSpec((tokens, width), lambda i, w: (0, 0)),
            scratch_shapes=[pltpu.VMEM((tokens, width), F32)],
        ),
        out_shape=jax.ShapeDtypeStruct((tokens, width), BF),
        compiler_params=params(),
        cost_estimate=cost(3 * count * rows * width * hidden, 10),
    )(jnp.stack([first // 2, column]).astype(jnp.int32), gates, slots, mid, w_down, *deps)


def finish_kernel(layout, where, *refs):
    outs, last = refs[2:-1], refs[-1]
    for g in range(2):
        for out, to, start, size in layout[g]:
            at = slice(start, start + size)
            v = jnp.where(where[0] == g, refs[0][:, at], refs[1][:, at])
            outs[out][:, to : to + size] = v.astype(F32)
    start = refs[0].shape[1] - last.shape[2]
    last[where[0]] = refs[0][:, start:].astype(F32)
    last[1 - where[0]] = refs[1][:, start:].astype(F32)


def finish(core, mine, other, layout, widths, out_width):
    rows, columns = mine.shape
    tile = rows // 4

    def row(i, w):
        return (i, 0)

    return pl.pallas_call(
        functools.partial(finish_kernel, layout),
        grid_spec=pltpu.PrefetchScalarGridSpec(
            num_scalar_prefetch=1,
            grid=(4,),
            in_specs=[pl.BlockSpec((tile, columns), row)] * 2,
            out_specs=[pl.BlockSpec((tile, w), row) for w in widths]
            + [pl.BlockSpec((2, tile, out_width), lambda i, w: (0, i, 0))],
        ),
        out_shape=[jax.ShapeDtypeStruct((rows, w), F32) for w in widths]
        + [jax.ShapeDtypeStruct((2, rows, out_width), F32)],
        compiler_params=params(),
        cost_estimate=cost(0, 12),
    )(jnp.reshape(core, (1,)).astype(jnp.int32), mine, other)


def finish_experts_kernel(per_core, half, where, *refs):
    mine, came, outs = refs[:per_core], refs[per_core : 2 * per_core], refs[2 * per_core :]
    rows = pl.ds(pl.multiple_of(where[0] * half, 16), half)
    for j in range(per_core):
        for source, at in ((mine, where[0] * per_core + j), ((came), (1 - where[0]) * per_core + j)):
            v = source[j][:, rows, :].astype(F32)
            outs[0][at] = v[0]
            outs[1][at] = v[1]
            outs[2][at] = v[2]


def finish_experts(core, mine, came):
    per_core = len(mine)
    _, rows, hidden = mine[0].shape
    half = rows // 2
    whole = pl.BlockSpec(memory_space=pltpu.VMEM)
    return pl.pallas_call(
        functools.partial(finish_experts_kernel, per_core, half),
        in_specs=[pl.BlockSpec(memory_space=pltpu.SMEM)] + [whole] * (2 * per_core),
        out_shape=[
            jax.ShapeDtypeStruct((2 * per_core, half, hidden), F32),
            jax.ShapeDtypeStruct((2 * per_core, half, hidden), F32),
            jax.ShapeDtypeStruct((2 * per_core, half, hidden), F32),
        ],
        compiler_params=params(),
        cost_estimate=cost(0, 10),
    )(jnp.reshape(core, (1,)), *mine, *came)


def local(
    tokens,
    norm_gain,
    w_query,
    key_weight,
    value_weight,
    w_out,
    ffn_gain,
    w_router,
    w_gate,
    w_up,
    w_down,
    parents,
    routes,
    cotangent,
):
    me = Mesh()
    paired = me.groups == 2
    tok_rows, width = tokens.shape
    tree_len = tok_rows * me.groups
    seg_len = tree_len // 16
    columns = width // me.groups
    all_q, all_k = w_query.shape[1], key_weight.shape[1]
    q_width, k_width = all_q // me.groups, all_k // me.groups
    kv_heads = k_width // HEAD_DIM
    parts = kv_heads // 2 if kv_heads % 2 == 0 else 1
    q_part, k_part = q_width // parts, k_width // parts
    gq, gk = q_part // HEAD_DIM, k_part // HEAD_DIM
    q_room, k_room = pairs(gq) * LANES, pairs(gk) * LANES
    lanes = q_room + 2 * k_room
    experts = w_gate.shape[0] * me.groups
    per_core = w_gate.shape[0] // 2
    partner = 1 - me.member

    def heads_of(member):
        found = []
        for weight, size, room in (
            (w_query, q_width, q_room),
            (key_weight, k_width, k_room),
            (value_weight, k_width, k_room),
        ):
            block = lax.dynamic_slice_in_dim(weight, member * size, size, 1)
            found.append(jnp.pad(block, ((0, 0), (0, room - size))))
        return jnp.concatenate(found, 1)

    projections = (w_query, key_weight, value_weight)
    gain_row = norm_gain[None]
    own, came = [], []
    along = jnp.split(cotangent, 2, 0)
    grad_came = []
    if paired:
        hot = jnp.any(
            routes.T[:, None, :] == jnp.arange(experts, dtype=jnp.int32)[None, :, None], axis=0
        )
        packet = jnp.concatenate(
            [
                w_router.T,
                jnp.pad(ffn_gain[None], ((0, 15), (0, 0))),
                jnp.pad(hot.astype(BF), ((0, 0), (0, columns - tok_rows))),
            ],
            0,
        )
        x_theirs, x_mine, packet_sent, gone = split(me.member, tokens, packet, along[0])
        x_came = me.swap_shard(x_theirs)
        grad_came.append(me.swap_shard(gone))
        packets = [packet_sent, me.swap_shard(packet_sent)]
        *theirs, hidden_first, x_columns, inv_one = project_theirs(
            me.member, parts, x_mine, x_came, gain_row, projections
        )
        came = [me.swap_shard(v) for v in theirs]
        own = project_own(me.member, parts, hidden_first, projections, (theirs[-1],))
    else:
        every_head = jnp.concatenate([heads_of(j) for j in range(me.groups)], 1)
        own_rows = tokens.astype(F32)
        inv_rows = lax.rsqrt(jnp.mean(own_rows * own_rows, axis=-1, keepdims=True) + EPS)
        x_columns = me.exchange(tokens, 1, 0)
        inv_one = me.gather(inv_rows, 0)
        hidden_first = (x_columns.astype(F32) * inv_one * norm_gain.astype(F32)).astype(BF)
        own.append(me.scatter(nn(hidden_first, every_head), 1))
        came.append(jnp.zeros(own[-1].shape, BF))

    gain_two = ffn_gain.astype(F32)

    index = jnp.arange(tree_len, dtype=jnp.int32)
    _, depth = tree_layout(index, seg_len)
    cos, sin = angle_tables(depth)
    visible = tree_mask(index, index, parents[0], seg_len)
    bias = jnp.where(visible, 0.0, -1e30).astype(F32)

    attended, lse, query, key, value, att_came = [], [], [], [], [], []
    for part in range(parts):
        a, b, c, d, e, f = attend(
            own[part], came[part], cos, sin, bias, along[1] if part == parts - 1 else cos, gq, gk
        )
        attended.append(a)
        lse.append(b)
        query.append(c)
        key.append(d)
        value.append(e)
        if paired:
            att_came.append(me.swap_shard(a))
    if paired:
        grad_came.append(me.swap_shard(f))
        mine = [cotangent, me.swap_core(cotangent)]
        others = [*grad_came, *(me.swap_core(v) for v in grad_came)]
        grad_all = jnp.where(
            me.member == 0,
            jnp.concatenate([mine[0], *others[:2], mine[1], *others[2:]], 0),
            jnp.concatenate([*others[:2], mine[0], *others[2:], mine[1]], 0),
        )
        starts = [
            member * q_width + part * q_part
            for member in (me.member, partner)
            for part in range(parts)
        ]
        middle, middle_low, squares = middle_of(
            attended + att_came, jnp.stack(starts).astype(jnp.int32), w_out, x_columns, True
        )
        attended_full = me.in_order(
            me.member, jnp.concatenate(attended, 1), jnp.concatenate(att_came, 1), 1
        )
        messages = [middle_low, me.swap_shard(middle_low)]
        hidden_all, gates_all, slots_all, inv_two = hidden_packed(
            me.member,
            [
                (*messages, *packets),
                (*(me.swap_core(v) for v in messages), *(me.swap_core(v) for v in packets)),
            ],
        )
    else:
        grad_tree = me.gather(cotangent, 0)
        grad_all = jnp.concatenate([grad_tree, me.swap_core(grad_tree)], 0)
        attended_full = me.gather(attended[0][:, :q_width], 1)
        where = jnp.zeros((1,), jnp.int32)
        middle, middle_low, squares = middle_of([attended_full], where, w_out, x_columns, False)
        route_hot = jnp.any(
            routes[:, :, None] == jnp.arange(experts, dtype=jnp.int32)[None, None, :], axis=1
        ).astype(F32)
        routed = me.gather(route_hot, 0)
        middle_low, squares = me.gather(middle_low, 1), me.total(squares)
        hidden_all, gates_all = hidden_of(
            [
                ([middle_low], [squares], routed),
                (
                    [me.swap_core(middle_low)],
                    [me.swap_core(squares)],
                    me.swap_core(routed),
                ),
            ],
            where,
            me.gather(ffn_gain, 0)[None],
            me.gather(w_router, 0),
        )
        inv_two = lax.rsqrt(squares / width + EPS)
    grad_tree = grad_all[:tree_len]
    hidden_all = hidden_all.reshape(2 * tree_len, width)
    normed_two = middle * inv_two
    hidden_own = (normed_two * gain_two).astype(BF)

    first = me.core * per_core
    chunk = width // me.chips
    def gates_grad(gates, grad, axis):
        return (gates * (grad - jnp.sum(gates * grad, axis=axis, keepdims=True))).astype(BF)

    def output_of(mixed_own, mixed_other, *deps):
        mixed = mixed_own.astype(F32) + me.swap_core(mixed_other).astype(F32)
        placed = lax.dynamic_update_slice_in_dim(
            jnp.zeros((tree_len, width), F32), middle, me.member * columns, 1
        )
        return me.scatter(tie((mixed + placed).astype(BF), deps), 0).astype(BF)

    def input_of(grad_middle, scaled, row_sums):
        normed = x_columns.astype(F32) * inv_one
        grad = grad_middle + inv_one * (scaled - normed * (me.total(row_sums) / width))
        return me.exchange(grad.astype(BF), 0, 1)

    flipped = bias.T
    if not paired:
        gates = gates_all[0]
        gates_all = gates_all.reshape(2 * tree_len, experts)
        before, rings = None, []
        for j in range(per_core):
            before = expert_grads(
                j, per_core, first + j, me.member * (2 * per_core) + first + j,
                hidden_all, grad_all, gates_all, w_gate, w_up, w_down, before, 0, 1, (),
            )
            mid, own_columns, grads = before
            ring = Scatter(me, lambda chip: lax.dynamic_slice_in_dim(grads, chip * chunk, chunk, 1))
            for _ in range(me.chips - 1):
                ring.start()
                ring.finish()
            rings.append(ring.held)
        grad_gates = me.total(own_columns[:tree_len] + me.swap_core(own_columns[tree_len:]))
        grad_logits = gates_grad(gates, grad_gates, -1)
        (grad_other,) = expert_hidden(first, me.member, mid, 1, w_gate, w_up, None, False, ())
        (grad_own,) = expert_hidden(
            first, me.member, mid, 0, w_gate, w_up, me.swap_core(grad_other), False, ()
        )
        mixed_other = expert_mix(first, mid, 1, w_down, ())
        mixed_own = expert_mix(first, mid, 0, w_down, ())
        result = output_of(mixed_own, mixed_other)
        grad_hidden_two = nt(grad_logits, w_router) + me.scatter(grad_own, 1)
        grad_gain_two = jnp.sum(grad_hidden_two * normed_two, axis=0)[None]
        scaled = grad_hidden_two * gain_two
        mean = me.total(jnp.sum(scaled * normed_two, axis=-1, keepdims=True)) / width
        grad_columns = me.part(grad_tree, 1, me.member).astype(F32)
        grad_middle = grad_columns + inv_two * (scaled - normed_two * mean)
        grad_branch = grad_middle.astype(BF)
        own = me.scatter(nt(grad_branch, w_out), 1)
        own = jnp.pad(own, ((0, 0), (0, q_room - q_width)))
        grad_heads = attend_back(
            own, jnp.zeros(own.shape, BF), query[0], key[0], value[0], lse[0],
            cos, sin, flipped, gq, gk, (),
        )
        grad_out = me.all_reduce(tn(attended_full, grad_branch))
        grad_full = me.gather(grad_heads, 1)
        every = me.all_reduce(tn(hidden_first, grad_full))
        every = every.reshape(columns, me.groups, lanes)
        grad_query, grad_key, grad_value = (
            every[:, :, start : start + size].reshape(columns, me.groups * size)
            for start, size in ((0, q_width), (q_room, k_width), (q_room + k_room, k_width))
        )
        grad_hidden_one = nt(grad_full, every_head)
        normed_one = x_columns.astype(F32) * inv_one
        grad_gain_one = jnp.sum(grad_hidden_one * normed_one, axis=0)[None]
        scaled = grad_hidden_one * norm_gain.astype(F32)
        row_sums = jnp.sum(scaled * normed_one, axis=-1, keepdims=True)
        input_grad = input_of(grad_middle, scaled, row_sums)
        grad_router = tn(hidden_own, grad_logits)
        small = me.butterfly(jnp.concatenate([grad_gain_one, grad_gain_two, grad_router.T], 0))
        sums = rings
        grad_gate, grad_up, grad_down = finish_experts(
            me.core, sums, [me.swap_core(v) for v in sums]
        )
    else:

        column = me.member * (2 * per_core) + first

        def pair_of(pair, before, deps):
            return expert_pair(
                pair, per_core, first + 2 * pair, column + 2 * pair,
                hidden_all, grad_all, gates_all, slots_all, w_gate, w_up, w_down, before, deps,
            )

        def hidden_grad(tree, came, deps):
            return pair_hidden(
                first, column, me.member, tree, gates_all, slots_all, mid, w_gate, w_up, came, deps
            )

        def mix_of(tree, deps):
            return pair_mix(first, column, tree, gates_all, slots_all, mid, w_down, deps)

        def ring_of(grads):
            return Scatter(me, lambda chip: lax.dynamic_slice_in_dim(grads, chip * chunk, chunk, 1))

        one = pair_of(0, None, ())
        ring_a = ring_of(one[2])
        sent = ring_a.start()
        mid, own_rows, grads = pair_of(1, one, ())
        sent_a = ring_a.hop(own_rows)
        ring_b = ring_of(grads)
        sent_b = ring_b.start()
        grad_gates = me.total(own_rows[:2] + me.swap_core(own_rows[2:]))
        grad_logits = gates_grad(gates_all[:2], grad_gates, 1)
        grad_logits = grad_logits.transpose(0, 2, 1).reshape(tree_len, experts)
        (grad_other,) = hidden_grad(1, None, (sent_a, sent_b))
        other_came = me.swap_core(grad_other)
        sent = ring_a.hop(grad_other)
        grad_mine, grad_theirs = hidden_grad(0, other_came, (sent,))
        hidden_came = me.swap_shard(grad_theirs)
        sent = ring_b.hop(grad_mine)
        mixed_other = mix_of(1, (sent,))
        sent = ring_a.hop(mixed_other)
        mixed_own = mix_of(0, (sent, grad_logits))
        sent = ring_b.hop(mixed_own)
        scaled, row_sums, grad_gain_two = norm_back(
            grad_mine, hidden_came, grad_logits, w_router, middle, inv_two, ffn_gain[None], (sent,),
        )
        sums_came = me.swap_shard(row_sums)
        grad_middle, grad_branch, *both = branch_back(
            me.member, parts, grad_all, scaled, middle, inv_two, row_sums, sums_came, w_out, ()
        )
        came = [me.swap_shard(v) for v in both[:parts]]
        own = both[parts:]
        sent = ring_a.hop(grad_branch)
        grad_out = out_grads(
            me.core == me.member,
            [attended + att_came, [me.swap_core(v) for v in attended + att_came]],
            [grad_branch, me.swap_core(grad_branch)],
            (sent,),
        )
        sent = ring_b.hop(grad_out)
        heads_a = attend_back(
            own[0], came[0], query[0], key[0], value[0], lse[0], cos, sin, flipped, gq, gk,
            (sent,),
        )
        back_a = me.swap_shard(heads_a)
        sent = ring_a.hop(heads_a)
        heads_b = attend_back(
            own[1], came[1], query[1], key[1], value[1], lse[1], cos, sin, flipped, gq, gk,
            (sent,),
        )
        back_b = me.swap_shard(heads_b)
        sent = ring_b.hop(heads_b)
        grad_pairs = [(heads_a, back_a), (heads_b, back_b)]
        grads_mine = weight_grads(
            me.member,
            me.core,
            (hidden_first, me.swap_core(hidden_first)),
            (grad_pairs, [tuple(me.swap_core(v) for v in pair) for pair in grad_pairs]),
            grad_out,
            (sent,),
        )
        head_chunk = grads_mine.shape[0] // me.chips
        ring_w = Scatter(
            me, lambda chip: lax.dynamic_slice_in_dim(grads_mine, chip * head_chunk, head_chunk, 0)
        )
        sent = ring_w.start()
        sent = ring_a.hop(sent)
        grad_router = tn(hidden_own, grad_logits)
        scaled, row_sums, grad_gain_one = project_back(
            me.member, x_columns, inv_one, gain_row, projections, grad_pairs, (sent,)
        )
        input_grad = input_of(grad_middle, scaled, row_sums)
        small = me.butterfly(jnp.concatenate([grad_gain_one, grad_gain_two, grad_router.T], 0))
        result = output_of(mixed_own, mixed_other, scaled)
        beside = {1: (scaled,), 5: (input_grad,), 9: (small,), 11: (result,)}
        hops, experts_done = me.chips - 1, None
        for hop in range(1, 2 * hops):
            w = ring_w.finish()
            if hop == hops:
                ring_w = Gather(me, ring_w.held)
            deps = beside.get(hop, ())
            ring = {1: ring_b, 3: ring_a, 4: ring_b, 6: ring_a, 7: ring_b, 9: ring_b}.get(hop)
            if ring is not None and ring.hops < hops:
                deps = (*deps, ring.finish(w))
                if ring.hops < hops:
                    ring.start()
                elif ring_a.hops == ring_b.hops:
                    sums = [h for r in (ring_a, ring_b) for h in jnp.split(r.held, 2, 0)]
                    experts_done = finish_experts(me.core, sums, [me.swap_core(v) for v in sums])
                    beside[12] = experts_done[:1]
            ring_w.start(*deps)
        ring_w.finish()
        grad_gate, grad_up, grad_down = experts_done
        layout = [
            [
                (out, j * step + part * size, j * lanes + start, size)
                for j in range(2)
                for out, step, start, size in (
                    (0, q_width, 0, q_part),
                    (1, k_width, q_room, k_part),
                    (2, k_width, q_room + k_room, k_part),
                )
            ]
            for part in range(parts)
        ]
        grad_query, grad_key, grad_value, grad_out = finish(
            me.core, ring_w.whole, me.swap_core(ring_w.whole), layout, (all_q, all_k, all_k), columns
        )
        grad_out = grad_out.reshape(-1, columns)

    return (
        result,
        input_grad,
        small[0],
        grad_query,
        grad_key,
        grad_value,
        grad_out,
        small[1],
        small[2:].T,
        grad_gate,
        grad_up,
        grad_down.transpose(0, 2, 1),
    )


def solution(mesh):
    return jax.shard_map(
        local,
        mesh=mesh,
        in_specs=(
            P(("rep", "shard"), None),
            P("shard"),
            P("shard", None),
            P("shard", None),
            P("shard", None),
            P(None, "shard"),
            P("shard"),
            P("shard", None),
            P("shard", None, None),
            P("shard", None, None),
            P("shard", None, None),
            P("rep", None),
            P(("rep", "shard"), None),
            P(("rep", "shard"), None),
        ),
        out_specs=(
            P(("rep", "shard"), None),
            P(("rep", "shard"), None),
            P("shard"),
            P("shard", None),
            P("shard", None),
            P("shard", None),
            P(None, "shard"),
            P("shard"),
            P("shard", None),
            P("shard", "rep", None),
            P("shard", "rep", None),
            P("shard", None, "rep"),
        ),
        check_vma=False,
    )
```

```python
import functools

import jax
import jax.numpy as jnp
from jax import lax
from jax.experimental import pallas as pl
from jax.experimental.pallas import tpu as pltpu
from jax.sharding import PartitionSpec as P

HEAD_DIM = 64
LANES = 128
EPS = 1e-06
BF = jnp.bfloat16
F32 = jnp.float32
VMEM_LIMIT = 60 << 20


def tree_layout(position, seg_len):
    trunk_len = 4 * seg_len
    beyond = position - trunk_len
    segment = jnp.where(position < trunk_len, 0, 1 + beyond // seg_len)
    inner = jnp.where(
        segment <= 4, trunk_len + beyond % seg_len, trunk_len + seg_len + beyond % seg_len
    )
    depth_position = jnp.where(position < trunk_len, position, inner)
    return (segment, depth_position)


def lookup(segment, parents_row):
    labels = jnp.arange(parents_row.shape[0], dtype=jnp.int32)
    picked = jnp.where(segment[:, None] == labels[None, :], parents_row[None, :], 0)
    return jnp.sum(picked, axis=1)


def tree_mask(query_index, key_index, parents_row, seg_len):
    query_seg, _ = tree_layout(query_index, seg_len)
    key_seg, _ = tree_layout(key_index, seg_len)
    parent_one = lookup(query_seg, parents_row)
    parent_two = lookup(parent_one, parents_row)
    key_row = key_seg[None, :]
    related = (
        (key_row == query_seg[:, None])
        | (key_row == parent_one[:, None])
        | (key_row == parent_two[:, None])
    )
    return related & (key_index[None, :] <= query_index[:, None])


def angle_tables(depth_position):
    half = HEAD_DIM // 2
    frequency = 10000.0 ** (-2.0 * jnp.arange(half, dtype=F32) / HEAD_DIM)
    angles = depth_position.astype(F32)[:, None] * frequency[None, :]
    cosine, sine = jnp.cos(angles), jnp.sin(angles)
    return (
        jnp.concatenate([cosine] * 4, 1),
        jnp.concatenate([-sine, sine, -sine, sine], 1),
    )


def dot(a, b, dims):
    return lax.dot_general(a, b, (dims, ((), ())), preferred_element_type=F32)


def nn(a, b):
    return dot(a, b, ((1,), (0,)))


def nt(a, b):
    return dot(a, b, ((1,), (1,)))


def tn(a, b):
    return dot(a, b, ((0,), (0,)))


class Mesh:
    def __init__(self):
        self.groups = lax.axis_size("shard")
        self.member = lax.axis_index("shard")
        self.reps = lax.axis_size("rep")
        self.rep = lax.axis_index("rep")
        self.core = self.rep % 2
        self.chip = self.rep // 2
        self.chips = self.reps // 2
        rows = self.chips // 2
        order = [2 * z for z in range(rows)] + [2 * z + 1 for z in range(rows - 1, -1, -1)]
        self.ring = []
        for place, chip in enumerate(order):
            after, before = order[(place + 1) % self.chips], order[place - 1]
            self.ring += [(2 * chip, 2 * after), (2 * chip + 1, 2 * before + 1)]
        self.place = jnp.where(
            self.chip % 2 == 0, self.chip // 2, self.chips - 1 - self.chip // 2
        )
        self.way = 1 - 2 * self.core

    def chip_at(self, place):
        place = place % self.chips
        rows = self.chips // 2
        return jnp.where(place < rows, 2 * place, 2 * (self.chips - 1 - place) + 1)

    def swap_shard(self, v):
        return lax.ppermute(v, "shard", [(0, 1), (1, 0)])

    def swap_core(self, v):
        return lax.ppermute(v, "rep", [(r, r ^ 1) for r in range(self.reps)])

    def along_ring(self, v):
        return lax.ppermute(v, "rep", self.ring)

    def part(self, v, axis, which):
        size = v.shape[axis] // self.groups
        return lax.dynamic_slice_in_dim(v, which * size, size, axis)

    def gather(self, v, axis):
        if self.groups != 2:
            return lax.all_gather(v, "shard", axis=axis, tiled=True)
        other = self.swap_shard(v)
        return self.in_order(self.member, v, other, axis)

    def in_order(self, which, mine, other, axis):
        return jnp.where(
            which == 0,
            jnp.concatenate([mine, other], axis),
            jnp.concatenate([other, mine], axis),
        )

    def exchange(self, v, split_axis, concat_axis):
        if self.groups != 2:
            return lax.all_to_all(v, "shard", split_axis, concat_axis, tiled=True)
        other = self.swap_shard(self.part(v, split_axis, 1 - self.member))
        mine = self.part(v, split_axis, self.member)
        return self.in_order(self.member, mine, other, concat_axis)

    def scatter(self, v, axis):
        if self.groups != 2:
            return lax.psum_scatter(
                v.astype(BF), "shard", scatter_dimension=axis, tiled=True
            ).astype(F32)
        other = self.swap_shard(self.part(v, axis, 1 - self.member).astype(BF))
        return self.part(v, axis, self.member).astype(F32) + other.astype(F32)

    def total(self, v):
        if self.groups != 2:
            return lax.psum(v, "shard")
        return v + self.swap_shard(v)

    def ring_sum(self, v):
        chunk = v.shape[0] // self.chips
        ring = Scatter(self, lambda chip: lax.dynamic_slice_in_dim(v, chip * chunk, chunk, 0))
        for _ in range(self.chips - 1):
            ring.start()
            ring.finish()
        ring = Gather(self, ring.held)
        for _ in range(self.chips - 1):
            ring.start()
            ring.finish()
        return ring.whole

    def all_reduce(self, v):
        half = v.shape[0] // 2
        v = v.astype(BF)
        mine = lax.dynamic_slice_in_dim(v, self.core * half, half, 0)
        other = self.swap_core(
            lax.dynamic_slice_in_dim(v, (1 - self.core) * half, half, 0)
        )
        whole = self.ring_sum((mine.astype(F32) + other.astype(F32)).astype(BF))
        return self.in_order(self.core, whole, self.swap_core(whole), 0).astype(F32)

    def butterfly(self, v):
        bit = 1
        while bit < self.reps:
            v = v + lax.ppermute(v, "rep", [(r, r ^ bit) for r in range(self.reps)])
            bit *= 2
        return v


class Scatter:
    def __init__(self, me, own):
        self.me, self.own, self.hops = me, own, 0
        self.held = own(me.chip_at(me.place - me.way))

    def start(self, *deps):
        sent = tie(self.held, deps)
        self.came = self.me.along_ring(sent)
        return sent

    def hop(self, *deps):
        self.finish(*deps)
        return self.start()

    def finish(self, *deps):
        self.hops += 1
        self.came = tie(self.came, deps)
        mine = self.own(self.me.chip_at(self.me.place - self.me.way * (self.hops + 1)))
        self.held = (self.came.astype(F32) + mine.astype(F32)).astype(BF)
        return self.came


class Gather:
    def __init__(self, me, held):
        self.me, self.held, self.hops = me, held, 0
        self.size = held.shape[0]
        whole = jnp.zeros((self.size * me.chips, held.shape[1]), held.dtype)
        self.whole = self.put(whole, me.place)

    def put(self, whole, place):
        at = self.me.chip_at(place) * self.size
        return lax.dynamic_update_slice_in_dim(whole, self.held, at, 0)

    def start(self, *deps):
        self.came = self.me.along_ring(tie(self.held, deps))

    def finish(self):
        self.hops += 1
        self.held = self.came
        self.whole = self.put(self.whole, self.me.place - self.me.way * self.hops)
        return self.came


def pairs(heads):
    return -(-heads // 2)


def rope(v, cos, sin, back):
    lane = lax.broadcasted_iota(jnp.int32, (1, LANES), 1)
    first = lane % HEAD_DIM < HEAD_DIM // 2
    out = []
    for i in range(v.shape[1] // LANES):
        x = v[:, i * LANES : (i + 1) * LANES]
        other = jnp.where(
            first,
            pltpu.roll(x, LANES - HEAD_DIM // 2, 1),
            pltpu.roll(x, HEAD_DIM // 2, 1),
        )
        out.append(x * cos - other * sin if back else x * cos + other * sin)
    return out


def halves(x, parity):
    low = lax.broadcasted_iota(jnp.int32, (1, LANES), 1) < HEAD_DIM
    zero = jnp.zeros_like(x)
    turned = pltpu.roll(x, HEAD_DIM, 1)
    a, b = (x, turned) if parity == 0 else (turned, x)
    return jnp.where(low, a, zero).astype(BF), jnp.where(low, zero, b).astype(BF)


def attend_kernel(
    q_heads, kv_heads, own_ref, came_ref, cos_ref, sin_ref, bias_ref,
    *refs,
):
    out_ref, lse_ref, q_ref, k_ref, v_ref = refs[-5:]
    per = q_heads // kv_heads
    rows = own_ref.shape[0]
    qp, kp = pairs(q_heads), pairs(kv_heads)
    cos, sin = cos_ref[...], sin_ref[...]
    raw = own_ref[...].astype(F32) + came_ref[...].astype(F32)
    scale = HEAD_DIM**-0.5
    q = [(t * scale).astype(BF) for t in rope(raw[:, : qp * LANES], cos, sin, False)]
    keys = rope(raw[:, qp * LANES : (qp + kp) * LANES], cos, sin, False)
    for i in range(qp):
        q_ref[:, i * LANES : (i + 1) * LANES] = q[i]
    ks, vs = [], []
    for g in range(kv_heads):
        at = (qp + kp + g // 2) * LANES
        ks.append(halves(keys[g // 2], g % 2))
        vs.append(halves(raw[:, at : at + LANES], g % 2))
        for p in range(2):
            k_ref[g, p] = ks[g][p]
            v_ref[g, p] = vs[g][p]
    half = rows // 2
    for lo, n in ((0, half), (half, rows)):
        bias = bias_ref[lo : lo + half, :n]
        for i in range(qp):
            out = jnp.zeros((half, LANES), F32)
            for h in range(2 * i, min(2 * i + 2, q_heads)):
                g, p = h // per, h % 2
                s = nt(q[i][lo : lo + half], ks[g][p][:n]) + bias
                peak = jnp.max(s, axis=-1, keepdims=True)
                e = jnp.exp(s - peak)
                total = jnp.sum(e, axis=-1, keepdims=True)
                lse_ref[lo : lo + half, h : h + 1] = peak + jnp.log(total)
                out = out + nn((e * (1.0 / total)).astype(BF), vs[g][p][:n])
            out_ref[lo : lo + half, i * LANES : (i + 1) * LANES] = out.astype(BF)


def attend(own, came, cos, sin, bias, q_heads, kv_heads, deps):
    rows = own.shape[0]
    qp = pairs(q_heads)
    specs, deps = after(deps)
    return pl.pallas_call(
        functools.partial(attend_kernel, q_heads, kv_heads),
        in_specs=[pl.BlockSpec(memory_space=pltpu.VMEM)] * 5 + specs,
        out_shape=[
            jax.ShapeDtypeStruct((rows, qp * LANES), BF),
            jax.ShapeDtypeStruct((rows, LANES), F32),
            jax.ShapeDtypeStruct((rows, qp * LANES), BF),
            jax.ShapeDtypeStruct((kv_heads, 2, rows, LANES), BF),
            jax.ShapeDtypeStruct((kv_heads, 2, rows, LANES), BF),
        ],
        compiler_params=pltpu.CompilerParams(vmem_limit_bytes=VMEM_LIMIT),
        cost_estimate=pl.CostEstimate(
            flops=1200 * rows * rows * q_heads,
            bytes_accessed=8 << 20,
            transcendentals=rows * rows * q_heads,
        ),
    )(own, came, cos, sin, bias, *deps)


def attend_back_kernel(
    q_heads, kv_heads, start, own_ref, came_ref, q_ref, k_ref, v_ref, lse_ref,
    cos_ref, sin_ref, bias_ref, *refs,
):
    per = q_heads // kv_heads
    rows = own_ref.shape[0]
    qp, kp = pairs(q_heads), pairs(kv_heads)
    cos, sin = cos_ref[...], sin_ref[...]
    scale = HEAD_DIM**-0.5
    low = lax.broadcasted_iota(jnp.int32, (1, LANES), 1) < HEAD_DIM
    at = slice(start, start + qp * LANES)
    grad = (own_ref[:, at].astype(F32) + came_ref[:, at].astype(F32)).astype(BF)
    lse = lse_ref[...].T
    half = rows // 2
    out_ref = refs[-1]

    def put(at, v):
        out_ref[:, at * LANES : (at + 1) * LANES] = v.astype(BF)

    def blocks():
        return [
            [[jnp.zeros((half, LANES), F32) for _ in range(2)] for _ in range(2)]
            for _ in range(kv_heads)
        ]

    dk, dv = blocks(), blocks()
    for i in range(qp):
        parts = []
        for lo, n in ((0, half), (half, rows)):
            q = q_ref[lo : lo + half, i * LANES : (i + 1) * LANES]
            go = grad[lo : lo + half, i * LANES : (i + 1) * LANES]
            bias = bias_ref[:n, lo : lo + half]
            dq = jnp.zeros((half, LANES), F32)
            for h in range(2 * i, min(2 * i + 2, q_heads)):
                g, p = h // per, h % 2
                k, v = k_ref[g, p, :n], v_ref[g, p, :n]
                s = nt(k, q) + bias
                probs = jnp.exp(s - lse[h : h + 1, lo : lo + half])
                dp = nt(v, go)
                delta = jnp.sum(probs * dp, axis=0, keepdims=True)
                ds = (probs * (dp - delta)).astype(BF)
                dq = dq + tn(ds, k)
                ck, cv = nn(ds, q), nn(probs.astype(BF), go)
                for b in range(n // half):
                    dk[g][p][b] = dk[g][p][b] + ck[b * half : (b + 1) * half]
                    dv[g][p][b] = dv[g][p][b] + cv[b * half : (b + 1) * half]
            parts.append(dq * scale)
        put(i, rope(jnp.concatenate(parts, 0), cos, sin, True)[0])

    def packed(d, j):
        got = jnp.zeros((rows, LANES), F32)
        for g in range(2 * j, min(2 * j + 2, kv_heads)):
            a, b = (jnp.concatenate(d[g][p], 0) for p in range(2))
            a, b = jnp.where(low, a, 0.0), jnp.where(low, 0.0, b)
            if g % 2 == 0:
                got = got + a + pltpu.roll(b, HEAD_DIM, 1)
            else:
                got = got + b + pltpu.roll(a, HEAD_DIM, 1)
        return got

    for j in range(kp):
        put(qp + j, rope(packed(dk, j), cos, sin, True)[0])
        put(qp + kp + j, packed(dv, j))


def attend_back(own, came, q, k, v, lse, cos, sin, bias, q_heads, kv_heads, start, deps):
    rows = own.shape[0]
    lanes = (pairs(q_heads) + 2 * pairs(kv_heads)) * LANES
    specs, deps = after(deps)
    return pl.pallas_call(
        functools.partial(attend_back_kernel, q_heads, kv_heads, start),
        in_specs=[pl.BlockSpec(memory_space=pltpu.VMEM)] * 9 + specs,
        out_shape=jax.ShapeDtypeStruct((rows, lanes), BF),
        compiler_params=pltpu.CompilerParams(vmem_limit_bytes=VMEM_LIMIT),
        cost_estimate=pl.CostEstimate(
            flops=1600 * rows * rows * q_heads,
            bytes_accessed=8 << 20,
            transcendentals=rows * rows * q_heads,
        ),
    )(own, came, q, k, v, lse, cos, sin, bias, *deps)


def after(arrays):
    return [pl.BlockSpec(memory_space=pl.ANY)] * len(arrays), tuple(arrays)


def row_tile(rows):
    return rows if rows <= 896 else 448


def params():
    return pltpu.CompilerParams(vmem_limit_bytes=VMEM_LIMIT)


def cost(flops, megabytes, transcendentals=0):
    return pl.CostEstimate(
        flops=int(flops), bytes_accessed=megabytes << 20, transcendentals=int(transcendentals)
    )


def to_row(column):
    rows = column.shape[0]
    return jnp.broadcast_to(column, (rows, LANES)).T[:1]


def to_column(row):
    return jnp.broadcast_to(row, (LANES, row.shape[1])).T[:, :1]


def put_column(ref, column):
    rows = column.shape[0]
    row = to_row(column)
    high = row.astype(BF)
    low = (row - high.astype(F32)).astype(BF)
    line = lax.broadcasted_iota(jnp.int32, (16, rows), 0)
    ref[rows : rows + 16, :] = jnp.zeros((16, ref.shape[1]), BF)
    ref[rows : rows + 16, :rows] = jnp.where(
        line == 0, high.astype(F32), jnp.where(line == 1, low.astype(F32), 0.0)
    ).astype(BF)


def get_column(ref):
    rows = ref.shape[0] - 16
    last = ref[rows : rows + 16, :rows].astype(F32)
    return to_column(last[0:1] + last[1:2])


def split_kernel(where, x_ref, theirs_ref, mine_ref):
    rows, size = x_ref.shape[0], mine_ref.shape[1]
    x = x_ref[...].astype(F32)
    squares = jnp.sum(x * x, axis=-1, keepdims=True)
    for ref, member in ((theirs_ref, 1 - where[0]), (mine_ref, where[0])):
        ref[:rows, :] = x_ref[:, pl.ds(pl.multiple_of(member * size, LANES), size)]
        put_column(ref, squares)


def split(member, x):
    rows, width = x.shape
    out = jax.ShapeDtypeStruct((rows + 16, width // 2), BF)
    return pl.pallas_call(
        split_kernel,
        in_specs=[pl.BlockSpec(memory_space=pltpu.SMEM), pl.BlockSpec(memory_space=pltpu.VMEM)],
        out_shape=[out, out],
        compiler_params=params(),
        cost_estimate=cost(0, 2),
    )(jnp.reshape(member, (1,)), x)


def heads_product(hidden, member, part, parts, weights):
    found = []
    for w in weights:
        size = w.shape[1] // (2 * parts)
        at = pl.ds(pl.multiple_of((member * parts + part) * size, LANES), size)
        found.append(nn(hidden, w[:, at]))
    return jnp.concatenate(found, 1)


def project_theirs_kernel(parts, where, mine_ref, came_ref, gain_ref, wq, wk, wv, *refs):
    outs, (hidden_ref, x_ref, inv_ref) = refs[:parts], refs[parts:]
    rows, columns = mine_ref.shape[0] - 16, mine_ref.shape[1]
    gain = gain_ref[...].astype(F32)
    for message, member in ((mine_ref, where[0]), (came_ref, 1 - where[0])):
        at = pl.ds(pl.multiple_of(member * rows, 16), rows)
        inv = lax.rsqrt(get_column(message) / (2 * columns) + EPS)
        inv_ref[at, :] = inv
        x = message[:rows, :]
        x_ref[at, :] = x
        hidden_ref[at, :] = (x.astype(F32) * inv * gain).astype(BF)
    for part in range(parts):
        outs[part][...] = heads_product(
            hidden_ref[...], 1 - where[0], part, parts, (wq, wk, wv)
        ).astype(BF)


def project_theirs(member, parts, mine, came, gain, weights):
    rows, columns = 2 * (mine.shape[0] - 16), mine.shape[1]
    lanes = sum(w.shape[1] for w in weights) // (2 * parts)
    return pl.pallas_call(
        functools.partial(project_theirs_kernel, parts),
        in_specs=[pl.BlockSpec(memory_space=pltpu.SMEM)]
        + [pl.BlockSpec(memory_space=pltpu.VMEM)] * 6,
        out_shape=[jax.ShapeDtypeStruct((rows, lanes), BF)] * parts
        + [
            jax.ShapeDtypeStruct((rows, columns), BF),
            jax.ShapeDtypeStruct((rows, columns), BF),
            jax.ShapeDtypeStruct((rows, 1), F32),
        ],
        compiler_params=params(),
        cost_estimate=cost(4 * rows * columns * lanes * parts, 6),
    )(jnp.reshape(member, (1,)), mine, came, gain, *weights)


def project_own_kernel(parts, where, hidden_ref, wq, wk, wv, *refs):
    for part in range(parts):
        refs[part - parts][...] = heads_product(
            hidden_ref[...], where[0], part, parts, (wq, wk, wv)
        )


def project_own(member, parts, hidden, weights, deps):
    rows, columns = hidden.shape
    lanes = sum(w.shape[1] for w in weights) // (2 * parts)
    specs, deps = after(deps)
    return pl.pallas_call(
        functools.partial(project_own_kernel, parts),
        in_specs=[pl.BlockSpec(memory_space=pltpu.SMEM)]
        + [pl.BlockSpec(memory_space=pltpu.VMEM)] * 4
        + specs,
        out_shape=[jax.ShapeDtypeStruct((rows, lanes), F32)] * parts,
        compiler_params=params(),
        cost_estimate=cost(4 * rows * columns * lanes * parts, 6),
    )(jnp.reshape(member, (1,)), hidden, *weights, *deps)


def project_back_kernel(
    parts, where, x_ref, inv_ref, gain_ref, wq_ref, wk_ref, wv_ref, *refs
):
    grads = refs[: 2 * parts]
    scaled_ref, sums_ref, gain_grad_ref = refs[-3:]
    total = jnp.zeros(x_ref.shape, F32)
    for part in range(parts):
        for grad, member in ((grads[2 * part], where[0]), (grads[2 * part + 1], 1 - where[0])):
            start = 0
            for w in (wq_ref, wk_ref, wv_ref):
                size = w.shape[1] // (2 * parts)
                at = pl.ds(pl.multiple_of((member * parts + part) * size, LANES), size)
                total += nt(grad[:, start : start + size], w[:, at])
                start += size
    normed = x_ref[...].astype(F32) * inv_ref[...]
    scaled = total * gain_ref[...].astype(F32)
    scaled_ref[...] = scaled
    sums_ref[...] = jnp.sum(scaled * normed, axis=-1, keepdims=True)
    gain_grad_ref[...] = jnp.sum(total * normed, axis=0, keepdims=True)


def project_back(member, x, inv, gain, weights, grads, deps):
    rows, columns = x.shape
    parts = len(grads)
    flat = [a for pair in grads for a in pair]
    specs, deps = after(deps)
    whole = pl.BlockSpec(memory_space=pltpu.VMEM)
    return pl.pallas_call(
        functools.partial(project_back_kernel, parts),
        in_specs=[pl.BlockSpec(memory_space=pltpu.SMEM)] + [whole] * (6 + len(flat)) + specs,
        out_shape=[
            jax.ShapeDtypeStruct((rows, columns), F32),
            jax.ShapeDtypeStruct((rows, 1), F32),
            jax.ShapeDtypeStruct((1, columns), F32),
        ],
        compiler_params=params(),
        cost_estimate=cost(2 * rows * columns * sum(w.shape[1] for w in weights), 10),
    )(jnp.reshape(member, (1,)), x, inv, gain, *weights, *flat, *deps)


def weight_grads_kernel(where, *refs):
    hidden, out_ref = refs[:2], refs[-1]
    size = refs[2].shape[1]
    out_ref[:, 2 * size :] = refs[10][...]
    for core in range(2):

        @pl.when(where[1] == core)
        def _():
            for i, member in ((0, where[0]), (1, 1 - where[0])):
                total = sum(tn(hidden[t][...], refs[2 + 4 * t + 2 * core + i][...]) for t in range(2))
                at = pl.ds(pl.multiple_of(member * size, LANES), size)
                out_ref[:, at] = total.astype(BF)


def weight_grads(member, core, hidden, grads, beside, deps):
    columns = hidden[0].shape[1]
    flat = [a for tree in grads for pair in tree for a in pair]
    rows, lanes = flat[0].shape
    specs, deps = after(deps)
    return pl.pallas_call(
        weight_grads_kernel,
        in_specs=[pl.BlockSpec(memory_space=pltpu.SMEM)]
        + [pl.BlockSpec(memory_space=pltpu.VMEM)] * (3 + len(flat))
        + specs,
        out_shape=jax.ShapeDtypeStruct((columns, 2 * lanes + beside.shape[1]), BF),
        compiler_params=params(),
        cost_estimate=cost(8 * rows * columns * lanes, 8),
    )(jnp.stack([member, core]), *hidden, *flat, beside, *deps)


def middle_kernel(count, where, *refs):
    pieces, (w_ref, x_ref) = refs[:count], refs[count : count + 2]
    middle_ref, low_ref, squares_ref = refs[-3:]
    total = x_ref[...].astype(F32)
    for i, piece in enumerate(pieces):
        size = piece.shape[1]
        total += nn(piece[...], w_ref[pl.ds(pl.multiple_of(where[i], 64), size), :])
    squares = jnp.sum(total * total, axis=-1, keepdims=True)
    middle_ref[...] = total
    low_ref[: total.shape[0], :] = total.astype(BF)
    squares_ref[...] = squares
    if low_ref.shape[0] > total.shape[0]:
        put_column(low_ref, squares)


def middle_of(pieces, where, w_out, x, packed, deps=()):
    rows, columns = x.shape
    tile = rows if packed else 448
    more = 16 if packed else 0
    specs, deps = after(deps)

    def row(i, w):
        return (i, 0)

    return pl.pallas_call(
        functools.partial(middle_kernel, len(pieces)),
        grid_spec=pltpu.PrefetchScalarGridSpec(
            num_scalar_prefetch=1,
            grid=(rows // tile,),
            in_specs=[pl.BlockSpec((tile, p.shape[1]), row) for p in pieces]
            + [
                pl.BlockSpec(w_out.shape, lambda i, w: (0, 0)),
                pl.BlockSpec((tile, columns), row),
            ]
            + specs,
            out_specs=[
                pl.BlockSpec((tile, columns), row),
                pl.BlockSpec((tile + more, columns), row),
                pl.BlockSpec((tile, 1), row),
            ],
        ),
        out_shape=[
            jax.ShapeDtypeStruct((rows, columns), F32),
            jax.ShapeDtypeStruct((rows + more, columns), BF),
            jax.ShapeDtypeStruct((rows, 1), F32),
        ],
        compiler_params=params(),
        cost_estimate=cost(2 * rows * columns * w_out.shape[0], 6),
    )(where, *pieces, w_out, x, *deps)


def hidden_kernel(count, parts, width, where, *refs):
    gain_ref, router_ref = refs[:2]
    h_ref, gates_ref = refs[-2:]
    for tree in range(2):
        mine = refs[2 + tree * (count + parts + 1) :]
        pieces, squares, on = mine[:count], mine[count : count + parts], mine[count + parts][...]
        total = squares[0][...]
        for more in squares[1:]:
            total += more[...]
        inv = lax.rsqrt(total / width + EPS)
        for i, piece in enumerate(pieces):
            size = piece.shape[1]
            at = pl.ds(pl.multiple_of(where[i] * size, LANES), size)
            gain = gain_ref[:, at].astype(F32)
            h_ref[tree, :, at] = (piece[...].astype(F32) * inv * gain).astype(BF)
        logits = jnp.where(on > 0, nn(h_ref[tree], router_ref[...]), -1e30)
        peak = jnp.max(logits, axis=-1, keepdims=True)
        e = jnp.exp(logits - peak) * on
        gates_ref[tree] = e / jnp.sum(e, axis=-1, keepdims=True)


def hidden_of(trees, where, gain, router):
    pieces, squares, on = trees[0]
    rows = on.shape[0]
    width, experts = router.shape
    tile = 448

    def row(i, w):
        return (i, 0)

    def all_of(i, w):
        return (0, 0)

    def both(i, w):
        return (0, i, 0)

    specs = [pl.BlockSpec((tile, p.shape[1]), row) for p in (*pieces, *squares, on)]
    return pl.pallas_call(
        functools.partial(hidden_kernel, len(pieces), len(squares), width),
        grid_spec=pltpu.PrefetchScalarGridSpec(
            num_scalar_prefetch=1,
            grid=(rows // tile,),
            in_specs=[pl.BlockSpec((1, width), all_of), pl.BlockSpec((width, experts), all_of)]
            + specs
            + specs,
            out_specs=[
                pl.BlockSpec((2, tile, width), both),
                pl.BlockSpec((2, tile, experts), both),
            ],
        ),
        out_shape=[
            jax.ShapeDtypeStruct((2, rows, width), BF),
            jax.ShapeDtypeStruct((2, rows, experts), F32),
        ],
        compiler_params=params(),
        cost_estimate=cost(4 * rows * width * 256, 8, rows * 32),
    )(where, gain, router, *(a for p, q, o in trees for a in (*p, *q, o)))


PACKET_ROWS = 48


def hidden_packed_kernel(where, *refs):
    h_ref, gates_ref, slots_ref, inv_ref, logits_ref, on_ref = refs[-6:]
    count = refs[0].shape[0] // 2 - 8
    before = (
        lax.broadcasted_iota(jnp.int32, (count, count), 0)
        < lax.broadcasted_iota(jnp.int32, (count, count), 1)
    )
    before = jnp.where(before, 1.0, 0.0).astype(BF)
    member = (where[0], 1 - where[0])
    for tree in range(2):
        messages, packets = refs[4 * tree : 4 * tree + 2], refs[4 * tree + 2 : 4 * tree + 4]
        rows, columns = messages[0].shape[0] - 16, messages[0].shape[1]
        squares = get_column(messages[0]) + get_column(messages[1])
        inv = lax.rsqrt(squares / (2 * columns) + EPS)
        if tree == 0:
            inv_ref[...] = inv
        logits = 0.0
        for i in range(2):
            at = pl.ds(pl.multiple_of(member[i] * columns, LANES), columns)
            gain = packets[i][16:32, :].astype(F32)[:1]
            h = (messages[i][:rows, :].astype(F32) * inv * gain).astype(BF)
            h_ref[tree, :, at] = h
            logits = logits + nt(h, packets[i][:16, :])
            tokens = rows // 2
            on_ref[pl.ds(pl.multiple_of(member[i] * tokens, 16), tokens), :] = (
                packets[i][32:48, :tokens].astype(F32).T
            )
        on = on_ref[...]
        logits = jnp.where(on > 0, logits, -1e30)
        if tree == 0:
            logits_ref[...] = logits
        peak = jnp.max(logits, axis=-1, keepdims=True)
        e = jnp.exp(logits - peak) * on
        gates = (e / jnp.sum(e, axis=-1, keepdims=True)).T
        for i in range(2):
            at = gates[:, i * count : (i + 1) * count]
            gates_ref[2 * tree + i] = at
            routed = jnp.where(at > 0.0, 1.0, 0.0).astype(BF)
            slots_ref[2 * tree + i] = nn(routed, before).astype(jnp.int32)


def hidden_packed(member, trees, deps):
    rows, columns = trees[0][0].shape[0] - 16, trees[0][0].shape[1]
    specs, deps = after(deps)
    return pl.pallas_call(
        hidden_packed_kernel,
        in_specs=[pl.BlockSpec(memory_space=pltpu.SMEM)]
        + [pl.BlockSpec(memory_space=pltpu.VMEM)] * 8
        + specs,
        out_shape=[
            jax.ShapeDtypeStruct((2, rows, 2 * columns), BF),
            jax.ShapeDtypeStruct((4, 16, rows // 2), F32),
            jax.ShapeDtypeStruct((4, 16, rows // 2), jnp.int32),
            jax.ShapeDtypeStruct((rows, 1), F32),
            jax.ShapeDtypeStruct((rows, 16), F32),
        ],
        scratch_shapes=[pltpu.VMEM((rows, 16), F32)],
        compiler_params=params(),
        cost_estimate=cost(4 * rows * columns * 256, 8),
    )(jnp.reshape(member, (1,)), *(a for tree in trees for a in tree), *deps)


def expert_grads_kernel(
    chained, steps, where, h_ref, g_ref, on_ref, wg_ref, wu_ref, wd_ref, *refs
):
    mid_ref, gg_ref, own_ref = refs[-3:] if steps == 1 else refs[-4:-1]
    step = pl.program_id(0)
    h, g = h_ref[...], g_ref[...]
    lane = lax.broadcasted_iota(jnp.int32, (1, on_ref.shape[1]), 1) == where[1]
    on = jnp.sum(jnp.where(lane, on_ref[...], 0.0), axis=-1, keepdims=True)
    gate_pre = nn(h, wg_ref[0])
    up_pre = nn(h, wu_ref[0])
    grad_mid = nt(g, wd_ref[0])
    sig = 1.0 / (1.0 + jnp.exp(-gate_pre))
    silu = gate_pre * sig
    mid = silu * up_pre
    column = jnp.where(lane, jnp.sum(grad_mid * mid, axis=-1, keepdims=True), 0.0)
    gg_ref[...] = refs[0][...] + column if chained else column
    act = (on * mid).astype(BF)
    grad_mid = on * grad_mid
    ggp = (grad_mid * up_pre * (sig * (1.0 + gate_pre * (1.0 - sig)))).astype(BF)
    gup = (grad_mid * silu).astype(BF)
    mid_ref[0, 0] = act
    mid_ref[0, 1] = ggp
    mid_ref[0, 2] = gup
    if steps == 1:
        own_ref[0] = tn(h, ggp).astype(BF)
        own_ref[1] = tn(h, gup).astype(BF)
        own_ref[2] = tn(g, act).astype(BF)
        return
    acc = refs[-1]

    @pl.when(step == 0)
    def _():
        acc[...] = jnp.zeros_like(acc)

    acc[0] += tn(h, ggp)
    acc[1] += tn(h, gup)
    acc[2] += tn(g, act)

    @pl.when(step == steps - 1)
    def _():
        own_ref[...] = acc[...].astype(BF)


def expert_grads(
    j, per_core, which, column, h, g, on, w_gate, w_up, w_down, before, slot, slots, deps
):
    rows, width = h.shape
    hidden = w_gate.shape[2]
    experts = on.shape[1]
    tile = row_tile(rows)
    steps = rows // tile

    def row(i, w):
        return (i, 0)

    def weight(i, w):
        return (w[0], 0, 0)

    chained = before is not None
    more = [pl.BlockSpec((tile, experts), row), pl.BlockSpec(memory_space=pl.ANY)] * chained
    aliases = {8: 0} if chained else {}
    if slot:
        aliases[9] = 2
        deps = (before[2], *deps)
    specs, deps = after(deps)
    return pl.pallas_call(
        functools.partial(expert_grads_kernel, chained, steps),
        grid_spec=pltpu.PrefetchScalarGridSpec(
            num_scalar_prefetch=1,
            grid=(steps,),
            in_specs=[
                pl.BlockSpec((tile, width), row),
                pl.BlockSpec((tile, width), row),
                pl.BlockSpec((tile, experts), row),
                pl.BlockSpec((1, width, hidden), weight),
                pl.BlockSpec((1, width, hidden), weight),
                pl.BlockSpec((1, hidden, width), weight),
            ]
            + more
            + specs,
            out_specs=[
                pl.BlockSpec((1, 3, tile, hidden), lambda i, w: (j, 0, i, 0)),
                pl.BlockSpec((tile, experts), row),
                pl.BlockSpec((3, width, hidden), lambda i, w: (slot, 0, 0)),
            ],
            scratch_shapes=[pltpu.VMEM((3, width, hidden), F32)] * (steps > 1),
        ),
        out_shape=[
            jax.ShapeDtypeStruct((per_core, 3, rows, hidden), BF),
            jax.ShapeDtypeStruct((rows, experts), F32),
            jax.ShapeDtypeStruct((3 * slots, width, hidden), BF),
        ],
        input_output_aliases=aliases,
        compiler_params=params(),
        cost_estimate=cost(16 * rows * width * hidden, 20, rows * hidden),
    )(
        jnp.stack([which, column]).astype(jnp.int32),
        h, g, on, w_gate, w_up, w_down,
        *((before[1], before[0]) if chained else ()),
        *deps,
    )


def expert_hidden_kernel(given, split, where, gate_ref, up_ref, wg_ref, wu_ref, *refs):
    e, count = pl.program_id(1), pl.num_programs(1)
    acc = refs[-1]
    part = nt(gate_ref[0, 0], wg_ref[0]) + nt(up_ref[0, 0], wu_ref[0])

    @pl.when(e == 0)
    def _():
        acc[...] = part + refs[0][...].astype(F32) if given else part

    @pl.when(e > 0)
    def _():
        acc[...] += part

    @pl.when(e == count - 1)
    def _():
        if not split:
            refs[-2][...] = acc[...].astype(BF)
            return
        size = refs[-2].shape[1]
        for out, member in ((refs[-3], where[1]), (refs[-2], 1 - where[1])):
            at = pl.ds(pl.multiple_of(member * size, LANES), size)
            out[...] = acc[:, at].astype(BF)


def expert_hidden(first, member, mid, tree, w_gate, w_up, came, split, deps):
    count, _, rows, hidden = mid.shape
    width = w_gate.shape[1]
    rows //= 2
    tile = 448
    tiles = rows // tile

    def weight(i, e, f):
        return (f[0] + e, 0, 0)

    def row(i, e, f):
        return (i, 0)

    given = [came] if came is not None else []
    specs, deps = after(deps)
    outs = 2 if split else 1
    return pl.pallas_call(
        functools.partial(expert_hidden_kernel, bool(given), split),
        grid_spec=pltpu.PrefetchScalarGridSpec(
            num_scalar_prefetch=1,
            grid=(tiles, count),
            in_specs=[
                pl.BlockSpec((1, 1, tile, hidden), lambda i, e, f: (e, 1, tree * tiles + i, 0)),
                pl.BlockSpec((1, 1, tile, hidden), lambda i, e, f: (e, 2, tree * tiles + i, 0)),
                pl.BlockSpec((1, width, hidden), weight),
                pl.BlockSpec((1, width, hidden), weight),
            ]
            + [pl.BlockSpec((tile, width), row) for _ in given]
            + specs,
            out_specs=[pl.BlockSpec((tile, width // outs), row)] * outs,
            scratch_shapes=[pltpu.VMEM((tile, width), F32)],
        ),
        out_shape=[jax.ShapeDtypeStruct((rows, width // outs), BF)] * outs,
        compiler_params=params(),
        cost_estimate=cost(6 * count * rows * width * hidden, 20),
    )(jnp.stack([first, member]).astype(jnp.int32), mid, mid, w_gate, w_up, *given, *deps)


def expert_mix_kernel(first, mid_ref, wd_ref, *refs):
    e, count = pl.program_id(1), pl.num_programs(1)
    acc = refs[-1]
    part = nn(mid_ref[0, 0], wd_ref[0])

    @pl.when(e == 0)
    def _():
        acc[...] = part

    @pl.when(e > 0)
    def _():
        acc[...] += part

    @pl.when(e == count - 1)
    def _():
        refs[-2][...] = acc[...].astype(BF)


def expert_mix(first, mid, tree, w_down, deps):
    count, _, rows, hidden = mid.shape
    width = w_down.shape[2]
    rows //= 2
    tile = 448
    tiles = rows // tile
    specs, deps = after(deps)
    return pl.pallas_call(
        expert_mix_kernel,
        grid_spec=pltpu.PrefetchScalarGridSpec(
            num_scalar_prefetch=1,
            grid=(tiles, count),
            in_specs=[
                pl.BlockSpec((1, 1, tile, hidden), lambda i, e, f: (e, 0, tree * tiles + i, 0)),
                pl.BlockSpec((1, hidden, width), lambda i, e, f: (f[0] + e, 0, 0)),
            ]
            + specs,
            out_specs=pl.BlockSpec((tile, width), lambda i, e, f: (i, 0)),
            scratch_shapes=[pltpu.VMEM((tile, width), F32)],
        ),
        out_shape=jax.ShapeDtypeStruct((rows, width), BF),
        compiler_params=params(),
        cost_estimate=cost(3 * count * rows * width * hidden, 10),
    )(jnp.reshape(first, (1,)).astype(jnp.int32), mid, w_down, *deps)


def out_grads_kernel(parts, where, *refs):
    branch, out_ref = refs[4 * parts : 4 * parts + 2], refs[-1]
    for own in range(2):

        @pl.when(where[0] == own)
        def _():
            for part in range(parts):
                at = (1 - own) * parts + part
                total = sum(
                    tn(refs[2 * parts * t + at][...], branch[t][...]) for t in range(2)
                )
                size = total.shape[0]
                out_ref[part * size : (part + 1) * size, :] = total.astype(BF)


def out_grads(own, attended, branch, deps):
    parts = len(attended[0]) // 2
    size, columns = attended[0][0].shape[1], branch[0].shape[1]
    specs, deps = after(deps)
    return pl.pallas_call(
        functools.partial(out_grads_kernel, parts),
        in_specs=[pl.BlockSpec(memory_space=pltpu.SMEM)]
        + [pl.BlockSpec(memory_space=pltpu.VMEM)] * (4 * parts + 2)
        + specs,
        out_shape=jax.ShapeDtypeStruct((parts * size, columns), BF),
        compiler_params=params(),
        cost_estimate=cost(4 * branch[0].shape[0] * columns * size * parts, 8),
    )(jnp.reshape(own, (1,)).astype(jnp.int32), *attended[0], *attended[1], *branch, *deps)


def tie_kernel(*refs):
    pass


def tie(v, deps):
    if not deps:
        return v
    specs, deps = after((v, *deps))
    return pl.pallas_call(
        tie_kernel,
        in_specs=specs,
        out_specs=pl.BlockSpec(memory_space=pl.ANY),
        out_shape=jax.ShapeDtypeStruct(v.shape, v.dtype),
        input_output_aliases={0: 0},
        cost_estimate=cost(0, 0),
    )(*deps)


def branch_kernel(
    where, mine_ref, came_ref, sums_ref, gl_ref, logits_ref, router_ref, middle_ref, inv_ref,
    gain_ref, grad_ref, w_ref, gain_grad_ref, full_ref, low_ref, theirs_ref, own_ref,
):
    rows, columns = middle_ref.shape
    gl = gl_ref[...]
    total = mine_ref[...].astype(F32) + came_ref[:rows, :].astype(F32)
    total += nt(gl, router_ref[...])
    products = jnp.sum(gl.astype(F32) * logits_ref[...], axis=-1, keepdims=True)
    mean = (sums_ref[...] + get_column(came_ref) + products) / (2 * columns)
    inv = inv_ref[...]
    normed = middle_ref[...] * inv
    gain_grad_ref[...] = jnp.sum(total * normed, axis=0, keepdims=True)
    at = pl.ds(pl.multiple_of(where[0] * columns, LANES), columns)
    grad = grad_ref[:, at].astype(F32)
    grad += inv * (total * gain_ref[...].astype(F32) - normed * mean)
    full_ref[...] = grad
    low = grad.astype(BF)
    low_ref[...] = low
    for out, member in ((theirs_ref, 1 - where[0]), (own_ref, where[0])):
        size = out.shape[1]
        heads = pl.ds(pl.multiple_of(member * size, 16), size)
        out[...] = nt(low, w_ref[heads, :]).astype(out.dtype)


def branch_back(member, mine, came, sums, gl, logits, router, middle, inv, gain, grad, w_out, deps):
    rows, columns = middle.shape
    size = w_out.shape[0] // 2
    specs, deps = after(deps)
    inputs = (mine, came, sums, gl, logits, router, middle, inv, gain)

    def all_of(i):
        return (0, 0)

    outs = [
        jax.ShapeDtypeStruct((1, columns), F32),
        jax.ShapeDtypeStruct((rows, columns), F32),
        jax.ShapeDtypeStruct((rows, columns), BF),
        jax.ShapeDtypeStruct((rows, size), BF),
        jax.ShapeDtypeStruct((rows, size), F32),
    ]

    def kernel(where, *refs):
        branch_kernel(where, *refs[:11], *refs[-5:])

    return pl.pallas_call(
        kernel,
        grid=(1,),
        in_specs=[pl.BlockSpec(memory_space=pltpu.SMEM)]
        + [pl.BlockSpec(a.shape, all_of) for a in inputs]
        + [pl.BlockSpec((rows, grad.shape[1]), all_of), pl.BlockSpec(w_out.shape, all_of)]
        + specs,
        out_specs=[pl.BlockSpec(o.shape, all_of) for o in outs],
        out_shape=outs,
        compiler_params=params(),
        cost_estimate=cost(2 * rows * columns * w_out.shape[0], 10),
    )(jnp.reshape(member, (1,)), *inputs, grad, w_out, *deps)


SLOTS = 128


def picked(gates_ref, slots_ref, block, expert):
    gates = gates_ref[block, pl.ds(expert, 1), :]
    slots = slots_ref[block, pl.ds(expert, 1), :]
    slot = lax.broadcasted_iota(jnp.int32, (SLOTS, gates.shape[1]), 0)
    return (slot == slots) & (gates > 0.0), gates


def one_hot(hit):
    return jnp.where(hit, 1.0, 0.0).astype(BF)


def expert_pair_kernel(
    chained, where, h_ref, g_ref, gates_ref, slots_ref, wg_ref, wu_ref, wd_ref, *refs
):
    mid_ref, gg_ref, own_ref, he_ref, ge_ref = refs[-5:]
    step = pl.program_id(0)
    expert = where[1] + step

    @pl.when(step == 0)
    def _():
        gg_ref[...] = refs[0][...] if chained else jnp.zeros_like(gg_ref)

    count = gates_ref.shape[2]
    hits, scales = [], []
    for b in range(4):
        hit, gates = picked(gates_ref, slots_ref, b, expert)
        pick = one_hot(hit)
        to = slice(b * SLOTS, (b + 1) * SLOTS)
        at = slice(b * count, (b + 1) * count)
        he_ref[to, :] = nn(pick, h_ref[at, :]).astype(BF)
        ge_ref[to, :] = nn(pick, g_ref[at, :]).astype(BF)
        hits.append(hit)
        scales.append(jnp.sum(jnp.where(hit, gates, 0.0), axis=-1, keepdims=True))
    on = jnp.concatenate(scales, 0)
    h, g = he_ref[...], ge_ref[...]
    gate_pre = nn(h, wg_ref[0])
    up_pre = nn(h, wu_ref[0])
    grad_mid = nt(g, wd_ref[0])
    sig = 1.0 / (1.0 + jnp.exp(-gate_pre))
    silu = gate_pre * sig
    mid = silu * up_pre
    column = jnp.sum(grad_mid * mid, axis=-1, keepdims=True)
    for b in range(4):
        part = jnp.where(hits[b], column[b * SLOTS : (b + 1) * SLOTS], 0.0)
        gg_ref[b, pl.ds(expert, 1), :] = jnp.sum(part, axis=0, keepdims=True)
    act = (on * mid).astype(BF)
    grad_mid = on * grad_mid
    ggp = (grad_mid * up_pre * (sig * (1.0 + gate_pre * (1.0 - sig)))).astype(BF)
    gup = (grad_mid * silu).astype(BF)
    mid_ref[0, 0] = act
    mid_ref[0, 1] = ggp
    mid_ref[0, 2] = gup
    own_ref[0] = tn(h, ggp).astype(BF)
    own_ref[1] = tn(h, gup).astype(BF)
    own_ref[2] = tn(g, act).astype(BF)


def expert_pair(pair, per_core, first, column, h, g, gates, slots, w_gate, w_up, w_down, before, deps):
    rows, width = h.shape
    hidden = w_gate.shape[2]

    def all_of(i, w):
        return (0, 0)

    def every(i, w):
        return (0, 0, 0)

    def weight(i, w):
        return (w[0] + i, 0, 0)

    chained = before is not None
    more = [pl.BlockSpec(gates.shape, every), pl.BlockSpec(memory_space=pl.ANY)] * chained
    specs, deps = after(deps)
    return pl.pallas_call(
        functools.partial(expert_pair_kernel, chained),
        grid_spec=pltpu.PrefetchScalarGridSpec(
            num_scalar_prefetch=1,
            grid=(2,),
            in_specs=[
                pl.BlockSpec((rows, width), all_of),
                pl.BlockSpec((rows, width), all_of),
                pl.BlockSpec(gates.shape, every),
                pl.BlockSpec(gates.shape, every),
                pl.BlockSpec((1, width, hidden), weight),
                pl.BlockSpec((1, width, hidden), weight),
                pl.BlockSpec((1, hidden, width), weight),
            ]
            + more
            + specs,
            out_specs=[
                pl.BlockSpec((1, 3, 4 * SLOTS, hidden), lambda i, w: (2 * pair + i, 0, 0, 0)),
                pl.BlockSpec(gates.shape, every),
                pl.BlockSpec((3, width, hidden), lambda i, w: (i, 0, 0)),
            ],
            scratch_shapes=[pltpu.VMEM((4 * SLOTS, width), BF)] * 2,
        ),
        out_shape=[
            jax.ShapeDtypeStruct((per_core, 3, 4 * SLOTS, hidden), BF),
            jax.ShapeDtypeStruct(gates.shape, F32),
            jax.ShapeDtypeStruct((6, width, hidden), BF),
        ],
        input_output_aliases={9: 0} if chained else {},
        compiler_params=params(),
        cost_estimate=cost(24 * 4 * SLOTS * width * hidden, 24, rows * hidden),
    )(
        jnp.stack([first, column]).astype(jnp.int32),
        h, g, gates, slots, w_gate, w_up, w_down,
        *((before[1], before[0]) if chained else ()),
        *deps,
    )


def add_picked(acc, tree, column, gates_ref, slots_ref, outs):
    step, steps = pl.program_id(0), pl.num_programs(0)
    count = gates_ref.shape[2]
    for b in range(2):
        pick = jnp.concatenate(
            [
                one_hot(picked(gates_ref, slots_ref, 2 * tree + b, column + 2 * step + i)[0])
                for i in range(2)
            ],
            0,
        )
        rows = jnp.concatenate([out[b * SLOTS : (b + 1) * SLOTS] for out in outs], 0)
        at = slice(b * count, (b + 1) * count)
        acc[at, :] += tn(pick, rows)


def pair_hidden_kernel(given, tree, where, gates_ref, slots_ref, gp_ref, up_ref, wg_ref, wu_ref, *refs):
    step, acc = pl.program_id(0), refs[-1]

    @pl.when(step == 0)
    def _():
        acc[...] = refs[0][...].astype(F32) if given else jnp.zeros_like(acc)

    outs = [
        (nt(gp_ref[i, 0], wg_ref[i]) + nt(up_ref[i, 0], wu_ref[i])).astype(BF) for i in range(2)
    ]
    add_picked(acc, tree, where[1], gates_ref, slots_ref, outs)

    @pl.when(step == pl.num_programs(0) - 1)
    def _():
        if not given:
            refs[-2][...] = acc[...].astype(BF)
            return
        mine, theirs, sums = refs[-4:-1]
        rows, size = mine.shape
        for out, member in ((mine, where[2]), (theirs, 1 - where[2])):
            at = pl.ds(pl.multiple_of(member * size, LANES), size)
            out[:rows, :] = acc[:, at].astype(BF)
        sums[...] = jnp.sum(acc[...] * refs[1][...].astype(F32), axis=-1, keepdims=True)
        put_column(theirs, sums[...])


def pair_hidden(first, column, member, tree, gates, slots, mid, w_gate, w_up, came, deps):
    count, _, rows, hidden = mid.shape
    width = w_gate.shape[1]
    tokens = 2 * gates.shape[2]
    given = came or ()

    def weight(i, w):
        return (w[0] + i, 0, 0)

    def every(i, w):
        return (0, 0, 0)

    def all_of(i, w):
        return (0, 0)

    specs, deps = after(deps)
    if given:
        half = width // 2
        outs = [((tokens, half), BF), ((tokens + 16, half), BF), ((tokens, 1), F32)]
    else:
        outs = [((tokens, width), BF)]
    return pl.pallas_call(
        functools.partial(pair_hidden_kernel, bool(given), tree),
        grid_spec=pltpu.PrefetchScalarGridSpec(
            num_scalar_prefetch=1,
            grid=(count // 2,),
            in_specs=[
                pl.BlockSpec(gates.shape, every),
                pl.BlockSpec(gates.shape, every),
                pl.BlockSpec((2, 1, rows // 2, hidden), lambda i, w: (i, 1, tree, 0)),
                pl.BlockSpec((2, 1, rows // 2, hidden), lambda i, w: (i, 2, tree, 0)),
                pl.BlockSpec((2, width, hidden), weight),
                pl.BlockSpec((2, width, hidden), weight),
            ]
            + [pl.BlockSpec((tokens, width), all_of) for _ in given]
            + specs,
            out_specs=[pl.BlockSpec(shape, all_of) for shape, _ in outs],
            scratch_shapes=[pltpu.VMEM((tokens, width), F32)],
        ),
        out_shape=[jax.ShapeDtypeStruct(*o) for o in outs],
        compiler_params=params(),
        cost_estimate=cost(6 * count * rows * width * hidden, 16),
    )(
        jnp.stack([first // 2, column, member]).astype(jnp.int32),
        gates, slots, mid, mid, w_gate, w_up, *given, *deps,
    )


def pair_mix_kernel(tree, where, gates_ref, slots_ref, act_ref, wd_ref, *refs):
    step, acc = pl.program_id(0), refs[-1]

    @pl.when(step == 0)
    def _():
        acc[...] = jnp.zeros_like(acc)

    outs = [nn(act_ref[i, 0], wd_ref[i]).astype(BF) for i in range(2)]
    add_picked(acc, tree, where[1], gates_ref, slots_ref, outs)

    @pl.when(step == pl.num_programs(0) - 1)
    def _():
        refs[-2][...] = acc[...].astype(BF)


def pair_mix(first, column, tree, gates, slots, mid, w_down, deps):
    count, _, rows, hidden = mid.shape
    width = w_down.shape[2]
    tokens = 2 * gates.shape[2]

    def every(i, w):
        return (0, 0, 0)

    specs, deps = after(deps)
    return pl.pallas_call(
        functools.partial(pair_mix_kernel, tree),
        grid_spec=pltpu.PrefetchScalarGridSpec(
            num_scalar_prefetch=1,
            grid=(count // 2,),
            in_specs=[
                pl.BlockSpec(gates.shape, every),
                pl.BlockSpec(gates.shape, every),
                pl.BlockSpec((2, 1, rows // 2, hidden), lambda i, w: (i, 0, tree, 0)),
                pl.BlockSpec((2, hidden, width), lambda i, w: (w[0] + i, 0, 0)),
            ]
            + specs,
            out_specs=pl.BlockSpec((tokens, width), lambda i, w: (0, 0)),
            scratch_shapes=[pltpu.VMEM((tokens, width), F32)],
        ),
        out_shape=jax.ShapeDtypeStruct((tokens, width), BF),
        compiler_params=params(),
        cost_estimate=cost(3 * count * rows * width * hidden, 10),
    )(jnp.stack([first // 2, column]).astype(jnp.int32), gates, slots, mid, w_down, *deps)


def finish_kernel(layout, where, *refs):
    outs, last = refs[2:-1], refs[-1]
    for g in range(2):
        for out, to, start, size in layout[g]:
            at = slice(start, start + size)
            v = jnp.where(where[0] == g, refs[0][:, at], refs[1][:, at])
            outs[out][:, to : to + size] = v.astype(F32)
    start = refs[0].shape[1] - last.shape[2]
    last[where[0]] = refs[0][:, start:].astype(F32)
    last[1 - where[0]] = refs[1][:, start:].astype(F32)


def finish(core, mine, other, layout, widths, out_width):
    rows, columns = mine.shape
    tile = rows // 4

    def row(i, w):
        return (i, 0)

    return pl.pallas_call(
        functools.partial(finish_kernel, layout),
        grid_spec=pltpu.PrefetchScalarGridSpec(
            num_scalar_prefetch=1,
            grid=(4,),
            in_specs=[pl.BlockSpec((tile, columns), row)] * 2,
            out_specs=[pl.BlockSpec((tile, w), row) for w in widths]
            + [pl.BlockSpec((2, tile, out_width), lambda i, w: (0, i, 0))],
        ),
        out_shape=[jax.ShapeDtypeStruct((rows, w), F32) for w in widths]
        + [jax.ShapeDtypeStruct((2, rows, out_width), F32)],
        compiler_params=params(),
        cost_estimate=cost(0, 12),
    )(jnp.reshape(core, (1,)).astype(jnp.int32), mine, other)


def finish_experts_kernel(per_core, half, where, *refs):
    mine, came, outs = refs[:per_core], refs[per_core : 2 * per_core], refs[2 * per_core :]
    rows = pl.ds(pl.multiple_of(where[0] * half, 16), half)
    for j in range(per_core):
        for source, at in ((mine, where[0] * per_core + j), ((came), (1 - where[0]) * per_core + j)):
            v = source[j][:, rows, :].astype(F32)
            outs[0][at] = v[0]
            outs[1][at] = v[1]
            outs[2][at] = v[2]


def finish_experts(core, mine, came):
    per_core = len(mine)
    _, rows, hidden = mine[0].shape
    half = rows // 2
    whole = pl.BlockSpec(memory_space=pltpu.VMEM)
    return pl.pallas_call(
        functools.partial(finish_experts_kernel, per_core, half),
        in_specs=[pl.BlockSpec(memory_space=pltpu.SMEM)] + [whole] * (2 * per_core),
        out_shape=[
            jax.ShapeDtypeStruct((2 * per_core, half, hidden), F32),
            jax.ShapeDtypeStruct((2 * per_core, half, hidden), F32),
            jax.ShapeDtypeStruct((2 * per_core, half, hidden), F32),
        ],
        compiler_params=params(),
        cost_estimate=cost(0, 10),
    )(jnp.reshape(core, (1,)), *mine, *came)


def local(
    tokens,
    norm_gain,
    w_query,
    key_weight,
    value_weight,
    w_out,
    ffn_gain,
    w_router,
    w_gate,
    w_up,
    w_down,
    parents,
    routes,
    cotangent,
):
    me = Mesh()
    paired = me.groups == 2
    tok_rows, width = tokens.shape
    tree_len = tok_rows * me.groups
    seg_len = tree_len // 16
    columns = width // me.groups
    all_q, all_k = w_query.shape[1], key_weight.shape[1]
    q_width, k_width = all_q // me.groups, all_k // me.groups
    kv_heads = k_width // HEAD_DIM
    parts = kv_heads // 2 if kv_heads % 2 == 0 else 1
    q_part, k_part = q_width // parts, k_width // parts
    gq, gk = q_part // HEAD_DIM, k_part // HEAD_DIM
    q_room, k_room = pairs(gq) * LANES, pairs(gk) * LANES
    lanes = q_room + 2 * k_room
    experts = w_gate.shape[0] * me.groups
    per_core = w_gate.shape[0] // 2
    partner = 1 - me.member

    def heads_of(member):
        found = []
        for weight, size, room in (
            (w_query, q_width, q_room),
            (key_weight, k_width, k_room),
            (value_weight, k_width, k_room),
        ):
            block = lax.dynamic_slice_in_dim(weight, member * size, size, 1)
            found.append(jnp.pad(block, ((0, 0), (0, room - size))))
        return jnp.concatenate(found, 1)

    projections = (w_query, key_weight, value_weight)
    gain_row = norm_gain[None]
    own, came = [], []
    along = jnp.split(cotangent, 2, 0)
    early = ()
    grad_came = []
    if paired:
        hot = jnp.any(
            routes.T[:, None, :] == jnp.arange(experts, dtype=jnp.int32)[None, :, None], axis=0
        )
        packet = jnp.concatenate(
            [
                w_router.T,
                jnp.pad(ffn_gain[None], ((0, 15), (0, 0))),
                jnp.pad(hot.astype(BF), ((0, 0), (0, columns - tok_rows))),
            ],
            0,
        )
        x_theirs, x_mine = split(me.member, tokens)
        x_came = me.swap_shard(x_theirs)
        packets = [packet, me.swap_shard(packet)]
        early = (packets[1],)
        grad_came.append(me.swap_shard(tie(along[0], (x_theirs,))))
        *theirs, hidden_first, x_columns, inv_one = project_theirs(
            me.member, parts, x_mine, x_came, gain_row, projections
        )
        own = project_own(me.member, parts, hidden_first, projections, (theirs[-1],))
        came = [me.swap_shard(theirs[0]), me.swap_shard(tie(theirs[1], own[:1]))]
    else:
        every_head = jnp.concatenate([heads_of(j) for j in range(me.groups)], 1)
        own_rows = tokens.astype(F32)
        inv_rows = lax.rsqrt(jnp.mean(own_rows * own_rows, axis=-1, keepdims=True) + EPS)
        x_columns = me.exchange(tokens, 1, 0)
        inv_one = me.gather(inv_rows, 0)
        hidden_first = (x_columns.astype(F32) * inv_one * norm_gain.astype(F32)).astype(BF)
        own.append(me.scatter(nn(hidden_first, every_head), 1))
        came.append(jnp.zeros(own[-1].shape, BF))

    gain_two = ffn_gain.astype(F32)

    index = jnp.arange(tree_len, dtype=jnp.int32)
    _, depth = tree_layout(index, seg_len)
    cos, sin = angle_tables(depth)
    visible = tree_mask(index, index, parents[0], seg_len)
    bias = jnp.where(visible, 0.0, -1e30).astype(F32)

    attended, lse, query, key, value, att_came = [], [], [], [], [], []
    for part in range(parts):
        a, b, c, d, e = attend(own[part], came[part], cos, sin, bias, gq, gk, (*early, *grad_came[:1]))
        attended.append(a)
        lse.append(b)
        query.append(c)
        key.append(d)
        value.append(e)
        if paired:
            att_came.append(me.swap_shard(a))
    if paired:
        sent = tie(along[1], att_came)
        grad_came.append(me.swap_shard(sent))
        mine = [cotangent, me.swap_core(cotangent)]
        others = [*grad_came, *(me.swap_core(v) for v in grad_came)]
        grad_all = jnp.where(
            me.member == 0,
            jnp.concatenate([mine[0], *others[:2], mine[1], *others[2:]], 0),
            jnp.concatenate([*others[:2], mine[0], *others[2:], mine[1]], 0),
        )
        starts = [
            member * q_width + part * q_part
            for member in (me.member, partner)
            for part in range(parts)
        ]
        middle, middle_low, squares = middle_of(
            attended + att_came, jnp.stack(starts).astype(jnp.int32), w_out, x_columns, True, (sent,)
        )
        attended_full = me.in_order(
            me.member, jnp.concatenate(attended, 1), jnp.concatenate(att_came, 1), 1
        )
        messages = [middle_low, me.swap_shard(middle_low)]
        hidden_all, gates_all, slots_all, inv_two, logits = hidden_packed(
            me.member,
            [
                (*messages, *packets),
                (*(me.swap_core(v) for v in messages), *(me.swap_core(v) for v in packets)),
            ],
            (grad_all,),
        )
    else:
        grad_tree = me.gather(cotangent, 0)
        grad_all = jnp.concatenate([grad_tree, me.swap_core(grad_tree)], 0)
        attended_full = me.gather(attended[0][:, :q_width], 1)
        where = jnp.zeros((1,), jnp.int32)
        middle, middle_low, squares = middle_of([attended_full], where, w_out, x_columns, False)
        route_hot = jnp.any(
            routes[:, :, None] == jnp.arange(experts, dtype=jnp.int32)[None, None, :], axis=1
        ).astype(F32)
        routed = me.gather(route_hot, 0)
        middle_low, squares = me.gather(middle_low, 1), me.total(squares)
        hidden_all, gates_all = hidden_of(
            [
                ([middle_low], [squares], routed),
                (
                    [me.swap_core(middle_low)],
                    [me.swap_core(squares)],
                    me.swap_core(routed),
                ),
            ],
            where,
            me.gather(ffn_gain, 0)[None],
            me.gather(w_router, 0),
        )
        inv_two = lax.rsqrt(squares / width + EPS)
    grad_tree = grad_all[:tree_len]
    hidden_all = hidden_all.reshape(2 * tree_len, width)
    normed_two = middle * inv_two
    hidden_own = (normed_two * gain_two).astype(BF)

    first = me.core * per_core
    chunk = width // me.chips
    def gates_grad(gates, grad, axis):
        return (gates * (grad - jnp.sum(gates * grad, axis=axis, keepdims=True))).astype(BF)

    def output_of(mixed_own, mixed_other):
        mixed = mixed_own.astype(F32) + me.swap_core(mixed_other).astype(F32)
        placed = lax.dynamic_update_slice_in_dim(
            jnp.zeros((tree_len, width), F32), middle, me.member * columns, 1
        )
        return mixed + placed

    def input_of(grad_middle, scaled, row_sums):
        normed = x_columns.astype(F32) * inv_one
        grad = grad_middle + inv_one * (scaled - normed * (me.total(row_sums) / width))
        return me.exchange(grad.astype(BF), 0, 1)

    flipped = bias.T
    if not paired:
        gates = gates_all[0]
        gates_all = gates_all.reshape(2 * tree_len, experts)
        before, rings = None, []
        for j in range(per_core):
            before = expert_grads(
                j, per_core, first + j, me.member * (2 * per_core) + first + j,
                hidden_all, grad_all, gates_all, w_gate, w_up, w_down, before, 0, 1, (),
            )
            mid, own_columns, grads = before
            ring = Scatter(me, lambda chip: lax.dynamic_slice_in_dim(grads, chip * chunk, chunk, 1))
            for _ in range(me.chips - 1):
                ring.start()
                ring.finish()
            rings.append(ring.held)
        grad_gates = me.total(own_columns[:tree_len] + me.swap_core(own_columns[tree_len:]))
        grad_logits = gates_grad(gates, grad_gates, -1)
        (grad_other,) = expert_hidden(first, me.member, mid, 1, w_gate, w_up, None, False, ())
        (grad_own,) = expert_hidden(
            first, me.member, mid, 0, w_gate, w_up, me.swap_core(grad_other), False, ()
        )
        mixed_other = expert_mix(first, mid, 1, w_down, ())
        mixed_own = expert_mix(first, mid, 0, w_down, ())
        result = me.scatter(output_of(mixed_own, mixed_other), 0).astype(BF)
        grad_hidden_two = nt(grad_logits, w_router) + me.scatter(grad_own, 1)
        grad_gain_two = jnp.sum(grad_hidden_two * normed_two, axis=0)[None]
        scaled = grad_hidden_two * gain_two
        mean = me.total(jnp.sum(scaled * normed_two, axis=-1, keepdims=True)) / width
        grad_columns = me.part(grad_tree, 1, me.member).astype(F32)
        grad_middle = grad_columns + inv_two * (scaled - normed_two * mean)
        grad_branch = grad_middle.astype(BF)
        own = me.scatter(nt(grad_branch, w_out), 1)
        own = jnp.pad(own, ((0, 0), (0, q_room - q_width)))
        grad_heads = attend_back(
            own, jnp.zeros(own.shape, BF), query[0], key[0], value[0], lse[0],
            cos, sin, flipped, gq, gk, 0, (),
        )
        grad_out = me.all_reduce(tn(attended_full, grad_branch))
        grad_full = me.gather(grad_heads, 1)
        every = me.all_reduce(tn(hidden_first, grad_full))
        every = every.reshape(columns, me.groups, lanes)
        grad_query, grad_key, grad_value = (
            every[:, :, start : start + size].reshape(columns, me.groups * size)
            for start, size in ((0, q_width), (q_room, k_width), (q_room + k_room, k_width))
        )
        grad_hidden_one = nt(grad_full, every_head)
        normed_one = x_columns.astype(F32) * inv_one
        grad_gain_one = jnp.sum(grad_hidden_one * normed_one, axis=0)[None]
        scaled = grad_hidden_one * norm_gain.astype(F32)
        row_sums = jnp.sum(scaled * normed_one, axis=-1, keepdims=True)
        input_grad = input_of(grad_middle, scaled, row_sums)
        grad_router = tn(hidden_own, grad_logits)
        small = me.butterfly(jnp.concatenate([grad_gain_one, grad_gain_two, grad_router.T], 0))
        sums = rings
        grad_gate, grad_up, grad_down = finish_experts(
            me.core, sums, [me.swap_core(v) for v in sums]
        )
    else:

        column = me.member * (2 * per_core) + first

        def pair_of(pair, before, deps):
            return expert_pair(
                pair, per_core, first + 2 * pair, column + 2 * pair,
                hidden_all, grad_all, gates_all, slots_all, w_gate, w_up, w_down, before, deps,
            )

        def hidden_grad(tree, came, deps):
            return pair_hidden(
                first, column, me.member, tree, gates_all, slots_all, mid, w_gate, w_up, came, deps
            )

        def mix_of(tree, deps):
            return pair_mix(first, column, tree, gates_all, slots_all, mid, w_down, deps)

        def ring_of(grads):
            return Scatter(me, lambda chip: lax.dynamic_slice_in_dim(grads, chip * chunk, chunk, 1))

        one = pair_of(0, None, ())
        ring_a = ring_of(one[2])
        sent = ring_a.start()
        mid, own_rows, grads = pair_of(1, one, ())
        sent_a = ring_a.hop(own_rows)
        ring_b = ring_of(grads)
        sent_b = ring_b.start()
        grad_gates = me.total(own_rows[:2] + me.swap_core(own_rows[2:]))
        grad_logits = gates_grad(gates_all[:2], grad_gates, 1)
        grad_logits = grad_logits.transpose(0, 2, 1).reshape(tree_len, experts)
        (grad_other,) = hidden_grad(1, None, (sent_a, sent_b))
        other_came = me.swap_core(grad_other)
        sent = ring_a.hop(grad_other)
        grad_mine, grad_theirs, row_sums = hidden_grad(0, (other_came, hidden_all), (sent,))
        hidden_came = me.swap_shard(grad_theirs)
        sent = ring_b.hop(grad_mine)
        mixed_other = mix_of(1, (sent,))
        sent = ring_a.hop(mixed_other)
        mixed_own = mix_of(0, (sent, grad_logits))
        sent = ring_b.hop(mixed_own)
        grad_gain_two, grad_middle, grad_branch, theirs, own = branch_back(
            me.member, grad_mine, hidden_came, row_sums, grad_logits, logits, w_router,
            middle, inv_two, ffn_gain[None], grad_all, w_out, (sent,),
        )
        came = me.swap_shard(theirs)
        sent = ring_a.hop(grad_branch)
        grad_out = out_grads(
            me.core == me.member,
            [attended + att_came, [me.swap_core(v) for v in attended + att_came]],
            [grad_branch, me.swap_core(grad_branch)],
            (sent,),
        )
        sent = ring_b.hop(grad_out)
        heads_a = attend_back(
            own, came, query[0], key[0], value[0], lse[0], cos, sin, flipped, gq, gk, 0,
            (sent,),
        )
        back_a = me.swap_shard(heads_a)
        sent = ring_a.hop(heads_a)
        heads_b = attend_back(
            own, came, query[1], key[1], value[1], lse[1], cos, sin, flipped, gq, gk, q_part,
            (sent,),
        )
        back_a = tie(back_a, (heads_b,))
        back_b = me.swap_shard(heads_b)
        summed = output_of(tie(mixed_own, (back_a,)), mixed_other).astype(BF)
        to_send = me.part(summed, 0, partner)
        sent = ring_b.hop(heads_b)
        grad_pairs = [(heads_a, back_a), (heads_b, back_b)]
        grads_mine = weight_grads(
            me.member,
            me.core,
            (hidden_first, me.swap_core(hidden_first)),
            (grad_pairs, [tuple(me.swap_core(v) for v in pair) for pair in grad_pairs]),
            grad_out,
            (sent, to_send),
        )
        head_chunk = grads_mine.shape[0] // me.chips
        ring_w = Scatter(
            me, lambda chip: lax.dynamic_slice_in_dim(grads_mine, chip * head_chunk, head_chunk, 0)
        )
        sent = ring_w.start()
        sent = ring_a.hop(sent)
        grad_router = tn(hidden_own, grad_logits)
        scaled, row_sums, grad_gain_one = project_back(
            me.member, x_columns, inv_one, gain_row, projections, grad_pairs, (sent,)
        )
        beside = {1: (scaled,)}

        def later(hop, v):
            beside[hop] = (*beside.get(hop, ()), v)

        hops, experts_done = me.chips - 1, None
        for hop in range(1, 2 * hops):
            w = ring_w.finish()
            if hop == hops:
                ring_w = Gather(me, ring_w.held)
            if hop == 1:
                result = me.swap_shard(tie(to_send, (w,))).astype(F32)
                result = (result + me.part(summed, 0, me.member).astype(F32)).astype(BF)
                later(6, result)
            if hop == 2:
                input_grad = input_of(grad_middle, scaled, tie(row_sums, (w,)))
                later(7, input_grad)
            if hop == hops + 1:
                small = me.butterfly(
                    tie(
                        jnp.concatenate([grad_gain_one, grad_gain_two, grad_router.T], 0), (w,)
                    )
                )
                later(2 * hops - 1, small)
            deps = beside.get(hop, ())
            ring = {1: ring_b, 3: ring_a, 4: ring_b, 6: ring_a, 7: ring_b, 9: ring_b}.get(hop)
            if ring is not None and ring.hops < hops:
                deps = (*deps, ring.finish(w))
                if ring.hops < hops:
                    ring.start()
                elif ring_a.hops == ring_b.hops:
                    sums = [h for r in (ring_a, ring_b) for h in jnp.split(r.held, 2, 0)]
                    experts_done = finish_experts(me.core, sums, [me.swap_core(v) for v in sums])
                    later(hop + 4, experts_done[0])
            ring_w.start(*deps)
        ring_w.finish()
        grad_gate, grad_up, grad_down = experts_done
        layout = [
            [
                (out, j * step + part * size, j * lanes + start, size)
                for j in range(2)
                for out, step, start, size in (
                    (0, q_width, 0, q_part),
                    (1, k_width, q_room, k_part),
                    (2, k_width, q_room + k_room, k_part),
                )
            ]
            for part in range(parts)
        ]
        grad_query, grad_key, grad_value, grad_out = finish(
            me.core, ring_w.whole, me.swap_core(ring_w.whole), layout, (all_q, all_k, all_k), columns
        )
        grad_out = grad_out.reshape(-1, columns)

    return (
        result,
        input_grad,
        small[0],
        grad_query,
        grad_key,
        grad_value,
        grad_out,
        small[1],
        small[2:].T,
        grad_gate,
        grad_up,
        grad_down.transpose(0, 2, 1),
    )


def solution(mesh):
    return jax.shard_map(
        local,
        mesh=mesh,
        in_specs=(
            P(("rep", "shard"), None),
            P("shard"),
            P("shard", None),
            P("shard", None),
            P("shard", None),
            P(None, "shard"),
            P("shard"),
            P("shard", None),
            P("shard", None, None),
            P("shard", None, None),
            P("shard", None, None),
            P("rep", None),
            P(("rep", "shard"), None),
            P(("rep", "shard"), None),
        ),
        out_specs=(
            P(("rep", "shard"), None),
            P(("rep", "shard"), None),
            P("shard"),
            P("shard", None),
            P("shard", None),
            P("shard", None),
            P(None, "shard"),
            P("shard"),
            P("shard", None),
            P("shard", "rep", None),
            P("shard", "rep", None),
            P("shard", None, "rep"),
        ),
        check_vma=False,
    )
```

```python
import functools

import jax
import jax.numpy as jnp
from jax import lax
from jax.experimental import pallas as pl
from jax.experimental.pallas import tpu as pltpu
from jax.sharding import PartitionSpec as P

HEAD_DIM = 64
LANES = 128
EPS = 1e-06
BF = jnp.bfloat16
F32 = jnp.float32
VMEM_LIMIT = 60 << 20


def tree_layout(position, seg_len):
    trunk_len = 4 * seg_len
    beyond = position - trunk_len
    segment = jnp.where(position < trunk_len, 0, 1 + beyond // seg_len)
    inner = jnp.where(
        segment <= 4, trunk_len + beyond % seg_len, trunk_len + seg_len + beyond % seg_len
    )
    depth_position = jnp.where(position < trunk_len, position, inner)
    return (segment, depth_position)


def lookup(segment, parents_row):
    labels = jnp.arange(parents_row.shape[0], dtype=jnp.int32)
    picked = jnp.where(segment[:, None] == labels[None, :], parents_row[None, :], 0)
    return jnp.sum(picked, axis=1)


def tree_mask(query_index, key_index, parents_row, seg_len):
    query_seg, _ = tree_layout(query_index, seg_len)
    key_seg, _ = tree_layout(key_index, seg_len)
    parent_one = lookup(query_seg, parents_row)
    parent_two = lookup(parent_one, parents_row)
    key_row = key_seg[None, :]
    related = (
        (key_row == query_seg[:, None])
        | (key_row == parent_one[:, None])
        | (key_row == parent_two[:, None])
    )
    return related & (key_index[None, :] <= query_index[:, None])


def angle_tables(depth_position):
    half = HEAD_DIM // 2
    frequency = 10000.0 ** (-2.0 * jnp.arange(half, dtype=F32) / HEAD_DIM)
    angles = depth_position.astype(F32)[:, None] * frequency[None, :]
    cosine, sine = jnp.cos(angles), jnp.sin(angles)
    return (
        jnp.concatenate([cosine] * 4, 1),
        jnp.concatenate([-sine, sine, -sine, sine], 1),
    )


def dot(a, b, dims):
    return lax.dot_general(a, b, (dims, ((), ())), preferred_element_type=F32)


def nn(a, b):
    return dot(a, b, ((1,), (0,)))


def nt(a, b):
    return dot(a, b, ((1,), (1,)))


def tn(a, b):
    return dot(a, b, ((0,), (0,)))


class Mesh:
    def __init__(self):
        self.groups = lax.axis_size("shard")
        self.member = lax.axis_index("shard")
        self.reps = lax.axis_size("rep")
        self.rep = lax.axis_index("rep")
        self.core = self.rep % 2
        self.chip = self.rep // 2
        self.chips = self.reps // 2
        rows = self.chips // 2
        order = [2 * z for z in range(rows)] + [2 * z + 1 for z in range(rows - 1, -1, -1)]
        self.ring = []
        for place, chip in enumerate(order):
            after, before = order[(place + 1) % self.chips], order[place - 1]
            self.ring += [(2 * chip, 2 * after), (2 * chip + 1, 2 * before + 1)]
        self.place = jnp.where(
            self.chip % 2 == 0, self.chip // 2, self.chips - 1 - self.chip // 2
        )
        self.way = 1 - 2 * self.core

    def chip_at(self, place):
        place = place % self.chips
        rows = self.chips // 2
        return jnp.where(place < rows, 2 * place, 2 * (self.chips - 1 - place) + 1)

    def swap_shard(self, v):
        return lax.ppermute(v, "shard", [(0, 1), (1, 0)])

    def swap_core(self, v):
        return lax.ppermute(v, "rep", [(r, r ^ 1) for r in range(self.reps)])

    def along_ring(self, v):
        return lax.ppermute(v, "rep", self.ring)

    def part(self, v, axis, which):
        size = v.shape[axis] // self.groups
        return lax.dynamic_slice_in_dim(v, which * size, size, axis)

    def gather(self, v, axis):
        if self.groups != 2:
            return lax.all_gather(v, "shard", axis=axis, tiled=True)
        other = self.swap_shard(v)
        return self.in_order(self.member, v, other, axis)

    def in_order(self, which, mine, other, axis):
        return jnp.where(
            which == 0,
            jnp.concatenate([mine, other], axis),
            jnp.concatenate([other, mine], axis),
        )

    def exchange(self, v, split_axis, concat_axis):
        if self.groups != 2:
            return lax.all_to_all(v, "shard", split_axis, concat_axis, tiled=True)
        other = self.swap_shard(self.part(v, split_axis, 1 - self.member))
        mine = self.part(v, split_axis, self.member)
        return self.in_order(self.member, mine, other, concat_axis)

    def scatter(self, v, axis):
        if self.groups != 2:
            return lax.psum_scatter(
                v.astype(BF), "shard", scatter_dimension=axis, tiled=True
            ).astype(F32)
        other = self.swap_shard(self.part(v, axis, 1 - self.member).astype(BF))
        return self.part(v, axis, self.member).astype(F32) + other.astype(F32)

    def total(self, v):
        if self.groups != 2:
            return lax.psum(v, "shard")
        return v + self.swap_shard(v)

    def ring_sum(self, v):
        chunk = v.shape[0] // self.chips
        ring = Scatter(self, lambda chip: lax.dynamic_slice_in_dim(v, chip * chunk, chunk, 0))
        for _ in range(self.chips - 1):
            ring.start()
            ring.finish()
        ring = Gather(self, ring.held)
        for _ in range(self.chips - 1):
            ring.start()
            ring.finish()
        whole = jnp.zeros(v.shape, v.dtype)
        for at, part in zip(ring.chips(), ring.chunks):
            whole = lax.dynamic_update_slice_in_dim(whole, part, at * chunk, 0)
        return whole

    def all_reduce(self, v):
        half = v.shape[0] // 2
        v = v.astype(BF)
        mine = lax.dynamic_slice_in_dim(v, self.core * half, half, 0)
        other = self.swap_core(
            lax.dynamic_slice_in_dim(v, (1 - self.core) * half, half, 0)
        )
        whole = self.ring_sum((mine.astype(F32) + other.astype(F32)).astype(BF))
        return self.in_order(self.core, whole, self.swap_core(whole), 0).astype(F32)

    def swap_rep(self, v, bit):
        return lax.ppermute(v, "rep", [(r, r ^ bit) for r in range(self.reps)])

    def butterfly(self, v):
        bit = 1
        while bit < self.reps:
            v = v + self.swap_rep(v, bit)
            bit *= 2
        return v


class Scatter:
    def __init__(self, me, own):
        self.me, self.own, self.hops = me, own, 0
        self.held = own(me.chip_at(me.place - me.way))

    def start(self, *deps):
        sent = tie(self.held, deps)
        self.came = self.me.along_ring(sent)
        return sent

    def hop(self, *deps):
        self.finish(*deps)
        return self.start()

    def finish(self, *deps):
        self.hops += 1
        self.came = tie(self.came, deps)
        mine = self.own(self.me.chip_at(self.me.place - self.me.way * (self.hops + 1)))
        self.held = (self.came.astype(F32) + mine.astype(F32)).astype(BF)
        return self.came


class Gather:
    def __init__(self, me, held):
        self.me, self.came, self.hops = me, held, 0
        self.chunks, self.other = [], []

    def chips(self):
        me = self.me
        return [me.chip_at(me.place - me.way * hop) for hop in range(me.chips)]

    def keep(self, chunk):
        self.chunks.append(chunk)
        self.other.append(self.me.swap_core(chunk))

    def start(self, *deps):
        sent = tie(self.came, deps)
        self.came = self.me.along_ring(sent)
        self.keep(sent)
        return sent

    def finish(self):
        self.hops += 1
        if self.hops == self.me.chips - 1:
            self.keep(self.came)


def pairs(heads):
    return -(-heads // 2)


def rope(v, cos, sin, back):
    lane = lax.broadcasted_iota(jnp.int32, (1, LANES), 1)
    first = lane % HEAD_DIM < HEAD_DIM // 2
    out = []
    for i in range(v.shape[1] // LANES):
        x = v[:, i * LANES : (i + 1) * LANES]
        other = jnp.where(
            first,
            pltpu.roll(x, LANES - HEAD_DIM // 2, 1),
            pltpu.roll(x, HEAD_DIM // 2, 1),
        )
        out.append(x * cos - other * sin if back else x * cos + other * sin)
    return out


def halves(x, parity):
    low = lax.broadcasted_iota(jnp.int32, (1, LANES), 1) < HEAD_DIM
    zero = jnp.zeros_like(x)
    turned = pltpu.roll(x, HEAD_DIM, 1)
    a, b = (x, turned) if parity == 0 else (turned, x)
    return jnp.where(low, a, zero).astype(BF), jnp.where(low, zero, b).astype(BF)


def attend_kernel(
    q_heads, kv_heads, own_ref, came_ref, cos_ref, sin_ref, bias_ref,
    *refs,
):
    out_ref, lse_ref, q_ref, k_ref, v_ref = refs[-5:]
    per = q_heads // kv_heads
    rows = own_ref.shape[0]
    qp, kp = pairs(q_heads), pairs(kv_heads)
    cos, sin = cos_ref[...], sin_ref[...]
    raw = own_ref[...].astype(F32) + came_ref[...].astype(F32)
    scale = HEAD_DIM**-0.5
    q = [(t * scale).astype(BF) for t in rope(raw[:, : qp * LANES], cos, sin, False)]
    keys = rope(raw[:, qp * LANES : (qp + kp) * LANES], cos, sin, False)
    for i in range(qp):
        q_ref[:, i * LANES : (i + 1) * LANES] = q[i]
    ks, vs = [], []
    for g in range(kv_heads):
        at = (qp + kp + g // 2) * LANES
        ks.append(halves(keys[g // 2], g % 2))
        vs.append(halves(raw[:, at : at + LANES], g % 2))
        for p in range(2):
            k_ref[g, p] = ks[g][p]
            v_ref[g, p] = vs[g][p]
    half = rows // 2
    for lo, n in ((0, half), (half, rows)):
        bias = bias_ref[lo : lo + half, :n]
        for i in range(qp):
            out = jnp.zeros((half, LANES), F32)
            for h in range(2 * i, min(2 * i + 2, q_heads)):
                g, p = h // per, h % 2
                s = nt(q[i][lo : lo + half], ks[g][p][:n]) + bias
                peak = jnp.max(s, axis=-1, keepdims=True)
                e = jnp.exp(s - peak)
                total = jnp.sum(e, axis=-1, keepdims=True)
                lse_ref[lo : lo + half, h : h + 1] = peak + jnp.log(total)
                out = out + nn((e * (1.0 / total)).astype(BF), vs[g][p][:n])
            out_ref[lo : lo + half, i * LANES : (i + 1) * LANES] = out.astype(BF)


def attend(own, came, cos, sin, bias, q_heads, kv_heads, deps):
    rows = own.shape[0]
    qp = pairs(q_heads)
    specs, deps = after(deps)
    return pl.pallas_call(
        functools.partial(attend_kernel, q_heads, kv_heads),
        in_specs=[pl.BlockSpec(memory_space=pltpu.VMEM)] * 5 + specs,
        out_shape=[
            jax.ShapeDtypeStruct((rows, qp * LANES), BF),
            jax.ShapeDtypeStruct((rows, LANES), F32),
            jax.ShapeDtypeStruct((rows, qp * LANES), BF),
            jax.ShapeDtypeStruct((kv_heads, 2, rows, LANES), BF),
            jax.ShapeDtypeStruct((kv_heads, 2, rows, LANES), BF),
        ],
        compiler_params=pltpu.CompilerParams(vmem_limit_bytes=VMEM_LIMIT),
        cost_estimate=pl.CostEstimate(
            flops=1200 * rows * rows * q_heads,
            bytes_accessed=8 << 20,
            transcendentals=rows * rows * q_heads,
        ),
    )(own, came, cos, sin, bias, *deps)


def attend_back_kernel(
    q_heads, kv_heads, start, own_ref, came_ref, q_ref, k_ref, v_ref, lse_ref,
    cos_ref, sin_ref, bias_ref, *refs,
):
    per = q_heads // kv_heads
    rows = own_ref.shape[0]
    qp, kp = pairs(q_heads), pairs(kv_heads)
    cos, sin = cos_ref[...], sin_ref[...]
    scale = HEAD_DIM**-0.5
    low = lax.broadcasted_iota(jnp.int32, (1, LANES), 1) < HEAD_DIM
    at = slice(start, start + qp * LANES)
    grad = (own_ref[:, at].astype(F32) + came_ref[:, at].astype(F32)).astype(BF)
    lse = lse_ref[...].T
    half = rows // 2
    out_ref = refs[-1]

    def put(at, v):
        out_ref[:, at * LANES : (at + 1) * LANES] = v.astype(BF)

    def blocks():
        return [
            [[jnp.zeros((half, LANES), F32) for _ in range(2)] for _ in range(2)]
            for _ in range(kv_heads)
        ]

    dk, dv = blocks(), blocks()
    for i in range(qp):
        parts = []
        for lo, n in ((0, half), (half, rows)):
            q = q_ref[lo : lo + half, i * LANES : (i + 1) * LANES]
            go = grad[lo : lo + half, i * LANES : (i + 1) * LANES]
            bias = bias_ref[:n, lo : lo + half]
            dq = jnp.zeros((half, LANES), F32)
            for h in range(2 * i, min(2 * i + 2, q_heads)):
                g, p = h // per, h % 2
                k, v = k_ref[g, p, :n], v_ref[g, p, :n]
                s = nt(k, q) + bias
                probs = jnp.exp(s - lse[h : h + 1, lo : lo + half])
                dp = nt(v, go)
                delta = jnp.sum(probs * dp, axis=0, keepdims=True)
                ds = (probs * (dp - delta)).astype(BF)
                dq = dq + tn(ds, k)
                ck, cv = nn(ds, q), nn(probs.astype(BF), go)
                for b in range(n // half):
                    dk[g][p][b] = dk[g][p][b] + ck[b * half : (b + 1) * half]
                    dv[g][p][b] = dv[g][p][b] + cv[b * half : (b + 1) * half]
            parts.append(dq * scale)
        put(i, rope(jnp.concatenate(parts, 0), cos, sin, True)[0])

    def packed(d, j):
        got = jnp.zeros((rows, LANES), F32)
        for g in range(2 * j, min(2 * j + 2, kv_heads)):
            a, b = (jnp.concatenate(d[g][p], 0) for p in range(2))
            a, b = jnp.where(low, a, 0.0), jnp.where(low, 0.0, b)
            if g % 2 == 0:
                got = got + a + pltpu.roll(b, HEAD_DIM, 1)
            else:
                got = got + b + pltpu.roll(a, HEAD_DIM, 1)
        return got

    for j in range(kp):
        put(qp + j, rope(packed(dk, j), cos, sin, True)[0])
        put(qp + kp + j, packed(dv, j))


def attend_back(own, came, q, k, v, lse, cos, sin, bias, q_heads, kv_heads, start, deps):
    rows = own.shape[0]
    lanes = (pairs(q_heads) + 2 * pairs(kv_heads)) * LANES
    specs, deps = after(deps)
    return pl.pallas_call(
        functools.partial(attend_back_kernel, q_heads, kv_heads, start),
        in_specs=[pl.BlockSpec(memory_space=pltpu.VMEM)] * 9 + specs,
        out_shape=jax.ShapeDtypeStruct((rows, lanes), BF),
        compiler_params=pltpu.CompilerParams(vmem_limit_bytes=VMEM_LIMIT),
        cost_estimate=pl.CostEstimate(
            flops=1600 * rows * rows * q_heads,
            bytes_accessed=8 << 20,
            transcendentals=rows * rows * q_heads,
        ),
    )(own, came, q, k, v, lse, cos, sin, bias, *deps)


def after(arrays):
    return [pl.BlockSpec(memory_space=pl.ANY)] * len(arrays), tuple(arrays)


def row_tile(rows):
    return rows if rows <= 896 else 448


def params():
    return pltpu.CompilerParams(vmem_limit_bytes=VMEM_LIMIT)


def cost(flops, megabytes, transcendentals=0):
    return pl.CostEstimate(
        flops=int(flops), bytes_accessed=megabytes << 20, transcendentals=int(transcendentals)
    )


def to_row(column):
    rows = column.shape[0]
    return jnp.broadcast_to(column, (rows, LANES)).T[:1]


def to_column(row):
    return jnp.broadcast_to(row, (LANES, row.shape[1])).T[:, :1]


def put_column(ref, column):
    rows = column.shape[0]
    row = to_row(column)
    high = row.astype(BF)
    low = (row - high.astype(F32)).astype(BF)
    line = lax.broadcasted_iota(jnp.int32, (16, rows), 0)
    ref[rows : rows + 16, :] = jnp.zeros((16, ref.shape[1]), BF)
    ref[rows : rows + 16, :rows] = jnp.where(
        line == 0, high.astype(F32), jnp.where(line == 1, low.astype(F32), 0.0)
    ).astype(BF)


def get_column(ref):
    rows = ref.shape[0] - 16
    last = ref[rows : rows + 16, :rows].astype(F32)
    return to_column(last[0:1] + last[1:2])


def split_kernel(where, x_ref, theirs_ref, mine_ref):
    rows, size = x_ref.shape[0], mine_ref.shape[1]
    x = x_ref[...].astype(F32)
    squares = jnp.sum(x * x, axis=-1, keepdims=True)
    for ref, member in ((theirs_ref, 1 - where[0]), (mine_ref, where[0])):
        ref[:rows, :] = x_ref[:, pl.ds(pl.multiple_of(member * size, LANES), size)]
        put_column(ref, squares)


def split(member, x):
    rows, width = x.shape
    out = jax.ShapeDtypeStruct((rows + 16, width // 2), BF)
    return pl.pallas_call(
        split_kernel,
        in_specs=[pl.BlockSpec(memory_space=pltpu.SMEM), pl.BlockSpec(memory_space=pltpu.VMEM)],
        out_shape=[out, out],
        compiler_params=params(),
        cost_estimate=cost(0, 2),
    )(jnp.reshape(member, (1,)), x)


def heads_product(hidden, member, part, parts, weights):
    found = []
    for w in weights:
        size = w.shape[1] // (2 * parts)
        at = pl.ds(pl.multiple_of((member * parts + part) * size, LANES), size)
        found.append(nn(hidden, w[:, at]))
    return jnp.concatenate(found, 1)


def project_theirs_kernel(parts, where, mine_ref, came_ref, gain_ref, wq, wk, wv, *refs):
    outs, (hidden_ref, x_ref, inv_ref) = refs[:parts], refs[parts:]
    rows, columns = mine_ref.shape[0] - 16, mine_ref.shape[1]
    gain = gain_ref[...].astype(F32)
    for message, member in ((mine_ref, where[0]), (came_ref, 1 - where[0])):
        at = pl.ds(pl.multiple_of(member * rows, 16), rows)
        inv = lax.rsqrt(get_column(message) / (2 * columns) + EPS)
        inv_ref[at, :] = inv
        x = message[:rows, :]
        x_ref[at, :] = x
        hidden_ref[at, :] = (x.astype(F32) * inv * gain).astype(BF)
    for part in range(parts):
        outs[part][...] = heads_product(
            hidden_ref[...], 1 - where[0], part, parts, (wq, wk, wv)
        ).astype(BF)


def project_theirs(member, parts, mine, came, gain, weights):
    rows, columns = 2 * (mine.shape[0] - 16), mine.shape[1]
    lanes = sum(w.shape[1] for w in weights) // (2 * parts)
    return pl.pallas_call(
        functools.partial(project_theirs_kernel, parts),
        in_specs=[pl.BlockSpec(memory_space=pltpu.SMEM)]
        + [pl.BlockSpec(memory_space=pltpu.VMEM)] * 6,
        out_shape=[jax.ShapeDtypeStruct((rows, lanes), BF)] * parts
        + [
            jax.ShapeDtypeStruct((rows, columns), BF),
            jax.ShapeDtypeStruct((rows, columns), BF),
            jax.ShapeDtypeStruct((rows, 1), F32),
        ],
        compiler_params=params(),
        cost_estimate=cost(4 * rows * columns * lanes * parts, 6),
    )(jnp.reshape(member, (1,)), mine, came, gain, *weights)


def project_own_kernel(parts, where, hidden_ref, wq, wk, wv, *refs):
    for part in range(parts):
        refs[part - parts][...] = heads_product(
            hidden_ref[...], where[0], part, parts, (wq, wk, wv)
        )


def project_own(member, parts, hidden, weights, deps):
    rows, columns = hidden.shape
    lanes = sum(w.shape[1] for w in weights) // (2 * parts)
    specs, deps = after(deps)
    return pl.pallas_call(
        functools.partial(project_own_kernel, parts),
        in_specs=[pl.BlockSpec(memory_space=pltpu.SMEM)]
        + [pl.BlockSpec(memory_space=pltpu.VMEM)] * 4
        + specs,
        out_shape=[jax.ShapeDtypeStruct((rows, lanes), F32)] * parts,
        compiler_params=params(),
        cost_estimate=cost(4 * rows * columns * lanes * parts, 6),
    )(jnp.reshape(member, (1,)), hidden, *weights, *deps)


def project_back_kernel(
    parts, where, x_ref, inv_ref, gain_ref, wq_ref, wk_ref, wv_ref, *refs
):
    grads = refs[: 2 * parts]
    scaled_ref, sums_ref, gain_grad_ref = refs[-3:]
    total = jnp.zeros(x_ref.shape, F32)
    for part in range(parts):
        for grad, member in ((grads[2 * part], where[0]), (grads[2 * part + 1], 1 - where[0])):
            start = 0
            for w in (wq_ref, wk_ref, wv_ref):
                size = w.shape[1] // (2 * parts)
                at = pl.ds(pl.multiple_of((member * parts + part) * size, LANES), size)
                total += nt(grad[:, start : start + size], w[:, at])
                start += size
    normed = x_ref[...].astype(F32) * inv_ref[...]
    scaled = total * gain_ref[...].astype(F32)
    scaled_ref[...] = scaled
    sums_ref[...] = jnp.sum(scaled * normed, axis=-1, keepdims=True)
    gain_grad_ref[...] = jnp.sum(total * normed, axis=0, keepdims=True)


def project_back(member, x, inv, gain, weights, grads, deps):
    rows, columns = x.shape
    parts = len(grads)
    flat = [a for pair in grads for a in pair]
    specs, deps = after(deps)
    whole = pl.BlockSpec(memory_space=pltpu.VMEM)
    return pl.pallas_call(
        functools.partial(project_back_kernel, parts),
        in_specs=[pl.BlockSpec(memory_space=pltpu.SMEM)] + [whole] * (6 + len(flat)) + specs,
        out_shape=[
            jax.ShapeDtypeStruct((rows, columns), F32),
            jax.ShapeDtypeStruct((rows, 1), F32),
            jax.ShapeDtypeStruct((1, columns), F32),
        ],
        compiler_params=params(),
        cost_estimate=cost(2 * rows * columns * sum(w.shape[1] for w in weights), 10),
    )(jnp.reshape(member, (1,)), x, inv, gain, *weights, *flat, *deps)


def weight_grads_kernel(where, *refs):
    hidden, out_ref = refs[:2], refs[-1]
    size = refs[2].shape[1]
    out_ref[:, 2 * size :] = refs[10][...]
    for core in range(2):

        @pl.when(where[1] == core)
        def _():
            for i, member in ((0, where[0]), (1, 1 - where[0])):
                total = sum(tn(hidden[t][...], refs[2 + 4 * t + 2 * core + i][...]) for t in range(2))
                at = pl.ds(pl.multiple_of(member * size, LANES), size)
                out_ref[:, at] = total.astype(BF)


def weight_grads(member, core, hidden, grads, beside, deps):
    columns = hidden[0].shape[1]
    flat = [a for tree in grads for pair in tree for a in pair]
    rows, lanes = flat[0].shape
    specs, deps = after(deps)
    return pl.pallas_call(
        weight_grads_kernel,
        in_specs=[pl.BlockSpec(memory_space=pltpu.SMEM)]
        + [pl.BlockSpec(memory_space=pltpu.VMEM)] * (3 + len(flat))
        + specs,
        out_shape=jax.ShapeDtypeStruct((columns, 2 * lanes + beside.shape[1]), BF),
        compiler_params=params(),
        cost_estimate=cost(8 * rows * columns * lanes, 8),
    )(jnp.stack([member, core]), *hidden, *flat, beside, *deps)


def middle_kernel(count, where, *refs):
    pieces, (w_ref, x_ref) = refs[:count], refs[count : count + 2]
    middle_ref, low_ref, squares_ref = refs[-3:]
    total = x_ref[...].astype(F32)
    for i, piece in enumerate(pieces):
        size = piece.shape[1]
        total += nn(piece[...], w_ref[pl.ds(pl.multiple_of(where[i], 64), size), :])
    squares = jnp.sum(total * total, axis=-1, keepdims=True)
    middle_ref[...] = total
    low_ref[: total.shape[0], :] = total.astype(BF)
    squares_ref[...] = squares
    if low_ref.shape[0] > total.shape[0]:
        put_column(low_ref, squares)


def middle_of(pieces, where, w_out, x, packed, deps=()):
    rows, columns = x.shape
    tile = rows if packed else 448
    more = 16 if packed else 0
    specs, deps = after(deps)

    def row(i, w):
        return (i, 0)

    return pl.pallas_call(
        functools.partial(middle_kernel, len(pieces)),
        grid_spec=pltpu.PrefetchScalarGridSpec(
            num_scalar_prefetch=1,
            grid=(rows // tile,),
            in_specs=[pl.BlockSpec((tile, p.shape[1]), row) for p in pieces]
            + [
                pl.BlockSpec(w_out.shape, lambda i, w: (0, 0)),
                pl.BlockSpec((tile, columns), row),
            ]
            + specs,
            out_specs=[
                pl.BlockSpec((tile, columns), row),
                pl.BlockSpec((tile + more, columns), row),
                pl.BlockSpec((tile, 1), row),
            ],
        ),
        out_shape=[
            jax.ShapeDtypeStruct((rows, columns), F32),
            jax.ShapeDtypeStruct((rows + more, columns), BF),
            jax.ShapeDtypeStruct((rows, 1), F32),
        ],
        compiler_params=params(),
        cost_estimate=cost(2 * rows * columns * w_out.shape[0], 6),
    )(where, *pieces, w_out, x, *deps)


def hidden_kernel(count, parts, width, where, *refs):
    gain_ref, router_ref = refs[:2]
    h_ref, gates_ref = refs[-2:]
    for tree in range(2):
        mine = refs[2 + tree * (count + parts + 1) :]
        pieces, squares, on = mine[:count], mine[count : count + parts], mine[count + parts][...]
        total = squares[0][...]
        for more in squares[1:]:
            total += more[...]
        inv = lax.rsqrt(total / width + EPS)
        for i, piece in enumerate(pieces):
            size = piece.shape[1]
            at = pl.ds(pl.multiple_of(where[i] * size, LANES), size)
            gain = gain_ref[:, at].astype(F32)
            h_ref[tree, :, at] = (piece[...].astype(F32) * inv * gain).astype(BF)
        logits = jnp.where(on > 0, nn(h_ref[tree], router_ref[...]), -1e30)
        peak = jnp.max(logits, axis=-1, keepdims=True)
        e = jnp.exp(logits - peak) * on
        gates_ref[tree] = e / jnp.sum(e, axis=-1, keepdims=True)


def hidden_of(trees, where, gain, router):
    pieces, squares, on = trees[0]
    rows = on.shape[0]
    width, experts = router.shape
    tile = 448

    def row(i, w):
        return (i, 0)

    def all_of(i, w):
        return (0, 0)

    def both(i, w):
        return (0, i, 0)

    specs = [pl.BlockSpec((tile, p.shape[1]), row) for p in (*pieces, *squares, on)]
    return pl.pallas_call(
        functools.partial(hidden_kernel, len(pieces), len(squares), width),
        grid_spec=pltpu.PrefetchScalarGridSpec(
            num_scalar_prefetch=1,
            grid=(rows // tile,),
            in_specs=[pl.BlockSpec((1, width), all_of), pl.BlockSpec((width, experts), all_of)]
            + specs
            + specs,
            out_specs=[
                pl.BlockSpec((2, tile, width), both),
                pl.BlockSpec((2, tile, experts), both),
            ],
        ),
        out_shape=[
            jax.ShapeDtypeStruct((2, rows, width), BF),
            jax.ShapeDtypeStruct((2, rows, experts), F32),
        ],
        compiler_params=params(),
        cost_estimate=cost(4 * rows * width * 256, 8, rows * 32),
    )(where, gain, router, *(a for p, q, o in trees for a in (*p, *q, o)))


PACKET_ROWS = 48


def hidden_packed_kernel(where, *refs):
    h_ref, gates_ref, slots_ref, inv_ref, logits_ref, on_ref = refs[-6:]
    count = refs[0].shape[0] // 2 - 8
    before = (
        lax.broadcasted_iota(jnp.int32, (count, count), 0)
        < lax.broadcasted_iota(jnp.int32, (count, count), 1)
    )
    before = jnp.where(before, 1.0, 0.0).astype(BF)
    member = (where[0], 1 - where[0])
    for tree in range(2):
        messages, packets = refs[4 * tree : 4 * tree + 2], refs[4 * tree + 2 : 4 * tree + 4]
        rows, columns = messages[0].shape[0] - 16, messages[0].shape[1]
        squares = get_column(messages[0]) + get_column(messages[1])
        inv = lax.rsqrt(squares / (2 * columns) + EPS)
        if tree == 0:
            inv_ref[...] = inv
        logits = 0.0
        for i in range(2):
            at = pl.ds(pl.multiple_of(member[i] * columns, LANES), columns)
            gain = packets[i][16:32, :].astype(F32)[:1]
            h = (messages[i][:rows, :].astype(F32) * inv * gain).astype(BF)
            h_ref[tree, :, at] = h
            logits = logits + nt(h, packets[i][:16, :])
            tokens = rows // 2
            on_ref[pl.ds(pl.multiple_of(member[i] * tokens, 16), tokens), :] = (
                packets[i][32:48, :tokens].astype(F32).T
            )
        on = on_ref[...]
        logits = jnp.where(on > 0, logits, -1e30)
        if tree == 0:
            logits_ref[...] = logits
        peak = jnp.max(logits, axis=-1, keepdims=True)
        e = jnp.exp(logits - peak) * on
        gates = (e / jnp.sum(e, axis=-1, keepdims=True)).T
        for i in range(2):
            at = gates[:, i * count : (i + 1) * count]
            gates_ref[2 * tree + i] = at
            routed = jnp.where(at > 0.0, 1.0, 0.0).astype(BF)
            slots_ref[2 * tree + i] = nn(routed, before).astype(jnp.int32)


def hidden_packed(member, trees, deps):
    rows, columns = trees[0][0].shape[0] - 16, trees[0][0].shape[1]
    specs, deps = after(deps)
    return pl.pallas_call(
        hidden_packed_kernel,
        in_specs=[pl.BlockSpec(memory_space=pltpu.SMEM)]
        + [pl.BlockSpec(memory_space=pltpu.VMEM)] * 8
        + specs,
        out_shape=[
            jax.ShapeDtypeStruct((2, rows, 2 * columns), BF),
            jax.ShapeDtypeStruct((4, 16, rows // 2), F32),
            jax.ShapeDtypeStruct((4, 16, rows // 2), jnp.int32),
            jax.ShapeDtypeStruct((rows, 1), F32),
            jax.ShapeDtypeStruct((rows, 16), F32),
        ],
        scratch_shapes=[pltpu.VMEM((rows, 16), F32)],
        compiler_params=params(),
        cost_estimate=cost(4 * rows * columns * 256, 8),
    )(jnp.reshape(member, (1,)), *(a for tree in trees for a in tree), *deps)


def expert_grads_kernel(
    chained, steps, where, h_ref, g_ref, on_ref, wg_ref, wu_ref, wd_ref, *refs
):
    mid_ref, gg_ref, own_ref = refs[-3:] if steps == 1 else refs[-4:-1]
    step = pl.program_id(0)
    h, g = h_ref[...], g_ref[...]
    lane = lax.broadcasted_iota(jnp.int32, (1, on_ref.shape[1]), 1) == where[1]
    on = jnp.sum(jnp.where(lane, on_ref[...], 0.0), axis=-1, keepdims=True)
    gate_pre = nn(h, wg_ref[0])
    up_pre = nn(h, wu_ref[0])
    grad_mid = nt(g, wd_ref[0])
    sig = 1.0 / (1.0 + jnp.exp(-gate_pre))
    silu = gate_pre * sig
    mid = silu * up_pre
    column = jnp.where(lane, jnp.sum(grad_mid * mid, axis=-1, keepdims=True), 0.0)
    gg_ref[...] = refs[0][...] + column if chained else column
    act = (on * mid).astype(BF)
    grad_mid = on * grad_mid
    ggp = (grad_mid * up_pre * (sig * (1.0 + gate_pre * (1.0 - sig)))).astype(BF)
    gup = (grad_mid * silu).astype(BF)
    mid_ref[0, 0] = act
    mid_ref[0, 1] = ggp
    mid_ref[0, 2] = gup
    if steps == 1:
        own_ref[0] = tn(h, ggp).astype(BF)
        own_ref[1] = tn(h, gup).astype(BF)
        own_ref[2] = tn(g, act).astype(BF)
        return
    acc = refs[-1]

    @pl.when(step == 0)
    def _():
        acc[...] = jnp.zeros_like(acc)

    acc[0] += tn(h, ggp)
    acc[1] += tn(h, gup)
    acc[2] += tn(g, act)

    @pl.when(step == steps - 1)
    def _():
        own_ref[...] = acc[...].astype(BF)


def expert_grads(
    j, per_core, which, column, h, g, on, w_gate, w_up, w_down, before, slot, slots, deps
):
    rows, width = h.shape
    hidden = w_gate.shape[2]
    experts = on.shape[1]
    tile = row_tile(rows)
    steps = rows // tile

    def row(i, w):
        return (i, 0)

    def weight(i, w):
        return (w[0], 0, 0)

    chained = before is not None
    more = [pl.BlockSpec((tile, experts), row), pl.BlockSpec(memory_space=pl.ANY)] * chained
    aliases = {8: 0} if chained else {}
    if slot:
        aliases[9] = 2
        deps = (before[2], *deps)
    specs, deps = after(deps)
    return pl.pallas_call(
        functools.partial(expert_grads_kernel, chained, steps),
        grid_spec=pltpu.PrefetchScalarGridSpec(
            num_scalar_prefetch=1,
            grid=(steps,),
            in_specs=[
                pl.BlockSpec((tile, width), row),
                pl.BlockSpec((tile, width), row),
                pl.BlockSpec((tile, experts), row),
                pl.BlockSpec((1, width, hidden), weight),
                pl.BlockSpec((1, width, hidden), weight),
                pl.BlockSpec((1, hidden, width), weight),
            ]
            + more
            + specs,
            out_specs=[
                pl.BlockSpec((1, 3, tile, hidden), lambda i, w: (j, 0, i, 0)),
                pl.BlockSpec((tile, experts), row),
                pl.BlockSpec((3, width, hidden), lambda i, w: (slot, 0, 0)),
            ],
            scratch_shapes=[pltpu.VMEM((3, width, hidden), F32)] * (steps > 1),
        ),
        out_shape=[
            jax.ShapeDtypeStruct((per_core, 3, rows, hidden), BF),
            jax.ShapeDtypeStruct((rows, experts), F32),
            jax.ShapeDtypeStruct((3 * slots, width, hidden), BF),
        ],
        input_output_aliases=aliases,
        compiler_params=params(),
        cost_estimate=cost(16 * rows * width * hidden, 20, rows * hidden),
    )(
        jnp.stack([which, column]).astype(jnp.int32),
        h, g, on, w_gate, w_up, w_down,
        *((before[1], before[0]) if chained else ()),
        *deps,
    )


def expert_hidden_kernel(given, split, where, gate_ref, up_ref, wg_ref, wu_ref, *refs):
    e, count = pl.program_id(1), pl.num_programs(1)
    acc = refs[-1]
    part = nt(gate_ref[0, 0], wg_ref[0]) + nt(up_ref[0, 0], wu_ref[0])

    @pl.when(e == 0)
    def _():
        acc[...] = part + refs[0][...].astype(F32) if given else part

    @pl.when(e > 0)
    def _():
        acc[...] += part

    @pl.when(e == count - 1)
    def _():
        if not split:
            refs[-2][...] = acc[...].astype(BF)
            return
        size = refs[-2].shape[1]
        for out, member in ((refs[-3], where[1]), (refs[-2], 1 - where[1])):
            at = pl.ds(pl.multiple_of(member * size, LANES), size)
            out[...] = acc[:, at].astype(BF)


def expert_hidden(first, member, mid, tree, w_gate, w_up, came, split, deps):
    count, _, rows, hidden = mid.shape
    width = w_gate.shape[1]
    rows //= 2
    tile = 448
    tiles = rows // tile

    def weight(i, e, f):
        return (f[0] + e, 0, 0)

    def row(i, e, f):
        return (i, 0)

    given = [came] if came is not None else []
    specs, deps = after(deps)
    outs = 2 if split else 1
    return pl.pallas_call(
        functools.partial(expert_hidden_kernel, bool(given), split),
        grid_spec=pltpu.PrefetchScalarGridSpec(
            num_scalar_prefetch=1,
            grid=(tiles, count),
            in_specs=[
                pl.BlockSpec((1, 1, tile, hidden), lambda i, e, f: (e, 1, tree * tiles + i, 0)),
                pl.BlockSpec((1, 1, tile, hidden), lambda i, e, f: (e, 2, tree * tiles + i, 0)),
                pl.BlockSpec((1, width, hidden), weight),
                pl.BlockSpec((1, width, hidden), weight),
            ]
            + [pl.BlockSpec((tile, width), row) for _ in given]
            + specs,
            out_specs=[pl.BlockSpec((tile, width // outs), row)] * outs,
            scratch_shapes=[pltpu.VMEM((tile, width), F32)],
        ),
        out_shape=[jax.ShapeDtypeStruct((rows, width // outs), BF)] * outs,
        compiler_params=params(),
        cost_estimate=cost(6 * count * rows * width * hidden, 20),
    )(jnp.stack([first, member]).astype(jnp.int32), mid, mid, w_gate, w_up, *given, *deps)


def expert_mix_kernel(first, mid_ref, wd_ref, *refs):
    e, count = pl.program_id(1), pl.num_programs(1)
    acc = refs[-1]
    part = nn(mid_ref[0, 0], wd_ref[0])

    @pl.when(e == 0)
    def _():
        acc[...] = part

    @pl.when(e > 0)
    def _():
        acc[...] += part

    @pl.when(e == count - 1)
    def _():
        refs[-2][...] = acc[...].astype(BF)


def expert_mix(first, mid, tree, w_down, deps):
    count, _, rows, hidden = mid.shape
    width = w_down.shape[2]
    rows //= 2
    tile = 448
    tiles = rows // tile
    specs, deps = after(deps)
    return pl.pallas_call(
        expert_mix_kernel,
        grid_spec=pltpu.PrefetchScalarGridSpec(
            num_scalar_prefetch=1,
            grid=(tiles, count),
            in_specs=[
                pl.BlockSpec((1, 1, tile, hidden), lambda i, e, f: (e, 0, tree * tiles + i, 0)),
                pl.BlockSpec((1, hidden, width), lambda i, e, f: (f[0] + e, 0, 0)),
            ]
            + specs,
            out_specs=pl.BlockSpec((tile, width), lambda i, e, f: (i, 0)),
            scratch_shapes=[pltpu.VMEM((tile, width), F32)],
        ),
        out_shape=jax.ShapeDtypeStruct((rows, width), BF),
        compiler_params=params(),
        cost_estimate=cost(3 * count * rows * width * hidden, 10),
    )(jnp.reshape(first, (1,)).astype(jnp.int32), mid, w_down, *deps)


def out_grads_kernel(parts, where, *refs):
    branch, out_ref = refs[4 * parts : 4 * parts + 2], refs[-1]
    for own in range(2):

        @pl.when(where[0] == own)
        def _():
            for part in range(parts):
                at = (1 - own) * parts + part
                total = sum(
                    tn(refs[2 * parts * t + at][...], branch[t][...]) for t in range(2)
                )
                size = total.shape[0]
                out_ref[part * size : (part + 1) * size, :] = total.astype(BF)


def out_grads(own, attended, branch, deps):
    parts = len(attended[0]) // 2
    size, columns = attended[0][0].shape[1], branch[0].shape[1]
    specs, deps = after(deps)
    return pl.pallas_call(
        functools.partial(out_grads_kernel, parts),
        in_specs=[pl.BlockSpec(memory_space=pltpu.SMEM)]
        + [pl.BlockSpec(memory_space=pltpu.VMEM)] * (4 * parts + 2)
        + specs,
        out_shape=jax.ShapeDtypeStruct((parts * size, columns), BF),
        compiler_params=params(),
        cost_estimate=cost(4 * branch[0].shape[0] * columns * size * parts, 8),
    )(jnp.reshape(own, (1,)).astype(jnp.int32), *attended[0], *attended[1], *branch, *deps)


def tie_kernel(*refs):
    pass


def tie(v, deps):
    if not deps:
        return v
    specs, deps = after((v, *deps))
    return pl.pallas_call(
        tie_kernel,
        in_specs=specs,
        out_specs=pl.BlockSpec(memory_space=pl.ANY),
        out_shape=jax.ShapeDtypeStruct(v.shape, v.dtype),
        input_output_aliases={0: 0},
        cost_estimate=cost(0, 0),
    )(*deps)


def branch_kernel(
    where, mine_ref, came_ref, sums_ref, gl_ref, logits_ref, router_ref, middle_ref, inv_ref,
    gain_ref, grad_ref, w_ref, gain_grad_ref, full_ref, low_ref, theirs_ref, own_ref,
):
    rows, columns = middle_ref.shape
    gl = gl_ref[...]
    total = mine_ref[...].astype(F32) + came_ref[:rows, :].astype(F32)
    total += nt(gl, router_ref[...])
    products = jnp.sum(gl.astype(F32) * logits_ref[...], axis=-1, keepdims=True)
    mean = (sums_ref[...] + get_column(came_ref) + products) / (2 * columns)
    inv = inv_ref[...]
    normed = middle_ref[...] * inv
    gain_grad_ref[...] = jnp.sum(total * normed, axis=0, keepdims=True)
    at = pl.ds(pl.multiple_of(where[0] * columns, LANES), columns)
    grad = grad_ref[:, at].astype(F32)
    grad += inv * (total * gain_ref[...].astype(F32) - normed * mean)
    full_ref[...] = grad
    low = grad.astype(BF)
    low_ref[...] = low
    for out, member in ((theirs_ref, 1 - where[0]), (own_ref, where[0])):
        size = out.shape[1]
        heads = pl.ds(pl.multiple_of(member * size, 16), size)
        out[...] = nt(low, w_ref[heads, :]).astype(out.dtype)


def branch_back(member, mine, came, sums, gl, logits, router, middle, inv, gain, grad, w_out, deps):
    rows, columns = middle.shape
    size = w_out.shape[0] // 2
    specs, deps = after(deps)
    inputs = (mine, came, sums, gl, logits, router, middle, inv, gain)

    def all_of(i):
        return (0, 0)

    outs = [
        jax.ShapeDtypeStruct((1, columns), F32),
        jax.ShapeDtypeStruct((rows, columns), F32),
        jax.ShapeDtypeStruct((rows, columns), BF),
        jax.ShapeDtypeStruct((rows, size), BF),
        jax.ShapeDtypeStruct((rows, size), F32),
    ]

    def kernel(where, *refs):
        branch_kernel(where, *refs[:11], *refs[-5:])

    return pl.pallas_call(
        kernel,
        grid=(1,),
        in_specs=[pl.BlockSpec(memory_space=pltpu.SMEM)]
        + [pl.BlockSpec(a.shape, all_of) for a in inputs]
        + [pl.BlockSpec((rows, grad.shape[1]), all_of), pl.BlockSpec(w_out.shape, all_of)]
        + specs,
        out_specs=[pl.BlockSpec(o.shape, all_of) for o in outs],
        out_shape=outs,
        compiler_params=params(),
        cost_estimate=cost(2 * rows * columns * w_out.shape[0], 10),
    )(jnp.reshape(member, (1,)), *inputs, grad, w_out, *deps)


SLOTS = 128


def picked(gates_ref, slots_ref, block, expert):
    gates = gates_ref[block, pl.ds(expert, 1), :]
    slots = slots_ref[block, pl.ds(expert, 1), :]
    slot = lax.broadcasted_iota(jnp.int32, (SLOTS, gates.shape[1]), 0)
    return (slot == slots) & (gates > 0.0), gates


def one_hot(hit):
    return jnp.where(hit, 1.0, 0.0).astype(BF)


def expert_pair_kernel(
    chained, where, h_ref, g_ref, gates_ref, slots_ref, wg_ref, wu_ref, wd_ref, *refs
):
    mid_ref, gg_ref, own_ref, he_ref, ge_ref = refs[-5:]
    step = pl.program_id(0)
    expert = where[1] + step

    @pl.when(step == 0)
    def _():
        gg_ref[...] = refs[0][...] if chained else jnp.zeros_like(gg_ref)

    count = gates_ref.shape[2]
    hits, scales = [], []
    for b in range(4):
        hit, gates = picked(gates_ref, slots_ref, b, expert)
        pick = one_hot(hit)
        to = slice(b * SLOTS, (b + 1) * SLOTS)
        at = slice(b * count, (b + 1) * count)
        he_ref[to, :] = nn(pick, h_ref[at, :]).astype(BF)
        ge_ref[to, :] = nn(pick, g_ref[at, :]).astype(BF)
        hits.append(hit)
        scales.append(jnp.sum(jnp.where(hit, gates, 0.0), axis=-1, keepdims=True))
    on = jnp.concatenate(scales, 0)
    h, g = he_ref[...], ge_ref[...]
    gate_pre = nn(h, wg_ref[0])
    up_pre = nn(h, wu_ref[0])
    grad_mid = nt(g, wd_ref[0])
    sig = 1.0 / (1.0 + jnp.exp(-gate_pre))
    silu = gate_pre * sig
    mid = silu * up_pre
    column = jnp.sum(grad_mid * mid, axis=-1, keepdims=True)
    for b in range(4):
        part = jnp.where(hits[b], column[b * SLOTS : (b + 1) * SLOTS], 0.0)
        gg_ref[b, pl.ds(expert, 1), :] = jnp.sum(part, axis=0, keepdims=True)
    act = (on * mid).astype(BF)
    grad_mid = on * grad_mid
    ggp = (grad_mid * up_pre * (sig * (1.0 + gate_pre * (1.0 - sig)))).astype(BF)
    gup = (grad_mid * silu).astype(BF)
    mid_ref[0, 0] = act
    mid_ref[0, 1] = ggp
    mid_ref[0, 2] = gup
    own_ref[0] = tn(h, ggp).astype(BF)
    own_ref[1] = tn(h, gup).astype(BF)
    own_ref[2] = tn(g, act).astype(BF)


def expert_pair(
    start, count, slot, per_core, first, column, h, g, gates, slots, w_gate, w_up, w_down, before, deps
):
    rows, width = h.shape
    hidden = w_gate.shape[2]

    def all_of(i, w):
        return (0, 0)

    def every(i, w):
        return (0, 0, 0)

    def weight(i, w):
        return (w[0] + i, 0, 0)

    chained = before is not None
    more = [pl.BlockSpec(gates.shape, every), pl.BlockSpec(memory_space=pl.ANY)] * chained
    aliases = {9: 0} if chained else {}
    if slot:
        aliases[10] = 2
        deps = (before[2], *deps)
    specs, deps = after(deps)
    return pl.pallas_call(
        functools.partial(expert_pair_kernel, chained),
        grid_spec=pltpu.PrefetchScalarGridSpec(
            num_scalar_prefetch=1,
            grid=(count,),
            in_specs=[
                pl.BlockSpec((rows, width), all_of),
                pl.BlockSpec((rows, width), all_of),
                pl.BlockSpec(gates.shape, every),
                pl.BlockSpec(gates.shape, every),
                pl.BlockSpec((1, width, hidden), weight),
                pl.BlockSpec((1, width, hidden), weight),
                pl.BlockSpec((1, hidden, width), weight),
            ]
            + more
            + specs,
            out_specs=[
                pl.BlockSpec((1, 3, 4 * SLOTS, hidden), lambda i, w: (start + i, 0, 0, 0)),
                pl.BlockSpec(gates.shape, every),
                pl.BlockSpec((3, width, hidden), lambda i, w: (slot + i, 0, 0)),
            ],
            scratch_shapes=[pltpu.VMEM((4 * SLOTS, width), BF)] * 2,
        ),
        out_shape=[
            jax.ShapeDtypeStruct((per_core, 3, 4 * SLOTS, hidden), BF),
            jax.ShapeDtypeStruct(gates.shape, F32),
            jax.ShapeDtypeStruct((6, width, hidden), BF),
        ],
        input_output_aliases=aliases,
        compiler_params=params(),
        cost_estimate=cost(12 * count * 4 * SLOTS * width * hidden, 12 * count, rows * hidden),
    )(
        jnp.stack([first, column]).astype(jnp.int32),
        h, g, gates, slots, w_gate, w_up, w_down,
        *((before[1], before[0]) if chained else ()),
        *deps,
    )


def add_picked(acc, tree, column, gates_ref, slots_ref, outs):
    step, steps = pl.program_id(0), pl.num_programs(0)
    count = gates_ref.shape[2]
    for b in range(2):
        pick = jnp.concatenate(
            [
                one_hot(picked(gates_ref, slots_ref, 2 * tree + b, column + 2 * step + i)[0])
                for i in range(2)
            ],
            0,
        )
        rows = jnp.concatenate([out[b * SLOTS : (b + 1) * SLOTS] for out in outs], 0)
        at = slice(b * count, (b + 1) * count)
        acc[at, :] += tn(pick, rows)


def pair_hidden_kernel(given, tree, where, gates_ref, slots_ref, gp_ref, up_ref, wg_ref, wu_ref, *refs):
    step, acc = pl.program_id(0), refs[-1]

    @pl.when(step == 0)
    def _():
        acc[...] = refs[0][...].astype(F32) if given else jnp.zeros_like(acc)

    outs = [
        (nt(gp_ref[i, 0], wg_ref[i]) + nt(up_ref[i, 0], wu_ref[i])).astype(BF) for i in range(2)
    ]
    add_picked(acc, tree, where[1], gates_ref, slots_ref, outs)

    @pl.when(step == pl.num_programs(0) - 1)
    def _():
        if not given:
            refs[-2][...] = acc[...].astype(BF)
            return
        mine, theirs, sums = refs[-4:-1]
        rows, size = mine.shape
        for out, member in ((mine, where[2]), (theirs, 1 - where[2])):
            at = pl.ds(pl.multiple_of(member * size, LANES), size)
            out[:rows, :] = acc[:, at].astype(BF)
        sums[...] = jnp.sum(acc[...] * refs[1][...].astype(F32), axis=-1, keepdims=True)
        put_column(theirs, sums[...])


def pair_hidden(first, column, member, tree, gates, slots, mid, w_gate, w_up, came, deps):
    count, _, rows, hidden = mid.shape
    width = w_gate.shape[1]
    tokens = 2 * gates.shape[2]
    given = came or ()

    def weight(i, w):
        return (w[0] + i, 0, 0)

    def every(i, w):
        return (0, 0, 0)

    def all_of(i, w):
        return (0, 0)

    specs, deps = after(deps)
    if given:
        half = width // 2
        outs = [((tokens, half), BF), ((tokens + 16, half), BF), ((tokens, 1), F32)]
    else:
        outs = [((tokens, width), BF)]
    return pl.pallas_call(
        functools.partial(pair_hidden_kernel, bool(given), tree),
        grid_spec=pltpu.PrefetchScalarGridSpec(
            num_scalar_prefetch=1,
            grid=(count // 2,),
            in_specs=[
                pl.BlockSpec(gates.shape, every),
                pl.BlockSpec(gates.shape, every),
                pl.BlockSpec((2, 1, rows // 2, hidden), lambda i, w: (i, 1, tree, 0)),
                pl.BlockSpec((2, 1, rows // 2, hidden), lambda i, w: (i, 2, tree, 0)),
                pl.BlockSpec((2, width, hidden), weight),
                pl.BlockSpec((2, width, hidden), weight),
            ]
            + [pl.BlockSpec((tokens, width), all_of) for _ in given]
            + specs,
            out_specs=[pl.BlockSpec(shape, all_of) for shape, _ in outs],
            scratch_shapes=[pltpu.VMEM((tokens, width), F32)],
        ),
        out_shape=[jax.ShapeDtypeStruct(*o) for o in outs],
        compiler_params=params(),
        cost_estimate=cost(6 * count * rows * width * hidden, 16),
    )(
        jnp.stack([first // 2, column, member]).astype(jnp.int32),
        gates, slots, mid, mid, w_gate, w_up, *given, *deps,
    )


def pair_mix_kernel(tree, where, gates_ref, slots_ref, act_ref, wd_ref, *refs):
    step, acc = pl.program_id(0), refs[-1]

    @pl.when(step == 0)
    def _():
        acc[...] = jnp.zeros_like(acc)

    outs = [nn(act_ref[i, 0], wd_ref[i]).astype(BF) for i in range(2)]
    add_picked(acc, tree, where[1], gates_ref, slots_ref, outs)

    @pl.when(step == pl.num_programs(0) - 1)
    def _():
        refs[-2][...] = acc[...].astype(BF)


def pair_mix(first, column, tree, gates, slots, mid, w_down, deps):
    count, _, rows, hidden = mid.shape
    width = w_down.shape[2]
    tokens = 2 * gates.shape[2]

    def every(i, w):
        return (0, 0, 0)

    specs, deps = after(deps)
    return pl.pallas_call(
        functools.partial(pair_mix_kernel, tree),
        grid_spec=pltpu.PrefetchScalarGridSpec(
            num_scalar_prefetch=1,
            grid=(count // 2,),
            in_specs=[
                pl.BlockSpec(gates.shape, every),
                pl.BlockSpec(gates.shape, every),
                pl.BlockSpec((2, 1, rows // 2, hidden), lambda i, w: (i, 0, tree, 0)),
                pl.BlockSpec((2, hidden, width), lambda i, w: (w[0] + i, 0, 0)),
            ]
            + specs,
            out_specs=pl.BlockSpec((tokens, width), lambda i, w: (0, 0)),
            scratch_shapes=[pltpu.VMEM((tokens, width), F32)],
        ),
        out_shape=jax.ShapeDtypeStruct((tokens, width), BF),
        compiler_params=params(),
        cost_estimate=cost(3 * count * rows * width * hidden, 10),
    )(jnp.stack([first // 2, column]).astype(jnp.int32), gates, slots, mid, w_down, *deps)


def finish_kernel(layout, chips, where, *refs):
    outs, (last, router, gains) = refs[2 * chips : -3], refs[-3:]
    rows, columns = last.shape[1], router.shape[1]

    @pl.when(pl.program_id(0) == 0)
    def _():
        total = sum(ref[rows:, : 2 * columns].astype(F32) for ref in refs[:chips])
        router[...] = total[:, :columns]
        gains[...] = total[0:2, columns:]

    for i in range(chips):

        @pl.when(pl.program_id(0) == i)
        def _():
            mine, other = refs[i], refs[chips + (chips - i) % chips]
            for g in range(2):
                for out, to, start, size in layout[g]:
                    at = slice(start, start + size)
                    v = jnp.where(where[0] == g, mine[:rows, at], other[:rows, at])
                    outs[out][:, to : to + size] = v.astype(F32)
            start = mine.shape[1] - last.shape[2]
            last[where[0]] = mine[:rows, start:].astype(F32)
            last[1 - where[0]] = other[:rows, start:].astype(F32)


def finish(core, ring, layout, widths, out_width):
    chips = len(ring.chunks)
    tile, columns = ring.chunks[0].shape
    whole = (tile, columns)
    tile -= 16
    rows = tile * chips

    def row(i, w):
        return (w[1 + i], 0)

    def all_of(i, w):
        return (0, 0)

    return pl.pallas_call(
        functools.partial(finish_kernel, layout, chips),
        grid_spec=pltpu.PrefetchScalarGridSpec(
            num_scalar_prefetch=1,
            grid=(chips,),
            in_specs=[pl.BlockSpec(whole, all_of)] * (2 * chips),
            out_specs=[pl.BlockSpec((tile, w), row) for w in widths]
            + [pl.BlockSpec((2, tile, out_width), lambda i, w: (0, w[1 + i], 0))]
            + [pl.BlockSpec((n, out_width), all_of) for n in (16, 2)],
        ),
        out_shape=[jax.ShapeDtypeStruct((rows, w), F32) for w in widths]
        + [jax.ShapeDtypeStruct((2, rows, out_width), F32)]
        + [jax.ShapeDtypeStruct((n, out_width), F32) for n in (16, 2)],
        compiler_params=params(),
        cost_estimate=cost(0, 20),
    )(jnp.stack([core, *ring.chips()]).astype(jnp.int32), *ring.chunks, *ring.other)


def finish_experts_kernel(per_core, half, where, *refs):
    mine, came, outs = refs[:per_core], refs[per_core : 2 * per_core], refs[2 * per_core :]
    rows = pl.ds(pl.multiple_of(where[0] * half, 16), half)
    for j in range(per_core):
        for source, at in ((mine, where[0] * per_core + j), ((came), (1 - where[0]) * per_core + j)):
            v = source[j][:, rows, :].astype(F32)
            outs[0][at] = v[0]
            outs[1][at] = v[1]
            outs[2][at] = v[2]


def finish_experts(core, mine, came):
    per_core = len(mine)
    _, rows, hidden = mine[0].shape
    half = rows // 2
    whole = pl.BlockSpec(memory_space=pltpu.VMEM)
    return pl.pallas_call(
        functools.partial(finish_experts_kernel, per_core, half),
        in_specs=[pl.BlockSpec(memory_space=pltpu.SMEM)] + [whole] * (2 * per_core),
        out_shape=[
            jax.ShapeDtypeStruct((2 * per_core, half, hidden), F32),
            jax.ShapeDtypeStruct((2 * per_core, half, hidden), F32),
            jax.ShapeDtypeStruct((2 * per_core, half, hidden), F32),
        ],
        compiler_params=params(),
        cost_estimate=cost(0, 10),
    )(jnp.reshape(core, (1,)), *mine, *came)


def local(
    tokens,
    norm_gain,
    w_query,
    key_weight,
    value_weight,
    w_out,
    ffn_gain,
    w_router,
    w_gate,
    w_up,
    w_down,
    parents,
    routes,
    cotangent,
):
    me = Mesh()
    paired = me.groups == 2
    tok_rows, width = tokens.shape
    tree_len = tok_rows * me.groups
    seg_len = tree_len // 16
    columns = width // me.groups
    all_q, all_k = w_query.shape[1], key_weight.shape[1]
    q_width, k_width = all_q // me.groups, all_k // me.groups
    kv_heads = k_width // HEAD_DIM
    parts = kv_heads // 2 if kv_heads % 2 == 0 else 1
    q_part, k_part = q_width // parts, k_width // parts
    gq, gk = q_part // HEAD_DIM, k_part // HEAD_DIM
    q_room, k_room = pairs(gq) * LANES, pairs(gk) * LANES
    lanes = q_room + 2 * k_room
    experts = w_gate.shape[0] * me.groups
    per_core = w_gate.shape[0] // 2
    partner = 1 - me.member

    def heads_of(member):
        found = []
        for weight, size, room in (
            (w_query, q_width, q_room),
            (key_weight, k_width, k_room),
            (value_weight, k_width, k_room),
        ):
            block = lax.dynamic_slice_in_dim(weight, member * size, size, 1)
            found.append(jnp.pad(block, ((0, 0), (0, room - size))))
        return jnp.concatenate(found, 1)

    projections = (w_query, key_weight, value_weight)
    gain_row = norm_gain[None]
    own, came = [], []
    along = jnp.split(cotangent, 2, 0)
    early = ()
    grad_came = []
    if paired:
        hot = jnp.any(
            routes.T[:, None, :] == jnp.arange(experts, dtype=jnp.int32)[None, :, None], axis=0
        )
        packet = jnp.concatenate(
            [
                w_router.T,
                jnp.pad(ffn_gain[None], ((0, 15), (0, 0))),
                jnp.pad(hot.astype(BF), ((0, 0), (0, columns - tok_rows))),
            ],
            0,
        )
        x_theirs, x_mine = split(me.member, tokens)
        x_came = me.swap_shard(x_theirs)
        packets = [packet, me.swap_shard(packet)]
        early = (packets[1],)
        grad_came.append(me.swap_shard(tie(along[0], (x_theirs,))))
        *theirs, hidden_first, x_columns, inv_one = project_theirs(
            me.member, parts, x_mine, x_came, gain_row, projections
        )
        own = project_own(me.member, parts, hidden_first, projections, (theirs[-1],))
        came = [me.swap_shard(theirs[0]), me.swap_shard(tie(theirs[1], own[:1]))]
    else:
        every_head = jnp.concatenate([heads_of(j) for j in range(me.groups)], 1)
        own_rows = tokens.astype(F32)
        inv_rows = lax.rsqrt(jnp.mean(own_rows * own_rows, axis=-1, keepdims=True) + EPS)
        x_columns = me.exchange(tokens, 1, 0)
        inv_one = me.gather(inv_rows, 0)
        hidden_first = (x_columns.astype(F32) * inv_one * norm_gain.astype(F32)).astype(BF)
        own.append(me.scatter(nn(hidden_first, every_head), 1))
        came.append(jnp.zeros(own[-1].shape, BF))

    gain_two = ffn_gain.astype(F32)

    index = jnp.arange(tree_len, dtype=jnp.int32)
    _, depth = tree_layout(index, seg_len)
    cos, sin = angle_tables(depth)
    visible = tree_mask(index, index, parents[0], seg_len)
    bias = jnp.where(visible, 0.0, -1e30).astype(F32)

    attended, lse, query, key, value, att_came = [], [], [], [], [], []
    for part in range(parts):
        a, b, c, d, e = attend(own[part], came[part], cos, sin, bias, gq, gk, (*early, *grad_came[:1]))
        attended.append(a)
        lse.append(b)
        query.append(c)
        key.append(d)
        value.append(e)
        if paired:
            att_came.append(me.swap_shard(a))
    if paired:
        sent = tie(along[1], att_came)
        grad_came.append(me.swap_shard(sent))
        mine = [cotangent, me.swap_core(cotangent)]
        others = [*grad_came, *(me.swap_core(v) for v in grad_came)]
        grad_all = jnp.where(
            me.member == 0,
            jnp.concatenate([mine[0], *others[:2], mine[1], *others[2:]], 0),
            jnp.concatenate([*others[:2], mine[0], *others[2:], mine[1]], 0),
        )
        starts = [
            member * q_width + part * q_part
            for member in (me.member, partner)
            for part in range(parts)
        ]
        middle, middle_low, squares = middle_of(
            attended + att_came, jnp.stack(starts).astype(jnp.int32), w_out, x_columns, True, (sent,)
        )
        attended_full = me.in_order(
            me.member, jnp.concatenate(attended, 1), jnp.concatenate(att_came, 1), 1
        )
        messages = [middle_low, me.swap_shard(middle_low)]
        hidden_all, gates_all, slots_all, inv_two, logits = hidden_packed(
            me.member,
            [
                (*messages, *packets),
                (*(me.swap_core(v) for v in messages), *(me.swap_core(v) for v in packets)),
            ],
            (grad_all,),
        )
    else:
        grad_tree = me.gather(cotangent, 0)
        grad_all = jnp.concatenate([grad_tree, me.swap_core(grad_tree)], 0)
        attended_full = me.gather(attended[0][:, :q_width], 1)
        where = jnp.zeros((1,), jnp.int32)
        middle, middle_low, squares = middle_of([attended_full], where, w_out, x_columns, False)
        route_hot = jnp.any(
            routes[:, :, None] == jnp.arange(experts, dtype=jnp.int32)[None, None, :], axis=1
        ).astype(F32)
        routed = me.gather(route_hot, 0)
        middle_low, squares = me.gather(middle_low, 1), me.total(squares)
        hidden_all, gates_all = hidden_of(
            [
                ([middle_low], [squares], routed),
                (
                    [me.swap_core(middle_low)],
                    [me.swap_core(squares)],
                    me.swap_core(routed),
                ),
            ],
            where,
            me.gather(ffn_gain, 0)[None],
            me.gather(w_router, 0),
        )
        inv_two = lax.rsqrt(squares / width + EPS)
    grad_tree = grad_all[:tree_len]
    hidden_all = hidden_all.reshape(2 * tree_len, width)
    normed_two = middle * inv_two
    hidden_own = (normed_two * gain_two).astype(BF)

    first = me.core * per_core
    chunk = width // me.chips
    def gates_grad(gates, grad, axis):
        return (gates * (grad - jnp.sum(gates * grad, axis=axis, keepdims=True))).astype(BF)

    def output_of(mixed_own, mixed_other):
        mixed = mixed_own.astype(F32) + me.swap_core(mixed_other).astype(F32)
        placed = lax.dynamic_update_slice_in_dim(
            jnp.zeros((tree_len, width), F32), middle, me.member * columns, 1
        )
        return mixed + placed

    def input_of(grad_middle, scaled, row_sums):
        normed = x_columns.astype(F32) * inv_one
        grad = grad_middle + inv_one * (scaled - normed * (row_sums / width))
        return me.exchange(grad.astype(BF), 0, 1)

    flipped = bias.T
    if not paired:
        gates = gates_all[0]
        gates_all = gates_all.reshape(2 * tree_len, experts)
        before, rings = None, []
        for j in range(per_core):
            before = expert_grads(
                j, per_core, first + j, me.member * (2 * per_core) + first + j,
                hidden_all, grad_all, gates_all, w_gate, w_up, w_down, before, 0, 1, (),
            )
            mid, own_columns, grads = before
            ring = Scatter(me, lambda chip: lax.dynamic_slice_in_dim(grads, chip * chunk, chunk, 1))
            for _ in range(me.chips - 1):
                ring.start()
                ring.finish()
            rings.append(ring.held)
        grad_gates = me.total(own_columns[:tree_len] + me.swap_core(own_columns[tree_len:]))
        grad_logits = gates_grad(gates, grad_gates, -1)
        (grad_other,) = expert_hidden(first, me.member, mid, 1, w_gate, w_up, None, False, ())
        (grad_own,) = expert_hidden(
            first, me.member, mid, 0, w_gate, w_up, me.swap_core(grad_other), False, ()
        )
        mixed_other = expert_mix(first, mid, 1, w_down, ())
        mixed_own = expert_mix(first, mid, 0, w_down, ())
        result = me.scatter(output_of(mixed_own, mixed_other), 0).astype(BF)
        grad_hidden_two = nt(grad_logits, w_router) + me.scatter(grad_own, 1)
        grad_gain_two = jnp.sum(grad_hidden_two * normed_two, axis=0)[None]
        scaled = grad_hidden_two * gain_two
        mean = me.total(jnp.sum(scaled * normed_two, axis=-1, keepdims=True)) / width
        grad_columns = me.part(grad_tree, 1, me.member).astype(F32)
        grad_middle = grad_columns + inv_two * (scaled - normed_two * mean)
        grad_branch = grad_middle.astype(BF)
        own = me.scatter(nt(grad_branch, w_out), 1)
        own = jnp.pad(own, ((0, 0), (0, q_room - q_width)))
        grad_heads = attend_back(
            own, jnp.zeros(own.shape, BF), query[0], key[0], value[0], lse[0],
            cos, sin, flipped, gq, gk, 0, (),
        )
        grad_out = me.all_reduce(tn(attended_full, grad_branch))
        grad_full = me.gather(grad_heads, 1)
        every = me.all_reduce(tn(hidden_first, grad_full))
        every = every.reshape(columns, me.groups, lanes)
        grad_query, grad_key, grad_value = (
            every[:, :, start : start + size].reshape(columns, me.groups * size)
            for start, size in ((0, q_width), (q_room, k_width), (q_room + k_room, k_width))
        )
        grad_hidden_one = nt(grad_full, every_head)
        normed_one = x_columns.astype(F32) * inv_one
        grad_gain_one = jnp.sum(grad_hidden_one * normed_one, axis=0)[None]
        scaled = grad_hidden_one * norm_gain.astype(F32)
        row_sums = jnp.sum(scaled * normed_one, axis=-1, keepdims=True)
        input_grad = input_of(grad_middle, scaled, me.total(row_sums))
        grad_router = tn(hidden_own, grad_logits)
        small = me.butterfly(jnp.concatenate([grad_gain_one, grad_gain_two, grad_router.T], 0))
        small = (small[0], small[1], small[2:].T)
        sums = rings
        grad_gate, grad_up, grad_down = finish_experts(
            me.core, sums, [me.swap_core(v) for v in sums]
        )
    else:

        column = me.member * (2 * per_core) + first

        def experts_of(start, count, slot, before, deps):
            return expert_pair(
                start, count, slot, per_core, first + start, column + start,
                hidden_all, grad_all, gates_all, slots_all, w_gate, w_up, w_down, before, deps,
            )

        def hidden_grad(tree, came, deps):
            return pair_hidden(
                first, column, me.member, tree, gates_all, slots_all, mid, w_gate, w_up, came, deps
            )

        def mix_of(tree, deps):
            return pair_mix(first, column, tree, gates_all, slots_all, mid, w_down, deps)

        def ring_of(grads):
            return Scatter(me, lambda chip: lax.dynamic_slice_in_dim(grads, chip * chunk, chunk, 1))

        one = experts_of(0, 2, 0, None, ())
        ring_a = ring_of(one[2])
        sent = ring_a.start()
        mid, own_rows, grads = experts_of(2, 2, 0, one, ())
        sent_a = ring_a.hop(own_rows)
        ring_b = ring_of(grads)
        sent_b = ring_b.start()
        grad_gates = me.total(own_rows[:2] + me.swap_core(own_rows[2:]))
        grad_logits = gates_grad(gates_all[:2], grad_gates, 1)
        grad_logits = grad_logits.transpose(0, 2, 1).reshape(tree_len, experts)
        (grad_other,) = hidden_grad(1, None, (sent_a, sent_b))
        other_came = me.swap_core(grad_other)
        sent = ring_a.hop(grad_other)
        grad_mine, grad_theirs, row_sums = hidden_grad(0, (other_came, hidden_all), (sent,))
        hidden_came = me.swap_shard(grad_theirs)
        sent = ring_b.hop(grad_mine)
        mixed_other = mix_of(1, (sent,))
        sent = ring_a.hop(mixed_other)
        mixed_own = mix_of(0, (sent, grad_logits))
        sent = ring_b.hop(mixed_own)
        grad_gain_two, grad_middle, grad_branch, theirs, own = branch_back(
            me.member, grad_mine, hidden_came, row_sums, grad_logits, logits, w_router,
            middle, inv_two, ffn_gain[None], grad_all, w_out, (sent,),
        )
        came = me.swap_shard(theirs)
        sent = ring_a.hop(grad_branch)
        grad_out = out_grads(
            me.core == me.member,
            [attended + att_came, [me.swap_core(v) for v in attended + att_came]],
            [grad_branch, me.swap_core(grad_branch)],
            (sent,),
        )
        sent = ring_b.hop(grad_out)
        heads_a = attend_back(
            own, came, query[0], key[0], value[0], lse[0], cos, sin, flipped, gq, gk, 0,
            (sent,),
        )
        back_a = me.swap_shard(heads_a)
        sent = ring_a.hop(heads_a)
        heads_b = attend_back(
            own, came, query[1], key[1], value[1], lse[1], cos, sin, flipped, gq, gk, q_part,
            (sent,),
        )
        back_a = tie(back_a, (heads_b,))
        back_b = me.swap_shard(heads_b)
        sent = (ring_b.hop(heads_b), ring_a.hop(heads_b))
        summed = output_of(tie(mixed_own, (back_a, *sent)), mixed_other).astype(BF)
        to_send = me.part(summed, 0, partner)
        grad_pairs = [(heads_a, back_a), (heads_b, back_b)]
        grads_mine = weight_grads(
            me.member,
            me.core,
            (hidden_first, me.swap_core(hidden_first)),
            (grad_pairs, [tuple(me.swap_core(v) for v in pair) for pair in grad_pairs]),
            grad_out,
            (*sent, to_send),
        )
        head_chunk = grads_mine.shape[0] // me.chips
        ring_w = Scatter(
            me, lambda chip: lax.dynamic_slice_in_dim(grads_mine, chip * head_chunk, head_chunk, 0)
        )
        sent = ring_w.start()
        grad_router = tn(hidden_own, grad_logits)
        scaled, row_sums, grad_gain_one = project_back(
            me.member, x_columns, inv_one, gain_row, projections, grad_pairs, (sent,)
        )
        beside = {1: (scaled,)}

        def later(hop, v):
            beside[hop] = (*beside.get(hop, ()), v)

        hops, experts_done, waiting = me.chips - 1, None, None
        for hop in range(1, 2 * hops):
            w = ring_w.finish() if hop <= hops else sent
            if hop > hops:
                ring_w.finish()
            if hop == hops:
                small = jnp.concatenate(
                    [
                        grad_router.T,
                        jnp.pad(jnp.concatenate([grad_gain_one, grad_gain_two]), ((0, 14), (0, 0))),
                    ],
                    1,
                )
                small = (small + me.swap_core(small)).astype(BF)
                small = jnp.pad(small, ((0, 0), (0, ring_w.held.shape[1] - small.shape[1])))
                ring_w = Gather(me, jnp.concatenate([ring_w.held, small], 0))
            if hop == 1:
                row_total = me.total(row_sums)
                later(2, row_total)
            if hop == 2:
                input_grad = input_of(grad_middle, scaled, row_total)
                later(5, input_grad)
            if hop == 3:
                result = me.swap_shard(tie(to_send, (w,))).astype(F32)
                result = (result + me.part(summed, 0, me.member).astype(F32)).astype(BF)
                later(2 * hops - 2, result)
            deps = beside.get(hop, ())
            ring = {1: ring_b, 2: ring_a, 4: ring_b, 6: ring_b}.get(hop)
            if ring is not None and ring.hops < hops:
                deps = (*deps, ring.finish(w))
                if ring.hops < hops:
                    waiting = ring
                elif ring_a.hops == ring_b.hops:
                    sums = [h for r in (ring_a, ring_b) for h in jnp.split(r.held, 2, 0)]
                    experts_done = finish_experts(me.core, sums, [me.swap_core(v) for v in sums])
                    later(hop + 4, experts_done[0])
            sent = ring_w.start(*deps)
            if waiting is not None:
                waiting.start(sent)
                waiting = None
        ring_w.finish()
        grad_gate, grad_up, grad_down = experts_done
        layout = [
            [
                (out, j * step + part * size, j * lanes + start, size)
                for j in range(2)
                for out, step, start, size in (
                    (0, q_width, 0, q_part),
                    (1, k_width, q_room, k_part),
                    (2, k_width, q_room + k_room, k_part),
                )
            ]
            for part in range(parts)
        ]
        grad_query, grad_key, grad_value, grad_out, *small = finish(
            me.core, ring_w, layout, (all_q, all_k, all_k), columns
        )
        grad_out = grad_out.reshape(-1, columns)
        small = (small[1][0], small[1][1], small[0].T)

    return (
        result,
        input_grad,
        small[0],
        grad_query,
        grad_key,
        grad_value,
        grad_out,
        small[1],
        small[2],
        grad_gate,
        grad_up,
        grad_down.transpose(0, 2, 1),
    )


def solution(mesh):
    return jax.shard_map(
        local,
        mesh=mesh,
        in_specs=(
            P(("rep", "shard"), None),
            P("shard"),
            P("shard", None),
            P("shard", None),
            P("shard", None),
            P(None, "shard"),
            P("shard"),
            P("shard", None),
            P("shard", None, None),
            P("shard", None, None),
            P("shard", None, None),
            P("rep", None),
            P(("rep", "shard"), None),
            P(("rep", "shard"), None),
        ),
        out_specs=(
            P(("rep", "shard"), None),
            P(("rep", "shard"), None),
            P("shard"),
            P("shard", None),
            P("shard", None),
            P("shard", None),
            P(None, "shard"),
            P("shard"),
            P("shard", None),
            P("shard", "rep", None),
            P("shard", "rep", None),
            P("shard", None, "rep"),
        ),
        check_vma=False,
    )
```

```python
import functools

import jax
import jax.numpy as jnp
from jax import lax
from jax.experimental import pallas as pl
from jax.experimental.pallas import tpu as pltpu
from jax.sharding import PartitionSpec as P

HEAD_DIM = 64
LANES = 128
EPS = 1e-06
BF = jnp.bfloat16
F32 = jnp.float32
VMEM_LIMIT = 60 << 20


def tree_layout(position, seg_len):
    trunk_len = 4 * seg_len
    beyond = position - trunk_len
    segment = jnp.where(position < trunk_len, 0, 1 + beyond // seg_len)
    inner = jnp.where(
        segment <= 4, trunk_len + beyond % seg_len, trunk_len + seg_len + beyond % seg_len
    )
    depth_position = jnp.where(position < trunk_len, position, inner)
    return (segment, depth_position)


def lookup(segment, parents_row):
    labels = jnp.arange(parents_row.shape[0], dtype=jnp.int32)
    picked = jnp.where(segment[:, None] == labels[None, :], parents_row[None, :], 0)
    return jnp.sum(picked, axis=1)


def tree_mask(query_index, key_index, parents_row, seg_len):
    query_seg, _ = tree_layout(query_index, seg_len)
    key_seg, _ = tree_layout(key_index, seg_len)
    parent_one = lookup(query_seg, parents_row)
    parent_two = lookup(parent_one, parents_row)
    key_row = key_seg[None, :]
    related = (
        (key_row == query_seg[:, None])
        | (key_row == parent_one[:, None])
        | (key_row == parent_two[:, None])
    )
    return related & (key_index[None, :] <= query_index[:, None])


def angle_tables(depth_position):
    half = HEAD_DIM // 2
    frequency = 10000.0 ** (-2.0 * jnp.arange(half, dtype=F32) / HEAD_DIM)
    angles = depth_position.astype(F32)[:, None] * frequency[None, :]
    cosine, sine = jnp.cos(angles), jnp.sin(angles)
    return (
        jnp.concatenate([cosine] * 4, 1),
        jnp.concatenate([-sine, sine, -sine, sine], 1),
    )


def dot(a, b, dims):
    return lax.dot_general(a, b, (dims, ((), ())), preferred_element_type=F32)


def nn(a, b):
    return dot(a, b, ((1,), (0,)))


def nt(a, b):
    return dot(a, b, ((1,), (1,)))


def tn(a, b):
    return dot(a, b, ((0,), (0,)))


class Mesh:
    def __init__(self):
        self.groups = lax.axis_size("shard")
        self.member = lax.axis_index("shard")
        self.reps = lax.axis_size("rep")
        self.rep = lax.axis_index("rep")
        self.core = self.rep % 2
        self.chip = self.rep // 2
        self.chips = self.reps // 2
        rows = self.chips // 2
        order = [2 * z for z in range(rows)] + [2 * z + 1 for z in range(rows - 1, -1, -1)]
        self.ring = []
        for place, chip in enumerate(order):
            after, before = order[(place + 1) % self.chips], order[place - 1]
            self.ring += [(2 * chip, 2 * after), (2 * chip + 1, 2 * before + 1)]
        self.place = jnp.where(
            self.chip % 2 == 0, self.chip // 2, self.chips - 1 - self.chip // 2
        )
        self.way = 1 - 2 * self.core

    def chip_at(self, place):
        place = place % self.chips
        rows = self.chips // 2
        return jnp.where(place < rows, 2 * place, 2 * (self.chips - 1 - place) + 1)

    def swap_shard(self, v):
        return lax.ppermute(v, "shard", [(0, 1), (1, 0)])

    def swap_core(self, v):
        return lax.ppermute(v, "rep", [(r, r ^ 1) for r in range(self.reps)])

    def along_ring(self, v):
        return lax.ppermute(v, "rep", self.ring)

    def part(self, v, axis, which):
        size = v.shape[axis] // self.groups
        return lax.dynamic_slice_in_dim(v, which * size, size, axis)

    def gather(self, v, axis):
        if self.groups != 2:
            return lax.all_gather(v, "shard", axis=axis, tiled=True)
        other = self.swap_shard(v)
        return self.in_order(self.member, v, other, axis)

    def in_order(self, which, mine, other, axis):
        return jnp.where(
            which == 0,
            jnp.concatenate([mine, other], axis),
            jnp.concatenate([other, mine], axis),
        )

    def exchange(self, v, split_axis, concat_axis):
        if self.groups != 2:
            return lax.all_to_all(v, "shard", split_axis, concat_axis, tiled=True)
        other = self.swap_shard(self.part(v, split_axis, 1 - self.member))
        mine = self.part(v, split_axis, self.member)
        return self.in_order(self.member, mine, other, concat_axis)

    def scatter(self, v, axis):
        if self.groups != 2:
            return lax.psum_scatter(
                v.astype(BF), "shard", scatter_dimension=axis, tiled=True
            ).astype(F32)
        other = self.swap_shard(self.part(v, axis, 1 - self.member).astype(BF))
        return self.part(v, axis, self.member).astype(F32) + other.astype(F32)

    def total(self, v):
        if self.groups != 2:
            return lax.psum(v, "shard")
        return v + self.swap_shard(v)

    def ring_sum(self, v):
        chunk = v.shape[0] // self.chips
        ring = Scatter(self, lambda chip: lax.dynamic_slice_in_dim(v, chip * chunk, chunk, 0))
        for _ in range(self.chips - 1):
            ring.start()
            ring.finish()
        ring = Gather(self, ring.held)
        for _ in range(self.chips - 1):
            ring.start()
            ring.finish()
        whole = jnp.zeros(v.shape, v.dtype)
        for at, part in zip(ring.chips(), ring.chunks):
            whole = lax.dynamic_update_slice_in_dim(whole, part, at * chunk, 0)
        return whole

    def all_reduce(self, v):
        half = v.shape[0] // 2
        v = v.astype(BF)
        mine = lax.dynamic_slice_in_dim(v, self.core * half, half, 0)
        other = self.swap_core(
            lax.dynamic_slice_in_dim(v, (1 - self.core) * half, half, 0)
        )
        whole = self.ring_sum((mine.astype(F32) + other.astype(F32)).astype(BF))
        return self.in_order(self.core, whole, self.swap_core(whole), 0).astype(F32)

    def swap_rep(self, v, bit):
        return lax.ppermute(v, "rep", [(r, r ^ bit) for r in range(self.reps)])

    def butterfly(self, v):
        bit = 1
        while bit < self.reps:
            v = v + self.swap_rep(v, bit)
            bit *= 2
        return v


class Scatter:
    def __init__(self, me, own):
        self.me, self.own, self.hops = me, own, 0
        self.held = own(me.chip_at(me.place - me.way))

    def start(self, *deps):
        sent = tie(self.held, deps)
        self.came = self.me.along_ring(sent)
        return sent

    def hop(self, *deps):
        self.finish(*deps)
        return self.start()

    def finish(self, *deps):
        self.hops += 1
        self.came = tie(self.came, deps)
        mine = self.own(self.me.chip_at(self.me.place - self.me.way * (self.hops + 1)))
        self.held = (self.came.astype(F32) + mine.astype(F32)).astype(BF)
        return self.came


class Gather:
    def __init__(self, me, held):
        self.me, self.came, self.hops = me, held, 0
        self.chunks, self.other = [], []

    def chips(self):
        me = self.me
        return [me.chip_at(me.place - me.way * hop) for hop in range(me.chips)]

    def keep(self, chunk):
        self.chunks.append(chunk)
        self.other.append(self.me.swap_core(chunk))

    def start(self, *deps):
        sent = tie(self.came, deps)
        self.came = self.me.along_ring(sent)
        self.keep(sent)
        return sent

    def finish(self):
        self.hops += 1
        if self.hops == self.me.chips - 1:
            self.keep(self.came)


def pairs(heads):
    return -(-heads // 2)


def rope(v, cos, sin, back):
    lane = lax.broadcasted_iota(jnp.int32, (1, LANES), 1)
    first = lane % HEAD_DIM < HEAD_DIM // 2
    out = []
    for i in range(v.shape[1] // LANES):
        x = v[:, i * LANES : (i + 1) * LANES]
        other = jnp.where(
            first,
            pltpu.roll(x, LANES - HEAD_DIM // 2, 1),
            pltpu.roll(x, HEAD_DIM // 2, 1),
        )
        out.append(x * cos - other * sin if back else x * cos + other * sin)
    return out


def halves(x, parity):
    low = lax.broadcasted_iota(jnp.int32, (1, LANES), 1) < HEAD_DIM
    zero = jnp.zeros_like(x)
    turned = pltpu.roll(x, HEAD_DIM, 1)
    a, b = (x, turned) if parity == 0 else (turned, x)
    return jnp.where(low, a, zero).astype(BF), jnp.where(low, zero, b).astype(BF)


def attend_kernel(
    q_heads, kv_heads, own_ref, came_ref, cos_ref, sin_ref, bias_ref,
    *refs,
):
    out_ref, lse_ref, q_ref, k_ref, v_ref = refs[-5:]
    per = q_heads // kv_heads
    rows = own_ref.shape[0]
    qp, kp = pairs(q_heads), pairs(kv_heads)
    cos, sin = cos_ref[...], sin_ref[...]
    raw = own_ref[...].astype(F32) + came_ref[...].astype(F32)
    scale = HEAD_DIM**-0.5
    q = [(t * scale).astype(BF) for t in rope(raw[:, : qp * LANES], cos, sin, False)]
    keys = rope(raw[:, qp * LANES : (qp + kp) * LANES], cos, sin, False)
    for i in range(qp):
        q_ref[:, i * LANES : (i + 1) * LANES] = q[i]
    ks, vs = [], []
    for g in range(kv_heads):
        at = (qp + kp + g // 2) * LANES
        ks.append(halves(keys[g // 2], g % 2))
        vs.append(halves(raw[:, at : at + LANES], g % 2))
        for p in range(2):
            k_ref[g, p] = ks[g][p]
            v_ref[g, p] = vs[g][p]
    half = rows // 2
    for lo, n in ((0, half), (half, rows)):
        bias = bias_ref[lo : lo + half, :n]
        for i in range(qp):
            out = jnp.zeros((half, LANES), F32)
            for h in range(2 * i, min(2 * i + 2, q_heads)):
                g, p = h // per, h % 2
                s = nt(q[i][lo : lo + half], ks[g][p][:n]) + bias
                peak = jnp.max(s, axis=-1, keepdims=True)
                e = jnp.exp(s - peak)
                total = jnp.sum(e, axis=-1, keepdims=True)
                lse_ref[lo : lo + half, h : h + 1] = peak + jnp.log(total)
                out = out + nn((e * (1.0 / total)).astype(BF), vs[g][p][:n])
            out_ref[lo : lo + half, i * LANES : (i + 1) * LANES] = out.astype(BF)


def attend(own, came, cos, sin, bias, q_heads, kv_heads, deps):
    rows = own.shape[0]
    qp = pairs(q_heads)
    specs, deps = after(deps)
    return pl.pallas_call(
        functools.partial(attend_kernel, q_heads, kv_heads),
        in_specs=[pl.BlockSpec(memory_space=pltpu.VMEM)] * 5 + specs,
        out_shape=[
            jax.ShapeDtypeStruct((rows, qp * LANES), BF),
            jax.ShapeDtypeStruct((rows, LANES), F32),
            jax.ShapeDtypeStruct((rows, qp * LANES), BF),
            jax.ShapeDtypeStruct((kv_heads, 2, rows, LANES), BF),
            jax.ShapeDtypeStruct((kv_heads, 2, rows, LANES), BF),
        ],
        compiler_params=pltpu.CompilerParams(vmem_limit_bytes=VMEM_LIMIT),
        cost_estimate=pl.CostEstimate(
            flops=1200 * rows * rows * q_heads,
            bytes_accessed=8 << 20,
            transcendentals=rows * rows * q_heads,
        ),
    )(own, came, cos, sin, bias, *deps)


def attend_back_kernel(
    q_heads, kv_heads, start, own_ref, came_ref, q_ref, k_ref, v_ref, lse_ref,
    cos_ref, sin_ref, bias_ref, *refs,
):
    per = q_heads // kv_heads
    rows = own_ref.shape[0]
    qp, kp = pairs(q_heads), pairs(kv_heads)
    cos, sin = cos_ref[...], sin_ref[...]
    scale = HEAD_DIM**-0.5
    low = lax.broadcasted_iota(jnp.int32, (1, LANES), 1) < HEAD_DIM
    at = slice(start, start + qp * LANES)
    grad = (own_ref[:, at].astype(F32) + came_ref[:, at].astype(F32)).astype(BF)
    lse = lse_ref[...].T
    half = rows // 2
    out_ref = refs[-1]

    def put(at, v):
        out_ref[:, at * LANES : (at + 1) * LANES] = v.astype(BF)

    def blocks():
        return [
            [[jnp.zeros((half, LANES), F32) for _ in range(2)] for _ in range(2)]
            for _ in range(kv_heads)
        ]

    dk, dv = blocks(), blocks()
    for i in range(qp):
        parts = []
        for lo, n in ((0, half), (half, rows)):
            q = q_ref[lo : lo + half, i * LANES : (i + 1) * LANES]
            go = grad[lo : lo + half, i * LANES : (i + 1) * LANES]
            bias = bias_ref[:n, lo : lo + half]
            dq = jnp.zeros((half, LANES), F32)
            for h in range(2 * i, min(2 * i + 2, q_heads)):
                g, p = h // per, h % 2
                k, v = k_ref[g, p, :n], v_ref[g, p, :n]
                s = nt(k, q) + bias
                probs = jnp.exp(s - lse[h : h + 1, lo : lo + half])
                dp = nt(v, go)
                delta = jnp.sum(probs * dp, axis=0, keepdims=True)
                ds = (probs * (dp - delta)).astype(BF)
                dq = dq + tn(ds, k)
                ck, cv = nn(ds, q), nn(probs.astype(BF), go)
                for b in range(n // half):
                    dk[g][p][b] = dk[g][p][b] + ck[b * half : (b + 1) * half]
                    dv[g][p][b] = dv[g][p][b] + cv[b * half : (b + 1) * half]
            parts.append(dq * scale)
        put(i, rope(jnp.concatenate(parts, 0), cos, sin, True)[0])

    def packed(d, j):
        got = jnp.zeros((rows, LANES), F32)
        for g in range(2 * j, min(2 * j + 2, kv_heads)):
            a, b = (jnp.concatenate(d[g][p], 0) for p in range(2))
            a, b = jnp.where(low, a, 0.0), jnp.where(low, 0.0, b)
            if g % 2 == 0:
                got = got + a + pltpu.roll(b, HEAD_DIM, 1)
            else:
                got = got + b + pltpu.roll(a, HEAD_DIM, 1)
        return got

    for j in range(kp):
        put(qp + j, rope(packed(dk, j), cos, sin, True)[0])
        put(qp + kp + j, packed(dv, j))


def attend_back(own, came, q, k, v, lse, cos, sin, bias, q_heads, kv_heads, start, deps):
    rows = own.shape[0]
    lanes = (pairs(q_heads) + 2 * pairs(kv_heads)) * LANES
    specs, deps = after(deps)
    return pl.pallas_call(
        functools.partial(attend_back_kernel, q_heads, kv_heads, start),
        in_specs=[pl.BlockSpec(memory_space=pltpu.VMEM)] * 9 + specs,
        out_shape=jax.ShapeDtypeStruct((rows, lanes), BF),
        compiler_params=pltpu.CompilerParams(vmem_limit_bytes=VMEM_LIMIT),
        cost_estimate=pl.CostEstimate(
            flops=1600 * rows * rows * q_heads,
            bytes_accessed=8 << 20,
            transcendentals=rows * rows * q_heads,
        ),
    )(own, came, q, k, v, lse, cos, sin, bias, *deps)


def after(arrays):
    return [pl.BlockSpec(memory_space=pl.ANY)] * len(arrays), tuple(arrays)


def row_tile(rows):
    return rows if rows <= 896 else 448


def params():
    return pltpu.CompilerParams(vmem_limit_bytes=VMEM_LIMIT)


def cost(flops, megabytes, transcendentals=0):
    return pl.CostEstimate(
        flops=int(flops), bytes_accessed=megabytes << 20, transcendentals=int(transcendentals)
    )


def to_row(column):
    rows = column.shape[0]
    return jnp.broadcast_to(column, (rows, LANES)).T[:1]


def to_column(row):
    return jnp.broadcast_to(row, (LANES, row.shape[1])).T[:, :1]


def put_column(ref, column):
    rows = column.shape[0]
    row = to_row(column)
    high = row.astype(BF)
    low = (row - high.astype(F32)).astype(BF)
    line = lax.broadcasted_iota(jnp.int32, (16, rows), 0)
    ref[rows : rows + 16, :] = jnp.zeros((16, ref.shape[1]), BF)
    ref[rows : rows + 16, :rows] = jnp.where(
        line == 0, high.astype(F32), jnp.where(line == 1, low.astype(F32), 0.0)
    ).astype(BF)


def get_column(ref):
    rows = ref.shape[0] - 16
    last = ref[rows : rows + 16, :rows].astype(F32)
    return to_column(last[0:1] + last[1:2])


def split_kernel(where, x_ref, theirs_ref, mine_ref):
    rows, size = x_ref.shape[0], mine_ref.shape[1]
    x = x_ref[...].astype(F32)
    squares = jnp.sum(x * x, axis=-1, keepdims=True)
    for ref, member in ((theirs_ref, 1 - where[0]), (mine_ref, where[0])):
        ref[:rows, :] = x_ref[:, pl.ds(pl.multiple_of(member * size, LANES), size)]
        put_column(ref, squares)


def split(member, x):
    rows, width = x.shape
    out = jax.ShapeDtypeStruct((rows + 16, width // 2), BF)
    return pl.pallas_call(
        split_kernel,
        in_specs=[pl.BlockSpec(memory_space=pltpu.SMEM), pl.BlockSpec(memory_space=pltpu.VMEM)],
        out_shape=[out, out],
        compiler_params=params(),
        cost_estimate=cost(0, 2),
    )(jnp.reshape(member, (1,)), x)


def heads_product(hidden, member, part, parts, weights):
    found = []
    for w in weights:
        size = w.shape[1] // (2 * parts)
        at = pl.ds(pl.multiple_of((member * parts + part) * size, LANES), size)
        found.append(nn(hidden, w[:, at]))
    return jnp.concatenate(found, 1)


def project_theirs_kernel(parts, where, mine_ref, came_ref, gain_ref, wq, wk, wv, *refs):
    outs, (hidden_ref, x_ref, inv_ref) = refs[:parts], refs[parts:]
    rows, columns = mine_ref.shape[0] - 16, mine_ref.shape[1]
    gain = gain_ref[...].astype(F32)
    for message, member in ((mine_ref, where[0]), (came_ref, 1 - where[0])):
        at = pl.ds(pl.multiple_of(member * rows, 16), rows)
        inv = lax.rsqrt(get_column(message) / (2 * columns) + EPS)
        inv_ref[at, :] = inv
        x = message[:rows, :]
        x_ref[at, :] = x
        hidden_ref[at, :] = (x.astype(F32) * inv * gain).astype(BF)
    for part in range(parts):
        outs[part][...] = heads_product(
            hidden_ref[...], 1 - where[0], part, parts, (wq, wk, wv)
        ).astype(BF)


def project_theirs(member, parts, mine, came, gain, weights):
    rows, columns = 2 * (mine.shape[0] - 16), mine.shape[1]
    lanes = sum(w.shape[1] for w in weights) // (2 * parts)
    return pl.pallas_call(
        functools.partial(project_theirs_kernel, parts),
        in_specs=[pl.BlockSpec(memory_space=pltpu.SMEM)]
        + [pl.BlockSpec(memory_space=pltpu.VMEM)] * 6,
        out_shape=[jax.ShapeDtypeStruct((rows, lanes), BF)] * parts
        + [
            jax.ShapeDtypeStruct((rows, columns), BF),
            jax.ShapeDtypeStruct((rows, columns), BF),
            jax.ShapeDtypeStruct((rows, 1), F32),
        ],
        compiler_params=params(),
        cost_estimate=cost(4 * rows * columns * lanes * parts, 6),
    )(jnp.reshape(member, (1,)), mine, came, gain, *weights)


def project_own_kernel(parts, where, hidden_ref, wq, wk, wv, *refs):
    for part in range(parts):
        refs[part - parts][...] = heads_product(
            hidden_ref[...], where[0], part, parts, (wq, wk, wv)
        )


def project_own(member, parts, hidden, weights, deps):
    rows, columns = hidden.shape
    lanes = sum(w.shape[1] for w in weights) // (2 * parts)
    specs, deps = after(deps)
    return pl.pallas_call(
        functools.partial(project_own_kernel, parts),
        in_specs=[pl.BlockSpec(memory_space=pltpu.SMEM)]
        + [pl.BlockSpec(memory_space=pltpu.VMEM)] * 4
        + specs,
        out_shape=[jax.ShapeDtypeStruct((rows, lanes), F32)] * parts,
        compiler_params=params(),
        cost_estimate=cost(4 * rows * columns * lanes * parts, 6),
    )(jnp.reshape(member, (1,)), hidden, *weights, *deps)


def project_back_kernel(
    parts, where, x_ref, inv_ref, gain_ref, wq_ref, wk_ref, wv_ref, *refs
):
    grads = refs[: 2 * parts]
    scaled_ref, sums_ref, gain_grad_ref = refs[-3:]
    total = jnp.zeros(x_ref.shape, F32)
    for part in range(parts):
        for grad, member in ((grads[2 * part], where[0]), (grads[2 * part + 1], 1 - where[0])):
            start = 0
            for w in (wq_ref, wk_ref, wv_ref):
                size = w.shape[1] // (2 * parts)
                at = pl.ds(pl.multiple_of((member * parts + part) * size, LANES), size)
                total += nt(grad[:, start : start + size], w[:, at])
                start += size
    normed = x_ref[...].astype(F32) * inv_ref[...]
    scaled = total * gain_ref[...].astype(F32)
    scaled_ref[...] = scaled
    sums_ref[...] = jnp.sum(scaled * normed, axis=-1, keepdims=True)
    gain_grad_ref[...] = jnp.sum(total * normed, axis=0, keepdims=True)


def project_back(member, x, inv, gain, weights, grads, deps):
    rows, columns = x.shape
    parts = len(grads)
    flat = [a for pair in grads for a in pair]
    specs, deps = after(deps)
    whole = pl.BlockSpec(memory_space=pltpu.VMEM)
    return pl.pallas_call(
        functools.partial(project_back_kernel, parts),
        in_specs=[pl.BlockSpec(memory_space=pltpu.SMEM)] + [whole] * (6 + len(flat)) + specs,
        out_shape=[
            jax.ShapeDtypeStruct((rows, columns), F32),
            jax.ShapeDtypeStruct((rows, 1), F32),
            jax.ShapeDtypeStruct((1, columns), F32),
        ],
        compiler_params=params(),
        cost_estimate=cost(2 * rows * columns * sum(w.shape[1] for w in weights), 10),
    )(jnp.reshape(member, (1,)), x, inv, gain, *weights, *flat, *deps)


def weight_grads_kernel(where, *refs):
    hidden, out_ref = refs[:2], refs[-1]
    size = refs[2].shape[1]
    out_ref[:, 2 * size :] = refs[10][...]
    for core in range(2):

        @pl.when(where[1] == core)
        def _():
            for i, member in ((0, where[0]), (1, 1 - where[0])):
                total = sum(tn(hidden[t][...], refs[2 + 4 * t + 2 * core + i][...]) for t in range(2))
                at = pl.ds(pl.multiple_of(member * size, LANES), size)
                out_ref[:, at] = total.astype(BF)


def weight_grads(member, core, hidden, grads, beside, deps):
    columns = hidden[0].shape[1]
    flat = [a for tree in grads for pair in tree for a in pair]
    rows, lanes = flat[0].shape
    specs, deps = after(deps)
    return pl.pallas_call(
        weight_grads_kernel,
        in_specs=[pl.BlockSpec(memory_space=pltpu.SMEM)]
        + [pl.BlockSpec(memory_space=pltpu.VMEM)] * (3 + len(flat))
        + specs,
        out_shape=jax.ShapeDtypeStruct((columns, 2 * lanes + beside.shape[1]), BF),
        compiler_params=params(),
        cost_estimate=cost(8 * rows * columns * lanes, 8),
    )(jnp.stack([member, core]), *hidden, *flat, beside, *deps)


def middle_kernel(count, where, *refs):
    pieces, (w_ref, x_ref) = refs[:count], refs[count : count + 2]
    middle_ref, low_ref, squares_ref = refs[-3:]
    total = x_ref[...].astype(F32)
    for i, piece in enumerate(pieces):
        size = piece.shape[1]
        total += nn(piece[...], w_ref[pl.ds(pl.multiple_of(where[i], 64), size), :])
    squares = jnp.sum(total * total, axis=-1, keepdims=True)
    middle_ref[...] = total
    low_ref[: total.shape[0], :] = total.astype(BF)
    squares_ref[...] = squares
    if low_ref.shape[0] > total.shape[0]:
        put_column(low_ref, squares)


def middle_of(pieces, where, w_out, x, packed, deps=()):
    rows, columns = x.shape
    tile = rows if packed else 448
    more = 16 if packed else 0
    specs, deps = after(deps)

    def row(i, w):
        return (i, 0)

    return pl.pallas_call(
        functools.partial(middle_kernel, len(pieces)),
        grid_spec=pltpu.PrefetchScalarGridSpec(
            num_scalar_prefetch=1,
            grid=(rows // tile,),
            in_specs=[pl.BlockSpec((tile, p.shape[1]), row) for p in pieces]
            + [
                pl.BlockSpec(w_out.shape, lambda i, w: (0, 0)),
                pl.BlockSpec((tile, columns), row),
            ]
            + specs,
            out_specs=[
                pl.BlockSpec((tile, columns), row),
                pl.BlockSpec((tile + more, columns), row),
                pl.BlockSpec((tile, 1), row),
            ],
        ),
        out_shape=[
            jax.ShapeDtypeStruct((rows, columns), F32),
            jax.ShapeDtypeStruct((rows + more, columns), BF),
            jax.ShapeDtypeStruct((rows, 1), F32),
        ],
        compiler_params=params(),
        cost_estimate=cost(2 * rows * columns * w_out.shape[0], 6),
    )(where, *pieces, w_out, x, *deps)


def hidden_kernel(count, parts, width, where, *refs):
    gain_ref, router_ref = refs[:2]
    h_ref, gates_ref = refs[-2:]
    for tree in range(2):
        mine = refs[2 + tree * (count + parts + 1) :]
        pieces, squares, on = mine[:count], mine[count : count + parts], mine[count + parts][...]
        total = squares[0][...]
        for more in squares[1:]:
            total += more[...]
        inv = lax.rsqrt(total / width + EPS)
        for i, piece in enumerate(pieces):
            size = piece.shape[1]
            at = pl.ds(pl.multiple_of(where[i] * size, LANES), size)
            gain = gain_ref[:, at].astype(F32)
            h_ref[tree, :, at] = (piece[...].astype(F32) * inv * gain).astype(BF)
        logits = jnp.where(on > 0, nn(h_ref[tree], router_ref[...]), -1e30)
        peak = jnp.max(logits, axis=-1, keepdims=True)
        e = jnp.exp(logits - peak) * on
        gates_ref[tree] = e / jnp.sum(e, axis=-1, keepdims=True)


def hidden_of(trees, where, gain, router):
    pieces, squares, on = trees[0]
    rows = on.shape[0]
    width, experts = router.shape
    tile = 448

    def row(i, w):
        return (i, 0)

    def all_of(i, w):
        return (0, 0)

    def both(i, w):
        return (0, i, 0)

    specs = [pl.BlockSpec((tile, p.shape[1]), row) for p in (*pieces, *squares, on)]
    return pl.pallas_call(
        functools.partial(hidden_kernel, len(pieces), len(squares), width),
        grid_spec=pltpu.PrefetchScalarGridSpec(
            num_scalar_prefetch=1,
            grid=(rows // tile,),
            in_specs=[pl.BlockSpec((1, width), all_of), pl.BlockSpec((width, experts), all_of)]
            + specs
            + specs,
            out_specs=[
                pl.BlockSpec((2, tile, width), both),
                pl.BlockSpec((2, tile, experts), both),
            ],
        ),
        out_shape=[
            jax.ShapeDtypeStruct((2, rows, width), BF),
            jax.ShapeDtypeStruct((2, rows, experts), F32),
        ],
        compiler_params=params(),
        cost_estimate=cost(4 * rows * width * 256, 8, rows * 32),
    )(where, gain, router, *(a for p, q, o in trees for a in (*p, *q, o)))


PACKET_ROWS = 48


def hidden_packed_kernel(where, *refs):
    h_ref, gates_ref, slots_ref, inv_ref, logits_ref, on_ref = refs[-6:]
    count = refs[0].shape[0] // 2 - 8
    before = (
        lax.broadcasted_iota(jnp.int32, (count, count), 0)
        < lax.broadcasted_iota(jnp.int32, (count, count), 1)
    )
    before = jnp.where(before, 1.0, 0.0).astype(BF)
    member = (where[0], 1 - where[0])
    for tree in range(2):
        messages, packets = refs[4 * tree : 4 * tree + 2], refs[4 * tree + 2 : 4 * tree + 4]
        rows, columns = messages[0].shape[0] - 16, messages[0].shape[1]
        squares = get_column(messages[0]) + get_column(messages[1])
        inv = lax.rsqrt(squares / (2 * columns) + EPS)
        if tree == 0:
            inv_ref[...] = inv
        logits = 0.0
        for i in range(2):
            at = pl.ds(pl.multiple_of(member[i] * columns, LANES), columns)
            gain = packets[i][16:32, :].astype(F32)[:1]
            h = (messages[i][:rows, :].astype(F32) * inv * gain).astype(BF)
            h_ref[tree, :, at] = h
            logits = logits + nt(h, packets[i][:16, :])
            tokens = rows // 2
            on_ref[pl.ds(pl.multiple_of(member[i] * tokens, 16), tokens), :] = (
                packets[i][32:48, :tokens].astype(F32).T
            )
        on = on_ref[...]
        logits = jnp.where(on > 0, logits, -1e30)
        if tree == 0:
            logits_ref[...] = logits
        peak = jnp.max(logits, axis=-1, keepdims=True)
        e = jnp.exp(logits - peak) * on
        gates = (e / jnp.sum(e, axis=-1, keepdims=True)).T
        for i in range(2):
            at = gates[:, i * count : (i + 1) * count]
            gates_ref[2 * tree + i] = at
            routed = jnp.where(at > 0.0, 1.0, 0.0).astype(BF)
            slots_ref[2 * tree + i] = nn(routed, before).astype(jnp.int32)


def hidden_packed(member, trees, deps):
    rows, columns = trees[0][0].shape[0] - 16, trees[0][0].shape[1]
    specs, deps = after(deps)
    return pl.pallas_call(
        hidden_packed_kernel,
        in_specs=[pl.BlockSpec(memory_space=pltpu.SMEM)]
        + [pl.BlockSpec(memory_space=pltpu.VMEM)] * 8
        + specs,
        out_shape=[
            jax.ShapeDtypeStruct((2, rows, 2 * columns), BF),
            jax.ShapeDtypeStruct((4, 16, rows // 2), F32),
            jax.ShapeDtypeStruct((4, 16, rows // 2), jnp.int32),
            jax.ShapeDtypeStruct((rows, 1), F32),
            jax.ShapeDtypeStruct((rows, 16), F32),
        ],
        scratch_shapes=[pltpu.VMEM((rows, 16), F32)],
        compiler_params=params(),
        cost_estimate=cost(4 * rows * columns * 256, 8),
    )(jnp.reshape(member, (1,)), *(a for tree in trees for a in tree), *deps)


def expert_grads_kernel(
    chained, steps, where, h_ref, g_ref, on_ref, wg_ref, wu_ref, wd_ref, *refs
):
    mid_ref, gg_ref, own_ref = refs[-3:] if steps == 1 else refs[-4:-1]
    step = pl.program_id(0)
    h, g = h_ref[...], g_ref[...]
    lane = lax.broadcasted_iota(jnp.int32, (1, on_ref.shape[1]), 1) == where[1]
    on = jnp.sum(jnp.where(lane, on_ref[...], 0.0), axis=-1, keepdims=True)
    gate_pre = nn(h, wg_ref[0])
    up_pre = nn(h, wu_ref[0])
    grad_mid = nt(g, wd_ref[0])
    sig = 1.0 / (1.0 + jnp.exp(-gate_pre))
    silu = gate_pre * sig
    mid = silu * up_pre
    column = jnp.where(lane, jnp.sum(grad_mid * mid, axis=-1, keepdims=True), 0.0)
    gg_ref[...] = refs[0][...] + column if chained else column
    act = (on * mid).astype(BF)
    grad_mid = on * grad_mid
    ggp = (grad_mid * up_pre * (sig * (1.0 + gate_pre * (1.0 - sig)))).astype(BF)
    gup = (grad_mid * silu).astype(BF)
    mid_ref[0, 0] = act
    mid_ref[0, 1] = ggp
    mid_ref[0, 2] = gup
    if steps == 1:
        own_ref[0] = tn(h, ggp).astype(BF)
        own_ref[1] = tn(h, gup).astype(BF)
        own_ref[2] = tn(g, act).astype(BF)
        return
    acc = refs[-1]

    @pl.when(step == 0)
    def _():
        acc[...] = jnp.zeros_like(acc)

    acc[0] += tn(h, ggp)
    acc[1] += tn(h, gup)
    acc[2] += tn(g, act)

    @pl.when(step == steps - 1)
    def _():
        own_ref[...] = acc[...].astype(BF)


def expert_grads(
    j, per_core, which, column, h, g, on, w_gate, w_up, w_down, before, slot, slots, deps
):
    rows, width = h.shape
    hidden = w_gate.shape[2]
    experts = on.shape[1]
    tile = row_tile(rows)
    steps = rows // tile

    def row(i, w):
        return (i, 0)

    def weight(i, w):
        return (w[0], 0, 0)

    chained = before is not None
    more = [pl.BlockSpec((tile, experts), row), pl.BlockSpec(memory_space=pl.ANY)] * chained
    aliases = {8: 0} if chained else {}
    if slot:
        aliases[9] = 2
        deps = (before[2], *deps)
    specs, deps = after(deps)
    return pl.pallas_call(
        functools.partial(expert_grads_kernel, chained, steps),
        grid_spec=pltpu.PrefetchScalarGridSpec(
            num_scalar_prefetch=1,
            grid=(steps,),
            in_specs=[
                pl.BlockSpec((tile, width), row),
                pl.BlockSpec((tile, width), row),
                pl.BlockSpec((tile, experts), row),
                pl.BlockSpec((1, width, hidden), weight),
                pl.BlockSpec((1, width, hidden), weight),
                pl.BlockSpec((1, hidden, width), weight),
            ]
            + more
            + specs,
            out_specs=[
                pl.BlockSpec((1, 3, tile, hidden), lambda i, w: (j, 0, i, 0)),
                pl.BlockSpec((tile, experts), row),
                pl.BlockSpec((3, width, hidden), lambda i, w: (slot, 0, 0)),
            ],
            scratch_shapes=[pltpu.VMEM((3, width, hidden), F32)] * (steps > 1),
        ),
        out_shape=[
            jax.ShapeDtypeStruct((per_core, 3, rows, hidden), BF),
            jax.ShapeDtypeStruct((rows, experts), F32),
            jax.ShapeDtypeStruct((3 * slots, width, hidden), BF),
        ],
        input_output_aliases=aliases,
        compiler_params=params(),
        cost_estimate=cost(16 * rows * width * hidden, 20, rows * hidden),
    )(
        jnp.stack([which, column]).astype(jnp.int32),
        h, g, on, w_gate, w_up, w_down,
        *((before[1], before[0]) if chained else ()),
        *deps,
    )


def expert_hidden_kernel(given, split, where, gate_ref, up_ref, wg_ref, wu_ref, *refs):
    e, count = pl.program_id(1), pl.num_programs(1)
    acc = refs[-1]
    part = nt(gate_ref[0, 0], wg_ref[0]) + nt(up_ref[0, 0], wu_ref[0])

    @pl.when(e == 0)
    def _():
        acc[...] = part + refs[0][...].astype(F32) if given else part

    @pl.when(e > 0)
    def _():
        acc[...] += part

    @pl.when(e == count - 1)
    def _():
        if not split:
            refs[-2][...] = acc[...].astype(BF)
            return
        size = refs[-2].shape[1]
        for out, member in ((refs[-3], where[1]), (refs[-2], 1 - where[1])):
            at = pl.ds(pl.multiple_of(member * size, LANES), size)
            out[...] = acc[:, at].astype(BF)


def expert_hidden(first, member, mid, tree, w_gate, w_up, came, split, deps):
    count, _, rows, hidden = mid.shape
    width = w_gate.shape[1]
    rows //= 2
    tile = 448
    tiles = rows // tile

    def weight(i, e, f):
        return (f[0] + e, 0, 0)

    def row(i, e, f):
        return (i, 0)

    given = [came] if came is not None else []
    specs, deps = after(deps)
    outs = 2 if split else 1
    return pl.pallas_call(
        functools.partial(expert_hidden_kernel, bool(given), split),
        grid_spec=pltpu.PrefetchScalarGridSpec(
            num_scalar_prefetch=1,
            grid=(tiles, count),
            in_specs=[
                pl.BlockSpec((1, 1, tile, hidden), lambda i, e, f: (e, 1, tree * tiles + i, 0)),
                pl.BlockSpec((1, 1, tile, hidden), lambda i, e, f: (e, 2, tree * tiles + i, 0)),
                pl.BlockSpec((1, width, hidden), weight),
                pl.BlockSpec((1, width, hidden), weight),
            ]
            + [pl.BlockSpec((tile, width), row) for _ in given]
            + specs,
            out_specs=[pl.BlockSpec((tile, width // outs), row)] * outs,
            scratch_shapes=[pltpu.VMEM((tile, width), F32)],
        ),
        out_shape=[jax.ShapeDtypeStruct((rows, width // outs), BF)] * outs,
        compiler_params=params(),
        cost_estimate=cost(6 * count * rows * width * hidden, 20),
    )(jnp.stack([first, member]).astype(jnp.int32), mid, mid, w_gate, w_up, *given, *deps)


def expert_mix_kernel(first, mid_ref, wd_ref, *refs):
    e, count = pl.program_id(1), pl.num_programs(1)
    acc = refs[-1]
    part = nn(mid_ref[0, 0], wd_ref[0])

    @pl.when(e == 0)
    def _():
        acc[...] = part

    @pl.when(e > 0)
    def _():
        acc[...] += part

    @pl.when(e == count - 1)
    def _():
        refs[-2][...] = acc[...].astype(BF)


def expert_mix(first, mid, tree, w_down, deps):
    count, _, rows, hidden = mid.shape
    width = w_down.shape[2]
    rows //= 2
    tile = 448
    tiles = rows // tile
    specs, deps = after(deps)
    return pl.pallas_call(
        expert_mix_kernel,
        grid_spec=pltpu.PrefetchScalarGridSpec(
            num_scalar_prefetch=1,
            grid=(tiles, count),
            in_specs=[
                pl.BlockSpec((1, 1, tile, hidden), lambda i, e, f: (e, 0, tree * tiles + i, 0)),
                pl.BlockSpec((1, hidden, width), lambda i, e, f: (f[0] + e, 0, 0)),
            ]
            + specs,
            out_specs=pl.BlockSpec((tile, width), lambda i, e, f: (i, 0)),
            scratch_shapes=[pltpu.VMEM((tile, width), F32)],
        ),
        out_shape=jax.ShapeDtypeStruct((rows, width), BF),
        compiler_params=params(),
        cost_estimate=cost(3 * count * rows * width * hidden, 10),
    )(jnp.reshape(first, (1,)).astype(jnp.int32), mid, w_down, *deps)


def out_grads_kernel(parts, where, *refs):
    branch, out_ref = refs[4 * parts : 4 * parts + 2], refs[-1]
    for own in range(2):

        @pl.when(where[0] == own)
        def _():
            for part in range(parts):
                at = (1 - own) * parts + part
                total = sum(
                    tn(refs[2 * parts * t + at][...], branch[t][...]) for t in range(2)
                )
                size = total.shape[0]
                out_ref[part * size : (part + 1) * size, :] = total.astype(BF)


def out_grads(own, attended, branch, deps):
    parts = len(attended[0]) // 2
    size, columns = attended[0][0].shape[1], branch[0].shape[1]
    specs, deps = after(deps)
    return pl.pallas_call(
        functools.partial(out_grads_kernel, parts),
        in_specs=[pl.BlockSpec(memory_space=pltpu.SMEM)]
        + [pl.BlockSpec(memory_space=pltpu.VMEM)] * (4 * parts + 2)
        + specs,
        out_shape=jax.ShapeDtypeStruct((parts * size, columns), BF),
        compiler_params=params(),
        cost_estimate=cost(4 * branch[0].shape[0] * columns * size * parts, 8),
    )(jnp.reshape(own, (1,)).astype(jnp.int32), *attended[0], *attended[1], *branch, *deps)


def tie_kernel(*refs):
    pass


def tie(v, deps):
    if not deps:
        return v
    specs, deps = after((v, *deps))
    return pl.pallas_call(
        tie_kernel,
        in_specs=specs,
        out_specs=pl.BlockSpec(memory_space=pl.ANY),
        out_shape=jax.ShapeDtypeStruct(v.shape, v.dtype),
        input_output_aliases={0: 0},
        cost_estimate=cost(0, 0),
    )(*deps)


def branch_kernel(
    where, mine_ref, came_ref, sums_ref, gl_ref, logits_ref, router_ref, middle_ref, inv_ref,
    gain_ref, grad_ref, w_ref, gain_grad_ref, full_ref, low_ref, theirs_ref, own_ref,
):
    rows, columns = middle_ref.shape
    gl = gl_ref[...]
    total = mine_ref[...].astype(F32) + came_ref[:rows, :].astype(F32)
    total += nt(gl, router_ref[...])
    products = jnp.sum(gl.astype(F32) * logits_ref[...], axis=-1, keepdims=True)
    mean = (sums_ref[...] + get_column(came_ref) + products) / (2 * columns)
    inv = inv_ref[...]
    normed = middle_ref[...] * inv
    gain_grad_ref[...] = jnp.sum(total * normed, axis=0, keepdims=True)
    at = pl.ds(pl.multiple_of(where[0] * columns, LANES), columns)
    grad = grad_ref[:, at].astype(F32)
    grad += inv * (total * gain_ref[...].astype(F32) - normed * mean)
    full_ref[...] = grad
    low = grad.astype(BF)
    low_ref[...] = low
    for out, member in ((theirs_ref, 1 - where[0]), (own_ref, where[0])):
        size = out.shape[1]
        heads = pl.ds(pl.multiple_of(member * size, 16), size)
        out[...] = nt(low, w_ref[heads, :]).astype(out.dtype)


def branch_back(member, mine, came, sums, gl, logits, router, middle, inv, gain, grad, w_out, deps):
    rows, columns = middle.shape
    size = w_out.shape[0] // 2
    specs, deps = after(deps)
    inputs = (mine, came, sums, gl, logits, router, middle, inv, gain)

    def all_of(i):
        return (0, 0)

    outs = [
        jax.ShapeDtypeStruct((1, columns), F32),
        jax.ShapeDtypeStruct((rows, columns), F32),
        jax.ShapeDtypeStruct((rows, columns), BF),
        jax.ShapeDtypeStruct((rows, size), BF),
        jax.ShapeDtypeStruct((rows, size), F32),
    ]

    def kernel(where, *refs):
        branch_kernel(where, *refs[:11], *refs[-5:])

    return pl.pallas_call(
        kernel,
        grid=(1,),
        in_specs=[pl.BlockSpec(memory_space=pltpu.SMEM)]
        + [pl.BlockSpec(a.shape, all_of) for a in inputs]
        + [pl.BlockSpec((rows, grad.shape[1]), all_of), pl.BlockSpec(w_out.shape, all_of)]
        + specs,
        out_specs=[pl.BlockSpec(o.shape, all_of) for o in outs],
        out_shape=outs,
        compiler_params=params(),
        cost_estimate=cost(2 * rows * columns * w_out.shape[0], 10),
    )(jnp.reshape(member, (1,)), *inputs, grad, w_out, *deps)


SLOTS = 128


def picked(gates_ref, slots_ref, block, expert):
    gates = gates_ref[block, pl.ds(expert, 1), :]
    slots = slots_ref[block, pl.ds(expert, 1), :]
    slot = lax.broadcasted_iota(jnp.int32, (SLOTS, gates.shape[1]), 0)
    return (slot == slots) & (gates > 0.0), gates


def one_hot(hit):
    return jnp.where(hit, 1.0, 0.0).astype(BF)


def expert_pair_kernel(
    chained, where, h_ref, g_ref, gates_ref, slots_ref, wg_ref, wu_ref, wd_ref, *refs
):
    mid_ref, gg_ref, own_ref, he_ref, ge_ref = refs[-5:]
    step = pl.program_id(0)
    expert = where[1] + step

    @pl.when(step == 0)
    def _():
        gg_ref[...] = refs[0][...] if chained else jnp.zeros_like(gg_ref)

    count = gates_ref.shape[2]
    hits, scales = [], []
    for b in range(4):
        hit, gates = picked(gates_ref, slots_ref, b, expert)
        pick = one_hot(hit)
        to = slice(b * SLOTS, (b + 1) * SLOTS)
        at = slice(b * count, (b + 1) * count)
        he_ref[to, :] = nn(pick, h_ref[at, :]).astype(BF)
        ge_ref[to, :] = nn(pick, g_ref[at, :]).astype(BF)
        hits.append(hit)
        scales.append(jnp.sum(jnp.where(hit, gates, 0.0), axis=-1, keepdims=True))
    on = jnp.concatenate(scales, 0)
    h, g = he_ref[...], ge_ref[...]
    gate_pre = nn(h, wg_ref[0])
    up_pre = nn(h, wu_ref[0])
    grad_mid = nt(g, wd_ref[0])
    sig = 1.0 / (1.0 + jnp.exp(-gate_pre))
    silu = gate_pre * sig
    mid = silu * up_pre
    column = jnp.sum(grad_mid * mid, axis=-1, keepdims=True)
    for b in range(4):
        part = jnp.where(hits[b], column[b * SLOTS : (b + 1) * SLOTS], 0.0)
        gg_ref[b, pl.ds(expert, 1), :] = jnp.sum(part, axis=0, keepdims=True)
    act = (on * mid).astype(BF)
    grad_mid = on * grad_mid
    ggp = (grad_mid * up_pre * (sig * (1.0 + gate_pre * (1.0 - sig)))).astype(BF)
    gup = (grad_mid * silu).astype(BF)
    mid_ref[0, 0] = act
    mid_ref[0, 1] = ggp
    mid_ref[0, 2] = gup
    own_ref[0] = tn(h, ggp).astype(BF)
    own_ref[1] = tn(h, gup).astype(BF)
    own_ref[2] = tn(g, act).astype(BF)


def expert_pair(
    start, count, slot, per_core, first, column, h, g, gates, slots, w_gate, w_up, w_down, before, deps
):
    rows, width = h.shape
    hidden = w_gate.shape[2]

    def all_of(i, w):
        return (0, 0)

    def every(i, w):
        return (0, 0, 0)

    def weight(i, w):
        return (w[0] + i, 0, 0)

    chained = before is not None
    more = [pl.BlockSpec(gates.shape, every), pl.BlockSpec(memory_space=pl.ANY)] * chained
    aliases = {9: 0} if chained else {}
    if slot:
        aliases[10] = 2
        deps = (before[2], *deps)
    specs, deps = after(deps)
    return pl.pallas_call(
        functools.partial(expert_pair_kernel, chained),
        grid_spec=pltpu.PrefetchScalarGridSpec(
            num_scalar_prefetch=1,
            grid=(count,),
            in_specs=[
                pl.BlockSpec((rows, width), all_of),
                pl.BlockSpec((rows, width), all_of),
                pl.BlockSpec(gates.shape, every),
                pl.BlockSpec(gates.shape, every),
                pl.BlockSpec((1, width, hidden), weight),
                pl.BlockSpec((1, width, hidden), weight),
                pl.BlockSpec((1, hidden, width), weight),
            ]
            + more
            + specs,
            out_specs=[
                pl.BlockSpec((1, 3, 4 * SLOTS, hidden), lambda i, w: (start + i, 0, 0, 0)),
                pl.BlockSpec(gates.shape, every),
                pl.BlockSpec((3, width, hidden), lambda i, w: (slot + i, 0, 0)),
            ],
            scratch_shapes=[pltpu.VMEM((4 * SLOTS, width), BF)] * 2,
        ),
        out_shape=[
            jax.ShapeDtypeStruct((per_core, 3, 4 * SLOTS, hidden), BF),
            jax.ShapeDtypeStruct(gates.shape, F32),
            jax.ShapeDtypeStruct((6, width, hidden), BF),
        ],
        input_output_aliases=aliases,
        compiler_params=params(),
        cost_estimate=cost(12 * count * 4 * SLOTS * width * hidden, 12 * count, rows * hidden),
    )(
        jnp.stack([first, column]).astype(jnp.int32),
        h, g, gates, slots, w_gate, w_up, w_down,
        *((before[1], before[0]) if chained else ()),
        *deps,
    )


def add_picked(acc, tree, column, gates_ref, slots_ref, outs):
    step, steps = pl.program_id(0), pl.num_programs(0)
    count = gates_ref.shape[2]
    for b in range(2):
        pick = jnp.concatenate(
            [
                one_hot(picked(gates_ref, slots_ref, 2 * tree + b, column + 2 * step + i)[0])
                for i in range(2)
            ],
            0,
        )
        rows = jnp.concatenate([out[b * SLOTS : (b + 1) * SLOTS] for out in outs], 0)
        at = slice(b * count, (b + 1) * count)
        acc[at, :] += tn(pick, rows)


def pair_hidden_kernel(given, tree, where, gates_ref, slots_ref, gp_ref, up_ref, wg_ref, wu_ref, *refs):
    step, acc = pl.program_id(0), refs[-1]

    @pl.when(step == 0)
    def _():
        acc[...] = refs[0][...].astype(F32) if given else jnp.zeros_like(acc)

    outs = [
        (nt(gp_ref[i, 0], wg_ref[i]) + nt(up_ref[i, 0], wu_ref[i])).astype(BF) for i in range(2)
    ]
    add_picked(acc, tree, where[1], gates_ref, slots_ref, outs)

    @pl.when(step == pl.num_programs(0) - 1)
    def _():
        if not given:
            refs[-2][...] = acc[...].astype(BF)
            return
        mine, theirs, sums = refs[-4:-1]
        rows, size = mine.shape
        for out, member in ((mine, where[2]), (theirs, 1 - where[2])):
            at = pl.ds(pl.multiple_of(member * size, LANES), size)
            out[:rows, :] = acc[:, at].astype(BF)
        sums[...] = jnp.sum(acc[...] * refs[1][...].astype(F32), axis=-1, keepdims=True)
        put_column(theirs, sums[...])


def pair_hidden(first, column, member, tree, gates, slots, mid, w_gate, w_up, came, deps):
    count, _, rows, hidden = mid.shape
    width = w_gate.shape[1]
    tokens = 2 * gates.shape[2]
    given = came or ()

    def weight(i, w):
        return (w[0] + i, 0, 0)

    def every(i, w):
        return (0, 0, 0)

    def all_of(i, w):
        return (0, 0)

    specs, deps = after(deps)
    if given:
        half = width // 2
        outs = [((tokens, half), BF), ((tokens + 16, half), BF), ((tokens, 1), F32)]
    else:
        outs = [((tokens, width), BF)]
    return pl.pallas_call(
        functools.partial(pair_hidden_kernel, bool(given), tree),
        grid_spec=pltpu.PrefetchScalarGridSpec(
            num_scalar_prefetch=1,
            grid=(count // 2,),
            in_specs=[
                pl.BlockSpec(gates.shape, every),
                pl.BlockSpec(gates.shape, every),
                pl.BlockSpec((2, 1, rows // 2, hidden), lambda i, w: (i, 1, tree, 0)),
                pl.BlockSpec((2, 1, rows // 2, hidden), lambda i, w: (i, 2, tree, 0)),
                pl.BlockSpec((2, width, hidden), weight),
                pl.BlockSpec((2, width, hidden), weight),
            ]
            + [pl.BlockSpec((tokens, width), all_of) for _ in given]
            + specs,
            out_specs=[pl.BlockSpec(shape, all_of) for shape, _ in outs],
            scratch_shapes=[pltpu.VMEM((tokens, width), F32)],
        ),
        out_shape=[jax.ShapeDtypeStruct(*o) for o in outs],
        compiler_params=params(),
        cost_estimate=cost(6 * count * rows * width * hidden, 16),
    )(
        jnp.stack([first // 2, column, member]).astype(jnp.int32),
        gates, slots, mid, mid, w_gate, w_up, *given, *deps,
    )


def pair_mix_kernel(tree, where, gates_ref, slots_ref, act_ref, wd_ref, *refs):
    step, acc = pl.program_id(0), refs[-1]

    @pl.when(step == 0)
    def _():
        acc[...] = jnp.zeros_like(acc)

    outs = [nn(act_ref[i, 0], wd_ref[i]).astype(BF) for i in range(2)]
    add_picked(acc, tree, where[1], gates_ref, slots_ref, outs)

    @pl.when(step == pl.num_programs(0) - 1)
    def _():
        refs[-2][...] = acc[...].astype(BF)


def pair_mix(first, column, tree, gates, slots, mid, w_down, deps):
    count, _, rows, hidden = mid.shape
    width = w_down.shape[2]
    tokens = 2 * gates.shape[2]

    def every(i, w):
        return (0, 0, 0)

    specs, deps = after(deps)
    return pl.pallas_call(
        functools.partial(pair_mix_kernel, tree),
        grid_spec=pltpu.PrefetchScalarGridSpec(
            num_scalar_prefetch=1,
            grid=(count // 2,),
            in_specs=[
                pl.BlockSpec(gates.shape, every),
                pl.BlockSpec(gates.shape, every),
                pl.BlockSpec((2, 1, rows // 2, hidden), lambda i, w: (i, 0, tree, 0)),
                pl.BlockSpec((2, hidden, width), lambda i, w: (w[0] + i, 0, 0)),
            ]
            + specs,
            out_specs=pl.BlockSpec((tokens, width), lambda i, w: (0, 0)),
            scratch_shapes=[pltpu.VMEM((tokens, width), F32)],
        ),
        out_shape=jax.ShapeDtypeStruct((tokens, width), BF),
        compiler_params=params(),
        cost_estimate=cost(3 * count * rows * width * hidden, 10),
    )(jnp.stack([first // 2, column]).astype(jnp.int32), gates, slots, mid, w_down, *deps)


def finish_kernel(layout, chips, where, *refs):
    outs, (last, router, gains) = refs[2 * chips : -3], refs[-3:]
    rows, columns = last.shape[1], router.shape[1]

    @pl.when(pl.program_id(0) == 0)
    def _():
        total = sum(ref[rows:, : 2 * columns].astype(F32) for ref in refs[:chips])
        router[...] = total[:, :columns]
        gains[...] = total[0:2, columns:]

    for i in range(chips):

        @pl.when(pl.program_id(0) == i)
        def _():
            mine, other = refs[i], refs[chips + (chips - i) % chips]
            for g in range(2):
                for out, to, start, size in layout[g]:
                    at = slice(start, start + size)
                    v = jnp.where(where[0] == g, mine[:rows, at], other[:rows, at])
                    outs[out][:, to : to + size] = v.astype(F32)
            start = mine.shape[1] - last.shape[2]
            last[where[0]] = mine[:rows, start:].astype(F32)
            last[1 - where[0]] = other[:rows, start:].astype(F32)


def finish(core, ring, layout, widths, out_width):
    chips = len(ring.chunks)
    tile, columns = ring.chunks[0].shape
    whole = (tile, columns)
    tile -= 16
    rows = tile * chips

    def row(i, w):
        return (w[1 + i], 0)

    def all_of(i, w):
        return (0, 0)

    return pl.pallas_call(
        functools.partial(finish_kernel, layout, chips),
        grid_spec=pltpu.PrefetchScalarGridSpec(
            num_scalar_prefetch=1,
            grid=(chips,),
            in_specs=[pl.BlockSpec(whole, all_of)] * (2 * chips),
            out_specs=[pl.BlockSpec((tile, w), row) for w in widths]
            + [pl.BlockSpec((2, tile, out_width), lambda i, w: (0, w[1 + i], 0))]
            + [pl.BlockSpec((n, out_width), all_of) for n in (16, 2)],
        ),
        out_shape=[jax.ShapeDtypeStruct((rows, w), F32) for w in widths]
        + [jax.ShapeDtypeStruct((2, rows, out_width), F32)]
        + [jax.ShapeDtypeStruct((n, out_width), F32) for n in (16, 2)],
        compiler_params=params(),
        cost_estimate=cost(0, 20),
    )(jnp.stack([core, *ring.chips()]).astype(jnp.int32), *ring.chunks, *ring.other)


def finish_experts_kernel(per_core, half, where, *refs):
    mine, came, outs = refs[:per_core], refs[per_core : 2 * per_core], refs[2 * per_core :]
    rows = pl.ds(pl.multiple_of(where[0] * half, 16), half)
    for j in range(per_core):
        for source, at in ((mine, where[0] * per_core + j), ((came), (1 - where[0]) * per_core + j)):
            v = source[j][:, rows, :].astype(F32)
            outs[0][at] = v[0]
            outs[1][at] = v[1]
            outs[2][at] = v[2]


def finish_experts(core, mine, came):
    per_core = len(mine)
    _, rows, hidden = mine[0].shape
    half = rows // 2
    whole = pl.BlockSpec(memory_space=pltpu.VMEM)
    return pl.pallas_call(
        functools.partial(finish_experts_kernel, per_core, half),
        in_specs=[pl.BlockSpec(memory_space=pltpu.SMEM)] + [whole] * (2 * per_core),
        out_shape=[
            jax.ShapeDtypeStruct((2 * per_core, half, hidden), F32),
            jax.ShapeDtypeStruct((2 * per_core, half, hidden), F32),
            jax.ShapeDtypeStruct((2 * per_core, half, hidden), F32),
        ],
        compiler_params=params(),
        cost_estimate=cost(0, 10),
    )(jnp.reshape(core, (1,)), *mine, *came)


def local(
    tokens,
    norm_gain,
    w_query,
    key_weight,
    value_weight,
    w_out,
    ffn_gain,
    w_router,
    w_gate,
    w_up,
    w_down,
    parents,
    routes,
    cotangent,
):
    me = Mesh()
    paired = me.groups == 2
    tok_rows, width = tokens.shape
    tree_len = tok_rows * me.groups
    seg_len = tree_len // 16
    columns = width // me.groups
    all_q, all_k = w_query.shape[1], key_weight.shape[1]
    q_width, k_width = all_q // me.groups, all_k // me.groups
    kv_heads = k_width // HEAD_DIM
    parts = kv_heads // 2 if kv_heads % 2 == 0 else 1
    q_part, k_part = q_width // parts, k_width // parts
    gq, gk = q_part // HEAD_DIM, k_part // HEAD_DIM
    q_room, k_room = pairs(gq) * LANES, pairs(gk) * LANES
    lanes = q_room + 2 * k_room
    experts = w_gate.shape[0] * me.groups
    per_core = w_gate.shape[0] // 2
    partner = 1 - me.member

    def heads_of(member):
        found = []
        for weight, size, room in (
            (w_query, q_width, q_room),
            (key_weight, k_width, k_room),
            (value_weight, k_width, k_room),
        ):
            block = lax.dynamic_slice_in_dim(weight, member * size, size, 1)
            found.append(jnp.pad(block, ((0, 0), (0, room - size))))
        return jnp.concatenate(found, 1)

    projections = (w_query, key_weight, value_weight)
    gain_row = norm_gain[None]
    own, came = [], []
    along = jnp.split(cotangent, 2, 0)
    early = ()
    grad_came = []
    if paired:
        hot = jnp.any(
            routes.T[:, None, :] == jnp.arange(experts, dtype=jnp.int32)[None, :, None], axis=0
        )
        packet = jnp.concatenate(
            [
                w_router.T,
                jnp.pad(ffn_gain[None], ((0, 15), (0, 0))),
                jnp.pad(hot.astype(BF), ((0, 0), (0, columns - tok_rows))),
            ],
            0,
        )
        x_theirs, x_mine = split(me.member, tokens)
        x_came = me.swap_shard(x_theirs)
        packets = [packet, me.swap_shard(packet)]
        early = (packets[1],)
        grad_came.append(me.swap_shard(tie(along[0], (x_theirs,))))
        *theirs, hidden_first, x_columns, inv_one = project_theirs(
            me.member, parts, x_mine, x_came, gain_row, projections
        )
        own = project_own(me.member, parts, hidden_first, projections, (theirs[-1],))
        came = [me.swap_shard(theirs[0]), me.swap_shard(tie(theirs[1], own[:1]))]
    else:
        every_head = jnp.concatenate([heads_of(j) for j in range(me.groups)], 1)
        own_rows = tokens.astype(F32)
        inv_rows = lax.rsqrt(jnp.mean(own_rows * own_rows, axis=-1, keepdims=True) + EPS)
        x_columns = me.exchange(tokens, 1, 0)
        inv_one = me.gather(inv_rows, 0)
        hidden_first = (x_columns.astype(F32) * inv_one * norm_gain.astype(F32)).astype(BF)
        own.append(me.scatter(nn(hidden_first, every_head), 1))
        came.append(jnp.zeros(own[-1].shape, BF))

    gain_two = ffn_gain.astype(F32)

    index = jnp.arange(tree_len, dtype=jnp.int32)
    _, depth = tree_layout(index, seg_len)
    cos, sin = angle_tables(depth)
    visible = tree_mask(index, index, parents[0], seg_len)
    bias = jnp.where(visible, 0.0, -1e30).astype(F32)

    attended, lse, query, key, value, att_came = [], [], [], [], [], []
    for part in range(parts):
        a, b, c, d, e = attend(own[part], came[part], cos, sin, bias, gq, gk, (*early, *grad_came[:1]))
        attended.append(a)
        lse.append(b)
        query.append(c)
        key.append(d)
        value.append(e)
        if paired:
            att_came.append(me.swap_shard(a))
    if paired:
        sent = tie(along[1], att_came)
        grad_came.append(me.swap_shard(sent))
        mine = [cotangent, me.swap_core(cotangent)]
        others = [*grad_came, *(me.swap_core(v) for v in grad_came)]
        grad_all = jnp.where(
            me.member == 0,
            jnp.concatenate([mine[0], *others[:2], mine[1], *others[2:]], 0),
            jnp.concatenate([*others[:2], mine[0], *others[2:], mine[1]], 0),
        )
        starts = [
            member * q_width + part * q_part
            for member in (me.member, partner)
            for part in range(parts)
        ]
        middle, middle_low, squares = middle_of(
            attended + att_came, jnp.stack(starts).astype(jnp.int32), w_out, x_columns, True, (sent,)
        )
        attended_full = me.in_order(
            me.member, jnp.concatenate(attended, 1), jnp.concatenate(att_came, 1), 1
        )
        messages = [middle_low, me.swap_shard(middle_low)]
        hidden_all, gates_all, slots_all, inv_two, logits = hidden_packed(
            me.member,
            [
                (*messages, *packets),
                (*(me.swap_core(v) for v in messages), *(me.swap_core(v) for v in packets)),
            ],
            (grad_all,),
        )
    else:
        grad_tree = me.gather(cotangent, 0)
        grad_all = jnp.concatenate([grad_tree, me.swap_core(grad_tree)], 0)
        attended_full = me.gather(attended[0][:, :q_width], 1)
        where = jnp.zeros((1,), jnp.int32)
        middle, middle_low, squares = middle_of([attended_full], where, w_out, x_columns, False)
        route_hot = jnp.any(
            routes[:, :, None] == jnp.arange(experts, dtype=jnp.int32)[None, None, :], axis=1
        ).astype(F32)
        routed = me.gather(route_hot, 0)
        middle_low, squares = me.gather(middle_low, 1), me.total(squares)
        hidden_all, gates_all = hidden_of(
            [
                ([middle_low], [squares], routed),
                (
                    [me.swap_core(middle_low)],
                    [me.swap_core(squares)],
                    me.swap_core(routed),
                ),
            ],
            where,
            me.gather(ffn_gain, 0)[None],
            me.gather(w_router, 0),
        )
        inv_two = lax.rsqrt(squares / width + EPS)
    grad_tree = grad_all[:tree_len]
    hidden_all = hidden_all.reshape(2 * tree_len, width)
    normed_two = middle * inv_two
    hidden_own = (normed_two * gain_two).astype(BF)

    first = me.core * per_core
    chunk = width // me.chips
    def gates_grad(gates, grad, axis):
        return (gates * (grad - jnp.sum(gates * grad, axis=axis, keepdims=True))).astype(BF)

    def output_of(mixed_own, mixed_other):
        mixed = mixed_own.astype(F32) + me.swap_core(mixed_other).astype(F32)
        placed = lax.dynamic_update_slice_in_dim(
            jnp.zeros((tree_len, width), F32), middle, me.member * columns, 1
        )
        return mixed + placed

    def input_of(grad_middle, scaled, row_sums):
        normed = x_columns.astype(F32) * inv_one
        grad = grad_middle + inv_one * (scaled - normed * (row_sums / width))
        return me.exchange(grad.astype(BF), 0, 1)

    flipped = bias.T
    if not paired:
        gates = gates_all[0]
        gates_all = gates_all.reshape(2 * tree_len, experts)
        before, rings = None, []
        for j in range(per_core):
            before = expert_grads(
                j, per_core, first + j, me.member * (2 * per_core) + first + j,
                hidden_all, grad_all, gates_all, w_gate, w_up, w_down, before, 0, 1, (),
            )
            mid, own_columns, grads = before
            ring = Scatter(me, lambda chip: lax.dynamic_slice_in_dim(grads, chip * chunk, chunk, 1))
            for _ in range(me.chips - 1):
                ring.start()
                ring.finish()
            rings.append(ring.held)
        grad_gates = me.total(own_columns[:tree_len] + me.swap_core(own_columns[tree_len:]))
        grad_logits = gates_grad(gates, grad_gates, -1)
        (grad_other,) = expert_hidden(first, me.member, mid, 1, w_gate, w_up, None, False, ())
        (grad_own,) = expert_hidden(
            first, me.member, mid, 0, w_gate, w_up, me.swap_core(grad_other), False, ()
        )
        mixed_other = expert_mix(first, mid, 1, w_down, ())
        mixed_own = expert_mix(first, mid, 0, w_down, ())
        result = me.scatter(output_of(mixed_own, mixed_other), 0).astype(BF)
        grad_hidden_two = nt(grad_logits, w_router) + me.scatter(grad_own, 1)
        grad_gain_two = jnp.sum(grad_hidden_two * normed_two, axis=0)[None]
        scaled = grad_hidden_two * gain_two
        mean = me.total(jnp.sum(scaled * normed_two, axis=-1, keepdims=True)) / width
        grad_columns = me.part(grad_tree, 1, me.member).astype(F32)
        grad_middle = grad_columns + inv_two * (scaled - normed_two * mean)
        grad_branch = grad_middle.astype(BF)
        own = me.scatter(nt(grad_branch, w_out), 1)
        own = jnp.pad(own, ((0, 0), (0, q_room - q_width)))
        grad_heads = attend_back(
            own, jnp.zeros(own.shape, BF), query[0], key[0], value[0], lse[0],
            cos, sin, flipped, gq, gk, 0, (),
        )
        grad_out = me.all_reduce(tn(attended_full, grad_branch))
        grad_full = me.gather(grad_heads, 1)
        every = me.all_reduce(tn(hidden_first, grad_full))
        every = every.reshape(columns, me.groups, lanes)
        grad_query, grad_key, grad_value = (
            every[:, :, start : start + size].reshape(columns, me.groups * size)
            for start, size in ((0, q_width), (q_room, k_width), (q_room + k_room, k_width))
        )
        grad_hidden_one = nt(grad_full, every_head)
        normed_one = x_columns.astype(F32) * inv_one
        grad_gain_one = jnp.sum(grad_hidden_one * normed_one, axis=0)[None]
        scaled = grad_hidden_one * norm_gain.astype(F32)
        row_sums = jnp.sum(scaled * normed_one, axis=-1, keepdims=True)
        input_grad = input_of(grad_middle, scaled, me.total(row_sums))
        grad_router = tn(hidden_own, grad_logits)
        small = me.butterfly(jnp.concatenate([grad_gain_one, grad_gain_two, grad_router.T], 0))
        small = (small[0], small[1], small[2:].T)
        sums = rings
        grad_gate, grad_up, grad_down = finish_experts(
            me.core, sums, [me.swap_core(v) for v in sums]
        )
    else:

        column = me.member * (2 * per_core) + first

        def experts_of(start, count, slot, before, deps):
            return expert_pair(
                start, count, slot, per_core, first + start, column + start,
                hidden_all, grad_all, gates_all, slots_all, w_gate, w_up, w_down, before, deps,
            )

        def hidden_grad(tree, came, deps):
            return pair_hidden(
                first, column, me.member, tree, gates_all, slots_all, mid, w_gate, w_up, came, deps
            )

        def mix_of(tree, deps):
            return pair_mix(first, column, tree, gates_all, slots_all, mid, w_down, deps)

        def ring_of(grads):
            return Scatter(me, lambda chip: lax.dynamic_slice_in_dim(grads, chip * chunk, chunk, 1))

        one = experts_of(0, 2, 0, None, ())
        ring_a = ring_of(one[2])
        sent = ring_a.start()
        mid, own_rows, grads = experts_of(2, 2, 0, one, ())
        sent_a = ring_a.hop(own_rows)
        ring_b = ring_of(grads)
        sent_b = ring_b.start()
        grad_gates = me.total(own_rows[:2] + me.swap_core(own_rows[2:]))
        grad_logits = gates_grad(gates_all[:2], grad_gates, 1)
        grad_logits = grad_logits.transpose(0, 2, 1).reshape(tree_len, experts)
        (grad_other,) = hidden_grad(1, None, (sent_a, sent_b))
        other_came = me.swap_core(grad_other)
        sent = ring_a.hop(grad_other)
        grad_mine, grad_theirs, row_sums = hidden_grad(0, (other_came, hidden_all), (sent,))
        hidden_came = me.swap_shard(grad_theirs)
        sent = ring_b.hop(grad_mine)
        mixed_other = mix_of(1, (sent,))
        sent = ring_a.hop(mixed_other)
        mixed_own = mix_of(0, (sent, grad_logits))
        sent = ring_b.hop(mixed_own)
        grad_gain_two, grad_middle, grad_branch, theirs, own = branch_back(
            me.member, grad_mine, hidden_came, row_sums, grad_logits, logits, w_router,
            middle, inv_two, ffn_gain[None], grad_all, w_out, (sent,),
        )
        came = me.swap_shard(theirs)
        sent = ring_a.hop(grad_branch)
        grad_out = out_grads(
            me.core == me.member,
            [attended + att_came, [me.swap_core(v) for v in attended + att_came]],
            [grad_branch, me.swap_core(grad_branch)],
            (sent,),
        )
        sent = ring_b.hop(grad_out)
        heads_a = attend_back(
            own, came, query[0], key[0], value[0], lse[0], cos, sin, flipped, gq, gk, 0,
            (sent,),
        )
        back_a = me.swap_shard(heads_a)
        sent = ring_a.hop(heads_a)
        heads_b = attend_back(
            own, came, query[1], key[1], value[1], lse[1], cos, sin, flipped, gq, gk, q_part,
            (sent,),
        )
        back_a = tie(back_a, (heads_b,))
        back_b = me.swap_shard(heads_b)
        sent = (ring_b.hop(heads_b), ring_a.hop(heads_b))
        summed = output_of(tie(mixed_own, (back_a, *sent)), mixed_other).astype(BF)
        to_send = me.part(summed, 0, partner)
        grad_pairs = [(heads_a, back_a), (heads_b, back_b)]
        grads_mine = weight_grads(
            me.member,
            me.core,
            (hidden_first, me.swap_core(hidden_first)),
            (grad_pairs, [tuple(me.swap_core(v) for v in pair) for pair in grad_pairs]),
            grad_out,
            (*sent, to_send),
        )
        head_chunk = grads_mine.shape[0] // me.chips
        ring_w = Scatter(
            me, lambda chip: lax.dynamic_slice_in_dim(grads_mine, chip * head_chunk, head_chunk, 0)
        )
        sent = ring_b.hop(ring_w.start())
        grad_router = tn(hidden_own, grad_logits)
        scaled, row_sums, grad_gain_one = project_back(
            me.member, x_columns, inv_one, gain_row, projections, grad_pairs, (sent,)
        )
        beside = {1: (scaled,)}

        def later(hop, v):
            beside[hop] = (*beside.get(hop, ()), v)

        hops, experts_done, waiting = me.chips - 1, None, None
        for hop in range(1, 2 * hops):
            w = ring_w.finish() if hop <= hops else sent
            if hop > hops:
                ring_w.finish()
            if hop == hops:
                small = jnp.concatenate(
                    [
                        grad_router.T,
                        jnp.pad(jnp.concatenate([grad_gain_one, grad_gain_two]), ((0, 14), (0, 0))),
                    ],
                    1,
                )
                small = (small + me.swap_core(small)).astype(BF)
                small = jnp.pad(small, ((0, 0), (0, ring_w.held.shape[1] - small.shape[1])))
                ring_w = Gather(me, jnp.concatenate([ring_w.held, small], 0))
            if hop == 1:
                row_total = me.total(row_sums)
                later(2, row_total)
            if hop == 2:
                input_grad = input_of(grad_middle, scaled, row_total)
                later(5, input_grad)
            if hop == 3:
                result = me.swap_shard(tie(to_send, (w,))).astype(F32)
                result = (result + me.part(summed, 0, me.member).astype(F32)).astype(BF)
                later(2 * hops - 2, result)
            deps = beside.get(hop, ())
            ring = {1: ring_a, 2: ring_b, 4: ring_b}.get(hop)
            if ring is not None and ring.hops < hops:
                deps = (*deps, ring.finish(w))
                if ring.hops < hops:
                    waiting = ring
                elif ring_a.hops == ring_b.hops:
                    sums = [h for r in (ring_a, ring_b) for h in jnp.split(r.held, 2, 0)]
                    experts_done = finish_experts(me.core, sums, [me.swap_core(v) for v in sums])
                    later(2 * hops - 3, experts_done[0])
            sent = ring_w.start(*deps)
            if waiting is not None:
                waiting.start(sent)
                waiting = None
        ring_w.finish()
        grad_gate, grad_up, grad_down = experts_done
        layout = [
            [
                (out, j * step + part * size, j * lanes + start, size)
                for j in range(2)
                for out, step, start, size in (
                    (0, q_width, 0, q_part),
                    (1, k_width, q_room, k_part),
                    (2, k_width, q_room + k_room, k_part),
                )
            ]
            for part in range(parts)
        ]
        grad_query, grad_key, grad_value, grad_out, *small = finish(
            me.core, ring_w, layout, (all_q, all_k, all_k), columns
        )
        grad_out = grad_out.reshape(-1, columns)
        small = (small[1][0], small[1][1], small[0].T)

    return (
        result,
        input_grad,
        small[0],
        grad_query,
        grad_key,
        grad_value,
        grad_out,
        small[1],
        small[2],
        grad_gate,
        grad_up,
        grad_down.transpose(0, 2, 1),
    )


def solution(mesh):
    return jax.shard_map(
        local,
        mesh=mesh,
        in_specs=(
            P(("rep", "shard"), None),
            P("shard"),
            P("shard", None),
            P("shard", None),
            P("shard", None),
            P(None, "shard"),
            P("shard"),
            P("shard", None),
            P("shard", None, None),
            P("shard", None, None),
            P("shard", None, None),
            P("rep", None),
            P(("rep", "shard"), None),
            P(("rep", "shard"), None),
        ),
        out_specs=(
            P(("rep", "shard"), None),
            P(("rep", "shard"), None),
            P("shard"),
            P("shard", None),
            P("shard", None),
            P("shard", None),
            P(None, "shard"),
            P("shard"),
            P("shard", None),
            P("shard", "rep", None),
            P("shard", "rep", None),
            P("shard", None, "rep"),
        ),
        check_vma=False,
    )
```

```python
import functools

import jax
import jax.numpy as jnp
from jax import lax
from jax.experimental import pallas as pl
from jax.experimental.pallas import tpu as pltpu
from jax.sharding import PartitionSpec as P

HEAD_DIM = 64
LANES = 128
EPS = 1e-06
BF = jnp.bfloat16
F32 = jnp.float32
VMEM_LIMIT = 60 << 20


def tree_layout(position, seg_len):
    trunk_len = 4 * seg_len
    beyond = position - trunk_len
    segment = jnp.where(position < trunk_len, 0, 1 + beyond // seg_len)
    inner = jnp.where(
        segment <= 4, trunk_len + beyond % seg_len, trunk_len + seg_len + beyond % seg_len
    )
    depth_position = jnp.where(position < trunk_len, position, inner)
    return (segment, depth_position)


def lookup(segment, parents_row):
    labels = jnp.arange(parents_row.shape[0], dtype=jnp.int32)
    picked = jnp.where(segment[:, None] == labels[None, :], parents_row[None, :], 0)
    return jnp.sum(picked, axis=1)


def tree_mask(query_index, key_index, parents_row, seg_len):
    query_seg, _ = tree_layout(query_index, seg_len)
    key_seg, _ = tree_layout(key_index, seg_len)
    parent_one = lookup(query_seg, parents_row)
    parent_two = lookup(parent_one, parents_row)
    key_row = key_seg[None, :]
    related = (
        (key_row == query_seg[:, None])
        | (key_row == parent_one[:, None])
        | (key_row == parent_two[:, None])
    )
    return related & (key_index[None, :] <= query_index[:, None])


def angle_tables(depth_position):
    half = HEAD_DIM // 2
    frequency = 10000.0 ** (-2.0 * jnp.arange(half, dtype=F32) / HEAD_DIM)
    angles = depth_position.astype(F32)[:, None] * frequency[None, :]
    cosine, sine = jnp.cos(angles), jnp.sin(angles)
    return (
        jnp.concatenate([cosine] * 4, 1),
        jnp.concatenate([-sine, sine, -sine, sine], 1),
    )


def dot(a, b, dims):
    return lax.dot_general(a, b, (dims, ((), ())), preferred_element_type=F32)


def nn(a, b):
    return dot(a, b, ((1,), (0,)))


def nt(a, b):
    return dot(a, b, ((1,), (1,)))


def tn(a, b):
    return dot(a, b, ((0,), (0,)))


class Mesh:
    def __init__(self):
        self.groups = lax.axis_size("shard")
        self.member = lax.axis_index("shard")
        self.reps = lax.axis_size("rep")
        self.rep = lax.axis_index("rep")
        self.core = self.rep % 2
        self.chip = self.rep // 2
        self.chips = self.reps // 2
        rows = self.chips // 2
        order = [2 * z for z in range(rows)] + [2 * z + 1 for z in range(rows - 1, -1, -1)]
        self.ring = []
        for place, chip in enumerate(order):
            after, before = order[(place + 1) % self.chips], order[place - 1]
            self.ring += [(2 * chip, 2 * after), (2 * chip + 1, 2 * before + 1)]
        self.place = jnp.where(
            self.chip % 2 == 0, self.chip // 2, self.chips - 1 - self.chip // 2
        )
        self.way = 1 - 2 * self.core

    def chip_at(self, place):
        place = place % self.chips
        rows = self.chips // 2
        return jnp.where(place < rows, 2 * place, 2 * (self.chips - 1 - place) + 1)

    def swap_shard(self, v):
        return lax.ppermute(v, "shard", [(0, 1), (1, 0)])

    def swap_core(self, v):
        return lax.ppermute(v, "rep", [(r, r ^ 1) for r in range(self.reps)])

    def along_ring(self, v):
        return lax.ppermute(v, "rep", self.ring)

    def part(self, v, axis, which):
        size = v.shape[axis] // self.groups
        return lax.dynamic_slice_in_dim(v, which * size, size, axis)

    def gather(self, v, axis):
        if self.groups != 2:
            return lax.all_gather(v, "shard", axis=axis, tiled=True)
        other = self.swap_shard(v)
        return self.in_order(self.member, v, other, axis)

    def in_order(self, which, mine, other, axis):
        return jnp.where(
            which == 0,
            jnp.concatenate([mine, other], axis),
            jnp.concatenate([other, mine], axis),
        )

    def exchange(self, v, split_axis, concat_axis):
        if self.groups != 2:
            return lax.all_to_all(v, "shard", split_axis, concat_axis, tiled=True)
        other = self.swap_shard(self.part(v, split_axis, 1 - self.member))
        mine = self.part(v, split_axis, self.member)
        return self.in_order(self.member, mine, other, concat_axis)

    def scatter(self, v, axis):
        if self.groups != 2:
            return lax.psum_scatter(
                v.astype(BF), "shard", scatter_dimension=axis, tiled=True
            ).astype(F32)
        other = self.swap_shard(self.part(v, axis, 1 - self.member).astype(BF))
        return self.part(v, axis, self.member).astype(F32) + other.astype(F32)

    def total(self, v):
        if self.groups != 2:
            return lax.psum(v, "shard")
        return v + self.swap_shard(v)

    def ring_sum(self, v):
        chunk = v.shape[0] // self.chips
        ring = Scatter(self, lambda chip: lax.dynamic_slice_in_dim(v, chip * chunk, chunk, 0))
        for _ in range(self.chips - 1):
            ring.start()
            ring.finish()
        ring = Gather(self, ring.held)
        for _ in range(self.chips - 1):
            ring.start()
            ring.finish()
        whole = jnp.zeros(v.shape, v.dtype)
        for at, part in zip(ring.chips(), ring.chunks):
            whole = lax.dynamic_update_slice_in_dim(whole, part, at * chunk, 0)
        return whole

    def all_reduce(self, v):
        half = v.shape[0] // 2
        v = v.astype(BF)
        mine = lax.dynamic_slice_in_dim(v, self.core * half, half, 0)
        other = self.swap_core(
            lax.dynamic_slice_in_dim(v, (1 - self.core) * half, half, 0)
        )
        whole = self.ring_sum((mine.astype(F32) + other.astype(F32)).astype(BF))
        return self.in_order(self.core, whole, self.swap_core(whole), 0).astype(F32)

    def swap_rep(self, v, bit):
        return lax.ppermute(v, "rep", [(r, r ^ bit) for r in range(self.reps)])

    def butterfly(self, v):
        bit = 1
        while bit < self.reps:
            v = v + self.swap_rep(v, bit)
            bit *= 2
        return v


class Scatter:
    def __init__(self, me, own):
        self.me, self.own, self.hops = me, own, 0
        self.held = own(me.chip_at(me.place - me.way))

    def start(self, *deps):
        sent = tie(self.held, deps)
        self.came = self.me.along_ring(sent)
        return sent

    def hop(self, *deps):
        self.finish(*deps)
        return self.start()

    def finish(self, *deps):
        self.hops += 1
        self.came = tie(self.came, deps)
        mine = self.own(self.me.chip_at(self.me.place - self.me.way * (self.hops + 1)))
        self.held = (self.came.astype(F32) + mine.astype(F32)).astype(BF)
        return self.came


class Gather:
    def __init__(self, me, held):
        self.me, self.came, self.hops = me, held, 0
        self.chunks, self.other = [], []

    def chips(self):
        me = self.me
        return [me.chip_at(me.place - me.way * hop) for hop in range(me.chips)]

    def keep(self, chunk):
        self.chunks.append(chunk)
        self.other.append(self.me.swap_core(chunk))

    def start(self, *deps):
        sent = tie(self.came, deps)
        self.came = self.me.along_ring(sent)
        self.keep(sent)
        return sent

    def finish(self):
        self.hops += 1
        if self.hops == self.me.chips - 1:
            self.keep(self.came)


def pairs(heads):
    return -(-heads // 2)


def rope(v, cos, sin, back):
    lane = lax.broadcasted_iota(jnp.int32, (1, LANES), 1)
    first = lane % HEAD_DIM < HEAD_DIM // 2
    out = []
    for i in range(v.shape[1] // LANES):
        x = v[:, i * LANES : (i + 1) * LANES]
        other = jnp.where(
            first,
            pltpu.roll(x, LANES - HEAD_DIM // 2, 1),
            pltpu.roll(x, HEAD_DIM // 2, 1),
        )
        out.append(x * cos - other * sin if back else x * cos + other * sin)
    return out


def halves(x, parity):
    low = lax.broadcasted_iota(jnp.int32, (1, LANES), 1) < HEAD_DIM
    zero = jnp.zeros_like(x)
    turned = pltpu.roll(x, HEAD_DIM, 1)
    a, b = (x, turned) if parity == 0 else (turned, x)
    return jnp.where(low, a, zero).astype(BF), jnp.where(low, zero, b).astype(BF)


def attend_kernel(
    q_heads, kv_heads, own_ref, came_ref, cos_ref, sin_ref, bias_ref,
    *refs,
):
    out_ref, lse_ref, q_ref, k_ref, v_ref = refs[-5:]
    per = q_heads // kv_heads
    rows = own_ref.shape[0]
    qp, kp = pairs(q_heads), pairs(kv_heads)
    cos, sin = cos_ref[...], sin_ref[...]
    raw = own_ref[...].astype(F32) + came_ref[...].astype(F32)
    scale = HEAD_DIM**-0.5
    q = [(t * scale).astype(BF) for t in rope(raw[:, : qp * LANES], cos, sin, False)]
    keys = rope(raw[:, qp * LANES : (qp + kp) * LANES], cos, sin, False)
    for i in range(qp):
        q_ref[:, i * LANES : (i + 1) * LANES] = q[i]
    ks, vs = [], []
    for g in range(kv_heads):
        at = (qp + kp + g // 2) * LANES
        ks.append(halves(keys[g // 2], g % 2))
        vs.append(halves(raw[:, at : at + LANES], g % 2))
        for p in range(2):
            k_ref[g, p] = ks[g][p]
            v_ref[g, p] = vs[g][p]
    half = rows // 2
    for lo, n in ((0, half), (half, rows)):
        bias = bias_ref[lo : lo + half, :n]
        for i in range(qp):
            out = jnp.zeros((half, LANES), F32)
            for h in range(2 * i, min(2 * i + 2, q_heads)):
                g, p = h // per, h % 2
                s = nt(q[i][lo : lo + half], ks[g][p][:n]) + bias
                peak = jnp.max(s, axis=-1, keepdims=True)
                e = jnp.exp(s - peak)
                total = jnp.sum(e, axis=-1, keepdims=True)
                lse_ref[lo : lo + half, h : h + 1] = peak + jnp.log(total)
                out = out + nn((e * (1.0 / total)).astype(BF), vs[g][p][:n])
            out_ref[lo : lo + half, i * LANES : (i + 1) * LANES] = out.astype(BF)


def attend(own, came, cos, sin, bias, q_heads, kv_heads, deps):
    rows = own.shape[0]
    qp = pairs(q_heads)
    specs, deps = after(deps)
    return pl.pallas_call(
        functools.partial(attend_kernel, q_heads, kv_heads),
        in_specs=[pl.BlockSpec(memory_space=pltpu.VMEM)] * 5 + specs,
        out_shape=[
            jax.ShapeDtypeStruct((rows, qp * LANES), BF),
            jax.ShapeDtypeStruct((rows, LANES), F32),
            jax.ShapeDtypeStruct((rows, qp * LANES), BF),
            jax.ShapeDtypeStruct((kv_heads, 2, rows, LANES), BF),
            jax.ShapeDtypeStruct((kv_heads, 2, rows, LANES), BF),
        ],
        compiler_params=pltpu.CompilerParams(vmem_limit_bytes=VMEM_LIMIT),
        cost_estimate=pl.CostEstimate(
            flops=1200 * rows * rows * q_heads,
            bytes_accessed=8 << 20,
            transcendentals=rows * rows * q_heads,
        ),
    )(own, came, cos, sin, bias, *deps)


def attend_back_kernel(
    q_heads, kv_heads, start, own_ref, came_ref, q_ref, k_ref, v_ref, lse_ref,
    cos_ref, sin_ref, bias_ref, *refs,
):
    per = q_heads // kv_heads
    rows = own_ref.shape[0]
    qp, kp = pairs(q_heads), pairs(kv_heads)
    cos, sin = cos_ref[...], sin_ref[...]
    scale = HEAD_DIM**-0.5
    low = lax.broadcasted_iota(jnp.int32, (1, LANES), 1) < HEAD_DIM
    at = slice(start, start + qp * LANES)
    grad = (own_ref[:, at].astype(F32) + came_ref[:, at].astype(F32)).astype(BF)
    lse = lse_ref[...].T
    half = rows // 2
    out_ref = refs[-1]

    def put(at, v):
        out_ref[:, at * LANES : (at + 1) * LANES] = v.astype(BF)

    def blocks():
        return [
            [[jnp.zeros((half, LANES), F32) for _ in range(2)] for _ in range(2)]
            for _ in range(kv_heads)
        ]

    dk, dv = blocks(), blocks()
    for i in range(qp):
        parts = []
        for lo, n in ((0, half), (half, rows)):
            q = q_ref[lo : lo + half, i * LANES : (i + 1) * LANES]
            go = grad[lo : lo + half, i * LANES : (i + 1) * LANES]
            bias = bias_ref[:n, lo : lo + half]
            dq = jnp.zeros((half, LANES), F32)
            for h in range(2 * i, min(2 * i + 2, q_heads)):
                g, p = h // per, h % 2
                k, v = k_ref[g, p, :n], v_ref[g, p, :n]
                s = nt(k, q) + bias
                probs = jnp.exp(s - lse[h : h + 1, lo : lo + half])
                dp = nt(v, go)
                delta = jnp.sum(probs * dp, axis=0, keepdims=True)
                ds = (probs * (dp - delta)).astype(BF)
                dq = dq + tn(ds, k)
                ck, cv = nn(ds, q), nn(probs.astype(BF), go)
                for b in range(n // half):
                    dk[g][p][b] = dk[g][p][b] + ck[b * half : (b + 1) * half]
                    dv[g][p][b] = dv[g][p][b] + cv[b * half : (b + 1) * half]
            parts.append(dq * scale)
        put(i, rope(jnp.concatenate(parts, 0), cos, sin, True)[0])

    def packed(d, j):
        got = jnp.zeros((rows, LANES), F32)
        for g in range(2 * j, min(2 * j + 2, kv_heads)):
            a, b = (jnp.concatenate(d[g][p], 0) for p in range(2))
            a, b = jnp.where(low, a, 0.0), jnp.where(low, 0.0, b)
            if g % 2 == 0:
                got = got + a + pltpu.roll(b, HEAD_DIM, 1)
            else:
                got = got + b + pltpu.roll(a, HEAD_DIM, 1)
        return got

    for j in range(kp):
        put(qp + j, rope(packed(dk, j), cos, sin, True)[0])
        put(qp + kp + j, packed(dv, j))


def attend_back(own, came, q, k, v, lse, cos, sin, bias, q_heads, kv_heads, start, deps):
    rows = own.shape[0]
    lanes = (pairs(q_heads) + 2 * pairs(kv_heads)) * LANES
    specs, deps = after(deps)
    return pl.pallas_call(
        functools.partial(attend_back_kernel, q_heads, kv_heads, start),
        in_specs=[pl.BlockSpec(memory_space=pltpu.VMEM)] * 9 + specs,
        out_shape=jax.ShapeDtypeStruct((rows, lanes), BF),
        compiler_params=pltpu.CompilerParams(vmem_limit_bytes=VMEM_LIMIT),
        cost_estimate=pl.CostEstimate(
            flops=1600 * rows * rows * q_heads,
            bytes_accessed=8 << 20,
            transcendentals=rows * rows * q_heads,
        ),
    )(own, came, q, k, v, lse, cos, sin, bias, *deps)


def after(arrays):
    return [pl.BlockSpec(memory_space=pl.ANY)] * len(arrays), tuple(arrays)


def row_tile(rows):
    return rows if rows <= 896 else 448


def params():
    return pltpu.CompilerParams(vmem_limit_bytes=VMEM_LIMIT)


def cost(flops, megabytes, transcendentals=0):
    return pl.CostEstimate(
        flops=int(flops), bytes_accessed=megabytes << 20, transcendentals=int(transcendentals)
    )


def to_row(column):
    rows = column.shape[0]
    return jnp.broadcast_to(column, (rows, LANES)).T[:1]


def to_column(row):
    return jnp.broadcast_to(row, (LANES, row.shape[1])).T[:, :1]


def put_column(ref, column):
    rows = column.shape[0]
    row = to_row(column)
    high = row.astype(BF)
    low = (row - high.astype(F32)).astype(BF)
    line = lax.broadcasted_iota(jnp.int32, (16, rows), 0)
    ref[rows : rows + 16, :] = jnp.zeros((16, ref.shape[1]), BF)
    ref[rows : rows + 16, :rows] = jnp.where(
        line == 0, high.astype(F32), jnp.where(line == 1, low.astype(F32), 0.0)
    ).astype(BF)


def get_column(ref):
    rows = ref.shape[0] - 16
    last = ref[rows : rows + 16, :rows].astype(F32)
    return to_column(last[0:1] + last[1:2])


def split_kernel(where, x_ref, theirs_ref, mine_ref):
    rows, size = x_ref.shape[0], mine_ref.shape[1]
    x = x_ref[...].astype(F32)
    squares = jnp.sum(x * x, axis=-1, keepdims=True)
    for ref, member in ((theirs_ref, 1 - where[0]), (mine_ref, where[0])):
        ref[:rows, :] = x_ref[:, pl.ds(pl.multiple_of(member * size, LANES), size)]
        put_column(ref, squares)


def split(member, x):
    rows, width = x.shape
    out = jax.ShapeDtypeStruct((rows + 16, width // 2), BF)
    return pl.pallas_call(
        split_kernel,
        in_specs=[pl.BlockSpec(memory_space=pltpu.SMEM), pl.BlockSpec(memory_space=pltpu.VMEM)],
        out_shape=[out, out],
        compiler_params=params(),
        cost_estimate=cost(0, 2),
    )(jnp.reshape(member, (1,)), x)


def heads_product(hidden, member, part, parts, weights):
    found = []
    for w in weights:
        size = w.shape[1] // (2 * parts)
        at = pl.ds(pl.multiple_of((member * parts + part) * size, LANES), size)
        found.append(nn(hidden, w[:, at]))
    return jnp.concatenate(found, 1)


def project_theirs_kernel(parts, where, mine_ref, came_ref, gain_ref, wq, wk, wv, *refs):
    outs, (hidden_ref, x_ref, inv_ref) = refs[:parts], refs[parts:]
    rows, columns = mine_ref.shape[0] - 16, mine_ref.shape[1]
    gain = gain_ref[...].astype(F32)
    for message, member in ((mine_ref, where[0]), (came_ref, 1 - where[0])):
        at = pl.ds(pl.multiple_of(member * rows, 16), rows)
        inv = lax.rsqrt(get_column(message) / (2 * columns) + EPS)
        inv_ref[at, :] = inv
        x = message[:rows, :]
        x_ref[at, :] = x
        hidden_ref[at, :] = (x.astype(F32) * inv * gain).astype(BF)
    for part in range(parts):
        outs[part][...] = heads_product(
            hidden_ref[...], 1 - where[0], part, parts, (wq, wk, wv)
        ).astype(BF)


def project_theirs(member, parts, mine, came, gain, weights):
    rows, columns = 2 * (mine.shape[0] - 16), mine.shape[1]
    lanes = sum(w.shape[1] for w in weights) // (2 * parts)
    return pl.pallas_call(
        functools.partial(project_theirs_kernel, parts),
        in_specs=[pl.BlockSpec(memory_space=pltpu.SMEM)]
        + [pl.BlockSpec(memory_space=pltpu.VMEM)] * 6,
        out_shape=[jax.ShapeDtypeStruct((rows, lanes), BF)] * parts
        + [
            jax.ShapeDtypeStruct((rows, columns), BF),
            jax.ShapeDtypeStruct((rows, columns), BF),
            jax.ShapeDtypeStruct((rows, 1), F32),
        ],
        compiler_params=params(),
        cost_estimate=cost(4 * rows * columns * lanes * parts, 6),
    )(jnp.reshape(member, (1,)), mine, came, gain, *weights)


def project_own_kernel(parts, where, hidden_ref, wq, wk, wv, *refs):
    for part in range(parts):
        refs[part - parts][...] = heads_product(
            hidden_ref[...], where[0], part, parts, (wq, wk, wv)
        )


def project_own(member, parts, hidden, weights, deps):
    rows, columns = hidden.shape
    lanes = sum(w.shape[1] for w in weights) // (2 * parts)
    specs, deps = after(deps)
    return pl.pallas_call(
        functools.partial(project_own_kernel, parts),
        in_specs=[pl.BlockSpec(memory_space=pltpu.SMEM)]
        + [pl.BlockSpec(memory_space=pltpu.VMEM)] * 4
        + specs,
        out_shape=[jax.ShapeDtypeStruct((rows, lanes), F32)] * parts,
        compiler_params=params(),
        cost_estimate=cost(4 * rows * columns * lanes * parts, 6),
    )(jnp.reshape(member, (1,)), hidden, *weights, *deps)


def project_back_kernel(
    parts, where, x_ref, inv_ref, gain_ref, wq_ref, wk_ref, wv_ref, *refs
):
    grads = refs[: 2 * parts]
    scaled_ref, sums_ref, gain_grad_ref = refs[-3:]
    total = jnp.zeros(x_ref.shape, F32)
    for part in range(parts):
        for grad, member in ((grads[2 * part], where[0]), (grads[2 * part + 1], 1 - where[0])):
            start = 0
            for w in (wq_ref, wk_ref, wv_ref):
                size = w.shape[1] // (2 * parts)
                at = pl.ds(pl.multiple_of((member * parts + part) * size, LANES), size)
                total += nt(grad[:, start : start + size], w[:, at])
                start += size
    normed = x_ref[...].astype(F32) * inv_ref[...]
    scaled = total * gain_ref[...].astype(F32)
    scaled_ref[...] = scaled
    sums_ref[...] = jnp.sum(scaled * normed, axis=-1, keepdims=True)
    gain_grad_ref[...] = jnp.sum(total * normed, axis=0, keepdims=True)


def project_back(member, x, inv, gain, weights, grads, deps):
    rows, columns = x.shape
    parts = len(grads)
    flat = [a for pair in grads for a in pair]
    specs, deps = after(deps)
    whole = pl.BlockSpec(memory_space=pltpu.VMEM)
    return pl.pallas_call(
        functools.partial(project_back_kernel, parts),
        in_specs=[pl.BlockSpec(memory_space=pltpu.SMEM)] + [whole] * (6 + len(flat)) + specs,
        out_shape=[
            jax.ShapeDtypeStruct((rows, columns), F32),
            jax.ShapeDtypeStruct((rows, 1), F32),
            jax.ShapeDtypeStruct((1, columns), F32),
        ],
        compiler_params=params(),
        cost_estimate=cost(2 * rows * columns * sum(w.shape[1] for w in weights), 10),
    )(jnp.reshape(member, (1,)), x, inv, gain, *weights, *flat, *deps)


def weight_grads_kernel(where, *refs):
    hidden, out_ref = refs[:2], refs[-1]
    size = refs[2].shape[1]
    out_ref[:, 2 * size :] = refs[10][...]
    for core in range(2):

        @pl.when(where[1] == core)
        def _():
            for i, member in ((0, where[0]), (1, 1 - where[0])):
                total = sum(tn(hidden[t][...], refs[2 + 4 * t + 2 * core + i][...]) for t in range(2))
                at = pl.ds(pl.multiple_of(member * size, LANES), size)
                out_ref[:, at] = total.astype(BF)


def weight_grads(member, core, hidden, grads, beside, deps):
    columns = hidden[0].shape[1]
    flat = [a for tree in grads for pair in tree for a in pair]
    rows, lanes = flat[0].shape
    specs, deps = after(deps)
    return pl.pallas_call(
        weight_grads_kernel,
        in_specs=[pl.BlockSpec(memory_space=pltpu.SMEM)]
        + [pl.BlockSpec(memory_space=pltpu.VMEM)] * (3 + len(flat))
        + specs,
        out_shape=jax.ShapeDtypeStruct((columns, 2 * lanes + beside.shape[1]), BF),
        compiler_params=params(),
        cost_estimate=cost(8 * rows * columns * lanes, 8),
    )(jnp.stack([member, core]), *hidden, *flat, beside, *deps)


def middle_kernel(count, where, *refs):
    pieces, (w_ref, x_ref) = refs[:count], refs[count : count + 2]
    middle_ref, low_ref, squares_ref = refs[-3:]
    total = x_ref[...].astype(F32)
    for i, piece in enumerate(pieces):
        size = piece.shape[1]
        total += nn(piece[...], w_ref[pl.ds(pl.multiple_of(where[i], 64), size), :])
    squares = jnp.sum(total * total, axis=-1, keepdims=True)
    middle_ref[...] = total
    low_ref[: total.shape[0], :] = total.astype(BF)
    squares_ref[...] = squares
    if low_ref.shape[0] > total.shape[0]:
        put_column(low_ref, squares)


def middle_of(pieces, where, w_out, x, packed, deps=()):
    rows, columns = x.shape
    tile = rows if packed else 448
    more = 16 if packed else 0
    specs, deps = after(deps)

    def row(i, w):
        return (i, 0)

    if packed:
        vmem = pl.BlockSpec(memory_space=pltpu.VMEM)
        return pl.pallas_call(
            functools.partial(middle_kernel, len(pieces)),
            in_specs=[pl.BlockSpec(memory_space=pltpu.SMEM)]
            + [vmem] * (len(pieces) + 2)
            + specs,
            out_shape=[
                jax.ShapeDtypeStruct((rows, columns), F32),
                jax.ShapeDtypeStruct((rows + more, columns), BF),
                jax.ShapeDtypeStruct((rows, 1), F32),
            ],
            compiler_params=params(),
            cost_estimate=cost(2 * rows * columns * w_out.shape[0], 6),
        )(where, *pieces, w_out, x, *deps)
    return pl.pallas_call(
        functools.partial(middle_kernel, len(pieces)),
        grid_spec=pltpu.PrefetchScalarGridSpec(
            num_scalar_prefetch=1,
            grid=(rows // tile,),
            in_specs=[pl.BlockSpec((tile, p.shape[1]), row) for p in pieces]
            + [
                pl.BlockSpec(w_out.shape, lambda i, w: (0, 0)),
                pl.BlockSpec((tile, columns), row),
            ]
            + specs,
            out_specs=[
                pl.BlockSpec((tile, columns), row),
                pl.BlockSpec((tile + more, columns), row),
                pl.BlockSpec((tile, 1), row),
            ],
        ),
        out_shape=[
            jax.ShapeDtypeStruct((rows, columns), F32),
            jax.ShapeDtypeStruct((rows + more, columns), BF),
            jax.ShapeDtypeStruct((rows, 1), F32),
        ],
        compiler_params=params(),
        cost_estimate=cost(2 * rows * columns * w_out.shape[0], 6),
    )(where, *pieces, w_out, x, *deps)


def hidden_kernel(count, parts, width, where, *refs):
    gain_ref, router_ref = refs[:2]
    h_ref, gates_ref = refs[-2:]
    for tree in range(2):
        mine = refs[2 + tree * (count + parts + 1) :]
        pieces, squares, on = mine[:count], mine[count : count + parts], mine[count + parts][...]
        total = squares[0][...]
        for more in squares[1:]:
            total += more[...]
        inv = lax.rsqrt(total / width + EPS)
        for i, piece in enumerate(pieces):
            size = piece.shape[1]
            at = pl.ds(pl.multiple_of(where[i] * size, LANES), size)
            gain = gain_ref[:, at].astype(F32)
            h_ref[tree, :, at] = (piece[...].astype(F32) * inv * gain).astype(BF)
        logits = jnp.where(on > 0, nn(h_ref[tree], router_ref[...]), -1e30)
        peak = jnp.max(logits, axis=-1, keepdims=True)
        e = jnp.exp(logits - peak) * on
        gates_ref[tree] = e / jnp.sum(e, axis=-1, keepdims=True)


def hidden_of(trees, where, gain, router):
    pieces, squares, on = trees[0]
    rows = on.shape[0]
    width, experts = router.shape
    tile = 448

    def row(i, w):
        return (i, 0)

    def all_of(i, w):
        return (0, 0)

    def both(i, w):
        return (0, i, 0)

    specs = [pl.BlockSpec((tile, p.shape[1]), row) for p in (*pieces, *squares, on)]
    return pl.pallas_call(
        functools.partial(hidden_kernel, len(pieces), len(squares), width),
        grid_spec=pltpu.PrefetchScalarGridSpec(
            num_scalar_prefetch=1,
            grid=(rows // tile,),
            in_specs=[pl.BlockSpec((1, width), all_of), pl.BlockSpec((width, experts), all_of)]
            + specs
            + specs,
            out_specs=[
                pl.BlockSpec((2, tile, width), both),
                pl.BlockSpec((2, tile, experts), both),
            ],
        ),
        out_shape=[
            jax.ShapeDtypeStruct((2, rows, width), BF),
            jax.ShapeDtypeStruct((2, rows, experts), F32),
        ],
        compiler_params=params(),
        cost_estimate=cost(4 * rows * width * 256, 8, rows * 32),
    )(where, gain, router, *(a for p, q, o in trees for a in (*p, *q, o)))


PACKET_ROWS = 48


def hidden_packed_kernel(where, *refs):
    h_ref, gates_ref, slots_ref, inv_ref, logits_ref, on_ref = refs[-6:]
    count = refs[0].shape[0] // 2 - 8
    before = (
        lax.broadcasted_iota(jnp.int32, (count, count), 0)
        < lax.broadcasted_iota(jnp.int32, (count, count), 1)
    )
    before = jnp.where(before, 1.0, 0.0).astype(BF)
    member = (where[0], 1 - where[0])
    for tree in range(2):
        messages, packets = refs[4 * tree : 4 * tree + 2], refs[4 * tree + 2 : 4 * tree + 4]
        rows, columns = messages[0].shape[0] - 16, messages[0].shape[1]
        squares = get_column(messages[0]) + get_column(messages[1])
        inv = lax.rsqrt(squares / (2 * columns) + EPS)
        if tree == 0:
            inv_ref[...] = inv
        logits = 0.0
        for i in range(2):
            at = pl.ds(pl.multiple_of(member[i] * columns, LANES), columns)
            gain = packets[i][16:32, :].astype(F32)[:1]
            h = (messages[i][:rows, :].astype(F32) * inv * gain).astype(BF)
            h_ref[tree, :, at] = h
            logits = logits + nt(h, packets[i][:16, :])
            tokens = rows // 2
            on_ref[pl.ds(pl.multiple_of(member[i] * tokens, 16), tokens), :] = (
                packets[i][32:48, :tokens].astype(F32).T
            )
        on = on_ref[...]
        logits = jnp.where(on > 0, logits, -1e30)
        if tree == 0:
            logits_ref[...] = logits
        peak = jnp.max(logits, axis=-1, keepdims=True)
        e = jnp.exp(logits - peak) * on
        gates = (e / jnp.sum(e, axis=-1, keepdims=True)).T
        for i in range(2):
            at = gates[:, i * count : (i + 1) * count]
            gates_ref[2 * tree + i] = at
            routed = jnp.where(at > 0.0, 1.0, 0.0).astype(BF)
            slots_ref[2 * tree + i] = nn(routed, before).astype(jnp.int32)


def hidden_packed(member, trees, deps):
    rows, columns = trees[0][0].shape[0] - 16, trees[0][0].shape[1]
    specs, deps = after(deps)
    return pl.pallas_call(
        hidden_packed_kernel,
        in_specs=[pl.BlockSpec(memory_space=pltpu.SMEM)]
        + [pl.BlockSpec(memory_space=pltpu.VMEM)] * 8
        + specs,
        out_shape=[
            jax.ShapeDtypeStruct((2, rows, 2 * columns), BF),
            jax.ShapeDtypeStruct((4, 16, rows // 2), F32),
            jax.ShapeDtypeStruct((4, 16, rows // 2), jnp.int32),
            jax.ShapeDtypeStruct((rows, 1), F32),
            jax.ShapeDtypeStruct((rows, 16), F32),
        ],
        scratch_shapes=[pltpu.VMEM((rows, 16), F32)],
        compiler_params=params(),
        cost_estimate=cost(4 * rows * columns * 256, 8),
    )(jnp.reshape(member, (1,)), *(a for tree in trees for a in tree), *deps)


def expert_grads_kernel(
    chained, steps, where, h_ref, g_ref, on_ref, wg_ref, wu_ref, wd_ref, *refs
):
    mid_ref, gg_ref, own_ref = refs[-3:] if steps == 1 else refs[-4:-1]
    step = pl.program_id(0)
    h, g = h_ref[...], g_ref[...]
    lane = lax.broadcasted_iota(jnp.int32, (1, on_ref.shape[1]), 1) == where[1]
    on = jnp.sum(jnp.where(lane, on_ref[...], 0.0), axis=-1, keepdims=True)
    gate_pre = nn(h, wg_ref[0])
    up_pre = nn(h, wu_ref[0])
    grad_mid = nt(g, wd_ref[0])
    sig = 1.0 / (1.0 + jnp.exp(-gate_pre))
    silu = gate_pre * sig
    mid = silu * up_pre
    column = jnp.where(lane, jnp.sum(grad_mid * mid, axis=-1, keepdims=True), 0.0)
    gg_ref[...] = refs[0][...] + column if chained else column
    act = (on * mid).astype(BF)
    grad_mid = on * grad_mid
    ggp = (grad_mid * up_pre * (sig * (1.0 + gate_pre * (1.0 - sig)))).astype(BF)
    gup = (grad_mid * silu).astype(BF)
    mid_ref[0, 0] = act
    mid_ref[0, 1] = ggp
    mid_ref[0, 2] = gup
    if steps == 1:
        own_ref[0] = tn(h, ggp).astype(BF)
        own_ref[1] = tn(h, gup).astype(BF)
        own_ref[2] = tn(g, act).astype(BF)
        return
    acc = refs[-1]

    @pl.when(step == 0)
    def _():
        acc[...] = jnp.zeros_like(acc)

    acc[0] += tn(h, ggp)
    acc[1] += tn(h, gup)
    acc[2] += tn(g, act)

    @pl.when(step == steps - 1)
    def _():
        own_ref[...] = acc[...].astype(BF)


def expert_grads(
    j, per_core, which, column, h, g, on, w_gate, w_up, w_down, before, slot, slots, deps
):
    rows, width = h.shape
    hidden = w_gate.shape[2]
    experts = on.shape[1]
    tile = row_tile(rows)
    steps = rows // tile

    def row(i, w):
        return (i, 0)

    def weight(i, w):
        return (w[0], 0, 0)

    chained = before is not None
    more = [pl.BlockSpec((tile, experts), row), pl.BlockSpec(memory_space=pl.ANY)] * chained
    aliases = {8: 0} if chained else {}
    if slot:
        aliases[9] = 2
        deps = (before[2], *deps)
    specs, deps = after(deps)
    return pl.pallas_call(
        functools.partial(expert_grads_kernel, chained, steps),
        grid_spec=pltpu.PrefetchScalarGridSpec(
            num_scalar_prefetch=1,
            grid=(steps,),
            in_specs=[
                pl.BlockSpec((tile, width), row),
                pl.BlockSpec((tile, width), row),
                pl.BlockSpec((tile, experts), row),
                pl.BlockSpec((1, width, hidden), weight),
                pl.BlockSpec((1, width, hidden), weight),
                pl.BlockSpec((1, hidden, width), weight),
            ]
            + more
            + specs,
            out_specs=[
                pl.BlockSpec((1, 3, tile, hidden), lambda i, w: (j, 0, i, 0)),
                pl.BlockSpec((tile, experts), row),
                pl.BlockSpec((3, width, hidden), lambda i, w: (slot, 0, 0)),
            ],
            scratch_shapes=[pltpu.VMEM((3, width, hidden), F32)] * (steps > 1),
        ),
        out_shape=[
            jax.ShapeDtypeStruct((per_core, 3, rows, hidden), BF),
            jax.ShapeDtypeStruct((rows, experts), F32),
            jax.ShapeDtypeStruct((3 * slots, width, hidden), BF),
        ],
        input_output_aliases=aliases,
        compiler_params=params(),
        cost_estimate=cost(16 * rows * width * hidden, 20, rows * hidden),
    )(
        jnp.stack([which, column]).astype(jnp.int32),
        h, g, on, w_gate, w_up, w_down,
        *((before[1], before[0]) if chained else ()),
        *deps,
    )


def expert_hidden_kernel(given, split, where, gate_ref, up_ref, wg_ref, wu_ref, *refs):
    e, count = pl.program_id(1), pl.num_programs(1)
    acc = refs[-1]
    part = nt(gate_ref[0, 0], wg_ref[0]) + nt(up_ref[0, 0], wu_ref[0])

    @pl.when(e == 0)
    def _():
        acc[...] = part + refs[0][...].astype(F32) if given else part

    @pl.when(e > 0)
    def _():
        acc[...] += part

    @pl.when(e == count - 1)
    def _():
        if not split:
            refs[-2][...] = acc[...].astype(BF)
            return
        size = refs[-2].shape[1]
        for out, member in ((refs[-3], where[1]), (refs[-2], 1 - where[1])):
            at = pl.ds(pl.multiple_of(member * size, LANES), size)
            out[...] = acc[:, at].astype(BF)


def expert_hidden(first, member, mid, tree, w_gate, w_up, came, split, deps):
    count, _, rows, hidden = mid.shape
    width = w_gate.shape[1]
    rows //= 2
    tile = 448
    tiles = rows // tile

    def weight(i, e, f):
        return (f[0] + e, 0, 0)

    def row(i, e, f):
        return (i, 0)

    given = [came] if came is not None else []
    specs, deps = after(deps)
    outs = 2 if split else 1
    return pl.pallas_call(
        functools.partial(expert_hidden_kernel, bool(given), split),
        grid_spec=pltpu.PrefetchScalarGridSpec(
            num_scalar_prefetch=1,
            grid=(tiles, count),
            in_specs=[
                pl.BlockSpec((1, 1, tile, hidden), lambda i, e, f: (e, 1, tree * tiles + i, 0)),
                pl.BlockSpec((1, 1, tile, hidden), lambda i, e, f: (e, 2, tree * tiles + i, 0)),
                pl.BlockSpec((1, width, hidden), weight),
                pl.BlockSpec((1, width, hidden), weight),
            ]
            + [pl.BlockSpec((tile, width), row) for _ in given]
            + specs,
            out_specs=[pl.BlockSpec((tile, width // outs), row)] * outs,
            scratch_shapes=[pltpu.VMEM((tile, width), F32)],
        ),
        out_shape=[jax.ShapeDtypeStruct((rows, width // outs), BF)] * outs,
        compiler_params=params(),
        cost_estimate=cost(6 * count * rows * width * hidden, 20),
    )(jnp.stack([first, member]).astype(jnp.int32), mid, mid, w_gate, w_up, *given, *deps)


def expert_mix_kernel(first, mid_ref, wd_ref, *refs):
    e, count = pl.program_id(1), pl.num_programs(1)
    acc = refs[-1]
    part = nn(mid_ref[0, 0], wd_ref[0])

    @pl.when(e == 0)
    def _():
        acc[...] = part

    @pl.when(e > 0)
    def _():
        acc[...] += part

    @pl.when(e == count - 1)
    def _():
        refs[-2][...] = acc[...].astype(BF)


def expert_mix(first, mid, tree, w_down, deps):
    count, _, rows, hidden = mid.shape
    width = w_down.shape[2]
    rows //= 2
    tile = 448
    tiles = rows // tile
    specs, deps = after(deps)
    return pl.pallas_call(
        expert_mix_kernel,
        grid_spec=pltpu.PrefetchScalarGridSpec(
            num_scalar_prefetch=1,
            grid=(tiles, count),
            in_specs=[
                pl.BlockSpec((1, 1, tile, hidden), lambda i, e, f: (e, 0, tree * tiles + i, 0)),
                pl.BlockSpec((1, hidden, width), lambda i, e, f: (f[0] + e, 0, 0)),
            ]
            + specs,
            out_specs=pl.BlockSpec((tile, width), lambda i, e, f: (i, 0)),
            scratch_shapes=[pltpu.VMEM((tile, width), F32)],
        ),
        out_shape=jax.ShapeDtypeStruct((rows, width), BF),
        compiler_params=params(),
        cost_estimate=cost(3 * count * rows * width * hidden, 10),
    )(jnp.reshape(first, (1,)).astype(jnp.int32), mid, w_down, *deps)


def out_grads_kernel(parts, where, *refs):
    branch, out_ref = refs[4 * parts : 4 * parts + 2], refs[-1]
    for own in range(2):

        @pl.when(where[0] == own)
        def _():
            for part in range(parts):
                at = (1 - own) * parts + part
                total = sum(
                    tn(refs[2 * parts * t + at][...], branch[t][...]) for t in range(2)
                )
                size = total.shape[0]
                out_ref[part * size : (part + 1) * size, :] = total.astype(BF)


def out_grads(own, attended, branch, deps):
    parts = len(attended[0]) // 2
    size, columns = attended[0][0].shape[1], branch[0].shape[1]
    specs, deps = after(deps)
    return pl.pallas_call(
        functools.partial(out_grads_kernel, parts),
        in_specs=[pl.BlockSpec(memory_space=pltpu.SMEM)]
        + [pl.BlockSpec(memory_space=pltpu.VMEM)] * (4 * parts + 2)
        + specs,
        out_shape=jax.ShapeDtypeStruct((parts * size, columns), BF),
        compiler_params=params(),
        cost_estimate=cost(4 * branch[0].shape[0] * columns * size * parts, 8),
    )(jnp.reshape(own, (1,)).astype(jnp.int32), *attended[0], *attended[1], *branch, *deps)


def tie_kernel(*refs):
    pass


def tie(v, deps):
    if not deps:
        return v
    specs, deps = after((v, *deps))
    return pl.pallas_call(
        tie_kernel,
        in_specs=specs,
        out_specs=pl.BlockSpec(memory_space=pl.ANY),
        out_shape=jax.ShapeDtypeStruct(v.shape, v.dtype),
        input_output_aliases={0: 0},
        cost_estimate=cost(0, 0),
    )(*deps)


def branch_kernel(
    where, mine_ref, came_ref, sums_ref, gl_ref, logits_ref, router_ref, middle_ref, inv_ref,
    gain_ref, grad_ref, w_ref, gain_grad_ref, full_ref, low_ref, theirs_ref, own_ref,
):
    rows, columns = middle_ref.shape
    gl = gl_ref[...]
    total = mine_ref[...].astype(F32) + came_ref[:rows, :].astype(F32)
    total += nt(gl, router_ref[...])
    products = jnp.sum(gl.astype(F32) * logits_ref[...], axis=-1, keepdims=True)
    mean = (sums_ref[...] + get_column(came_ref) + products) / (2 * columns)
    inv = inv_ref[...]
    normed = middle_ref[...] * inv
    gain_grad_ref[...] = jnp.sum(total * normed, axis=0, keepdims=True)
    at = pl.ds(pl.multiple_of(where[0] * columns, LANES), columns)
    grad = grad_ref[:, at].astype(F32)
    grad += inv * (total * gain_ref[...].astype(F32) - normed * mean)
    full_ref[...] = grad
    low = grad.astype(BF)
    low_ref[...] = low
    for out, member in ((theirs_ref, 1 - where[0]), (own_ref, where[0])):
        size = out.shape[1]
        heads = pl.ds(pl.multiple_of(member * size, 16), size)
        out[...] = nt(low, w_ref[heads, :]).astype(out.dtype)


def branch_back(member, mine, came, sums, gl, logits, router, middle, inv, gain, grad, w_out, deps):
    rows, columns = middle.shape
    size = w_out.shape[0] // 2
    specs, deps = after(deps)
    inputs = (mine, came, sums, gl, logits, router, middle, inv, gain)

    def all_of(i):
        return (0, 0)

    outs = [
        jax.ShapeDtypeStruct((1, columns), F32),
        jax.ShapeDtypeStruct((rows, columns), F32),
        jax.ShapeDtypeStruct((rows, columns), BF),
        jax.ShapeDtypeStruct((rows, size), BF),
        jax.ShapeDtypeStruct((rows, size), F32),
    ]

    def kernel(where, *refs):
        branch_kernel(where, *refs[:11], *refs[-5:])

    return pl.pallas_call(
        kernel,
        grid=(1,),
        in_specs=[pl.BlockSpec(memory_space=pltpu.SMEM)]
        + [pl.BlockSpec(a.shape, all_of) for a in inputs]
        + [pl.BlockSpec((rows, grad.shape[1]), all_of), pl.BlockSpec(w_out.shape, all_of)]
        + specs,
        out_specs=[pl.BlockSpec(o.shape, all_of) for o in outs],
        out_shape=outs,
        compiler_params=params(),
        cost_estimate=cost(2 * rows * columns * w_out.shape[0], 10),
    )(jnp.reshape(member, (1,)), *inputs, grad, w_out, *deps)


SLOTS = 128


def picked(gates_ref, slots_ref, block, expert):
    gates = gates_ref[block, pl.ds(expert, 1), :]
    slots = slots_ref[block, pl.ds(expert, 1), :]
    slot = lax.broadcasted_iota(jnp.int32, (SLOTS, gates.shape[1]), 0)
    return (slot == slots) & (gates > 0.0), gates


def one_hot(hit):
    return jnp.where(hit, 1.0, 0.0).astype(BF)


def expert_pair_kernel(
    chained, where, h_ref, g_ref, gates_ref, slots_ref, wg_ref, wu_ref, wd_ref, *refs
):
    mid_ref, gg_ref, own_ref, he_ref, ge_ref = refs[-5:]
    step = pl.program_id(0)
    expert = where[1] + step

    @pl.when(step == 0)
    def _():
        gg_ref[...] = refs[0][...] if chained else jnp.zeros_like(gg_ref)

    count = gates_ref.shape[2]
    hits, scales = [], []
    for b in range(4):
        hit, gates = picked(gates_ref, slots_ref, b, expert)
        pick = one_hot(hit)
        to = slice(b * SLOTS, (b + 1) * SLOTS)
        at = slice(b * count, (b + 1) * count)
        he_ref[to, :] = nn(pick, h_ref[at, :]).astype(BF)
        ge_ref[to, :] = nn(pick, g_ref[at, :]).astype(BF)
        hits.append(hit)
        scales.append(jnp.sum(jnp.where(hit, gates, 0.0), axis=-1, keepdims=True))
    on = jnp.concatenate(scales, 0)
    h, g = he_ref[...], ge_ref[...]
    gate_pre = nn(h, wg_ref[0])
    up_pre = nn(h, wu_ref[0])
    grad_mid = nt(g, wd_ref[0])
    sig = 1.0 / (1.0 + jnp.exp(-gate_pre))
    silu = gate_pre * sig
    mid = silu * up_pre
    column = jnp.sum(grad_mid * mid, axis=-1, keepdims=True)
    for b in range(4):
        part = jnp.where(hits[b], column[b * SLOTS : (b + 1) * SLOTS], 0.0)
        gg_ref[b, pl.ds(expert, 1), :] = jnp.sum(part, axis=0, keepdims=True)
    act = (on * mid).astype(BF)
    grad_mid = on * grad_mid
    ggp = (grad_mid * up_pre * (sig * (1.0 + gate_pre * (1.0 - sig)))).astype(BF)
    gup = (grad_mid * silu).astype(BF)
    mid_ref[0, 0] = act
    mid_ref[0, 1] = ggp
    mid_ref[0, 2] = gup
    own_ref[0] = tn(h, ggp).astype(BF)
    own_ref[1] = tn(h, gup).astype(BF)
    own_ref[2] = tn(g, act).astype(BF)


def expert_pair(
    start, count, slot, per_core, first, column, h, g, gates, slots, w_gate, w_up, w_down, before, deps
):
    rows, width = h.shape
    hidden = w_gate.shape[2]

    def all_of(i, w):
        return (0, 0)

    def every(i, w):
        return (0, 0, 0)

    def weight(i, w):
        return (w[0] + i, 0, 0)

    chained = before is not None
    more = [pl.BlockSpec(gates.shape, every), pl.BlockSpec(memory_space=pl.ANY)] * chained
    aliases = {9: 0} if chained else {}
    if slot:
        aliases[10] = 2
        deps = (before[2], *deps)
    specs, deps = after(deps)
    return pl.pallas_call(
        functools.partial(expert_pair_kernel, chained),
        grid_spec=pltpu.PrefetchScalarGridSpec(
            num_scalar_prefetch=1,
            grid=(count,),
            in_specs=[
                pl.BlockSpec((rows, width), all_of),
                pl.BlockSpec((rows, width), all_of),
                pl.BlockSpec(gates.shape, every),
                pl.BlockSpec(gates.shape, every),
                pl.BlockSpec((1, width, hidden), weight),
                pl.BlockSpec((1, width, hidden), weight),
                pl.BlockSpec((1, hidden, width), weight),
            ]
            + more
            + specs,
            out_specs=[
                pl.BlockSpec((1, 3, 4 * SLOTS, hidden), lambda i, w: (start + i, 0, 0, 0)),
                pl.BlockSpec(gates.shape, every),
                pl.BlockSpec((3, width, hidden), lambda i, w: (slot + i, 0, 0)),
            ],
            scratch_shapes=[pltpu.VMEM((4 * SLOTS, width), BF)] * 2,
        ),
        out_shape=[
            jax.ShapeDtypeStruct((per_core, 3, 4 * SLOTS, hidden), BF),
            jax.ShapeDtypeStruct(gates.shape, F32),
            jax.ShapeDtypeStruct((6, width, hidden), BF),
        ],
        input_output_aliases=aliases,
        compiler_params=params(),
        cost_estimate=cost(12 * count * 4 * SLOTS * width * hidden, 12 * count, rows * hidden),
    )(
        jnp.stack([first, column]).astype(jnp.int32),
        h, g, gates, slots, w_gate, w_up, w_down,
        *((before[1], before[0]) if chained else ()),
        *deps,
    )


def add_picked(acc, tree, column, gates_ref, slots_ref, outs):
    step, steps = pl.program_id(0), pl.num_programs(0)
    count = gates_ref.shape[2]
    for b in range(2):
        pick = jnp.concatenate(
            [
                one_hot(picked(gates_ref, slots_ref, 2 * tree + b, column + 2 * step + i)[0])
                for i in range(2)
            ],
            0,
        )
        rows = jnp.concatenate([out[b * SLOTS : (b + 1) * SLOTS] for out in outs], 0)
        at = slice(b * count, (b + 1) * count)
        acc[at, :] += tn(pick, rows)


def pair_hidden_kernel(given, tree, where, gates_ref, slots_ref, gp_ref, up_ref, wg_ref, wu_ref, *refs):
    step, acc = pl.program_id(0), refs[-1]

    @pl.when(step == 0)
    def _():
        acc[...] = refs[0][...].astype(F32) if given else jnp.zeros_like(acc)

    outs = [
        (nt(gp_ref[i, 0], wg_ref[i]) + nt(up_ref[i, 0], wu_ref[i])).astype(BF) for i in range(2)
    ]
    add_picked(acc, tree, where[1], gates_ref, slots_ref, outs)

    @pl.when(step == pl.num_programs(0) - 1)
    def _():
        if not given:
            refs[-2][...] = acc[...].astype(BF)
            return
        mine, theirs, sums = refs[-4:-1]
        rows, size = mine.shape
        for out, member in ((mine, where[2]), (theirs, 1 - where[2])):
            at = pl.ds(pl.multiple_of(member * size, LANES), size)
            out[:rows, :] = acc[:, at].astype(BF)
        sums[...] = jnp.sum(acc[...] * refs[1][...].astype(F32), axis=-1, keepdims=True)
        put_column(theirs, sums[...])


def pair_hidden(first, column, member, tree, gates, slots, mid, w_gate, w_up, came, deps):
    count, _, rows, hidden = mid.shape
    width = w_gate.shape[1]
    tokens = 2 * gates.shape[2]
    given = came or ()

    def weight(i, w):
        return (w[0] + i, 0, 0)

    def every(i, w):
        return (0, 0, 0)

    def all_of(i, w):
        return (0, 0)

    specs, deps = after(deps)
    if given:
        half = width // 2
        outs = [((tokens, half), BF), ((tokens + 16, half), BF), ((tokens, 1), F32)]
    else:
        outs = [((tokens, width), BF)]
    return pl.pallas_call(
        functools.partial(pair_hidden_kernel, bool(given), tree),
        grid_spec=pltpu.PrefetchScalarGridSpec(
            num_scalar_prefetch=1,
            grid=(count // 2,),
            in_specs=[
                pl.BlockSpec(gates.shape, every),
                pl.BlockSpec(gates.shape, every),
                pl.BlockSpec((2, 1, rows // 2, hidden), lambda i, w: (i, 1, tree, 0)),
                pl.BlockSpec((2, 1, rows // 2, hidden), lambda i, w: (i, 2, tree, 0)),
                pl.BlockSpec((2, width, hidden), weight),
                pl.BlockSpec((2, width, hidden), weight),
            ]
            + [pl.BlockSpec((tokens, width), all_of) for _ in given]
            + specs,
            out_specs=[pl.BlockSpec(shape, all_of) for shape, _ in outs],
            scratch_shapes=[pltpu.VMEM((tokens, width), F32)],
        ),
        out_shape=[jax.ShapeDtypeStruct(*o) for o in outs],
        compiler_params=params(),
        cost_estimate=cost(6 * count * rows * width * hidden, 16),
    )(
        jnp.stack([first // 2, column, member]).astype(jnp.int32),
        gates, slots, mid, mid, w_gate, w_up, *given, *deps,
    )


def pair_mix_kernel(tree, where, gates_ref, slots_ref, act_ref, wd_ref, *refs):
    step, acc = pl.program_id(0), refs[-1]

    @pl.when(step == 0)
    def _():
        acc[...] = jnp.zeros_like(acc)

    outs = [nn(act_ref[i, 0], wd_ref[i]).astype(BF) for i in range(2)]
    add_picked(acc, tree, where[1], gates_ref, slots_ref, outs)

    @pl.when(step == pl.num_programs(0) - 1)
    def _():
        refs[-2][...] = acc[...].astype(BF)


def pair_mix(first, column, tree, gates, slots, mid, w_down, deps):
    count, _, rows, hidden = mid.shape
    width = w_down.shape[2]
    tokens = 2 * gates.shape[2]

    def every(i, w):
        return (0, 0, 0)

    specs, deps = after(deps)
    return pl.pallas_call(
        functools.partial(pair_mix_kernel, tree),
        grid_spec=pltpu.PrefetchScalarGridSpec(
            num_scalar_prefetch=1,
            grid=(count // 2,),
            in_specs=[
                pl.BlockSpec(gates.shape, every),
                pl.BlockSpec(gates.shape, every),
                pl.BlockSpec((2, 1, rows // 2, hidden), lambda i, w: (i, 0, tree, 0)),
                pl.BlockSpec((2, hidden, width), lambda i, w: (w[0] + i, 0, 0)),
            ]
            + specs,
            out_specs=pl.BlockSpec((tokens, width), lambda i, w: (0, 0)),
            scratch_shapes=[pltpu.VMEM((tokens, width), F32)],
        ),
        out_shape=jax.ShapeDtypeStruct((tokens, width), BF),
        compiler_params=params(),
        cost_estimate=cost(3 * count * rows * width * hidden, 10),
    )(jnp.stack([first // 2, column]).astype(jnp.int32), gates, slots, mid, w_down, *deps)


def finish_kernel(layout, chips, where, *refs):
    outs, (last, router, gains) = refs[2 * chips : -3], refs[-3:]
    rows, columns = last.shape[1], router.shape[1]

    @pl.when(pl.program_id(0) == 0)
    def _():
        total = sum(ref[rows:, : 2 * columns].astype(F32) for ref in refs[:chips])
        router[...] = total[:, :columns]
        gains[...] = total[0:2, columns:]

    for i in range(chips):

        @pl.when(pl.program_id(0) == i)
        def _():
            mine, other = refs[i], refs[chips + (chips - i) % chips]
            for g in range(2):
                for out, to, start, size in layout[g]:
                    at = slice(start, start + size)
                    v = jnp.where(where[0] == g, mine[:rows, at], other[:rows, at])
                    outs[out][:, to : to + size] = v.astype(F32)
            start = mine.shape[1] - last.shape[2]
            last[where[0]] = mine[:rows, start:].astype(F32)
            last[1 - where[0]] = other[:rows, start:].astype(F32)


def finish(core, ring, layout, widths, out_width):
    chips = len(ring.chunks)
    tile, columns = ring.chunks[0].shape
    whole = (tile, columns)
    tile -= 16
    rows = tile * chips

    def row(i, w):
        return (w[1 + i], 0)

    def all_of(i, w):
        return (0, 0)

    return pl.pallas_call(
        functools.partial(finish_kernel, layout, chips),
        grid_spec=pltpu.PrefetchScalarGridSpec(
            num_scalar_prefetch=1,
            grid=(chips,),
            in_specs=[pl.BlockSpec(whole, all_of)] * (2 * chips),
            out_specs=[pl.BlockSpec((tile, w), row) for w in widths]
            + [pl.BlockSpec((2, tile, out_width), lambda i, w: (0, w[1 + i], 0))]
            + [pl.BlockSpec((n, out_width), all_of) for n in (16, 2)],
        ),
        out_shape=[jax.ShapeDtypeStruct((rows, w), F32) for w in widths]
        + [jax.ShapeDtypeStruct((2, rows, out_width), F32)]
        + [jax.ShapeDtypeStruct((n, out_width), F32) for n in (16, 2)],
        compiler_params=params(),
        cost_estimate=cost(0, 20),
    )(jnp.stack([core, *ring.chips()]).astype(jnp.int32), *ring.chunks, *ring.other)


def finish_experts_kernel(per_core, half, where, *refs):
    mine, came, outs = refs[:per_core], refs[per_core : 2 * per_core], refs[2 * per_core :]
    rows = pl.ds(pl.multiple_of(where[0] * half, 16), half)
    for j in range(per_core):
        for source, at in ((mine, where[0] * per_core + j), ((came), (1 - where[0]) * per_core + j)):
            v = source[j][:, rows, :].astype(F32)
            outs[0][at] = v[0]
            outs[1][at] = v[1]
            outs[2][at] = v[2]


def finish_experts(core, mine, came):
    per_core = len(mine)
    _, rows, hidden = mine[0].shape
    half = rows // 2
    whole = pl.BlockSpec(memory_space=pltpu.VMEM)
    return pl.pallas_call(
        functools.partial(finish_experts_kernel, per_core, half),
        in_specs=[pl.BlockSpec(memory_space=pltpu.SMEM)] + [whole] * (2 * per_core),
        out_shape=[
            jax.ShapeDtypeStruct((2 * per_core, half, hidden), F32),
            jax.ShapeDtypeStruct((2 * per_core, half, hidden), F32),
            jax.ShapeDtypeStruct((2 * per_core, half, hidden), F32),
        ],
        compiler_params=params(),
        cost_estimate=cost(0, 10),
    )(jnp.reshape(core, (1,)), *mine, *came)


def local(
    tokens,
    norm_gain,
    w_query,
    key_weight,
    value_weight,
    w_out,
    ffn_gain,
    w_router,
    w_gate,
    w_up,
    w_down,
    parents,
    routes,
    cotangent,
):
    me = Mesh()
    paired = me.groups == 2
    tok_rows, width = tokens.shape
    tree_len = tok_rows * me.groups
    seg_len = tree_len // 16
    columns = width // me.groups
    all_q, all_k = w_query.shape[1], key_weight.shape[1]
    q_width, k_width = all_q // me.groups, all_k // me.groups
    kv_heads = k_width // HEAD_DIM
    parts = kv_heads // 2 if kv_heads % 2 == 0 else 1
    q_part, k_part = q_width // parts, k_width // parts
    gq, gk = q_part // HEAD_DIM, k_part // HEAD_DIM
    q_room, k_room = pairs(gq) * LANES, pairs(gk) * LANES
    lanes = q_room + 2 * k_room
    experts = w_gate.shape[0] * me.groups
    per_core = w_gate.shape[0] // 2
    partner = 1 - me.member

    def heads_of(member):
        found = []
        for weight, size, room in (
            (w_query, q_width, q_room),
            (key_weight, k_width, k_room),
            (value_weight, k_width, k_room),
        ):
            block = lax.dynamic_slice_in_dim(weight, member * size, size, 1)
            found.append(jnp.pad(block, ((0, 0), (0, room - size))))
        return jnp.concatenate(found, 1)

    projections = (w_query, key_weight, value_weight)
    gain_row = norm_gain[None]
    own, came = [], []
    along = jnp.split(cotangent, 2, 0)
    early = ()
    grad_came = []
    if paired:
        hot = jnp.any(
            routes.T[:, None, :] == jnp.arange(experts, dtype=jnp.int32)[None, :, None], axis=0
        )
        packet = jnp.concatenate(
            [
                w_router.T,
                jnp.pad(ffn_gain[None], ((0, 15), (0, 0))),
                jnp.pad(hot.astype(BF), ((0, 0), (0, columns - tok_rows))),
            ],
            0,
        )
        x_theirs, x_mine = split(me.member, tokens)
        x_came = me.swap_shard(x_theirs)
        packets = [packet, me.swap_shard(packet)]
        early = (packets[1],)
        grad_came.append(me.swap_shard(tie(along[0], (x_theirs,))))
        *theirs, hidden_first, x_columns, inv_one = project_theirs(
            me.member, parts, x_mine, x_came, gain_row, projections
        )
        own = project_own(me.member, parts, hidden_first, projections, (theirs[-1],))
        came = [me.swap_shard(theirs[0]), me.swap_shard(tie(theirs[1], own[:1]))]
    else:
        every_head = jnp.concatenate([heads_of(j) for j in range(me.groups)], 1)
        own_rows = tokens.astype(F32)
        inv_rows = lax.rsqrt(jnp.mean(own_rows * own_rows, axis=-1, keepdims=True) + EPS)
        x_columns = me.exchange(tokens, 1, 0)
        inv_one = me.gather(inv_rows, 0)
        hidden_first = (x_columns.astype(F32) * inv_one * norm_gain.astype(F32)).astype(BF)
        own.append(me.scatter(nn(hidden_first, every_head), 1))
        came.append(jnp.zeros(own[-1].shape, BF))

    gain_two = ffn_gain.astype(F32)

    index = jnp.arange(tree_len, dtype=jnp.int32)
    _, depth = tree_layout(index, seg_len)
    cos, sin = angle_tables(depth)
    visible = tree_mask(index, index, parents[0], seg_len)
    bias = jnp.where(visible, 0.0, -1e30).astype(F32)

    attended, lse, query, key, value, att_came = [], [], [], [], [], []
    for part in range(parts):
        a, b, c, d, e = attend(own[part], came[part], cos, sin, bias, gq, gk, (*early, *grad_came[:1]))
        attended.append(a)
        lse.append(b)
        query.append(c)
        key.append(d)
        value.append(e)
        if paired:
            att_came.append(me.swap_shard(a))
    if paired:
        sent = tie(along[1], att_came)
        grad_came.append(me.swap_shard(sent))
        mine = [cotangent, me.swap_core(cotangent)]
        others = [*grad_came, *(me.swap_core(v) for v in grad_came)]
        grad_all = jnp.where(
            me.member == 0,
            jnp.concatenate([mine[0], *others[:2], mine[1], *others[2:]], 0),
            jnp.concatenate([*others[:2], mine[0], *others[2:], mine[1]], 0),
        )
        starts = [
            member * q_width + part * q_part
            for member in (me.member, partner)
            for part in range(parts)
        ]
        middle, middle_low, squares = middle_of(
            attended + att_came, jnp.stack(starts).astype(jnp.int32), w_out, x_columns, True, (sent,)
        )
        attended_full = me.in_order(
            me.member, jnp.concatenate(attended, 1), jnp.concatenate(att_came, 1), 1
        )
        messages = [middle_low, me.swap_shard(middle_low)]
        hidden_all, gates_all, slots_all, inv_two, logits = hidden_packed(
            me.member,
            [
                (*messages, *packets),
                (*(me.swap_core(v) for v in messages), *(me.swap_core(v) for v in packets)),
            ],
            (),
        )
    else:
        grad_tree = me.gather(cotangent, 0)
        grad_all = jnp.concatenate([grad_tree, me.swap_core(grad_tree)], 0)
        attended_full = me.gather(attended[0][:, :q_width], 1)
        where = jnp.zeros((1,), jnp.int32)
        middle, middle_low, squares = middle_of([attended_full], where, w_out, x_columns, False)
        route_hot = jnp.any(
            routes[:, :, None] == jnp.arange(experts, dtype=jnp.int32)[None, None, :], axis=1
        ).astype(F32)
        routed = me.gather(route_hot, 0)
        middle_low, squares = me.gather(middle_low, 1), me.total(squares)
        hidden_all, gates_all = hidden_of(
            [
                ([middle_low], [squares], routed),
                (
                    [me.swap_core(middle_low)],
                    [me.swap_core(squares)],
                    me.swap_core(routed),
                ),
            ],
            where,
            me.gather(ffn_gain, 0)[None],
            me.gather(w_router, 0),
        )
        inv_two = lax.rsqrt(squares / width + EPS)
    grad_tree = grad_all[:tree_len]
    hidden_all = hidden_all.reshape(2 * tree_len, width)
    normed_two = middle * inv_two
    hidden_own = (normed_two * gain_two).astype(BF)

    first = me.core * per_core
    chunk = width // me.chips
    def gates_grad(gates, grad, axis):
        return (gates * (grad - jnp.sum(gates * grad, axis=axis, keepdims=True))).astype(BF)

    def output_of(mixed_own, mixed_other):
        mixed = mixed_own.astype(F32) + me.swap_core(mixed_other).astype(F32)
        placed = lax.dynamic_update_slice_in_dim(
            jnp.zeros((tree_len, width), F32), middle, me.member * columns, 1
        )
        return mixed + placed

    def input_of(grad_middle, scaled, row_sums):
        normed = x_columns.astype(F32) * inv_one
        grad = grad_middle + inv_one * (scaled - normed * (row_sums / width))
        return me.exchange(grad.astype(BF), 0, 1)

    flipped = bias.T
    if not paired:
        gates = gates_all[0]
        gates_all = gates_all.reshape(2 * tree_len, experts)
        before, rings = None, []
        for j in range(per_core):
            before = expert_grads(
                j, per_core, first + j, me.member * (2 * per_core) + first + j,
                hidden_all, grad_all, gates_all, w_gate, w_up, w_down, before, 0, 1, (),
            )
            mid, own_columns, grads = before
            ring = Scatter(me, lambda chip: lax.dynamic_slice_in_dim(grads, chip * chunk, chunk, 1))
            for _ in range(me.chips - 1):
                ring.start()
                ring.finish()
            rings.append(ring.held)
        grad_gates = me.total(own_columns[:tree_len] + me.swap_core(own_columns[tree_len:]))
        grad_logits = gates_grad(gates, grad_gates, -1)
        (grad_other,) = expert_hidden(first, me.member, mid, 1, w_gate, w_up, None, False, ())
        (grad_own,) = expert_hidden(
            first, me.member, mid, 0, w_gate, w_up, me.swap_core(grad_other), False, ()
        )
        mixed_other = expert_mix(first, mid, 1, w_down, ())
        mixed_own = expert_mix(first, mid, 0, w_down, ())
        result = me.scatter(output_of(mixed_own, mixed_other), 0).astype(BF)
        grad_hidden_two = nt(grad_logits, w_router) + me.scatter(grad_own, 1)
        grad_gain_two = jnp.sum(grad_hidden_two * normed_two, axis=0)[None]
        scaled = grad_hidden_two * gain_two
        mean = me.total(jnp.sum(scaled * normed_two, axis=-1, keepdims=True)) / width
        grad_columns = me.part(grad_tree, 1, me.member).astype(F32)
        grad_middle = grad_columns + inv_two * (scaled - normed_two * mean)
        grad_branch = grad_middle.astype(BF)
        own = me.scatter(nt(grad_branch, w_out), 1)
        own = jnp.pad(own, ((0, 0), (0, q_room - q_width)))
        grad_heads = attend_back(
            own, jnp.zeros(own.shape, BF), query[0], key[0], value[0], lse[0],
            cos, sin, flipped, gq, gk, 0, (),
        )
        grad_out = me.all_reduce(tn(attended_full, grad_branch))
        grad_full = me.gather(grad_heads, 1)
        every = me.all_reduce(tn(hidden_first, grad_full))
        every = every.reshape(columns, me.groups, lanes)
        grad_query, grad_key, grad_value = (
            every[:, :, start : start + size].reshape(columns, me.groups * size)
            for start, size in ((0, q_width), (q_room, k_width), (q_room + k_room, k_width))
        )
        grad_hidden_one = nt(grad_full, every_head)
        normed_one = x_columns.astype(F32) * inv_one
        grad_gain_one = jnp.sum(grad_hidden_one * normed_one, axis=0)[None]
        scaled = grad_hidden_one * norm_gain.astype(F32)
        row_sums = jnp.sum(scaled * normed_one, axis=-1, keepdims=True)
        input_grad = input_of(grad_middle, scaled, me.total(row_sums))
        grad_router = tn(hidden_own, grad_logits)
        small = me.butterfly(jnp.concatenate([grad_gain_one, grad_gain_two, grad_router.T], 0))
        small = (small[0], small[1], small[2:].T)
        sums = rings
        grad_gate, grad_up, grad_down = finish_experts(
            me.core, sums, [me.swap_core(v) for v in sums]
        )
    else:

        column = me.member * (2 * per_core) + first

        def experts_of(start, count, slot, before, deps):
            return expert_pair(
                start, count, slot, per_core, first + start, column + start,
                hidden_all, grad_all, gates_all, slots_all, w_gate, w_up, w_down, before, deps,
            )

        def hidden_grad(tree, came, deps):
            return pair_hidden(
                first, column, me.member, tree, gates_all, slots_all, mid, w_gate, w_up, came, deps
            )

        def mix_of(tree, deps):
            return pair_mix(first, column, tree, gates_all, slots_all, mid, w_down, deps)

        def ring_of(grads):
            return Scatter(me, lambda chip: lax.dynamic_slice_in_dim(grads, chip * chunk, chunk, 1))

        one = experts_of(0, 2, 0, None, ())
        ring_a = ring_of(one[2])
        sent = ring_a.start()
        mid, own_rows, grads = experts_of(2, 2, 0, one, ())
        sent_a = ring_a.hop(own_rows)
        ring_b = ring_of(grads)
        sent_b = ring_b.start()
        grad_gates = me.total(own_rows[:2] + me.swap_core(own_rows[2:]))
        grad_logits = gates_grad(gates_all[:2], grad_gates, 1)
        grad_logits = grad_logits.transpose(0, 2, 1).reshape(tree_len, experts)
        (grad_other,) = hidden_grad(1, None, (sent_a, sent_b))
        other_came = me.swap_core(grad_other)
        sent = ring_a.hop(grad_other)
        grad_mine, grad_theirs, row_sums = hidden_grad(0, (other_came, hidden_all), (sent,))
        hidden_came = me.swap_shard(grad_theirs)
        sent = ring_b.hop(grad_mine)
        mixed_other = mix_of(1, (sent,))
        sent = ring_a.hop(mixed_other)
        mixed_own = mix_of(0, (sent, grad_logits))
        sent = ring_b.hop(mixed_own)
        grad_gain_two, grad_middle, grad_branch, theirs, own = branch_back(
            me.member, grad_mine, hidden_came, row_sums, grad_logits, logits, w_router,
            middle, inv_two, ffn_gain[None], grad_all, w_out, (sent,),
        )
        came = me.swap_shard(theirs)
        sent = ring_a.hop(grad_branch)
        grad_out = out_grads(
            me.core == me.member,
            [attended + att_came, [me.swap_core(v) for v in attended + att_came]],
            [grad_branch, me.swap_core(grad_branch)],
            (sent,),
        )
        sent = ring_b.hop(grad_out)
        heads_a = attend_back(
            own, came, query[0], key[0], value[0], lse[0], cos, sin, flipped, gq, gk, 0,
            (sent,),
        )
        back_a = me.swap_shard(heads_a)
        sent = ring_a.hop(heads_a)
        heads_b = attend_back(
            own, came, query[1], key[1], value[1], lse[1], cos, sin, flipped, gq, gk, q_part,
            (sent,),
        )
        back_a = tie(back_a, (heads_b,))
        back_b = me.swap_shard(heads_b)
        sent = (ring_b.hop(heads_b), ring_a.hop(heads_b))
        summed = output_of(tie(mixed_own, (back_a, *sent)), mixed_other).astype(BF)
        to_send = me.part(summed, 0, partner)
        grad_pairs = [(heads_a, back_a), (heads_b, back_b)]
        grads_mine = weight_grads(
            me.member,
            me.core,
            (hidden_first, me.swap_core(hidden_first)),
            (grad_pairs, [tuple(me.swap_core(v) for v in pair) for pair in grad_pairs]),
            grad_out,
            (*sent, to_send),
        )
        head_chunk = grads_mine.shape[0] // me.chips
        ring_w = Scatter(
            me, lambda chip: lax.dynamic_slice_in_dim(grads_mine, chip * head_chunk, head_chunk, 0)
        )
        sent = ring_b.hop(ring_w.start())
        grad_router = tn(hidden_own, grad_logits)
        scaled, row_sums, grad_gain_one = project_back(
            me.member, x_columns, inv_one, gain_row, projections, grad_pairs, (sent,)
        )
        beside = {1: (scaled,)}

        def later(hop, v):
            beside[hop] = (*beside.get(hop, ()), v)

        hops, experts_done, waiting = me.chips - 1, None, None
        for hop in range(1, 2 * hops):
            w = ring_w.finish() if hop <= hops else sent
            if hop > hops:
                ring_w.finish()
            if hop == hops:
                small = jnp.concatenate(
                    [
                        grad_router.T,
                        jnp.pad(jnp.concatenate([grad_gain_one, grad_gain_two]), ((0, 14), (0, 0))),
                    ],
                    1,
                )
                small = (small + me.swap_core(small)).astype(BF)
                small = jnp.pad(small, ((0, 0), (0, ring_w.held.shape[1] - small.shape[1])))
                ring_w = Gather(me, jnp.concatenate([ring_w.held, small], 0))
            if hop == 1:
                row_total = me.total(row_sums)
                later(2, row_total)
            if hop == 2:
                input_grad = input_of(grad_middle, scaled, row_total)
                later(5, input_grad)
            if hop == 3:
                result = me.swap_shard(tie(to_send, (w,))).astype(F32)
                result = (result + me.part(summed, 0, me.member).astype(F32)).astype(BF)
                later(2 * hops - 2, result)
            deps = beside.get(hop, ())
            ring = {1: ring_a, 2: ring_b, 4: ring_b}.get(hop)
            if ring is not None and ring.hops < hops:
                deps = (*deps, ring.finish(w))
                if ring.hops < hops:
                    waiting = ring
                elif ring_a.hops == ring_b.hops:
                    sums = [h for r in (ring_a, ring_b) for h in jnp.split(r.held, 2, 0)]
                    experts_done = finish_experts(me.core, sums, [me.swap_core(v) for v in sums])
                    later(2 * hops - 3, experts_done[0])
            sent = ring_w.start(*deps)
            if waiting is not None:
                waiting.start(sent)
                waiting = None
        ring_w.finish()
        grad_gate, grad_up, grad_down = experts_done
        layout = [
            [
                (out, j * step + part * size, j * lanes + start, size)
                for j in range(2)
                for out, step, start, size in (
                    (0, q_width, 0, q_part),
                    (1, k_width, q_room, k_part),
                    (2, k_width, q_room + k_room, k_part),
                )
            ]
            for part in range(parts)
        ]
        grad_query, grad_key, grad_value, grad_out, *small = finish(
            me.core, ring_w, layout, (all_q, all_k, all_k), columns
        )
        grad_out = grad_out.reshape(-1, columns)
        small = (small[1][0], small[1][1], small[0].T)

    return (
        result,
        input_grad,
        small[0],
        grad_query,
        grad_key,
        grad_value,
        grad_out,
        small[1],
        small[2],
        grad_gate,
        grad_up,
        grad_down.transpose(0, 2, 1),
    )


def solution(mesh):
    return jax.shard_map(
        local,
        mesh=mesh,
        in_specs=(
            P(("rep", "shard"), None),
            P("shard"),
            P("shard", None),
            P("shard", None),
            P("shard", None),
            P(None, "shard"),
            P("shard"),
            P("shard", None),
            P("shard", None, None),
            P("shard", None, None),
            P("shard", None, None),
            P("rep", None),
            P(("rep", "shard"), None),
            P(("rep", "shard"), None),
        ),
        out_specs=(
            P(("rep", "shard"), None),
            P(("rep", "shard"), None),
            P("shard"),
            P("shard", None),
            P("shard", None),
            P("shard", None),
            P(None, "shard"),
            P("shard"),
            P("shard", None),
            P("shard", "rep", None),
            P("shard", "rep", None),
            P("shard", None, "rep"),
        ),
        check_vma=False,
    )
```
